32 devices in a mesh: groups: 2 (over y), seq: 4 (over z), head: 2 (over x), inner: 2 (over core).
Axes of the slice: x: 2, y: 2, z: 4, core: 2. Of those that a mesh axis runs over, the one named last changes fastest.
Arguments:
- query_rows: bfloat16 [16, 640, 1024], P(('groups', 'seq'), 'inner', 'head'), parts along dimension 0, may hold values from -100 to 100
- key_rows: bfloat16 [16, 640, 128], P(('groups', 'seq')), parts along dimension 0, may hold values from -5 to 5
- value_rows: bfloat16 [16, 640, 128], P(('groups', 'seq')), parts along dimension 0, may hold values from -6 to 6
- slot_block: int32 [8], replicated, may hold values from 0 to 7, as said below
Outputs:
- attended: bfloat16 [16, 640, 1024], P(('groups', 'seq'), 'inner', 'head'), parts along dimension 0
- log_total: float32 [16, 8, 640], P(('groups', 'seq'), 'head', 'inner'), parts along dimension 0
The draws below stay inside these ranges and needn't reach their ends.
There are 2 independent parts, one for each index of `groups`. The reference program is written for one: setup_inputs(seed, part) draws one part's arguments, and reference() takes and returns one part's arrays. A program takes and returns all parts, laid end to end along the dimension named above; an argument that names none is the same for every part. Nothing has to cross between parts.
Inputs may be any that keep to these rules, and one draw needn't show every extreme that they name: slot_block is a permutation of 0 .. 7; slots 2 s and 2 s + 1 hold blocks b and 7 - b.
All inputs are finite; a program needn't handle non-finite values.
Results may differ from the reference program's by a relative error of at most 0.017.
Values may be sent and summed in bfloat16 or wider, within the bound.
No kernel may reach another device: no remote copies, remote signals or barrier semaphores. Data moves between devices by JAX's collectives and lax.ppermute only.
A program may use at most 64 MiB of HBM per device.

```python
import jax
import jax.numpy as jnp
from jax import lax

HD = 128
GROUP_HEADS = 8
BLK = 640
NBLOCKS = 8


def shared_keys(key):
    base = jnp.clip(jax.random.normal(key, (NBLOCKS, BLK, HD), jnp.float32), -5.0, 5.0)
    row_ids = jnp.arange(BLK)
    chosen = row_ids % 37 == 5
    before = jnp.roll(chosen, -1)
    blended = jnp.where(before[None, :, None], base, base)
    return blended


def draw_key_rows(key, part):
    blended = shared_keys(key)
    return blended.astype(jnp.bfloat16)


def draw_query_rows(key, part):
    key = jax.random.fold_in(key, 11)
    fresh = jnp.clip(jax.random.normal(key, (NBLOCKS, BLK, GROUP_HEADS, HD), jnp.float32), -5.0, 5.0)
    return fresh.reshape(NBLOCKS, BLK, GROUP_HEADS * HD).astype(jnp.bfloat16)


def draw_slot_block(key, part):
    key = jax.random.fold_in(key, 23)
    order = jax.random.permutation(key, NBLOCKS // 2).astype(jnp.int32)
    paired = jnp.stack([order, NBLOCKS - 1 - order], axis=1).reshape(NBLOCKS)
    return paired.astype(jnp.int32)


def steps_of(own_key, shape, shards, smallest, top_value):
    factor_of, own = 1.0, jax.random.fold_in(own_key, 6)
    for dim, shards_of in shards:
        heights = jnp.exp(jax.random.uniform(jax.random.fold_in(own, dim), (shards_of,), jnp.float32, smallest / len(shards), top_value / len(shards)))
        factor_of = factor_of * jnp.repeat(heights, shape[dim] // shards_of).reshape([-1 if axis == dim else 1 for axis in range(len(shape))])
    return factor_of


def scatter_about(stream_key, shape, deviation, most, cuts=(), held_as=jnp.bfloat16):
    entries = deviation * jax.random.normal(stream_key, shape, jnp.float32)
    if cuts:
        entries = entries * steps_of(stream_key, shape, cuts, -0.22, 0.18)
    return jnp.clip(entries, -most, most).astype(held_as)


def setup_inputs(seed: int = 0, part: int = 0) -> dict:
    seeds = jax.random.split(jax.random.key(seed), 5)
    part_splits = jax.random.split(jax.random.fold_in(seeds[4], part), 5)
    query_rows = draw_query_rows(jax.random.fold_in(jax.random.fold_in(seeds[4], part), 71), part)
    key_rows = draw_key_rows(jax.random.fold_in(jax.random.fold_in(seeds[4], part), 71), part)
    value_rows = scatter_about(part_splits[2], (NBLOCKS, BLK, HD), 1.0, 6.0, ((0, 4),))
    slot_block = draw_slot_block(jax.random.fold_in(seeds[4], 71), part)
    return {"query_rows": query_rows, "key_rows": key_rows, "value_rows": value_rows, "slot_block": slot_block}


def reference(query_rows, key_rows, value_rows, slot_block):
    positions = (slot_block[:, None] * BLK + jnp.arange(BLK, dtype=jnp.int32)[None, :]).astype(jnp.int32)
    key_pos = positions.reshape(-1)
    flat_keys = key_rows.reshape(-1, HD).astype(jnp.float32)
    flat_values = value_rows.reshape(-1, HD).astype(jnp.float32)
    score_scale = 1.0 / (HD ** 0.5)

    def per_slot(operands):
        slot_queries, query_pos = operands
        queries = slot_queries.reshape(BLK, GROUP_HEADS, HD).astype(jnp.float32)
        scores = jnp.einsum("rhd,cd->hrc", queries, flat_keys) * score_scale
        allowed = key_pos[None, None, :] <= query_pos[None, :, None]
        scores = jnp.where(allowed, scores, -jnp.inf)
        highest = jnp.max(scores, axis=-1)
        log_total = highest + jnp.log(jnp.sum(jnp.exp(scores - highest[..., None]), axis=-1))
        weights = jnp.where(allowed, jnp.exp(scores - log_total[..., None]), 0.0).astype(jnp.bfloat16)
        outputs = jnp.einsum("hrc,cd->rhd", weights.astype(jnp.float32), flat_values)
        return outputs.reshape(BLK, GROUP_HEADS * HD).astype(jnp.bfloat16), log_total

    attended, log_total = lax.map(per_slot, (query_rows, positions))
    return attended, log_total
```

```python
import functools
import math

import jax
import jax.numpy as jnp
from jax import lax
from jax.experimental import pallas as pl
from jax.experimental.pallas import tpu as pltpu
from jax.sharding import PartitionSpec as P

NEG = -1e30
SUM_LIMIT = 1e36


def score_dot(q, k):
    return lax.dot_general(q, k, (((1,), (1,)), ((), ())), preferred_element_type=jnp.float32)


def widen(x, width):
    return jnp.concatenate([x] * (width // x.shape[1]), axis=1)


def with_ones(v):
    return jnp.concatenate([v, jnp.ones_like(v)], axis=1)


def local_kernel(coef, sb, q_ref, k_ref, v_ref, acc_ref, top_ref):
    rows, block_len = q_ref.shape[1], k_ref.shape[1]
    me = lax.axis_index("seq")
    inner = lax.axis_index("inner")
    b0, b1 = sb[2 * me], sb[2 * me + 1]
    hi = jnp.where(b1 > b0, 1, 0)
    lo = 1 - hi
    row = lax.broadcasted_iota(jnp.int32, (rows, block_len), 0) + inner * rows
    col = lax.broadcasted_iota(jnp.int32, (rows, block_len), 1)
    causal = col <= row

    def lanes_max(s):
        top = jnp.max(s, axis=1, keepdims=True)
        return jnp.broadcast_to(top, (rows, 128))

    s_diag = jnp.where(causal, score_dot(q_ref[hi], k_ref[hi]) * coef, NEG)
    s_past = score_dot(q_ref[hi], k_ref[lo]) * coef
    s_low = jnp.where(causal, score_dot(q_ref[lo], k_ref[lo]) * coef, NEG)
    top = lanes_max(jnp.maximum(s_diag, s_past))
    wide = widen(top, block_len)
    p_diag = jnp.exp2(s_diag - wide).astype(jnp.bfloat16)
    p_past = jnp.exp2(s_past - wide).astype(jnp.bfloat16)
    v_hi, v_lo = with_ones(v_ref[hi]), with_ones(v_ref[lo])
    acc = jnp.dot(p_diag, v_hi, preferred_element_type=jnp.float32)
    acc += jnp.dot(p_past, v_lo, preferred_element_type=jnp.float32)
    top_ref[hi, 0] = top
    acc_ref[hi, 0] = acc
    top = lanes_max(s_low)
    p_low = jnp.exp2(s_low - widen(top, block_len)).astype(jnp.bfloat16)
    top_ref[lo, 0] = top
    acc_ref[lo, 0] = jnp.dot(p_low, v_lo, preferred_element_type=jnp.float32)


def remote_kernel(coef, count, sb, q_ref, acc_in, top_ref, kv_hbm, out_ref, lse_ref, k_buf, v_buf, acc, run_top, sems):
    rows, block_len = q_ref.shape[1], k_buf.shape[2]
    head = pl.program_id(0)
    me = lax.axis_index("seq")
    inner = lax.axis_index("inner")
    b0, b1 = sb[2 * me], sb[2 * me + 1]
    hi = jnp.where(b1 > b0, 1, 0)
    lo = 1 - hi

    def copies(step):
        source = lax.rem(me + step, count)
        found = []
        for slot in range(2):
            piece = source * 4 + slot * 2
            found.append(
                pltpu.make_async_copy(kv_hbm.at[piece], k_buf.at[step, slot], sems.at[step, slot, 0])
            )
            found.append(
                pltpu.make_async_copy(
                    kv_hbm.at[piece + 1], v_buf.at[step, slot, :, pl.ds(0, 128)], sems.at[step, slot, 1]
                )
            )
        return found

    order = list(range(1, count)) + [0]

    @pl.when(head == 0)
    def _():
        for step in order:
            for copy in copies(step):
                copy.start()
        v_buf[:, :, :, 128:] = jnp.ones((count, 2, block_len, 128), jnp.bfloat16)
        for step in order:
            for copy in copies(step):
                copy.wait()

    acc[...] = acc_in[:, 0]

    def weights(slot, keys):
        s = score_dot(q_ref[slot], keys) * coef
        return jnp.exp2(s - widen(top_ref[slot, 0], block_len)).astype(jnp.bfloat16)

    total = None
    for step in range(1, count):
        source = lax.rem(me + step, count)
        c0, c1 = sb[2 * source], sb[2 * source + 1]
        other_hi = jnp.where(c1 > c0, 1, 0)
        other_lo = 1 - other_hi
        above = jnp.maximum(b0, b1) > jnp.maximum(c0, c1)
        q_slot = jnp.where(above, hi, lo)
        k_slot = jnp.where(above, other_hi, other_lo)
        part = jnp.dot(
            weights(hi, k_buf[step, other_lo]), v_buf[step, other_lo], preferred_element_type=jnp.float32
        )
        total = part if total is None else total + part
        acc[q_slot] += jnp.dot(
            weights(q_slot, k_buf[step, k_slot]), v_buf[step, k_slot], preferred_element_type=jnp.float32
        )
    acc[hi] += total

    largest = jnp.max(acc[:, :, 128:])

    @pl.when(largest < SUM_LIMIT)
    def _():
        run_top[...] = top_ref[:, 0]

    @pl.when(jnp.logical_not(largest < SUM_LIMIT))
    def _():
        run_top[...] = jnp.full_like(run_top, NEG)
        acc[...] = jnp.zeros_like(acc)

        @pl.loop(0, count * 4)
        def _(i):
            step, slot, q_slot = i // 4, lax.rem(i, 4) // 2, lax.rem(i, 2)
            source = lax.rem(me + step, count)
            shift = (sb[2 * me + q_slot] - sb[2 * source + slot]) * block_len + inner * rows

            @pl.when(shift + rows > 0)
            def _():
                s = score_dot(q_ref[q_slot], k_buf[step, slot]) * coef
                row = lax.broadcasted_iota(jnp.int32, s.shape, 0) + shift
                allowed = lax.broadcasted_iota(jnp.int32, s.shape, 1) <= row
                s = jnp.where(allowed, s, NEG)
                before = run_top[q_slot]
                top = jnp.maximum(before, jnp.broadcast_to(jnp.max(s, axis=1, keepdims=True), before.shape))
                p = jnp.where(allowed, jnp.exp2(s - widen(top, block_len)), 0.0).astype(jnp.bfloat16)
                run_top[q_slot] = top
                acc[q_slot] = acc[q_slot] * widen(jnp.exp2(before - top), 256) + jnp.dot(
                    p, v_buf[step, slot], preferred_element_type=jnp.float32
                )

    for slot in range(2):
        sums = acc[slot, :, 128:]
        out_ref[slot] = (acc[slot, :, :128] / sums).astype(out_ref.dtype)
        log_total = run_top[slot] * math.log(2.0) + jnp.log(sums)
        lse_ref[slot, pl.ds(head, 1), :] = jnp.transpose(log_total)[:1]


def body(query_rows, key_rows, value_rows, slot_block):
    _, block_len, width = key_rows.shape
    _, rows, feats = query_rows.shape
    heads = feats // width
    count = lax.axis_size("seq")
    coef = math.log2(math.e) / math.sqrt(width)

    head_index, inner_index = lax.axis_index("head"), lax.axis_index("inner")
    with jax.named_scope("pieces"):
        kv = jnp.where(inner_index == 0, key_rows, value_rows)
        piece = jnp.where(head_index == 0, kv[0], kv[1])
    with jax.named_scope("gather_kv"):
        gathered = lax.all_gather(piece, ("seq", "head", "inner"), axis=0, tiled=False)

    q_spec = pl.BlockSpec((2, rows, width), lambda h, sb: (0, 0, h))
    kv_spec = pl.BlockSpec((2, block_len, width), lambda h, sb: (0, 0, 0))
    acc_spec = pl.BlockSpec((2, 1, rows, 2 * width), lambda h, sb: (0, h, 0, 0))
    top_spec = pl.BlockSpec((2, 1, rows, width), lambda h, sb: (0, h, 0, 0))
    unit = 2 * rows * heads * block_len * width * 2
    acc, top = pl.pallas_call(
        functools.partial(local_kernel, coef),
        grid_spec=pltpu.PrefetchScalarGridSpec(
            num_scalar_prefetch=1,
            grid=(heads,),
            in_specs=[q_spec, kv_spec, kv_spec],
            out_specs=[acc_spec, top_spec],
        ),
        out_shape=[
            jax.ShapeDtypeStruct((2, heads, rows, 2 * width), jnp.float32),
            jax.ShapeDtypeStruct((2, heads, rows, width), jnp.float32),
        ],
        cost_estimate=pl.CostEstimate(flops=3 * unit, bytes_accessed=6_000_000, transcendentals=0),
        compiler_params=pltpu.CompilerParams(vmem_limit_bytes=48 * 1024 * 1024),
        name="local_part",
    )(slot_block, query_rows, key_rows, value_rows)

    attended, log_total = pl.pallas_call(
        functools.partial(remote_kernel, coef, count),
        grid_spec=pltpu.PrefetchScalarGridSpec(
            num_scalar_prefetch=1,
            grid=(heads,),
            in_specs=[q_spec, acc_spec, top_spec, pl.BlockSpec(memory_space=pl.ANY)],
            out_specs=[q_spec, pl.BlockSpec((2, heads, rows), lambda h, sb: (0, 0, 0))],
            scratch_shapes=[
                pltpu.VMEM((count, 2, block_len, width), jnp.bfloat16),
                pltpu.VMEM((count, 2, block_len, 2 * width), jnp.bfloat16),
                pltpu.VMEM((2, rows, 2 * width), jnp.float32),
                pltpu.VMEM((2, rows, width), jnp.float32),
                pltpu.SemaphoreType.DMA((count, 2, 2)),
            ],
        ),
        out_shape=[
            jax.ShapeDtypeStruct(query_rows.shape, query_rows.dtype),
            jax.ShapeDtypeStruct((2, heads, rows), jnp.float32),
        ],
        cost_estimate=pl.CostEstimate(flops=2 * (count - 1) * unit, bytes_accessed=8_000_000, transcendentals=0),
        compiler_params=pltpu.CompilerParams(vmem_limit_bytes=48 * 1024 * 1024),
        name="remote_part",
    )(slot_block, query_rows, acc, top, gathered)
    return attended, log_total


def solution(mesh):
    placed = (
        P(("groups", "seq"), "inner", "head"),
        P(("groups", "seq"), None, None),
        P(("groups", "seq"), None, None),
        P(),
    )
    return jax.shard_map(
        body,
        mesh=mesh,
        in_specs=placed,
        out_specs=(P(("groups", "seq"), "inner", "head"), P(("groups", "seq"), "head", "inner")),
        check_vma=False,
    )
```

```python
import functools
import math

import jax
import jax.numpy as jnp
from jax import lax
from jax.experimental import pallas as pl
from jax.experimental.pallas import tpu as pltpu
from jax.sharding import PartitionSpec as P

NEG = -1e30
SUM_LIMIT = 1e36


def score_dot(q, k):
    return lax.dot_general(q, k, (((1,), (1,)), ((), ())), preferred_element_type=jnp.float32)


def value_dot(p, v):
    return jnp.dot(p, v, preferred_element_type=jnp.float32)


def widen(x, width):
    return jnp.concatenate([x] * (width // x.shape[1]), axis=1)


def with_ones(x):
    return jnp.concatenate([x, jnp.ones_like(x)], axis=1)


def partner(index, distance, count):
    if count & (count - 1) == 0:
        return index ^ distance
    return (index + distance) % count


def source_of(index, distance, count):
    if count & (count - 1) == 0:
        return index ^ distance
    return lax.rem(index - distance + count, count)


def high_slot(sb, seq_index):
    b0, b1 = sb[2 * seq_index], sb[2 * seq_index + 1]
    return jnp.where(b1 > b0, 1, 0), jnp.maximum(b0, b1)


def minus_columns(top):
    high = top.astype(jnp.bfloat16)
    rest = top - high.astype(jnp.float32)
    middle = rest.astype(jnp.bfloat16)
    low = (rest - middle.astype(jnp.float32)).astype(jnp.bfloat16)
    lane = lax.broadcasted_iota(jnp.int32, top.shape, 1)
    high, middle, low = (x.astype(jnp.float32) for x in (high, middle, low))
    picked = jnp.where(lane == 0, high, jnp.where(lane == 1, middle, jnp.where(lane == 2, low, 0.0)))
    return (-picked).astype(jnp.bfloat16)


def local_kernel(coef, sb, q_ref, k_ref, v_ref, qx_ref, acc_ref):
    rows, block_len, width = q_ref.shape[1], k_ref.shape[1], k_ref.shape[2]
    inner = lax.axis_index("inner")
    hi, _ = high_slot(sb, lax.axis_index("seq"))
    lo = 1 - hi
    row = lax.broadcasted_iota(jnp.int32, (rows, block_len), 0) + inner * rows
    col = lax.broadcasted_iota(jnp.int32, (rows, block_len), 1)
    causal = col <= row

    def lanes_max(s):
        return jnp.broadcast_to(jnp.max(s, axis=1, keepdims=True), (rows, width))

    def weights(s, wide):
        return jnp.exp2((s - wide) * coef).astype(jnp.bfloat16)

    q_hi, q_lo = q_ref[hi], q_ref[lo]
    s_diag = jnp.where(causal, score_dot(q_hi, k_ref[hi]), NEG)
    s_past = score_dot(q_hi, k_ref[lo])
    s_low = jnp.where(causal, score_dot(q_lo, k_ref[lo]), NEG)
    top = lanes_max(jnp.maximum(s_diag, s_past))
    wide = widen(top, block_len)
    v_hi, v_lo = with_ones(v_ref[hi]), with_ones(v_ref[lo])
    acc = value_dot(weights(s_diag, wide), v_hi)
    top_low = lanes_max(s_low)
    acc += value_dot(weights(s_past, wide), v_lo)
    acc_low = value_dot(weights(s_low, widen(top_low, block_len)), v_lo)
    acc_ref[hi, 0] = acc
    acc_ref[lo, 0] = acc_low
    qx_ref[hi, 0] = jnp.concatenate([q_hi, minus_columns(top)], axis=1)
    qx_ref[lo, 0] = jnp.concatenate([q_lo, minus_columns(top_low)], axis=1)


def visit(coef, distance, sb, qx_ref, acc_in, parts, k_buf, v_buf, acc_out):
    width = qx_ref.shape[3] // 2
    count = lax.axis_size("seq")
    me = lax.axis_index("seq")
    head_index = lax.axis_index("head")
    inner = lax.axis_index("inner")
    hi, top_block = high_slot(sb, me)

    @pl.when(pl.program_id(0) == 0)
    def _():
        k_buf[:, :, width:] = jnp.ones((2, k_buf.shape[1], width), jnp.bfloat16)
        v_buf[:, :, width:] = jnp.ones((2, k_buf.shape[1], width), jnp.bfloat16)
        for value, (own_buf, twin_buf) in enumerate([(k_buf, v_buf), (v_buf, k_buf)]):

            @pl.when(inner == value)
            def _():
                for turn in range(2):
                    slot = head_index if turn == 0 else 1 - head_index
                    own_buf[slot, :, :width] = parts[turn][...]
                    twin_buf[slot, :, :width] = parts[2 + turn][...]

    other_hi, other_top = high_slot(sb, source_of(me, distance, count))
    above = top_block > other_top
    q_slot = jnp.where(above, hi, 1 - hi)
    k_slot = jnp.where(above, other_hi, 1 - other_hi)

    def weights(s):
        return jnp.exp2(s * coef).astype(jnp.bfloat16)

    acc_out[...] = acc_in[:, 0]
    s_first = score_dot(qx_ref[hi, 0], k_buf[1 - other_hi])
    s_second = score_dot(qx_ref[q_slot, 0], k_buf[k_slot])
    acc_out[hi] += value_dot(weights(s_first), v_buf[1 - other_hi])
    acc_out[q_slot] += value_dot(weights(s_second), v_buf[k_slot])


def middle_kernel(coef, distance, sb, qx_ref, acc_in, p0, p1, p2, p3, acc_out, k_buf, v_buf, acc):
    visit(coef, distance, sb, qx_ref, acc_in, (p0, p1, p2, p3), k_buf, v_buf, acc)
    acc_out[:, 0] = acc[...]


def last_kernel(coef, distance, distances, sb, qx_ref, acc_in, p0, p1, p2, p3, *rest):
    every = rest[: 4 * len(distances) + 2]
    out_ref, lse_ref, k_buf, v_buf, acc, run_top, sem = rest[4 * len(distances) + 2 :]
    visit(coef, distance, sb, qx_ref, acc_in, (p0, p1, p2, p3), k_buf, v_buf, acc)
    _, rows, width = run_top.shape
    block_len = k_buf.shape[1]
    count = lax.axis_size("seq")
    me = lax.axis_index("seq")
    head_index = lax.axis_index("head")
    inner = lax.axis_index("inner")
    fits = jnp.max(acc[:, :, width:]) < SUM_LIMIT

    @pl.when(fits)
    def _():
        for slot in range(2):
            minus = jnp.sum(qx_ref[slot, 0, :, width:].astype(jnp.float32), axis=1, keepdims=True)
            run_top[slot] = jnp.broadcast_to(-minus, (rows, width))

    @pl.when(jnp.logical_not(fits))
    def _():
        run_top[...] = jnp.full_like(run_top, NEG)
        acc[...] = jnp.zeros_like(acc)

        def fetch(src, buf, slot):
            copy = pltpu.make_async_copy(src, buf.at[slot, :, pl.ds(0, width)], sem)
            copy.start()
            copy.wait()

        def online(source):
            @pl.loop(0, 4)
            def _(i):
                slot, q_slot = i // 2, lax.rem(i, 2)
                shift = (sb[2 * me + q_slot] - sb[2 * source + slot]) * block_len + inner * rows

                @pl.when(shift + rows > 0)
                def _():
                    s = score_dot(qx_ref[q_slot, 0, :, :width], k_buf[slot, :, :width])
                    row = lax.broadcasted_iota(jnp.int32, s.shape, 0) + shift
                    allowed = lax.broadcasted_iota(jnp.int32, s.shape, 1) <= row
                    s = jnp.where(allowed, s, NEG)
                    before = run_top[q_slot]
                    top = jnp.maximum(before, jnp.broadcast_to(jnp.max(s, axis=1, keepdims=True), before.shape))
                    p = jnp.where(allowed, jnp.exp2((s - widen(top, block_len)) * coef), 0.0)
                    run_top[q_slot] = top
                    shrink = widen(jnp.exp2((before - top) * coef), 2 * width)
                    acc[q_slot] = acc[q_slot] * shrink + value_dot(p.astype(jnp.bfloat16), v_buf[slot])

        for slot in range(2):
            fetch(every[0].at[slot], k_buf, slot)
            fetch(every[1].at[slot], v_buf, slot)
        online(me)
        for place, other in enumerate(distances):
            pieces = every[2 + 4 * place : 6 + 4 * place]
            for value, (own_buf, twin_buf) in enumerate([(k_buf, v_buf), (v_buf, k_buf)]):

                @pl.when(inner == value)
                def _():
                    for turn in range(2):
                        slot = head_index if turn == 0 else 1 - head_index
                        fetch(pieces[turn], own_buf, slot)
                        fetch(pieces[2 + turn], twin_buf, slot)

            online(source_of(me, other, count))

    for slot in range(2):
        sums = acc[slot, :, width:]
        out_ref[slot] = (acc[slot, :, :width] / sums).astype(out_ref.dtype)
        log_total = run_top[slot] * (coef * math.log(2.0)) + jnp.log(sums)
        lse_ref[slot, pl.ds(pl.program_id(0), 1), :] = jnp.transpose(log_total)[:1]


def body(query_rows, key_rows, value_rows, slot_block):
    _, block_len, width = key_rows.shape
    _, rows, feats = query_rows.shape
    heads = feats // width
    count = lax.axis_size("seq")
    coef = math.log2(math.e) / math.sqrt(width)
    distances = list(range(1, count))

    head_index, inner_index = lax.axis_index("head"), lax.axis_index("inner")
    with jax.named_scope("pieces"):
        held = [
            jnp.where(inner_index == 0, key_rows[slot], value_rows[slot]) for slot in range(2)
        ]
        piece = jnp.where(head_index == 0, held[0], held[1])
    swap = [(0, 1), (1, 0)]
    with jax.named_scope("along_seq"):
        arrived = [
            lax.ppermute(piece, "seq", [(i, partner(i, d, count)) for i in range(count)])
            for d in distances
        ]
    q_spec = pl.BlockSpec((2, rows, width), lambda h, sb: (0, 0, h))
    kv_spec = pl.BlockSpec((2, block_len, width), lambda h, sb: (0, 0, 0))
    head_spec = pl.BlockSpec((2, 1, rows, 2 * width), lambda h, sb: (0, h, 0, 0))
    piece_spec = pl.BlockSpec((block_len, width), lambda h, sb: (0, 0))
    any_spec = pl.BlockSpec(memory_space=pl.ANY)
    acc_shape = jax.ShapeDtypeStruct((2, heads, rows, 2 * width), jnp.float32)
    params = pltpu.CompilerParams(vmem_limit_bytes=40 * 1024 * 1024)
    unit = rows * heads * block_len * width * 4
    exps = rows * heads * block_len

    def cost(units, size):
        return pl.CostEstimate(flops=2 * units * unit, bytes_accessed=size, transcendentals=units * exps)

    qx, acc = pl.pallas_call(
        functools.partial(local_kernel, coef),
        grid_spec=pltpu.PrefetchScalarGridSpec(
            num_scalar_prefetch=1,
            grid=(heads,),
            in_specs=[q_spec, kv_spec, kv_spec],
            out_specs=[head_spec, head_spec],
        ),
        out_shape=[jax.ShapeDtypeStruct(acc_shape.shape, jnp.bfloat16), acc_shape],
        cost_estimate=cost(3, 6_000_000),
        compiler_params=params,
        name="local_part",
    )(slot_block, query_rows, key_rows, value_rows)

    buffers = [
        pltpu.VMEM((2, block_len, 2 * width), jnp.bfloat16),
        pltpu.VMEM((2, block_len, 2 * width), jnp.bfloat16),
        pltpu.VMEM((2, rows, 2 * width), jnp.float32),
    ]
    visitors = []

    def attend(acc, distance, pieces):
        return pl.pallas_call(
            functools.partial(middle_kernel, coef, distance),
            grid_spec=pltpu.PrefetchScalarGridSpec(
                num_scalar_prefetch=1,
                grid=(heads,),
                in_specs=[head_spec, head_spec] + [piece_spec] * 4,
                out_specs=head_spec,
                scratch_shapes=buffers,
            ),
            out_shape=acc_shape,
            input_output_aliases={2: 0},
            cost_estimate=cost(2, 7_000_000),
            compiler_params=params,
            name=f"visitor_{distance}",
        )(slot_block, qx, acc, *pieces)

    for place, own in enumerate(arrived):
        if place >= 2:
            acc = attend(acc, distances[place - 2], visitors[place - 2])
        own, acc = lax.optimization_barrier((own, acc))
        with jax.named_scope("along_head"):
            across = lax.ppermute(own, "head", swap)
        with jax.named_scope("along_inner"):
            visitors.append((own, across, lax.ppermute(own, "inner", swap), lax.ppermute(across, "inner", swap)))
    if count > 2:
        acc = attend(acc, distances[-2], visitors[-2])

    flat = [part for pieces in visitors for part in pieces]
    attended, log_total = pl.pallas_call(
        functools.partial(last_kernel, coef, distances[-1], distances),
        grid_spec=pltpu.PrefetchScalarGridSpec(
            num_scalar_prefetch=1,
            grid=(heads,),
            in_specs=[head_spec, head_spec] + [piece_spec] * 4 + [any_spec] * (2 + len(flat)),
            out_specs=[q_spec, pl.BlockSpec((2, heads, rows), lambda h, sb: (0, 0, 0))],
            scratch_shapes=buffers + [pltpu.VMEM((2, rows, width), jnp.float32), pltpu.SemaphoreType.DMA],
        ),
        out_shape=[
            jax.ShapeDtypeStruct(query_rows.shape, query_rows.dtype),
            jax.ShapeDtypeStruct((2, heads, rows), jnp.float32),
        ],
        cost_estimate=cost(2, 7_000_000),
        compiler_params=params,
        name="last_visitor",
    )(slot_block, qx, acc, *visitors[-1], key_rows, value_rows, *flat)
    return attended, log_total


def solution(mesh):
    placed = (
        P(("groups", "seq"), "inner", "head"),
        P(("groups", "seq"), None, None),
        P(("groups", "seq"), None, None),
        P(),
    )
    return jax.shard_map(
        body,
        mesh=mesh,
        in_specs=placed,
        out_specs=(P(("groups", "seq"), "inner", "head"), P(("groups", "seq"), "head", "inner")),
        check_vma=False,
    )
```

```python
import functools
import math

import jax
import jax.numpy as jnp
from jax import lax
from jax.experimental import pallas as pl
from jax.experimental.pallas import tpu as pltpu
from jax.sharding import PartitionSpec as P

NEG = -1e30
SUM_LIMIT = 1e36
LO, HI = 0, 1


def score_dot(q, k):
    return lax.dot_general(q, k, (((1,), (1,)), ((), ())), preferred_element_type=jnp.float32)


def value_dot(p, v):
    return jnp.dot(p, v, preferred_element_type=jnp.float32)


def widen(x, width):
    return jnp.concatenate([x] * (width // x.shape[1]), axis=1)


def with_ones(x):
    return jnp.concatenate([x, jnp.ones_like(x)], axis=1)


def is_power(count):
    return count & (count - 1) == 0


def source_of(index, distance, count):
    if is_power(count):
        return index ^ distance
    return lax.rem(index - distance + count, count)


def blocks_of(sb, seq_index):
    b0, b1 = sb[2 * seq_index], sb[2 * seq_index + 1]
    return jnp.where(b1 > b0, 1, 0), jnp.minimum(b0, b1), jnp.maximum(b0, b1)


def minus_columns(top):
    high = top.astype(jnp.bfloat16)
    rest = top - high.astype(jnp.float32)
    middle = rest.astype(jnp.bfloat16)
    low = (rest - middle.astype(jnp.float32)).astype(jnp.bfloat16)
    lane = lax.broadcasted_iota(jnp.int32, top.shape, 1)
    high, middle, low = (x.astype(jnp.float32) for x in (high, middle, low))
    picked = jnp.where(lane == 0, high, jnp.where(lane == 1, middle, jnp.where(lane == 2, low, 0.0)))
    return (-picked).astype(jnp.bfloat16)


def local_kernel(coef, sb, q_hbm, k_hbm, v_hbm, qx_ref, acc_ref, q_buf, k_buf, v_buf, sems):
    heads = qx_ref.shape[1]
    _, block_len, width = k_buf.shape
    rows = q_buf.shape[1]
    inner = lax.axis_index("inner")
    hi, _, _ = blocks_of(sb, lax.axis_index("seq"))
    copies = []
    for place, (src, dst) in enumerate([(k_hbm, k_buf), (q_hbm, q_buf), (v_hbm, v_buf)]):
        for order, slot in ((LO, 1 - hi), (HI, hi)):
            copies.append(pltpu.make_async_copy(src.at[slot], dst.at[order], sems.at[place, order]))
    for copy in copies:
        copy.start()
    row = lax.broadcasted_iota(jnp.int32, (rows, block_len), 0) + inner * rows
    col = lax.broadcasted_iota(jnp.int32, (rows, block_len), 1)
    causal = col <= row

    def lanes_max(s):
        return jnp.broadcast_to(jnp.max(s, axis=1, keepdims=True), (rows, width))

    def weights(s, top):
        return jnp.exp2((s - widen(top, block_len)) * coef).astype(jnp.bfloat16)

    for copy in copies[:4]:
        copy.wait()

    def scores(h):
        q_lo = q_buf[LO, :, h * width : (h + 1) * width]
        q_hi = q_buf[HI, :, h * width : (h + 1) * width]
        past = score_dot(q_hi, k_buf[LO])
        diag = jnp.where(causal, score_dot(q_hi, k_buf[HI]), NEG)
        low = jnp.where(causal, score_dot(q_lo, k_buf[LO]), NEG)
        return q_lo, q_hi, past, diag, low

    ready = scores(0)
    for copy in copies[4:]:
        copy.wait()
    for h in range(heads):
        q_lo, q_hi, past, diag, low = ready
        if h + 1 < heads:
            ready = scores(h + 1)
        v_lo, v_hi = with_ones(v_buf[LO]), with_ones(v_buf[HI])
        top = lanes_max(jnp.maximum(past, diag))
        acc_ref[HI, h] = value_dot(weights(past, top), v_lo) + value_dot(weights(diag, top), v_hi)
        qx_ref[HI, h] = jnp.concatenate([q_hi, minus_columns(top)], axis=1)
        top = lanes_max(low)
        acc_ref[LO, h] = value_dot(weights(low, top), v_lo)
        qx_ref[LO, h] = jnp.concatenate([q_lo, minus_columns(top)], axis=1)


def visit(coef, distance, sb, qx_ref, acc_ref, parts, k_buf, v_buf):
    _, heads, rows, _ = qx_ref.shape
    _, block_len, width = k_buf.shape
    count = lax.axis_size("seq")
    me = lax.axis_index("seq")
    head_index = lax.axis_index("head")
    inner = lax.axis_index("inner")
    for value, (own_buf, twin_buf) in enumerate([(k_buf, v_buf), (v_buf, k_buf)]):

        @pl.when(inner == value)
        def _():
            for turn in range(2):
                slot = head_index if turn == 0 else 1 - head_index
                own_buf[slot] = parts[turn][...]
                twin_buf[slot] = parts[2 + turn][...]

    _, _, top_block = blocks_of(sb, me)
    other_hi, _, other_top = blocks_of(sb, source_of(me, distance, count))
    other_lo = 1 - other_hi
    above = top_block > other_top

    def weights(s):
        return jnp.exp2(s * coef).astype(jnp.bfloat16)

    def in_turn(chunks, score, finish):
        ready = score(*chunks[0])
        for place, chunk in enumerate(chunks):
            now = ready
            if place + 1 < len(chunks):
                ready = score(*chunks[place + 1])
            finish(weights(now), *chunk)

    @pl.when(above)
    def _():
        def score(h):
            return score_dot(qx_ref[HI, h], with_ones(k_buf[...].reshape(2 * block_len, width)))

        def finish(p, h):
            acc_ref[HI, h] += value_dot(p, with_ones(v_buf[...].reshape(2 * block_len, width)))

        in_turn([(h,) for h in range(heads)], score, finish)

    @pl.when(jnp.logical_not(above))
    def _():
        def score(h, order):
            return score_dot(qx_ref[order, h], with_ones(k_buf[other_lo]))

        def finish(p, h, order):
            acc_ref[order, h] += value_dot(p, with_ones(v_buf[other_lo]))

        in_turn([(h, order) for h in range(heads) for order in (HI, LO)], score, finish)


def middle_kernel(coef, distance, sb, qx_ref, acc_in, p0, p1, p2, p3, acc_ref, k_buf, v_buf):
    visit(coef, distance, sb, qx_ref, acc_ref, (p0, p1, p2, p3), k_buf, v_buf)


def last_kernel(coef, distance, distances, sb, qx_ref, acc_ref, p0, p1, p2, p3, *rest):
    every = rest[: 4 * len(distances) + 2]
    out_ref, lse_ref, k_buf, v_buf, run_top, run_acc, sem = rest[4 * len(distances) + 2 :]
    visit(coef, distance, sb, qx_ref, acc_ref, (p0, p1, p2, p3), k_buf, v_buf)
    _, heads, rows, _ = qx_ref.shape
    _, block_len, width = k_buf.shape
    count = lax.axis_size("seq")
    me = lax.axis_index("seq")
    head_index = lax.axis_index("head")
    inner = lax.axis_index("inner")
    hi, lo_block, hi_block = blocks_of(sb, me)

    def first_row(x):
        return jnp.transpose(x)[:1]

    def emit(order, h, acc, top_row):
        slot = hi if order == HI else 1 - hi
        sums = acc[:, width:]
        out_ref[slot, :, h * width : (h + 1) * width] = (acc[:, :width] / sums).astype(out_ref.dtype)
        lse_ref[slot, h : h + 1, :] = top_row * (coef * math.log(2.0)) + jnp.log(first_row(sums))

    for order in (LO, HI):
        for h in range(heads):
            columns = jnp.transpose(qx_ref[order, h, :, width:].astype(jnp.float32))
            emit(order, h, acc_ref[order, h], -(columns[0:1] + columns[1:2] + columns[2:3]))

    @pl.when(jnp.logical_not(jnp.max(acc_ref[:, :, :, width:]) < SUM_LIMIT))
    def _():
        def fetch(src, buf, slot):
            copy = pltpu.make_async_copy(src, buf.at[slot], sem)
            copy.start()
            copy.wait()

        def online(source):
            @pl.loop(0, 4 * heads)
            def _(i):
                h, slot, order = i // 4, lax.rem(i, 4) // 2, lax.rem(i, 2)
                own_block = jnp.where(order == HI, hi_block, lo_block)
                shift = (own_block - sb[2 * source + slot]) * block_len + inner * rows

                @pl.when(shift + rows > 0)
                def _():
                    s = score_dot(qx_ref[order, h, :, :width], k_buf[slot])
                    row = lax.broadcasted_iota(jnp.int32, s.shape, 0) + shift
                    allowed = lax.broadcasted_iota(jnp.int32, s.shape, 1) <= row
                    s = jnp.where(allowed, s, NEG)
                    before = run_top[order, h]
                    top = jnp.maximum(before, jnp.broadcast_to(jnp.max(s, axis=1, keepdims=True), before.shape))
                    p = jnp.where(allowed, jnp.exp2((s - widen(top, block_len)) * coef), 0.0)
                    run_top[order, h] = top
                    shrink = widen(jnp.exp2((before - top) * coef), 2 * width)
                    part = value_dot(p.astype(jnp.bfloat16), with_ones(v_buf[slot]))
                    run_acc[order, h] = run_acc[order, h] * shrink + part

        run_top[...] = jnp.full_like(run_top, NEG)
        run_acc[...] = jnp.zeros_like(run_acc)
        for slot in range(2):
            fetch(every[0].at[slot], k_buf, slot)
            fetch(every[1].at[slot], v_buf, slot)
        online(me)
        for place, other in enumerate(distances):
            pieces = every[2 + 4 * place : 6 + 4 * place]
            for value, (own_buf, twin_buf) in enumerate([(k_buf, v_buf), (v_buf, k_buf)]):

                @pl.when(inner == value)
                def _():
                    for turn in range(2):
                        slot = head_index if turn == 0 else 1 - head_index
                        fetch(pieces[turn], own_buf, slot)
                        fetch(pieces[2 + turn], twin_buf, slot)

            online(source_of(me, other, count))
        for order in (LO, HI):
            for h in range(heads):
                emit(order, h, run_acc[order, h], first_row(run_top[order, h]))


def body(query_rows, key_rows, value_rows, slot_block):
    _, block_len, width = key_rows.shape
    _, rows, feats = query_rows.shape
    heads = feats // width
    count = lax.axis_size("seq")
    coef = math.log2(math.e) / math.sqrt(width)
    distances = list(range(1, count))
    swap = [(0, 1), (1, 0)]

    def along_seq(block, distance):
        if is_power(count):
            route = [(i, i ^ distance) for i in range(count)]
        else:
            route = [(i, (i + distance) % count) for i in range(count)]
        with jax.named_scope("along_seq"):
            return lax.ppermute(block, "seq", route)

    head_index, inner_index = lax.axis_index("head"), lax.axis_index("inner")
    with jax.named_scope("pieces"):
        held = [
            jnp.where(inner_index == 0, key_rows[slot], value_rows[slot]) for slot in range(2)
        ]
        piece = jnp.where(head_index == 0, held[0], held[1])
    arrived = {}
    for distance in distances:
        if not is_power(count) or is_power(distance):
            arrived[distance] = along_seq(piece, distance)

    whole = pl.BlockSpec(memory_space=pltpu.VMEM)
    anywhere = pl.BlockSpec(memory_space=pl.ANY)
    in_hbm = pl.BlockSpec(memory_space=pltpu.HBM)
    scalars = pl.BlockSpec(memory_space=pltpu.SMEM)
    acc_shape = jax.ShapeDtypeStruct((2, heads, rows, 2 * width), jnp.float32)
    qx_shape = jax.ShapeDtypeStruct(acc_shape.shape, jnp.bfloat16)
    params = pltpu.CompilerParams(vmem_limit_bytes=40 * 1024 * 1024)
    unit = rows * heads * block_len * width * 4
    exps = rows * heads * block_len

    def cost(units, size):
        return pl.CostEstimate(flops=2 * units * unit, bytes_accessed=size, transcendentals=units * exps)

    kv_buffers = [pltpu.VMEM((2, block_len, width), jnp.bfloat16)] * 2
    qx, acc = pl.pallas_call(
        functools.partial(local_kernel, coef),
        in_specs=[scalars] + [in_hbm] * 3,
        out_specs=[whole, whole],
        out_shape=[qx_shape, acc_shape],
        scratch_shapes=[pltpu.VMEM((2, rows, feats), jnp.bfloat16)] + kv_buffers + [pltpu.SemaphoreType.DMA((3, 2))],
        cost_estimate=cost(3, 6_000_000),
        compiler_params=params,
        name="local_part",
    )(slot_block, query_rows, key_rows, value_rows)

    def attend(acc, distance):
        return pl.pallas_call(
            functools.partial(middle_kernel, coef, distance),
            in_specs=[scalars] + [whole] * 6,
            out_specs=whole,
            out_shape=acc_shape,
            scratch_shapes=kv_buffers,
            input_output_aliases={2: 0},
            cost_estimate=cost(2, 7_000_000),
            compiler_params=params,
            name=f"visitor_{distance}",
        )(slot_block, qx, acc, *visitors[distance])

    visitors = {}
    first, acc = lax.optimization_barrier((arrived, acc))
    arrived = dict(first)
    for place, distance in enumerate(distances):
        if distance not in arrived:
            near = distance & -distance
            arrived[distance] = along_seq(arrived[distance ^ near], near)
        if place >= 2:
            acc = attend(acc, distances[place - 2])
        own, acc = lax.optimization_barrier((arrived[distance], acc))
        arrived[distance] = own
        with jax.named_scope("along_head"):
            across = lax.ppermute(own, "head", swap)
        with jax.named_scope("along_inner"):
            visitors[distance] = (own, across, lax.ppermute(own, "inner", swap), lax.ppermute(across, "inner", swap))
    if count > 2:
        acc = attend(acc, distances[-2])

    flat = [part for distance in distances for part in visitors[distance]]
    attended, log_total = pl.pallas_call(
        functools.partial(last_kernel, coef, distances[-1], distances),
        in_specs=[scalars] + [whole] * 6 + [in_hbm] * 2 + [anywhere] * len(flat),
        out_specs=[pl.BlockSpec(query_rows.shape), pl.BlockSpec((2, heads, rows))],
        out_shape=[
            jax.ShapeDtypeStruct(query_rows.shape, query_rows.dtype),
            jax.ShapeDtypeStruct((2, heads, rows), jnp.float32),
        ],
        scratch_shapes=kv_buffers
        + [
            pltpu.VMEM((2, heads, rows, width), jnp.float32),
            pltpu.VMEM(acc_shape.shape, jnp.float32),
            pltpu.SemaphoreType.DMA,
        ],
        cost_estimate=cost(2, 7_000_000),
        compiler_params=params,
        name="last_visitor",
    )(slot_block, qx, acc, *visitors[distances[-1]], key_rows, value_rows, *flat)
    return attended, log_total


def solution(mesh):
    placed = (
        P(("groups", "seq"), "inner", "head"),
        P(("groups", "seq"), None, None),
        P(("groups", "seq"), None, None),
        P(),
    )
    return jax.shard_map(
        body,
        mesh=mesh,
        in_specs=placed,
        out_specs=(P(("groups", "seq"), "inner", "head"), P(("groups", "seq"), "head", "inner")),
        check_vma=False,
    )
```

```python
import functools
import math

import jax
import jax.numpy as jnp
from jax import lax
from jax.experimental import pallas as pl
from jax.experimental.pallas import tpu as pltpu
from jax.sharding import PartitionSpec as P

NEG = -1e30
SUM_LIMIT = 1e36
LO, HI = 0, 1


def score_dot(q, k):
    return lax.dot_general(q, k, (((1,), (1,)), ((), ())), preferred_element_type=jnp.float32)


def value_dot(p, v):
    return jnp.dot(p, v, preferred_element_type=jnp.float32)


def widen(x, width):
    return jnp.concatenate([x] * (width // x.shape[1]), axis=1)


def with_ones(x):
    return jnp.concatenate([x, jnp.ones_like(x)], axis=1)


def is_power(count):
    return count & (count - 1) == 0


def source_of(index, distance, count):
    if is_power(count):
        return index ^ distance
    return lax.rem(index - distance + count, count)


def blocks_of(sb, seq_index):
    b0, b1 = sb[2 * seq_index], sb[2 * seq_index + 1]
    return jnp.where(b1 > b0, 1, 0), jnp.minimum(b0, b1), jnp.maximum(b0, b1)


def minus_columns(top):
    high = top.astype(jnp.bfloat16)
    rest = top - high.astype(jnp.float32)
    middle = rest.astype(jnp.bfloat16)
    low = (rest - middle.astype(jnp.float32)).astype(jnp.bfloat16)
    lane = lax.broadcasted_iota(jnp.int32, top.shape, 1)
    high, middle, low = (x.astype(jnp.float32) for x in (high, middle, low))
    picked = jnp.where(lane == 0, high, jnp.where(lane == 1, middle, jnp.where(lane == 2, low, 0.0)))
    return (-picked).astype(jnp.bfloat16)


def local_heads(coef, inner, q_buf, k_buf, v_buf, qx_ref, acc_ref, first, ready_values):
    heads = qx_ref.shape[1]
    _, block_len, width = k_buf.shape
    rows = q_buf.shape[1]
    row = lax.broadcasted_iota(jnp.int32, (rows, block_len), 0) + inner * rows
    col = lax.broadcasted_iota(jnp.int32, (rows, block_len), 1)
    causal = col <= row

    def lanes_max(s):
        return jnp.broadcast_to(jnp.max(s, axis=1, keepdims=True), (rows, width))

    def weights(s, top):
        return jnp.exp2((s - widen(top, block_len)) * coef).astype(jnp.bfloat16)

    def scores(h):
        q_lo = q_buf[LO, :, (first + h) * width : (first + h + 1) * width]
        q_hi = q_buf[HI, :, (first + h) * width : (first + h + 1) * width]
        past = score_dot(q_hi, k_buf[LO])
        diag = jnp.where(causal, score_dot(q_hi, k_buf[HI]), NEG)
        low = jnp.where(causal, score_dot(q_lo, k_buf[LO]), NEG)
        return q_lo, q_hi, past, diag, low

    ready = scores(0)
    ready_values()
    for h in range(heads):
        q_lo, q_hi, past, diag, low = ready
        if h + 1 < heads:
            ready = scores(h + 1)
        v_lo, v_hi = with_ones(v_buf[LO]), with_ones(v_buf[HI])
        top = lanes_max(jnp.maximum(past, diag))
        acc_ref[HI, h] = value_dot(weights(past, top), v_lo) + value_dot(weights(diag, top), v_hi)
        qx_ref[HI, h] = jnp.concatenate([q_hi, minus_columns(top)], axis=1)
        top = lanes_max(low)
        acc_ref[LO, h] = value_dot(weights(low, top), v_lo)
        qx_ref[LO, h] = jnp.concatenate([q_lo, minus_columns(top)], axis=1)


def local_first(coef, sb, q_hbm, k_hbm, v_hbm, qx_ref, acc_ref, q_buf, k_buf, v_buf, sems):
    hi, _, _ = blocks_of(sb, lax.axis_index("seq"))
    copies = []
    for place, (src, dst) in enumerate([(k_hbm, k_buf), (q_hbm, q_buf), (v_hbm, v_buf)]):
        for order, slot in ((LO, 1 - hi), (HI, hi)):
            copies.append(pltpu.make_async_copy(src.at[slot], dst.at[order], sems.at[place, order]))
    for copy in copies:
        copy.start()
    for copy in copies[:4]:
        copy.wait()

    def ready_values():
        for copy in copies[4:]:
            copy.wait()

    local_heads(coef, lax.axis_index("inner"), q_buf, k_buf, v_buf, qx_ref, acc_ref, 0, ready_values)


def local_second(coef, first, q_buf, k_buf, v_buf, qx_ref, acc_ref):
    local_heads(coef, lax.axis_index("inner"), q_buf, k_buf, v_buf, qx_ref, acc_ref, first, lambda: None)


def head_places(parts):
    return [(part, h) for part in parts for h in range(part.shape[1])]


def visit(coef, distance, sb, qx, acc, parts, k_buf, v_buf, store):
    places = head_places(qx)
    heads = len(places)
    _, block_len, width = k_buf.shape
    count = lax.axis_size("seq")
    me = lax.axis_index("seq")
    head_index = lax.rem(lax.axis_index("head"), 2)
    inner = lax.axis_index("inner")
    for value, (own_buf, twin_buf) in enumerate([(k_buf, v_buf), (v_buf, k_buf)]):

        @pl.when(inner == value)
        def _():
            for turn in range(2):
                slot = head_index if turn == 0 else 1 - head_index
                own_buf[slot] = parts[turn][...]
                twin_buf[slot] = parts[2 + turn][...]

    _, _, top_block = blocks_of(sb, me)
    other_hi, _, other_top = blocks_of(sb, source_of(me, distance, count))
    other_lo = 1 - other_hi
    above = top_block > other_top

    def weights(s):
        return jnp.exp2(s * coef).astype(jnp.bfloat16)

    def in_turn(chunks, score, finish):
        ready = score(*chunks[0])
        for place, chunk in enumerate(chunks):
            now = ready
            if place + 1 < len(chunks):
                ready = score(*chunks[place + 1])
            finish(weights(now), *chunk)

    @pl.when(above)
    def _():
        def score(h):
            keys = with_ones(k_buf[...].reshape(2 * block_len, width))
            return score_dot(places[h][0][HI, places[h][1]], keys)

        def finish(p, h):
            values = with_ones(v_buf[...].reshape(2 * block_len, width))
            store(HI, h, acc[h][0][HI, acc[h][1]] + value_dot(p, values))
            store(LO, h, None)

        in_turn([(h,) for h in range(heads)], score, finish)

    @pl.when(jnp.logical_not(above))
    def _():
        def score(h, order):
            return score_dot(places[h][0][order, places[h][1]], with_ones(k_buf[other_lo]))

        def finish(p, h, order):
            store(order, h, acc[h][0][order, acc[h][1]] + value_dot(p, with_ones(v_buf[other_lo])))

        in_turn([(h, order) for h in range(heads) for order in (HI, LO)], score, finish)


def first_row(x):
    return jnp.transpose(x)[:1]


def middle_kernel(coef, distance, n, sb, *refs):
    qx, pieces, outs = refs[:n], refs[2 * n : 2 * n + 4], refs[2 * n + 4 : 3 * n + 4]
    *tops, k_buf, v_buf = refs[3 * n + 4 :]
    acc = head_places(outs)
    width = k_buf.shape[2]

    def store(order, h, value):
        if value is not None:
            acc[h][0][order, acc[h][1]] = value

    visit(coef, distance, sb, qx, acc, pieces, k_buf, v_buf, store)
    for top_ref in tops:
        for order in (LO, HI):
            for h, (part, place) in enumerate(head_places(qx)):
                columns = jnp.transpose(part[order, place, :, width:].astype(jnp.float32))
                top_ref[order, h : h + 1, :] = -(columns[0:1] + columns[1:2] + columns[2:3])


def last_kernel(coef, distance, distances, n, sb, *refs):
    qx, acc, top_ref, pieces = refs[:n], head_places(refs[n : 2 * n]), refs[2 * n], refs[2 * n + 1 : 2 * n + 5]
    every, rest = refs[2 * n + 5 :][: 4 * len(distances) + 2], refs[2 * n + 5 :][4 * len(distances) + 2 :]
    out_hbm, lse_ref, out_buf, k_buf, v_buf, worst, run_top, run_acc, sem, out_sems = rest
    heads = len(acc)
    rows = worst.shape[0]
    _, block_len, width = k_buf.shape
    count = lax.axis_size("seq")
    me = lax.axis_index("seq")
    head_index = lax.rem(lax.axis_index("head"), 2)
    inner = lax.axis_index("inner")
    hi, lo_block, hi_block = blocks_of(sb, me)

    def out_copy(h):
        columns = pl.ds(h * width, width)
        return pltpu.make_async_copy(out_buf.at[:, :, columns], out_hbm.at[:, :, columns], out_sems.at[h])

    def emit(order, h, value, top_row):
        slot = hi if order == HI else 1 - hi
        sums = value[:, width:]
        out_buf[slot, :, h * width : (h + 1) * width] = (value[:, :width] / sums).astype(out_buf.dtype)
        lse_ref[slot, h : h + 1, :] = top_row * (coef * math.log(2.0)) + jnp.log(first_row(sums))
        return sums

    worst[...] = jnp.zeros_like(worst)

    def store(order, h, value):
        if value is None:
            value = acc[h][0][order, acc[h][1]]
        sums = emit(order, h, value, top_ref[order, h : h + 1, :])
        worst[...] = jnp.maximum(worst[...], sums)
        if order == LO:
            out_copy(h).start()

    visit(coef, distance, sb, qx, acc, pieces, k_buf, v_buf, store)
    for h in range(heads):
        out_copy(h).wait()

    @pl.when(jnp.logical_not(jnp.max(worst[...]) < SUM_LIMIT))
    def _():
        def fetch(src, buf, slot):
            copy = pltpu.make_async_copy(src, buf.at[slot], sem)
            copy.start()
            copy.wait()

        def online(source):
            base = 0
            for part in qx:

                @pl.loop(0, 4 * part.shape[1])
                def _(i):
                    h, slot, order = i // 4, lax.rem(i, 4) // 2, lax.rem(i, 2)
                    own_block = jnp.where(order == HI, hi_block, lo_block)
                    shift = (own_block - sb[2 * source + slot]) * block_len + inner * rows

                    @pl.when(shift + rows > 0)
                    def _():
                        s = score_dot(part[order, h, :, :width], k_buf[slot])
                        row = lax.broadcasted_iota(jnp.int32, s.shape, 0) + shift
                        allowed = lax.broadcasted_iota(jnp.int32, s.shape, 1) <= row
                        s = jnp.where(allowed, s, NEG)
                        before = run_top[order, base + h]
                        top = jnp.maximum(before, jnp.broadcast_to(jnp.max(s, axis=1, keepdims=True), before.shape))
                        p = jnp.where(allowed, jnp.exp2((s - widen(top, block_len)) * coef), 0.0)
                        run_top[order, base + h] = top
                        shrink = widen(jnp.exp2((before - top) * coef), 2 * width)
                        fresh = value_dot(p.astype(jnp.bfloat16), with_ones(v_buf[slot]))
                        run_acc[order, base + h] = run_acc[order, base + h] * shrink + fresh

                base += part.shape[1]

        run_top[...] = jnp.full_like(run_top, NEG)
        run_acc[...] = jnp.zeros_like(run_acc)
        for slot in range(2):
            fetch(every[0].at[slot], k_buf, slot)
            fetch(every[1].at[slot], v_buf, slot)
        online(me)
        for place, other in enumerate(distances):
            others = every[2 + 4 * place : 6 + 4 * place]
            for value, (own_buf, twin_buf) in enumerate([(k_buf, v_buf), (v_buf, k_buf)]):

                @pl.when(inner == value)
                def _():
                    for turn in range(2):
                        slot = head_index if turn == 0 else 1 - head_index
                        fetch(others[turn], own_buf, slot)
                        fetch(others[2 + turn], twin_buf, slot)

            online(source_of(me, other, count))
        for h in range(heads):
            for order in (LO, HI):
                emit(order, h, run_acc[order, h], first_row(run_top[order, h]))
            out_copy(h).start()
            out_copy(h).wait()


def body(query_rows, key_rows, value_rows, slot_block):
    _, block_len, width = key_rows.shape
    _, rows, feats = query_rows.shape
    heads = feats // width
    sizes = [heads] if heads == 1 else [heads // 2, heads - heads // 2]
    count = lax.axis_size("seq")
    coef = math.log2(math.e) / math.sqrt(width)
    distances = list(range(1, count))

    def along_seq(block, distance):
        if is_power(count):
            route = [(i, i ^ distance) for i in range(count)]
        else:
            route = [(i, (i + distance) % count) for i in range(count)]
        with jax.named_scope("along_seq"):
            return lax.ppermute(block, "seq", route)

    def along_head(block):
        with jax.named_scope("along_head"):
            return lax.ppermute(block, "head", [(i, i ^ 1) for i in range(lax.axis_size("head"))])

    def along_inner(block):
        with jax.named_scope("along_inner"):
            return lax.ppermute(block, "inner", [(0, 1), (1, 0)])

    head_index, inner_index = lax.rem(lax.axis_index("head"), 2), lax.axis_index("inner")
    with jax.named_scope("pieces"):
        held = [
            jnp.where(inner_index == 0, key_rows[slot], value_rows[slot]) for slot in range(2)
        ]
        piece = jnp.where(head_index == 0, held[0], held[1])
    arrived = {}
    for distance in distances:
        if not is_power(count) or is_power(distance):
            arrived[distance] = along_seq(piece, distance)

    whole = pl.BlockSpec(memory_space=pltpu.VMEM)
    anywhere = pl.BlockSpec(memory_space=pl.ANY)
    scalars = pl.BlockSpec(memory_space=pltpu.SMEM)
    acc_shapes = [jax.ShapeDtypeStruct((2, size, rows, 2 * width), jnp.float32) for size in sizes]
    qx_shapes = [jax.ShapeDtypeStruct(shape.shape, jnp.bfloat16) for shape in acc_shapes]
    top_shape = jax.ShapeDtypeStruct((2, heads, rows), jnp.float32)
    params = pltpu.CompilerParams(vmem_limit_bytes=40 * 1024 * 1024)
    unit = rows * heads * block_len * width * 4
    exps = rows * heads * block_len

    def cost(units, size):
        return pl.CostEstimate(flops=int(2 * units * unit), bytes_accessed=size, transcendentals=int(units * exps))

    query_rows, key_rows, value_rows, slot_hbm = (
        pltpu.with_memory_space_constraint(x, pltpu.HBM) for x in (query_rows, key_rows, value_rows, slot_block)
    )
    kv_shape = jax.ShapeDtypeStruct(key_rows.shape, key_rows.dtype)
    qx0, acc0, q_sorted, k_sorted, v_sorted = pl.pallas_call(
        functools.partial(local_first, coef),
        in_specs=[scalars] + [anywhere] * 3,
        out_specs=[whole] * 5,
        out_shape=[qx_shapes[0], acc_shapes[0], jax.ShapeDtypeStruct(query_rows.shape, query_rows.dtype), kv_shape, kv_shape],
        scratch_shapes=[pltpu.SemaphoreType.DMA((3, 2))],
        cost_estimate=cost(1.5, 4_000_000),
        compiler_params=params,
        name="local_first",
    )(slot_hbm, query_rows, key_rows, value_rows)

    kv_buffers = [pltpu.VMEM((2, block_len, width), jnp.bfloat16)] * 2
    across, beside, beside_across = {}, {}, {}

    arrived[1], q_sorted = lax.optimization_barrier((arrived[1], q_sorted))
    across[1] = along_head(arrived[1])
    qx, acc = [qx0], [acc0]
    for size, qx_shape, acc_shape in zip(sizes[1:], qx_shapes[1:], acc_shapes[1:]):
        more_qx, more_acc = pl.pallas_call(
            functools.partial(local_second, coef, heads - size),
            in_specs=[whole] * 3,
            out_specs=[whole] * 2,
            out_shape=[qx_shape, acc_shape],
            cost_estimate=cost(1.5, 4_000_000),
            compiler_params=params,
            name="local_second",
        )(q_sorted, k_sorted, v_sorted)
        qx.append(more_qx)
        acc.append(more_acc)
    n = len(sizes)

    def attend(acc, distance, with_tops):
        return pl.pallas_call(
            functools.partial(middle_kernel, coef, distance, n),
            in_specs=[scalars] + [whole] * (2 * n + 4),
            out_specs=[whole] * (n + with_tops),
            out_shape=acc_shapes + [top_shape] * with_tops,
            scratch_shapes=kv_buffers,
            input_output_aliases={1 + n + i: i for i in range(n)},
            cost_estimate=cost(2, 7_000_000),
            compiler_params=params,
            name=f"visitor_{distance}",
        )(slot_block, *qx, *acc, arrived[distance], across[distance], beside[distance], beside_across[distance])

    for place, distance in enumerate(distances):
        following = distances[place + 1] if place + 1 < len(distances) else None
        tied = (acc, across[distance], arrived.get(following))
        acc, across[distance], ahead = lax.optimization_barrier(tied)
        if following is None:
            beside[distance] = along_inner(arrived[distance])
            beside_across[distance] = along_inner(across[distance])
            break
        arrived[following] = ahead
        after = distances[place + 2] if place + 2 < len(distances) else None
        if after is not None and after not in arrived:
            near = after & -after
            arrived[after] = along_seq(arrived[after ^ near], near)
        across[following] = along_head(arrived[following])
        beside[distance] = along_inner(arrived[distance])
        beside_across[distance] = along_inner(across[distance])
        found = attend(acc, distance, int(after is None))
        acc, tops = found[:n], found[n:]

    last = distances[-1]
    flat = [part for d in distances for part in (arrived[d], across[d], beside[d], beside_across[d])]
    attended, log_total = pl.pallas_call(
        functools.partial(last_kernel, coef, last, distances, n),
        in_specs=[scalars] + [whole] * (2 * n + 5) + [anywhere] * (2 + len(flat)),
        out_specs=[anywhere, pl.BlockSpec(top_shape.shape)],
        out_shape=[jax.ShapeDtypeStruct(query_rows.shape, query_rows.dtype), top_shape],
        scratch_shapes=[pltpu.VMEM(query_rows.shape, query_rows.dtype)]
        + kv_buffers
        + [
            pltpu.VMEM((rows, width), jnp.float32),
            pltpu.VMEM((2, heads, rows, width), jnp.float32),
            pltpu.VMEM((2, heads, rows, 2 * width), jnp.float32),
            pltpu.SemaphoreType.DMA,
            pltpu.SemaphoreType.DMA((heads,)),
        ],
        cost_estimate=cost(2, 7_000_000),
        compiler_params=params,
        name="last_visitor",
    )(slot_block, *qx, *acc, *tops, *flat[-4:], key_rows, value_rows, *flat)
    return attended, log_total


def solution(mesh):
    placed = (
        P(("groups", "seq"), "inner", "head"),
        P(("groups", "seq"), None, None),
        P(("groups", "seq"), None, None),
        P(),
    )
    return jax.shard_map(
        body,
        mesh=mesh,
        in_specs=placed,
        out_specs=(P(("groups", "seq"), "inner", "head"), P(("groups", "seq"), "head", "inner")),
        check_vma=False,
    )
```

```python
import functools
import math

import jax
import jax.numpy as jnp
from jax import lax
from jax.experimental import pallas as pl
from jax.experimental.pallas import tpu as pltpu
from jax.sharding import PartitionSpec as P

NEG = -1e30
SUM_LIMIT = 1e36
LO, HI = 0, 1


def score_dot(q, k):
    return lax.dot_general(q, k, (((1,), (1,)), ((), ())), preferred_element_type=jnp.float32)


def value_dot(p, v):
    return jnp.dot(p, v, preferred_element_type=jnp.float32)


def widen(x, width):
    return jnp.concatenate([x] * (width // x.shape[1]), axis=1)


def with_ones(x):
    return jnp.concatenate([x, jnp.ones_like(x)], axis=1)


def is_power(count):
    return count & (count - 1) == 0


def source_of(index, distance, count):
    if is_power(count):
        return index ^ distance
    return lax.rem(index - distance + count, count)


def blocks_of(sb, seq_index):
    b0, b1 = sb[2 * seq_index], sb[2 * seq_index + 1]
    return jnp.where(b1 > b0, 1, 0), jnp.minimum(b0, b1), jnp.maximum(b0, b1)


def minus_columns(top):
    high = top.astype(jnp.bfloat16)
    rest = top - high.astype(jnp.float32)
    middle = rest.astype(jnp.bfloat16)
    low = (rest - middle.astype(jnp.float32)).astype(jnp.bfloat16)
    lane = lax.broadcasted_iota(jnp.int32, top.shape, 1)
    high, middle, low = (x.astype(jnp.float32) for x in (high, middle, low))
    picked = jnp.where(lane == 0, high, jnp.where(lane == 1, middle, jnp.where(lane == 2, low, 0.0)))
    return (-picked).astype(jnp.bfloat16)


def load_kernel(q_hbm, k_hbm, v_hbm, sb_hbm, piece, q_out, k_out, v_out, sb_out, sems):
    half = piece.shape[1]
    inner = lax.axis_index("inner")
    rows = pl.ds(pl.multiple_of(lax.rem(lax.axis_index("head"), 2) * half, half), half)
    for value, src in enumerate((k_hbm, v_hbm)):

        @pl.when(inner == value)
        def _():
            pltpu.make_async_copy(src.at[:, rows], piece, sems.at[0]).start()

    copies = [pltpu.make_async_copy(k_hbm.at[:, rows], piece, sems.at[0])]
    for place, (src, dst) in enumerate([(k_hbm, k_out), (q_hbm, q_out), (v_hbm, v_out), (sb_hbm, sb_out)]):
        copy = pltpu.make_async_copy(src, dst, sems.at[1 + place])
        copy.start()
        copies.append(copy)
    for copy in copies:
        copy.wait()


def local_kernel(coef, first, sb, q_buf, k_buf, v_buf, qx_ref, acc_ref):
    heads = qx_ref.shape[1]
    _, block_len, width = k_buf.shape
    rows = q_buf.shape[1]
    hi, _, _ = blocks_of(sb, lax.axis_index("seq"))
    lo = 1 - hi
    row = lax.broadcasted_iota(jnp.int32, (rows, block_len), 0) + lax.axis_index("inner") * rows
    col = lax.broadcasted_iota(jnp.int32, (rows, block_len), 1)
    causal = col <= row

    def lanes_max(s):
        return jnp.broadcast_to(jnp.max(s, axis=1, keepdims=True), (rows, width))

    def weights(s, top):
        return jnp.exp2((s - widen(top, block_len)) * coef).astype(jnp.bfloat16)

    def scores(h):
        q_lo = q_buf[lo, :, (first + h) * width : (first + h + 1) * width]
        q_hi = q_buf[hi, :, (first + h) * width : (first + h + 1) * width]
        past = score_dot(q_hi, k_buf[lo])
        diag = jnp.where(causal, score_dot(q_hi, k_buf[hi]), NEG)
        low = jnp.where(causal, score_dot(q_lo, k_buf[lo]), NEG)
        return q_lo, q_hi, past, diag, low

    ready = scores(0)
    for h in range(heads):
        q_lo, q_hi, past, diag, low = ready
        if h + 1 < heads:
            ready = scores(h + 1)
        v_lo, v_hi = with_ones(v_buf[lo]), with_ones(v_buf[hi])
        top = lanes_max(jnp.maximum(past, diag))
        acc_ref[HI, h] = value_dot(weights(past, top), v_lo) + value_dot(weights(diag, top), v_hi)
        qx_ref[HI, h] = jnp.concatenate([q_hi, minus_columns(top)], axis=1)
        top = lanes_max(low)
        acc_ref[LO, h] = value_dot(weights(low, top), v_lo)
        qx_ref[LO, h] = jnp.concatenate([q_lo, minus_columns(top)], axis=1)


def head_places(parts):
    return [(part, h) for part in parts for h in range(part.shape[1])]


def place_pieces(parts, own_half, k_buf, v_buf):
    inner = lax.axis_index("inner")
    for value, (own_buf, twin_buf) in enumerate([(k_buf, v_buf), (v_buf, k_buf)]):

        @pl.when(inner == value)
        def _():
            for turn, (own, twin) in enumerate(parts):
                half = own_half if turn == 0 else 1 - own_half
                own_buf[:, half] = own[...]
                twin_buf[:, half] = twin[...]


def visit(coef, distance, parts, sb, qx, acc, buffers, store):
    places = head_places(qx)
    heads = len(places)
    count = lax.axis_size("seq")
    me = lax.axis_index("seq")
    k_buf, v_buf = buffers[:2] if len(parts) == 2 else buffers[2:]
    own_half = lax.rem(lax.axis_index("head"), 2) if len(parts) == 2 else 0
    place_pieces(parts, own_half, k_buf, v_buf)
    _, halves, half_len, width = k_buf.shape
    keys_here = halves * half_len

    _, _, top_block = blocks_of(sb, me)
    other_hi, _, other_top = blocks_of(sb, source_of(me, distance, count))
    other_lo = 1 - other_hi
    above = top_block > other_top

    def weights(s):
        return jnp.exp2(s * coef).astype(jnp.bfloat16)

    def in_turn(chunks, score, finish):
        ready = score(*chunks[0])
        for place, chunk in enumerate(chunks):
            now = ready
            if place + 1 < len(chunks):
                ready = score(*chunks[place + 1])
            finish(weights(now), *chunk)

    @pl.when(above)
    def _():
        def score(h):
            keys = with_ones(k_buf[...].reshape(2 * keys_here, width))
            return score_dot(places[h][0][HI, places[h][1]], keys)

        def finish(p, h):
            values = with_ones(v_buf[...].reshape(2 * keys_here, width))
            store(HI, h, acc[h][0][HI, acc[h][1]] + value_dot(p, values))
            store(LO, h, None)

        in_turn([(h,) for h in range(heads)], score, finish)

    @pl.when(jnp.logical_not(above))
    def _():
        def score(h, order):
            keys = with_ones(k_buf[other_lo].reshape(keys_here, width))
            return score_dot(places[h][0][order, places[h][1]], keys)

        def finish(p, h, order):
            values = with_ones(v_buf[other_lo].reshape(keys_here, width))
            store(order, h, acc[h][0][order, acc[h][1]] + value_dot(p, values))

        in_turn([(h, order) for h in range(heads) for order in (HI, LO)], score, finish)


def first_row(x):
    return jnp.transpose(x)[:1]


def middle_kernel(coef, visits, n, sb, *refs):
    qx, refs = refs[:n], refs[2 * n :]
    taken = []
    for distance, pairs in visits:
        taken.append((distance, [refs[2 * i : 2 * i + 2] for i in range(pairs)]))
        refs = refs[2 * pairs :]
    outs, tops, buffers = refs[:n], refs[n:-4], refs[-4:]
    acc = head_places(outs)
    width = buffers[0].shape[3]

    def store(order, h, value):
        if value is not None:
            acc[h][0][order, acc[h][1]] = value

    for distance, parts in taken:
        visit(coef, distance, parts, sb, qx, acc, buffers, store)
    for top_ref in tops:
        for order in (LO, HI):
            for h, (part, place) in enumerate(head_places(qx)):
                columns = jnp.transpose(part[order, place, :, width:].astype(jnp.float32))
                top_ref[order, h : h + 1, :] = -(columns[0:1] + columns[1:2] + columns[2:3])


def last_kernel(coef, distances, n, sb, *refs):
    qx, acc, top_ref, parts = refs[:n], head_places(refs[n : 2 * n]), refs[2 * n], [refs[2 * n + 1 : 2 * n + 3]]
    every, rest = refs[2 * n + 3 :][: 4 * len(distances) + 2], refs[2 * n + 3 :][4 * len(distances) + 2 :]
    out_hbm, lse_hbm, out_buf, lse_ref, *buffers, worst, run_top, run_acc, sem, out_sems = rest
    heads = len(acc)
    rows = worst.shape[0]
    k_buf, v_buf = buffers[:2]
    _, halves, half_len, width = k_buf.shape
    block_len = halves * half_len
    count = lax.axis_size("seq")
    me = lax.axis_index("seq")
    own_half = lax.rem(lax.axis_index("head"), 2)
    inner = lax.axis_index("inner")
    hi, lo_block, hi_block = blocks_of(sb, me)
    lse_copy = pltpu.make_async_copy(lse_ref, lse_hbm, sem)

    def out_copy(h):
        columns = pl.ds(h * width, width)
        return pltpu.make_async_copy(out_buf.at[:, :, columns], out_hbm.at[:, :, columns], out_sems.at[h])

    def emit(order, h, value, top_row):
        slot = hi if order == HI else 1 - hi
        sums = value[:, width:]
        out_buf[slot, :, h * width : (h + 1) * width] = (value[:, :width] / sums).astype(out_buf.dtype)
        lse_ref[slot, h : h + 1, :] = top_row * (coef * math.log(2.0)) + jnp.log(first_row(sums))
        return sums

    worst[...] = jnp.zeros_like(worst)

    def store(order, h, value):
        if value is None:
            value = acc[h][0][order, acc[h][1]]
        sums = emit(order, h, value, top_ref[order, h : h + 1, :])
        worst[...] = jnp.maximum(worst[...], sums)
        if order == LO:
            out_copy(h).start()

    visit(coef, distances[-1], parts, sb, qx, acc, buffers, store)
    lse_copy.start()
    for h in range(heads):
        out_copy(h).wait()
    lse_copy.wait()

    @pl.when(jnp.logical_not(jnp.max(worst[...]) < SUM_LIMIT))
    def _():
        def fetch(src, dst):
            copy = pltpu.make_async_copy(src, dst, sem)
            copy.start()
            copy.wait()

        def online(source):
            base = 0
            for part in qx:

                @pl.loop(0, 4 * part.shape[1])
                def _(i):
                    h, slot, order = i // 4, lax.rem(i, 4) // 2, lax.rem(i, 2)
                    own_block = jnp.where(order == HI, hi_block, lo_block)
                    shift = (own_block - sb[2 * source + slot]) * block_len + inner * rows

                    @pl.when(shift + rows > 0)
                    def _():
                        s = score_dot(part[order, h, :, :width], k_buf[slot].reshape(block_len, width))
                        row = lax.broadcasted_iota(jnp.int32, s.shape, 0) + shift
                        allowed = lax.broadcasted_iota(jnp.int32, s.shape, 1) <= row
                        s = jnp.where(allowed, s, NEG)
                        before = run_top[order, base + h]
                        top = jnp.maximum(before, jnp.broadcast_to(jnp.max(s, axis=1, keepdims=True), before.shape))
                        p = jnp.where(allowed, jnp.exp2((s - widen(top, block_len)) * coef), 0.0)
                        run_top[order, base + h] = top
                        shrink = widen(jnp.exp2((before - top) * coef), 2 * width)
                        fresh = value_dot(p.astype(jnp.bfloat16), with_ones(v_buf[slot].reshape(block_len, width)))
                        run_acc[order, base + h] = run_acc[order, base + h] * shrink + fresh

                base += part.shape[1]

        run_top[...] = jnp.full_like(run_top, NEG)
        run_acc[...] = jnp.zeros_like(run_acc)
        for half in range(2):
            fetch(every[0].at[:, pl.ds(half * half_len, half_len)], k_buf.at[:, half])
            fetch(every[1].at[:, pl.ds(half * half_len, half_len)], v_buf.at[:, half])
        online(me)
        for place, other in enumerate(distances):
            others = every[2 + 4 * place : 6 + 4 * place]
            for value, (own_buf, twin_buf) in enumerate([(k_buf, v_buf), (v_buf, k_buf)]):

                @pl.when(inner == value)
                def _():
                    for turn in range(2):
                        half = own_half if turn == 0 else 1 - own_half
                        fetch(others[2 * turn], own_buf.at[:, half])
                        fetch(others[2 * turn + 1], twin_buf.at[:, half])

            online(source_of(me, other, count))
        for h in range(heads):
            for order in (LO, HI):
                emit(order, h, run_acc[order, h], first_row(run_top[order, h]))
            out_copy(h).start()
            out_copy(h).wait()
        lse_copy.start()
        lse_copy.wait()


def body(query_rows, key_rows, value_rows, slot_block):
    _, block_len, width = key_rows.shape
    _, rows, feats = query_rows.shape
    heads = feats // width
    sizes = [heads] if heads == 1 else [heads // 2, heads - heads // 2]
    count = lax.axis_size("seq")
    coef = math.log2(math.e) / math.sqrt(width)
    distances = list(range(1, count))

    def along_seq(block, distance):
        if is_power(count):
            route = [(i, i ^ distance) for i in range(count)]
        else:
            route = [(i, (i + distance) % count) for i in range(count)]
        with jax.named_scope("along_seq"):
            return lax.ppermute(block, "seq", route)

    def along_head(block):
        with jax.named_scope("along_head"):
            return lax.ppermute(block, "head", [(i, i ^ 1) for i in range(lax.axis_size("head"))])

    def along_inner(block):
        with jax.named_scope("along_inner"):
            return lax.ppermute(block, "inner", [(0, 1), (1, 0)])

    whole = pl.BlockSpec(memory_space=pltpu.VMEM)
    anywhere = pl.BlockSpec(memory_space=pl.ANY)
    scalars = pl.BlockSpec(memory_space=pltpu.SMEM)
    acc_shapes = [jax.ShapeDtypeStruct((2, size, rows, 2 * width), jnp.float32) for size in sizes]
    qx_shapes = [jax.ShapeDtypeStruct(shape.shape, jnp.bfloat16) for shape in acc_shapes]
    top_shape = jax.ShapeDtypeStruct((2, heads, rows), jnp.float32)
    params = pltpu.CompilerParams(vmem_limit_bytes=40 * 1024 * 1024)
    unit = rows * heads * block_len * width * 4
    exps = rows * heads * block_len

    def cost(units, size):
        return pl.CostEstimate(flops=int(2 * units * unit), bytes_accessed=size, transcendentals=int(units * exps))

    in_hbm = [
        pltpu.with_memory_space_constraint(x, pltpu.HBM) for x in (query_rows, key_rows, value_rows, slot_block)
    ]
    half_shape = jax.ShapeDtypeStruct((2, block_len // 2, width), key_rows.dtype)
    piece, q_here, k_here, v_here, sb_here = pl.pallas_call(
        load_kernel,
        in_specs=[anywhere] * 4,
        out_specs=[whole] * 5,
        out_shape=[half_shape] + [jax.ShapeDtypeStruct(x.shape, x.dtype) for x in in_hbm],
        scratch_shapes=[pltpu.SemaphoreType.DMA((5,))],
        cost_estimate=pl.CostEstimate(flops=0, bytes_accessed=3_000_000, transcendentals=0),
        compiler_params=params,
        name="load",
    )(*in_hbm)
    arrived, across, beside, beside_across = {}, {}, {}, {}
    for distance in distances:
        if not is_power(count) or is_power(distance):
            arrived[distance] = along_seq(piece, distance)

    qx, acc = [], []
    first = 0
    for size, qx_shape, acc_shape in zip(sizes, qx_shapes, acc_shapes):
        more_qx, more_acc = pl.pallas_call(
            functools.partial(local_kernel, coef, first),
            in_specs=[scalars] + [whole] * 3,
            out_specs=[whole] * 2,
            out_shape=[qx_shape, acc_shape],
            cost_estimate=cost(1.5, 4_000_000),
            compiler_params=params,
            name=f"local_{first}",
        )(sb_here, q_here, k_here, v_here)
        qx.append(more_qx)
        acc.append(more_acc)
        if first == 0:
            arrived[1], q_here, acc[0] = lax.optimization_barrier((arrived[1], q_here, acc[0]))
            across[1] = along_head(arrived[1])
            beside[1] = along_inner(arrived[1])
        first += size
    kv_buffers = [pltpu.VMEM((2, 2, block_len // 2, width), jnp.bfloat16)] * 2
    kv_buffers += [pltpu.VMEM((2, 1, block_len // 2, width), jnp.bfloat16)] * 2
    n = len(sizes)

    def attend(acc, visits, with_tops):
        pieces = [part for _, pairs in visits for pair in pairs for part in pair]
        return pl.pallas_call(
            functools.partial(middle_kernel, coef, [(distance, len(pairs)) for distance, pairs in visits], n),
            in_specs=[scalars] + [whole] * (2 * n + len(pieces)),
            out_specs=[whole] * (n + with_tops),
            out_shape=acc_shapes + [top_shape] * with_tops,
            scratch_shapes=kv_buffers,
            input_output_aliases={1 + n + i: i for i in range(n)},
            cost_estimate=cost(len(pieces) / 2, 7_000_000),
            compiler_params=params,
            name=f"visitors_{visits[0][0]}_{visits[1][0]}",
        )(sb_here, *qx, *acc, *pieces)

    for place, distance in enumerate(distances):
        if place == 0:
            continue
        before = distances[place - 1]
        acc, arrived[distance] = lax.optimization_barrier((acc, arrived[distance]))
        following = distances[place + 1] if place + 1 < len(distances) else None
        if following is not None and following not in arrived:
            near = following & -following
            arrived[following] = along_seq(arrived[following ^ near], near)
        across[distance] = along_head(arrived[distance])
        beside[distance] = along_inner(arrived[distance])
        beside_across[before] = along_inner(across[before])
        second = (across[before], beside_across[before])
        waiting = [(arrived[before], beside[before]), second] if place == 1 else [second]
        visits = [(before, waiting), (distance, [(arrived[distance], beside[distance])])]
        found = attend(acc, visits, int(following is None))
        acc, tops = found[:n], found[n:]
    beside_across[distances[-1]] = along_inner(across[distances[-1]])

    pairs = [(arrived[d], beside[d], across[d], beside_across[d]) for d in distances]
    flat = [part for pair in pairs for part in pair]
    attended, log_total = pl.pallas_call(
        functools.partial(last_kernel, coef, distances, n),
        in_specs=[scalars] + [whole] * (2 * n + 3) + [anywhere] * (2 + len(flat)),
        out_specs=[anywhere, anywhere],
        out_shape=[jax.ShapeDtypeStruct(query_rows.shape, query_rows.dtype), top_shape],
        scratch_shapes=[
            pltpu.VMEM(query_rows.shape, query_rows.dtype),
            pltpu.VMEM(top_shape.shape, jnp.float32),
        ]
        + kv_buffers
        + [
            pltpu.VMEM((rows, width), jnp.float32),
            pltpu.VMEM((2, heads, rows, width), jnp.float32),
            pltpu.VMEM((2, heads, rows, 2 * width), jnp.float32),
            pltpu.SemaphoreType.DMA,
            pltpu.SemaphoreType.DMA((heads,)),
        ],
        cost_estimate=cost(1, 7_000_000),
        compiler_params=params,
        name="last_visitor",
    )(sb_here, *qx, *acc, *tops, *flat[-2:], in_hbm[1], in_hbm[2], *flat)
    return attended, log_total


def solution(mesh):
    placed = (
        P(("groups", "seq"), "inner", "head"),
        P(("groups", "seq"), None, None),
        P(("groups", "seq"), None, None),
        P(),
    )
    return jax.shard_map(
        body,
        mesh=mesh,
        in_specs=placed,
        out_specs=(P(("groups", "seq"), "inner", "head"), P(("groups", "seq"), "head", "inner")),
        check_vma=False,
    )
```

```python
import functools
import math

import jax
import jax.numpy as jnp
from jax import lax
from jax.experimental import pallas as pl
from jax.experimental.pallas import tpu as pltpu
from jax.sharding import PartitionSpec as P

NEG = -1e30
SUM_LIMIT = 1e36
LO, HI = 0, 1
TILE = 256


def score_dot(q, k):
    return lax.dot_general(q, k, (((1,), (1,)), ((), ())), preferred_element_type=jnp.float32)


def value_dot(p, v):
    return jnp.dot(p, v, preferred_element_type=jnp.float32)


def widen(x, width):
    return jnp.concatenate([x] * (width // x.shape[1]), axis=1)


def with_ones(x):
    return jnp.concatenate([x, jnp.ones_like(x)], axis=1)


def is_power(count):
    return count & (count - 1) == 0


def source_of(index, distance, count):
    if is_power(count):
        return index ^ distance
    return lax.rem(index - distance + count, count)


def blocks_of(sb, seq_index):
    b0, b1 = sb[2 * seq_index], sb[2 * seq_index + 1]
    return jnp.where(b1 > b0, 1, 0), jnp.minimum(b0, b1), jnp.maximum(b0, b1)


def minus_columns(top):
    high = top.astype(jnp.bfloat16)
    rest = top - high.astype(jnp.float32)
    middle = rest.astype(jnp.bfloat16)
    low = (rest - middle.astype(jnp.float32)).astype(jnp.bfloat16)
    lane = lax.broadcasted_iota(jnp.int32, top.shape, 1)
    high, middle, low = (x.astype(jnp.float32) for x in (high, middle, low))
    picked = jnp.where(lane == 0, high, jnp.where(lane == 1, middle, jnp.where(lane == 2, low, 0.0)))
    return (-picked).astype(jnp.bfloat16)


def key_tiles(count):
    return [(start, min(TILE, count - start)) for start in range(0, count, TILE)]


def load_kernel(q_hbm, k_hbm, v_hbm, sb_hbm, piece, q_out, k_out, v_out, sb_out, sems):
    half = piece.shape[1]
    rows, width = q_hbm.shape[1], q_out.shape[2]
    inner = lax.axis_index("inner")
    mine = pl.ds(pl.multiple_of(lax.rem(lax.axis_index("head"), 2) * half, half), half)
    for value, src in enumerate((k_hbm, v_hbm)):

        @pl.when(inner == value)
        def _():
            pltpu.make_async_copy(src.at[:, mine], piece, sems.at[0]).start()

    copies = [pltpu.make_async_copy(k_hbm.at[:, mine], piece, sems.at[0])]
    pairs = [(k_hbm, k_out), (v_hbm, v_out), (sb_hbm, sb_out)]
    for h in range(q_hbm.shape[2] // width):
        pairs.append((q_hbm.at[:, :, pl.ds(h * width, width)], q_out.at[:, pl.ds(h * rows, rows)]))
    for place, (src, dst) in enumerate(pairs):
        copy = pltpu.make_async_copy(src, dst, sems.at[1 + place])
        copy.start()
        copies.append(copy)
    for copy in copies:
        copy.wait()


def scaled_exp(coef, s):
    return jnp.exp2(s * coef).astype(jnp.bfloat16)


def in_turn(coef, chunks, score, finish):
    ready = score(*chunks[0])
    for place, chunk in enumerate(chunks):
        now = ready
        if place + 1 < len(chunks):
            ready = score(*chunks[place + 1])
        finish(scaled_exp(coef, now), *chunk)


def local_kernel(coef, rows, sb, q_ref, k_ref, v_ref, qx_ref, acc_ref):
    _, all_rows, width = q_ref.shape
    block_len = k_ref.shape[1]
    heads = all_rows // rows
    hi, _, _ = blocks_of(sb, lax.axis_index("seq"))
    slots = {HI: hi, LO: 1 - hi}
    tiles = key_tiles(block_len)

    def keys(slot, start, size):
        return k_ref[slot, pl.ds(start, size)]

    def values(slot, start, size):
        return with_ones(v_ref[slot, pl.ds(start, size)])

    def masked(order, start, size):
        row = lax.broadcasted_iota(jnp.int32, (rows, size), 0) + lax.axis_index("inner") * rows
        col = lax.broadcasted_iota(jnp.int32, (rows, size), 1) + start
        bias = jnp.where(col <= row, 0.0, NEG)
        s = score_dot(q_ref[slots[order]], keys(slots[order], start, size))
        return s + jnp.concatenate([bias] * heads, axis=0)

    def highest(scores):
        parts = [s[:, at : at + width] for s in scores for at in range(0, s.shape[1], width)]
        top = functools.reduce(jnp.maximum, parts)
        return jnp.broadcast_to(jnp.max(top, axis=1, keepdims=True), (all_rows, width))

    def settle(order, scores, top):
        total = None
        for (start, size), s in zip(tiles, scores):
            p = scaled_exp(coef, s - widen(top, size))
            part = value_dot(p, values(slots[order], start, size))
            total = part if total is None else total + part
        acc_ref[order] = total

    def extend(order, top):
        qx_ref[order] = jnp.concatenate([q_ref[slots[order]], minus_columns(top)], axis=1)

    diag = [masked(HI, *tile) for tile in tiles]
    top = highest(diag)
    extend(HI, top)
    low = [masked(LO, *tile) for tile in tiles]
    settle(HI, diag, top)
    top = highest(low)
    extend(LO, top)

    def score(start, size):
        return score_dot(qx_ref[HI], with_ones(keys(slots[LO], start, size)))

    def finish(p, start, size):
        acc_ref[HI] += value_dot(p, values(slots[LO], start, size))

    settle(LO, low, top)
    in_turn(coef, tiles, score, finish)


def place_pieces(parts, own_half, k_buf, v_buf):
    inner = lax.axis_index("inner")
    for value, (own_buf, twin_buf) in enumerate([(k_buf, v_buf), (v_buf, k_buf)]):

        @pl.when(inner == value)
        def _():
            for turn, pair in enumerate(parts):
                half = own_half if turn == 0 else 1 - own_half
                for piece, buf in zip(pair, (own_buf, twin_buf)):
                    size = piece.shape[1]
                    for slot in range(2):
                        start = pl.multiple_of((slot * len(parts) + half) * size, size)
                        buf[pl.ds(start, size)] = piece[slot]


def visit(coef, distance, parts, sb, qx_ref, acc_ref, buffers, group, store):
    all_rows = qx_ref.shape[1]
    count = lax.axis_size("seq")
    me = lax.axis_index("seq")
    k_buf, v_buf = buffers[:2] if len(parts) == 2 else buffers[2:]
    own_half = lax.rem(lax.axis_index("head"), 2) if len(parts) == 2 else 0
    place_pieces(parts, own_half, k_buf, v_buf)
    keys_here = k_buf.shape[0] // 2

    _, _, top_block = blocks_of(sb, me)
    other_hi, _, other_top = blocks_of(sb, source_of(me, distance, count))
    above = top_block > other_top

    def run(orders, first_key, key_count):
        tiles = key_tiles(key_count)
        totals = {}

        def chosen(buf, start, size):
            return with_ones(buf[pl.ds(first_key + start, size)])

        def score(order, row, start, size):
            return score_dot(qx_ref[order, pl.ds(row, group)], chosen(k_buf, start, size))

        def finish(p, order, row, start, size):
            part = value_dot(p, chosen(v_buf, start, size))
            before = acc_ref[order, pl.ds(row, group)] if start == 0 else totals[order, row]
            totals[order, row] = before + part
            if start == tiles[-1][0]:
                store(order, row, totals[order, row])

        chunks = [(order, row, *tile) for row in range(0, all_rows, group) for order in orders for tile in tiles]
        in_turn(coef, chunks, score, finish)

    @pl.when(above)
    def _():
        for row in range(0, all_rows, group):
            store(LO, row, None)
        run((HI,), 0, 2 * keys_here)

    @pl.when(jnp.logical_not(above))
    def _():
        run((HI, LO), pl.multiple_of((1 - other_hi) * keys_here, keys_here), keys_here)


def first_row(x):
    return jnp.transpose(x)[:1]


def middle_kernel(coef, visits, rows, sb, qx_ref, acc_in, *refs):
    taken = []
    for distance, pairs in visits:
        taken.append((distance, [refs[2 * i : 2 * i + 2] for i in range(pairs)]))
        refs = refs[2 * pairs :]
    acc_ref, tops, buffers = refs[0], refs[1:-4], refs[-4:]
    _, all_rows, double = qx_ref.shape

    def store(order, row, value):
        if value is not None:
            acc_ref[order, pl.ds(row, all_rows)] = value

    for distance, parts in taken:
        visit(coef, distance, parts, sb, qx_ref, acc_ref, buffers, all_rows, store)
    for top_ref in tops:
        for order in (LO, HI):
            for h in range(all_rows // rows):
                columns = qx_ref[order, pl.ds(h * rows, rows), pl.ds(double // 2, double // 2)]
                columns = jnp.transpose(columns.astype(jnp.float32))
                top_ref[order, h : h + 1, :] = -(columns[0:1] + columns[1:2] + columns[2:3])


def last_kernel(coef, distances, sb, qx_ref, acc_ref, top_ref, *refs):
    parts, every, rest = [refs[:2]], refs[2 : 4 * len(distances) + 4], refs[4 * len(distances) + 4 :]
    out_hbm, lse_hbm, out_buf, lse_ref, *buffers, worst, run_top, run_acc, sem, out_sems = rest
    rows = out_buf.shape[1]
    all_rows = qx_ref.shape[1]
    heads = all_rows // rows
    k_buf, v_buf = buffers[:2]
    block_len, width = k_buf.shape[0] // 2, k_buf.shape[1]
    half_len = block_len // 2
    count = lax.axis_size("seq")
    me = lax.axis_index("seq")
    own_half = lax.rem(lax.axis_index("head"), 2)
    inner = lax.axis_index("inner")
    hi, lo_block, hi_block = blocks_of(sb, me)
    lse_copy = pltpu.make_async_copy(lse_ref, lse_hbm, sem)

    def out_copy(h):
        columns = pl.ds(h * width, width)
        return pltpu.make_async_copy(out_buf.at[:, :, columns], out_hbm.at[:, :, columns], out_sems.at[h])

    def emit(order, h, value, top_row):
        slot = hi if order == HI else 1 - hi
        sums = value[:, width:]
        out_buf[slot, :, h * width : (h + 1) * width] = (value[:, :width] / sums).astype(out_buf.dtype)
        lse_ref[slot, h : h + 1, :] = top_row * (coef * math.log(2.0)) + jnp.log(first_row(sums))
        return sums

    worst[...] = jnp.zeros_like(worst)

    def store(order, row, value):
        group = all_rows // 2 if heads > 1 else all_rows
        if value is None:
            value = acc_ref[order, pl.ds(row, group)]
        for at in range(0, group, rows):
            h = (row + at) // rows
            sums = emit(order, h, value[at : at + rows], top_ref[order, h : h + 1, :])
            worst[...] = jnp.maximum(worst[...], sums)

    visit(coef, distances[-1], parts, sb, qx_ref, acc_ref, buffers, all_rows // 2 if heads > 1 else all_rows, store)
    for h in range(heads):
        out_copy(h).start()
    lse_copy.start()
    for h in range(heads):
        out_copy(h).wait()
    lse_copy.wait()

    @pl.when(jnp.logical_not(jnp.max(worst[...]) < SUM_LIMIT))
    def _():
        def fetch(src, dst):
            copy = pltpu.make_async_copy(src, dst, sem)
            copy.start()
            copy.wait()

        def online(source):
            @pl.loop(0, 4 * heads)
            def _(i):
                h, slot, order = i // 4, lax.rem(i, 4) // 2, lax.rem(i, 2)
                own_block = jnp.where(order == HI, hi_block, lo_block)
                shift = (own_block - sb[2 * source + slot]) * block_len + inner * rows

                @pl.when(shift + rows > 0)
                def _():
                    queries = qx_ref[order, pl.ds(pl.multiple_of(h * rows, rows), rows), pl.ds(0, width)]
                    at = pl.ds(pl.multiple_of(slot * block_len, block_len), block_len)
                    s = score_dot(queries, k_buf[at])
                    row = lax.broadcasted_iota(jnp.int32, s.shape, 0) + shift
                    allowed = lax.broadcasted_iota(jnp.int32, s.shape, 1) <= row
                    s = jnp.where(allowed, s, NEG)
                    before = run_top[order, h]
                    top = jnp.maximum(before, jnp.broadcast_to(jnp.max(s, axis=1, keepdims=True), before.shape))
                    p = jnp.where(allowed, jnp.exp2((s - widen(top, block_len)) * coef), 0.0)
                    run_top[order, h] = top
                    shrink = widen(jnp.exp2((before - top) * coef), 2 * width)
                    fresh = value_dot(p.astype(jnp.bfloat16), with_ones(v_buf[at]))
                    run_acc[order, h] = run_acc[order, h] * shrink + fresh

        run_top[...] = jnp.full_like(run_top, NEG)
        run_acc[...] = jnp.zeros_like(run_acc)
        def rows_of(slot, half):
            return pl.ds(pl.multiple_of((slot * 2 + half) * half_len, half_len), half_len)

        for slot in range(2):
            fetch(every[0].at[slot], k_buf.at[pl.ds(slot * block_len, block_len)])
            fetch(every[1].at[slot], v_buf.at[pl.ds(slot * block_len, block_len)])
        online(me)
        for place, other in enumerate(distances):
            others = every[2 + 4 * place : 6 + 4 * place]
            for value, (own_buf, twin_buf) in enumerate([(k_buf, v_buf), (v_buf, k_buf)]):

                @pl.when(inner == value)
                def _():
                    for turn in range(2):
                        half = own_half if turn == 0 else 1 - own_half
                        for slot in range(2):
                            fetch(others[2 * turn].at[slot], own_buf.at[rows_of(slot, half)])
                            fetch(others[2 * turn + 1].at[slot], twin_buf.at[rows_of(slot, half)])

            online(source_of(me, other, count))
        for h in range(heads):
            for order in (LO, HI):
                emit(order, h, run_acc[order, h], first_row(run_top[order, h]))
            out_copy(h).start()
            out_copy(h).wait()
        lse_copy.start()
        lse_copy.wait()


def body(query_rows, key_rows, value_rows, slot_block):
    _, block_len, width = key_rows.shape
    _, rows, feats = query_rows.shape
    heads = feats // width
    all_rows = heads * rows
    count = lax.axis_size("seq")
    coef = math.log2(math.e) / math.sqrt(width)
    distances = list(range(1, count))

    def along_seq(block, distance):
        if is_power(count):
            route = [(i, i ^ distance) for i in range(count)]
        else:
            route = [(i, (i + distance) % count) for i in range(count)]
        with jax.named_scope("along_seq"):
            return lax.ppermute(block, "seq", route)

    def along_head(block):
        with jax.named_scope("along_head"):
            return lax.ppermute(block, "head", [(i, i ^ 1) for i in range(lax.axis_size("head"))])

    def along_inner(block):
        with jax.named_scope("along_inner"):
            return lax.ppermute(block, "inner", [(0, 1), (1, 0)])

    whole = pl.BlockSpec(memory_space=pltpu.VMEM)
    anywhere = pl.BlockSpec(memory_space=pl.ANY)
    scalars = pl.BlockSpec(memory_space=pltpu.SMEM)
    acc_shape = jax.ShapeDtypeStruct((2, all_rows, 2 * width), jnp.float32)
    qx_shape = jax.ShapeDtypeStruct(acc_shape.shape, jnp.bfloat16)
    top_shape = jax.ShapeDtypeStruct((2, heads, rows), jnp.float32)
    params = pltpu.CompilerParams(vmem_limit_bytes=40 * 1024 * 1024)
    unit = rows * heads * block_len * width * 4
    exps = rows * heads * block_len

    def cost(units, size):
        return pl.CostEstimate(flops=int(2 * units * unit), bytes_accessed=size, transcendentals=int(units * exps))

    in_hbm = [
        pltpu.with_memory_space_constraint(x, pltpu.HBM) for x in (query_rows, key_rows, value_rows, slot_block)
    ]
    half_shape = jax.ShapeDtypeStruct((2, block_len // 2, width), key_rows.dtype)
    piece, q_here, k_here, v_here, sb_here = pl.pallas_call(
        load_kernel,
        in_specs=[anywhere] * 4,
        out_specs=[whole] * 5,
        out_shape=[half_shape, jax.ShapeDtypeStruct((2, all_rows, width), query_rows.dtype)]
        + [jax.ShapeDtypeStruct(x.shape, x.dtype) for x in in_hbm[1:]],
        scratch_shapes=[pltpu.SemaphoreType.DMA((4 + heads,))],
        cost_estimate=pl.CostEstimate(flops=0, bytes_accessed=3_000_000, transcendentals=0),
        compiler_params=params,
        name="load",
    )(*in_hbm)
    arrived, across, beside, beside_across = {}, {}, {}, {}
    for distance in distances:
        if not is_power(count) or is_power(distance):
            arrived[distance] = along_seq(piece, distance)

    qx, acc = pl.pallas_call(
        functools.partial(local_kernel, coef, rows),
        in_specs=[scalars] + [whole] * 3,
        out_specs=[whole] * 2,
        out_shape=[qx_shape, acc_shape],
        cost_estimate=cost(3, 6_000_000),
        compiler_params=params,
        name="local_part",
    )(sb_here, q_here, k_here, v_here)
    kv_buffers = [pltpu.VMEM((2 * block_len, width), jnp.bfloat16)] * 2
    kv_buffers += [pltpu.VMEM((block_len, width), jnp.bfloat16)] * 2

    def attend(acc, visits, with_tops):
        pieces = [part for _, pairs in visits for pair in pairs for part in pair]
        return pl.pallas_call(
            functools.partial(middle_kernel, coef, [(distance, len(pairs)) for distance, pairs in visits], rows),
            in_specs=[scalars] + [whole] * (2 + len(pieces)),
            out_specs=[whole] * (1 + with_tops),
            out_shape=[acc_shape] + [top_shape] * with_tops,
            scratch_shapes=kv_buffers,
            input_output_aliases={2: 0},
            cost_estimate=cost(len(pieces) / 2, 7_000_000),
            compiler_params=params,
            name=f"visitors_from_{visits[0][0]}",
        )(sb_here, qx, acc, *pieces)

    def relay(distance):
        if distance in distances and distance not in arrived:
            near = distance & -distance
            arrived[distance] = along_seq(arrived[distance ^ near], near)

    def spread(distance):
        if distance in distances:
            across[distance] = along_head(arrived[distance])
            beside[distance] = along_inner(arrived[distance])

    def own_pair(distance):
        return arrived[distance], beside[distance]

    def far_pair(distance):
        beside_across[distance] = along_inner(across[distance])
        return across[distance], beside_across[distance]

    last = distances[-1]
    first, acc = lax.optimization_barrier((dict(arrived), acc))
    arrived.update(first)
    spread(1)
    relay(3)
    spread(2)
    for distance in distances[:-1]:
        ahead = distance + 2
        tied = lax.optimization_barrier((across[distance], arrived.get(ahead), acc))
        across[distance], arrived_ahead, acc = tied
        if ahead in distances:
            arrived[ahead] = arrived_ahead
        visits = [(distance, [own_pair(distance), far_pair(distance)])]
        if distance + 1 == last:
            visits.append((last, [own_pair(last)]))
        acc, *tops = attend(acc, visits, int(distance + 1 == last))
        relay(ahead + 1)
        spread(ahead)
    across[last], acc = lax.optimization_barrier((across[last], acc))
    far_pair(last)

    pairs = [(arrived[d], beside[d], across[d], beside_across[d]) for d in distances]
    flat = [part for pair in pairs for part in pair]
    attended, log_total = pl.pallas_call(
        functools.partial(last_kernel, coef, distances),
        in_specs=[scalars] + [whole] * 5 + [anywhere] * (2 + len(flat)),
        out_specs=[anywhere, anywhere],
        out_shape=[jax.ShapeDtypeStruct(query_rows.shape, query_rows.dtype), top_shape],
        scratch_shapes=[
            pltpu.VMEM(query_rows.shape, query_rows.dtype),
            pltpu.VMEM(top_shape.shape, jnp.float32),
        ]
        + kv_buffers
        + [
            pltpu.VMEM((rows, width), jnp.float32),
            pltpu.VMEM((2, heads, rows, width), jnp.float32),
            pltpu.VMEM((2, heads, rows, 2 * width), jnp.float32),
            pltpu.SemaphoreType.DMA,
            pltpu.SemaphoreType.DMA((heads,)),
        ],
        cost_estimate=cost(1, 7_000_000),
        compiler_params=params,
        name="last_visitor",
    )(sb_here, qx, acc, *tops, *flat[-2:], in_hbm[1], in_hbm[2], *flat)
    return attended, log_total


def solution(mesh):
    placed = (
        P(("groups", "seq"), "inner", "head"),
        P(("groups", "seq"), None, None),
        P(("groups", "seq"), None, None),
        P(),
    )
    return jax.shard_map(
        body,
        mesh=mesh,
        in_specs=placed,
        out_specs=(P(("groups", "seq"), "inner", "head"), P(("groups", "seq"), "head", "inner")),
        check_vma=False,
    )
```

```python
import functools
import math

import jax
import jax.numpy as jnp
from jax import lax
from jax.experimental import pallas as pl
from jax.experimental.pallas import tpu as pltpu
from jax.sharding import PartitionSpec as P

NEG = -1e30
SUM_LIMIT = 1e36
LO, HI = 0, 1


def score_dot(q, k):
    return lax.dot_general(q, k, (((1,), (1,)), ((), ())), preferred_element_type=jnp.float32)


def value_dot(p, v):
    return jnp.dot(p, v, preferred_element_type=jnp.float32)


def widen(x, width):
    return jnp.concatenate([x] * (width // x.shape[1]), axis=1)


def with_ones(x):
    return jnp.concatenate([x, jnp.ones_like(x)], axis=1)


def is_power(count):
    return count & (count - 1) == 0


def source_of(index, distance, count):
    if is_power(count):
        return index ^ distance
    return lax.rem(index - distance + count, count)


def blocks_of(sb, seq_index):
    b0, b1 = sb[2 * seq_index], sb[2 * seq_index + 1]
    return jnp.where(b1 > b0, 1, 0), jnp.minimum(b0, b1), jnp.maximum(b0, b1)


def minus_columns(top):
    high = top.astype(jnp.bfloat16)
    rest = top - high.astype(jnp.float32)
    middle = rest.astype(jnp.bfloat16)
    low = (rest - middle.astype(jnp.float32)).astype(jnp.bfloat16)
    lane = lax.broadcasted_iota(jnp.int32, top.shape, 1)
    high, middle, low = (x.astype(jnp.float32) for x in (high, middle, low))
    picked = jnp.where(lane == 0, high, jnp.where(lane == 1, middle, jnp.where(lane == 2, low, 0.0)))
    return (-picked).astype(jnp.bfloat16)


def load_kernel(q_hbm, k_hbm, v_hbm, sb_hbm, piece, q_out, k_out, v_out, sb_out, sems):
    half = piece.shape[1]
    rows, width = q_hbm.shape[1], q_out.shape[2]
    inner = lax.axis_index("inner")
    mine = pl.ds(pl.multiple_of(lax.rem(lax.axis_index("head"), 2) * half, half), half)
    for value, src in enumerate((k_hbm, v_hbm)):

        @pl.when(inner == value)
        def _():
            pltpu.make_async_copy(src.at[:, mine], piece, sems.at[0]).start()

    copies = [pltpu.make_async_copy(k_hbm.at[:, mine], piece, sems.at[0])]
    pairs = [(k_hbm, k_out), (v_hbm, v_out), (sb_hbm, sb_out)]
    for h in range(q_hbm.shape[2] // width):
        pairs.append((q_hbm.at[:, :, pl.ds(h * width, width)], q_out.at[:, pl.ds(h * rows, rows)]))
    for place, (src, dst) in enumerate(pairs):
        copy = pltpu.make_async_copy(src, dst, sems.at[1 + place])
        copy.start()
        copies.append(copy)
    for copy in copies:
        copy.wait()


def scaled_exp(coef, s):
    return jnp.exp2(s * coef).astype(jnp.bfloat16)


def pipelined(steps, buffers, score, finish, done=None):
    even, odd = buffers
    score(0, even)
    if steps == 1:
        finish(0, even)
        return

    @pl.loop(0, steps // 2)
    def _(pair):
        first = 2 * pair
        score(first + 1, odd)
        finish(first, even)
        score(jnp.minimum(first + 2, steps - 1), even)
        finish(first + 1, odd)
        if done is not None:
            done(pair)


def sweep(coef, steps, chunk, rows, block_len, qx_ref, acc_ref, k_ref, v_ref, buffers, done=None):
    def place(i):
        order, row, start = chunk(i)
        return order, pl.ds(pl.multiple_of(row, rows), rows), pl.ds(pl.multiple_of(start, block_len), block_len)

    def score(i, buf):
        order, mine, keys = place(i)
        buf[...] = score_dot(qx_ref[order, mine], with_ones(k_ref[keys]))

    def finish(i, buf):
        order, mine, keys = place(i)
        acc_ref[order, mine] += value_dot(scaled_exp(coef, buf[...]), with_ones(v_ref[keys]))

    pipelined(steps, buffers, score, finish, done)


def diagonal_kernel(coef, rows, sb, q_ref, k_ref, v_ref, qx_ref, acc_ref, bias, *buffers):
    _, all_rows, width = q_ref.shape
    block_len = bias.shape[1]
    hi, _, _ = blocks_of(sb, lax.axis_index("seq"))
    row = lax.broadcasted_iota(jnp.int32, bias.shape, 0) + lax.axis_index("inner") * rows
    bias[...] = jnp.where(lax.broadcasted_iota(jnp.int32, bias.shape, 1) <= row, 0.0, NEG)

    def place(i):
        order = lax.rem(i, 2)
        slot = jnp.where(order == HI, hi, 1 - hi)
        return order, slot, pl.ds(pl.multiple_of(i // 2 * rows, rows), rows)

    def keys_of(slot):
        return pl.ds(pl.multiple_of(slot * block_len, block_len), block_len)

    def score(i, buf):
        _, slot, mine = place(i)
        buf[...] = score_dot(q_ref[slot, mine], k_ref[keys_of(slot)]) + bias[...]

    def finish(i, buf):
        order, slot, mine = place(i)
        parts = [buf[:, at : at + width] for at in range(0, block_len, width)]
        top = jnp.max(functools.reduce(jnp.maximum, parts), axis=1, keepdims=True)
        top = jnp.broadcast_to(top, (rows, width))
        p = scaled_exp(coef, buf[...] - widen(top, block_len))
        acc_ref[order, mine] = value_dot(p, with_ones(v_ref[keys_of(slot)]))
        qx_ref[order, mine] = jnp.concatenate([q_ref[slot, mine], minus_columns(top)], axis=1)

    pipelined(2 * all_rows // rows, buffers, score, finish)


def past_kernel(coef, rows, sb, qx_ref, acc_in, k_ref, v_ref, acc_ref, *buffers):
    block_len = buffers[0].shape[1]
    hi, _, _ = blocks_of(sb, lax.axis_index("seq"))

    def chunk(i):
        return HI, i * rows, (1 - hi) * block_len

    sweep(coef, qx_ref.shape[1] // rows, chunk, rows, block_len, qx_ref, acc_ref, k_ref, v_ref, buffers)


def place_pieces(parts, k_buf, v_buf):
    inner = lax.axis_index("inner")
    own_half = lax.rem(lax.axis_index("head"), 2)
    for value, (own_buf, twin_buf) in enumerate([(k_buf, v_buf), (v_buf, k_buf)]):

        @pl.when(inner == value)
        def _():
            for turn in range(2):
                half = own_half if turn == 0 else 1 - own_half
                for piece, buf in zip(parts[2 * turn : 2 * turn + 2], (own_buf, twin_buf)):
                    size = piece.shape[1]
                    for slot in range(2):
                        buf[pl.ds(pl.multiple_of((slot * 2 + half) * size, size), size)] = piece[slot]


def visit(coef, distance, rows, parts, sb, qx_ref, acc_ref, k_buf, v_buf, buffers, done=None):
    me = lax.axis_index("seq")
    block_len = buffers[0].shape[1]
    place_pieces(parts, k_buf, v_buf)
    _, _, top_block = blocks_of(sb, me)
    other_hi, _, other_top = blocks_of(sb, source_of(me, distance, lax.axis_size("seq")))
    above = top_block > other_top

    def chunk(i):
        turn = lax.rem(i, 2)
        order = jnp.where(above, HI, turn)
        slot = jnp.where(above, turn, 1 - other_hi)
        return order, i // 2 * rows, slot * block_len

    steps = 2 * qx_ref.shape[1] // rows
    sweep(coef, steps, chunk, rows, block_len, qx_ref, acc_ref, k_buf, v_buf, buffers, done)


def first_row(x):
    return jnp.transpose(x)[:1]


def middle_kernel(coef, distance, rows, sb, qx_ref, acc_in, p0, p1, p2, p3, acc_ref, *refs):
    *tops, k_buf, v_buf, even, odd = refs
    _, all_rows, double = qx_ref.shape
    visit(coef, distance, rows, (p0, p1, p2, p3), sb, qx_ref, acc_ref, k_buf, v_buf, (even, odd))
    for top_ref in tops:
        for order in (LO, HI):
            for h in range(all_rows // rows):
                columns = qx_ref[order, pl.ds(h * rows, rows), pl.ds(double // 2, double // 2)]
                columns = jnp.transpose(columns.astype(jnp.float32))
                top_ref[order, h : h + 1, :] = -(columns[0:1] + columns[1:2] + columns[2:3])


def last_kernel(coef, distances, sb, qx_ref, acc_ref, top_ref, *refs):
    parts, every, rest = refs[:4], refs[4 : 4 * len(distances) + 6], refs[4 * len(distances) + 6 :]
    out_hbm, lse_hbm, out_buf, lse_ref, k_buf, v_buf, even, odd, worst, run_top, run_acc, sem, out_sems = rest
    rows = out_buf.shape[1]
    all_rows = qx_ref.shape[1]
    heads = all_rows // rows
    block_len, width = k_buf.shape[0] // 2, k_buf.shape[1]
    half_len = block_len // 2
    count = lax.axis_size("seq")
    me = lax.axis_index("seq")
    own_half = lax.rem(lax.axis_index("head"), 2)
    inner = lax.axis_index("inner")
    hi, lo_block, hi_block = blocks_of(sb, me)
    lse_copy = pltpu.make_async_copy(lse_ref, lse_hbm, sem)

    def out_copy(h):
        columns = pl.ds(pl.multiple_of(h * width, width), width)
        return pltpu.make_async_copy(out_buf.at[:, :, columns], out_hbm.at[:, :, columns], out_sems.at[h])

    def emit(order, h, value, top_row):
        slot = hi if order == HI else 1 - hi
        sums = value[:, width:]
        columns = pl.ds(pl.multiple_of(h * width, width), width)
        out_buf[slot, :, columns] = (value[:, :width] / sums).astype(out_buf.dtype)
        lse_ref[slot, pl.ds(h, 1), :] = top_row * (coef * math.log(2.0)) + jnp.log(first_row(sums))
        return sums

    worst[...] = jnp.zeros_like(worst)

    def done(h):
        mine = pl.ds(pl.multiple_of(h * rows, rows), rows)
        for order in (LO, HI):
            sums = emit(order, h, acc_ref[order, mine], top_ref[order, pl.ds(h, 1), :])
            worst[...] = jnp.maximum(worst[...], sums)
        out_copy(h).start()

    visit(coef, distances[-1], rows, parts, sb, qx_ref, acc_ref, k_buf, v_buf, (even, odd), done)
    lse_copy.start()
    for h in range(heads):
        out_copy(h).wait()
    lse_copy.wait()

    @pl.when(jnp.logical_not(jnp.max(worst[...]) < SUM_LIMIT))
    def _():
        def fetch(src, dst):
            copy = pltpu.make_async_copy(src, dst, sem)
            copy.start()
            copy.wait()

        def online(source):
            @pl.loop(0, 4 * heads)
            def _(i):
                h, slot, order = i // 4, lax.rem(i, 4) // 2, lax.rem(i, 2)
                own_block = jnp.where(order == HI, hi_block, lo_block)
                shift = (own_block - sb[2 * source + slot]) * block_len + inner * rows

                @pl.when(shift + rows > 0)
                def _():
                    queries = qx_ref[order, pl.ds(pl.multiple_of(h * rows, rows), rows), pl.ds(0, width)]
                    at = pl.ds(pl.multiple_of(slot * block_len, block_len), block_len)
                    s = score_dot(queries, k_buf[at])
                    row = lax.broadcasted_iota(jnp.int32, s.shape, 0) + shift
                    allowed = lax.broadcasted_iota(jnp.int32, s.shape, 1) <= row
                    s = jnp.where(allowed, s, NEG)
                    before = run_top[order, h]
                    top = jnp.maximum(before, jnp.broadcast_to(jnp.max(s, axis=1, keepdims=True), before.shape))
                    p = jnp.where(allowed, jnp.exp2((s - widen(top, block_len)) * coef), 0.0)
                    run_top[order, h] = top
                    shrink = widen(jnp.exp2((before - top) * coef), 2 * width)
                    fresh = value_dot(p.astype(jnp.bfloat16), with_ones(v_buf[at]))
                    run_acc[order, h] = run_acc[order, h] * shrink + fresh

        run_top[...] = jnp.full_like(run_top, NEG)
        run_acc[...] = jnp.zeros_like(run_acc)
        def rows_of(slot, half):
            return pl.ds(pl.multiple_of((slot * 2 + half) * half_len, half_len), half_len)

        for slot in range(2):
            fetch(every[0].at[slot], k_buf.at[pl.ds(slot * block_len, block_len)])
            fetch(every[1].at[slot], v_buf.at[pl.ds(slot * block_len, block_len)])
        online(me)
        for place, other in enumerate(distances):
            others = every[2 + 4 * place : 6 + 4 * place]
            for value, (own_buf, twin_buf) in enumerate([(k_buf, v_buf), (v_buf, k_buf)]):

                @pl.when(inner == value)
                def _():
                    for turn in range(2):
                        half = own_half if turn == 0 else 1 - own_half
                        for slot in range(2):
                            fetch(others[2 * turn].at[slot], own_buf.at[rows_of(slot, half)])
                            fetch(others[2 * turn + 1].at[slot], twin_buf.at[rows_of(slot, half)])

            online(source_of(me, other, count))
        for h in range(heads):
            for order in (LO, HI):
                emit(order, h, run_acc[order, h], first_row(run_top[order, h]))
            out_copy(h).start()
            out_copy(h).wait()
        lse_copy.start()
        lse_copy.wait()


def body(query_rows, key_rows, value_rows, slot_block):
    _, block_len, width = key_rows.shape
    _, rows, feats = query_rows.shape
    heads = feats // width
    all_rows = heads * rows
    count = lax.axis_size("seq")
    coef = math.log2(math.e) / math.sqrt(width)
    distances = list(range(1, count))

    def along_seq(block, distance):
        if is_power(count):
            route = [(i, i ^ distance) for i in range(count)]
        else:
            route = [(i, (i + distance) % count) for i in range(count)]
        with jax.named_scope("along_seq"):
            return lax.ppermute(block, "seq", route)

    def along_head(block):
        with jax.named_scope("along_head"):
            return lax.ppermute(block, "head", [(i, i ^ 1) for i in range(lax.axis_size("head"))])

    def along_inner(block):
        with jax.named_scope("along_inner"):
            return lax.ppermute(block, "inner", [(0, 1), (1, 0)])

    whole = pl.BlockSpec(memory_space=pltpu.VMEM)
    anywhere = pl.BlockSpec(memory_space=pl.ANY)
    scalars = pl.BlockSpec(memory_space=pltpu.SMEM)
    acc_shape = jax.ShapeDtypeStruct((2, all_rows, 2 * width), jnp.float32)
    qx_shape = jax.ShapeDtypeStruct(acc_shape.shape, jnp.bfloat16)
    top_shape = jax.ShapeDtypeStruct((2, heads, rows), jnp.float32)
    params = pltpu.CompilerParams(vmem_limit_bytes=40 * 1024 * 1024)
    unit = rows * heads * block_len * width * 4
    exps = rows * heads * block_len

    def cost(units, size):
        return pl.CostEstimate(flops=int(2 * units * unit), bytes_accessed=size, transcendentals=int(units * exps))

    in_hbm = [
        pltpu.with_memory_space_constraint(x, pltpu.HBM) for x in (query_rows, key_rows, value_rows, slot_block)
    ]
    half_shape = jax.ShapeDtypeStruct((2, block_len // 2, width), key_rows.dtype)
    piece, q_here, k_here, v_here, sb_here = pl.pallas_call(
        load_kernel,
        in_specs=[anywhere] * 4,
        out_specs=[whole] * 5,
        out_shape=[half_shape, jax.ShapeDtypeStruct((2, all_rows, width), query_rows.dtype)]
        + [jax.ShapeDtypeStruct(x.shape, x.dtype) for x in in_hbm[1:]],
        scratch_shapes=[pltpu.SemaphoreType.DMA((4 + heads,))],
        cost_estimate=pl.CostEstimate(flops=0, bytes_accessed=3_000_000, transcendentals=0),
        compiler_params=params,
        name="load",
    )(*in_hbm)
    arrived, across, beside, beside_across = {}, {}, {}, {}
    for distance in distances:
        if not is_power(count) or is_power(distance):
            arrived[distance] = along_seq(piece, distance)

    k_flat, v_flat = (x.reshape(2 * block_len, width) for x in (k_here, v_here))
    score_buffers = [pltpu.VMEM((rows, block_len), jnp.float32)] * 2
    qx, acc = pl.pallas_call(
        functools.partial(diagonal_kernel, coef, rows),
        in_specs=[scalars] + [whole] * 3,
        out_specs=[whole] * 2,
        out_shape=[qx_shape, acc_shape],
        scratch_shapes=[pltpu.VMEM((rows, block_len), jnp.float32)] + score_buffers,
        cost_estimate=cost(2, 6_000_000),
        compiler_params=params,
        name="diagonal",
    )(sb_here, q_here, k_flat, v_flat)
    kv_buffers = [pltpu.VMEM((2 * block_len, width), jnp.bfloat16)] * 2

    def spread(distance):
        if distance in distances:
            across[distance] = along_head(arrived[distance])
            beside[distance] = along_inner(arrived[distance])

    def relay(distance):
        if distance in distances and distance not in arrived:
            near = distance & -distance
            arrived[distance] = along_seq(arrived[distance ^ near], near)

    def attend(acc, distance, with_tops):
        return pl.pallas_call(
            functools.partial(middle_kernel, coef, distance, rows),
            in_specs=[scalars] + [whole] * 6,
            out_specs=[whole] * (1 + with_tops),
            out_shape=[acc_shape] + [top_shape] * with_tops,
            scratch_shapes=kv_buffers + score_buffers,
            input_output_aliases={2: 0},
            cost_estimate=cost(2, 7_000_000),
            compiler_params=params,
            name=f"visitor_{distance}",
        )(sb_here, qx, acc, arrived[distance], beside[distance], across[distance], beside_across[distance])

    last = distances[-1]
    arrived[1], acc = lax.optimization_barrier((arrived[1], acc))
    spread(1)
    acc = pl.pallas_call(
        functools.partial(past_kernel, coef, rows),
        in_specs=[scalars] + [whole] * 4,
        out_specs=whole,
        out_shape=acc_shape,
        scratch_shapes=score_buffers,
        input_output_aliases={2: 0},
        cost_estimate=cost(1, 6_000_000),
        compiler_params=params,
        name="past",
    )(sb_here, qx, acc, k_flat, v_flat)
    for distance in distances[:-1]:
        following = distance + 1
        tied = lax.optimization_barrier((across[distance], arrived[following], acc))
        across[distance], arrived[following], acc = tied
        relay(following + 1)
        spread(following)
        beside_across[distance] = along_inner(across[distance])
        acc, *tops = attend(acc, distance, int(following == last))
    across[last], acc = lax.optimization_barrier((across[last], acc))
    beside_across[last] = along_inner(across[last])

    flat = [part[d] for d in distances for part in (arrived, beside, across, beside_across)]
    attended, log_total = pl.pallas_call(
        functools.partial(last_kernel, coef, distances),
        in_specs=[scalars] + [whole] * 7 + [anywhere] * (2 + len(flat)),
        out_specs=[anywhere, anywhere],
        out_shape=[jax.ShapeDtypeStruct(query_rows.shape, query_rows.dtype), top_shape],
        scratch_shapes=[
            pltpu.VMEM(query_rows.shape, query_rows.dtype),
            pltpu.VMEM(top_shape.shape, jnp.float32),
        ]
        + kv_buffers
        + score_buffers
        + [
            pltpu.VMEM((rows, width), jnp.float32),
            pltpu.VMEM((2, heads, rows, width), jnp.float32),
            pltpu.VMEM((2, heads, rows, 2 * width), jnp.float32),
            pltpu.SemaphoreType.DMA,
            pltpu.SemaphoreType.DMA((heads,)),
        ],
        cost_estimate=cost(1, 7_000_000),
        compiler_params=params,
        name="last_visitor",
    )(sb_here, qx, acc, *tops, *flat[-4:], in_hbm[1], in_hbm[2], *flat)
    return attended, log_total


def solution(mesh):
    placed = (
        P(("groups", "seq"), "inner", "head"),
        P(("groups", "seq"), None, None),
        P(("groups", "seq"), None, None),
        P(),
    )
    return jax.shard_map(
        body,
        mesh=mesh,
        in_specs=placed,
        out_specs=(P(("groups", "seq"), "inner", "head"), P(("groups", "seq"), "head", "inner")),
        check_vma=False,
    )
```

```python
import functools
import math

import jax
import jax.numpy as jnp
from jax import lax
from jax.experimental import pallas as pl
from jax.experimental.pallas import tpu as pltpu
from jax.sharding import PartitionSpec as P

NEG = -1e30
SUM_LIMIT = 1e36
LO, HI = 0, 1
TILE = 256


def score_dot(q, k):
    return lax.dot_general(q, k, (((1,), (1,)), ((), ())), preferred_element_type=jnp.float32)


def flat_dot(q, k_turned):
    return jnp.dot(q, k_turned, preferred_element_type=jnp.float32)


def value_dot(p, v):
    return jnp.dot(p, v, preferred_element_type=jnp.float32)


def widen(x, width):
    return jnp.concatenate([x] * (width // x.shape[1]), axis=1)


def with_ones(x):
    return jnp.concatenate([x, jnp.ones_like(x)], axis=1)


def over_ones(x):
    return jnp.concatenate([x, jnp.ones_like(x)], axis=0)


def is_power(count):
    return count & (count - 1) == 0


def source_of(index, distance, count):
    if is_power(count):
        return index ^ distance
    return lax.rem(index - distance + count, count)


def blocks_of(sb, seq_index):
    b0, b1 = sb[2 * seq_index], sb[2 * seq_index + 1]
    return jnp.where(b1 > b0, 1, 0), jnp.minimum(b0, b1), jnp.maximum(b0, b1)


def minus_columns(top):
    high = top.astype(jnp.bfloat16)
    rest = top - high.astype(jnp.float32)
    middle = rest.astype(jnp.bfloat16)
    low = (rest - middle.astype(jnp.float32)).astype(jnp.bfloat16)
    lane = lax.broadcasted_iota(jnp.int32, top.shape, 1)
    high, middle, low = (x.astype(jnp.float32) for x in (high, middle, low))
    picked = jnp.where(lane == 0, high, jnp.where(lane == 1, middle, jnp.where(lane == 2, low, 0.0)))
    return (-picked).astype(jnp.bfloat16)


def key_tiles(count):
    return [(start, min(TILE, count - start)) for start in range(0, count, TILE)]


def load_kernel(q_hbm, k_hbm, v_hbm, sb_hbm, piece, q_out, k_out, v_out, sb_out, sems):
    half = piece.shape[1]
    rows, width = q_hbm.shape[1], q_out.shape[2]
    inner = lax.axis_index("inner")
    mine = pl.ds(pl.multiple_of(lax.rem(lax.axis_index("head"), 2) * half, half), half)
    for value, src in enumerate((k_hbm, v_hbm)):

        @pl.when(inner == value)
        def _():
            pltpu.make_async_copy(src.at[:, mine], piece, sems.at[0]).start()

    copies = [pltpu.make_async_copy(k_hbm.at[:, mine], piece, sems.at[0])]
    pairs = [(k_hbm, k_out), (v_hbm, v_out), (sb_hbm, sb_out)]
    for h in range(q_hbm.shape[2] // width):
        pairs.append((q_hbm.at[:, :, pl.ds(h * width, width)], q_out.at[:, pl.ds(h * rows, rows)]))
    for place, (src, dst) in enumerate(pairs):
        copy = pltpu.make_async_copy(src, dst, sems.at[1 + place])
        copy.start()
        copies.append(copy)
    for copy in copies:
        copy.wait()


def scaled_exp(coef, s):
    return jnp.exp2(s * coef).astype(jnp.bfloat16)


def in_turn(coef, chunks, score, finish):
    ready = score(*chunks[0])
    for place, chunk in enumerate(chunks):
        now = ready
        if place + 1 < len(chunks):
            ready = score(*chunks[place + 1])
        finish(scaled_exp(coef, now), *chunk)


def local_kernel(coef, rows, sb, q_ref, k_ref, v_ref, qx_ref, acc_ref, turned):
    _, all_rows, width = q_ref.shape
    block_len = k_ref.shape[1]
    heads = all_rows // rows
    hi, _, _ = blocks_of(sb, lax.axis_index("seq"))
    slots = {HI: hi, LO: 1 - hi}
    tiles = key_tiles(block_len)

    for order in (HI, LO):
        turned[order] = jnp.transpose(k_ref[slots[order]])

    def keys(order, start, size):
        return turned[order, :, start : start + size]

    def values(slot, start, size):
        return with_ones(v_ref[slot, pl.ds(start, size)])

    def masked(order, start, size):
        row = lax.broadcasted_iota(jnp.int32, (rows, size), 0) + lax.axis_index("inner") * rows
        col = lax.broadcasted_iota(jnp.int32, (rows, size), 1) + start
        bias = jnp.where(col <= row, 0.0, NEG)
        s = flat_dot(q_ref[slots[order]], keys(order, start, size))
        return s + jnp.concatenate([bias] * heads, axis=0)

    def highest(scores):
        parts = [s[:, at : at + width] for s in scores for at in range(0, s.shape[1], width)]
        top = functools.reduce(jnp.maximum, parts)
        return jnp.broadcast_to(jnp.max(top, axis=1, keepdims=True), (all_rows, width))

    def settle(order, scores, top):
        total = None
        for (start, size), s in zip(tiles, scores):
            p = scaled_exp(coef, s - widen(top, size))
            part = value_dot(p, values(slots[order], start, size))
            total = part if total is None else total + part
        acc_ref[order] = total

    def extend(order, top):
        qx_ref[order] = jnp.concatenate([q_ref[slots[order]], minus_columns(top)], axis=1)

    diag = [masked(HI, *tile) for tile in tiles]
    top = highest(diag)
    extend(HI, top)
    low = [masked(LO, *tile) for tile in tiles]
    settle(HI, diag, top)
    top = highest(low)
    extend(LO, top)

    def score(start, size):
        return flat_dot(qx_ref[HI], over_ones(keys(LO, start, size)))

    def finish(p, start, size):
        acc_ref[HI] += value_dot(p, values(slots[LO], start, size))

    settle(LO, low, top)
    in_turn(coef, tiles, score, finish)


def place_pieces(parts, k_buf, v_buf, turned):
    inner = lax.axis_index("inner")
    own_half = lax.rem(lax.axis_index("head"), 2)
    for value, (own_buf, twin_buf) in enumerate([(k_buf, v_buf), (v_buf, k_buf)]):

        @pl.when(inner == value)
        def _():
            for turn in range(2):
                half = own_half if turn == 0 else 1 - own_half
                for piece, buf in zip(parts[2 * turn : 2 * turn + 2], (own_buf, twin_buf)):
                    size = piece.shape[1]
                    for slot in range(2):
                        buf[pl.ds(pl.multiple_of((slot * 2 + half) * size, size), size)] = piece[slot]

    turned[...] = jnp.transpose(k_buf[...])


def visit(coef, distance, parts, sb, qx_ref, acc_ref, buffers, group, store):
    all_rows = qx_ref.shape[1]
    count = lax.axis_size("seq")
    me = lax.axis_index("seq")
    k_buf, v_buf, turned = buffers
    place_pieces(parts, k_buf, v_buf, turned)
    keys_here = k_buf.shape[0] // 2

    _, _, top_block = blocks_of(sb, me)
    other_hi, _, other_top = blocks_of(sb, source_of(me, distance, count))
    above = top_block > other_top

    def run(orders, first_key, key_count):
        tiles = key_tiles(key_count)
        totals = {}

        def keys(start, size):
            at = first_key + start
            at = at if isinstance(at, int) else pl.multiple_of(at, 128)
            return over_ones(turned[:, pl.ds(at, size)])

        def values(start, size):
            return with_ones(v_buf[pl.ds(first_key + start, size)])

        def score(order, row, start, size):
            return flat_dot(qx_ref[order, pl.ds(row, group)], keys(start, size))

        def finish(p, order, row, start, size):
            part = value_dot(p, values(start, size))
            before = acc_ref[order, pl.ds(row, group)] if start == 0 else totals[order, row]
            totals[order, row] = before + part
            if start == tiles[-1][0]:
                store(order, row, totals[order, row])

        chunks = [(order, row, *tile) for row in range(0, all_rows, group) for order in orders for tile in tiles]
        in_turn(coef, chunks, score, finish)

    @pl.when(above)
    def _():
        for row in range(0, all_rows, group):
            store(LO, row, None)
        run((HI,), 0, 2 * keys_here)

    @pl.when(jnp.logical_not(above))
    def _():
        run((HI, LO), pl.multiple_of((1 - other_hi) * keys_here, keys_here), keys_here)


def first_row(x):
    return jnp.transpose(x)[:1]


def middle_kernel(coef, visits, rows, sb, qx_ref, acc_in, *refs):
    pieces, (acc_ref, *tops), buffers = refs[: 4 * len(visits)], refs[4 * len(visits) : -3], refs[-3:]
    _, all_rows, double = qx_ref.shape

    def store(order, row, value):
        if value is not None:
            acc_ref[order, pl.ds(row, all_rows)] = value

    for place, distance in enumerate(visits):
        parts = pieces[4 * place : 4 * place + 4]
        visit(coef, distance, parts, sb, qx_ref, acc_ref, buffers, all_rows, store)
    for top_ref in tops:
        for order in (LO, HI):
            for h in range(all_rows // rows):
                columns = qx_ref[order, pl.ds(h * rows, rows), pl.ds(double // 2, double // 2)]
                columns = jnp.transpose(columns.astype(jnp.float32))
                top_ref[order, h : h + 1, :] = -(columns[0:1] + columns[1:2] + columns[2:3])


def last_kernel(coef, distances, sb, qx_ref, acc_ref, top_ref, *refs):
    parts, every, rest = refs[:4], refs[4 : 4 * len(distances) + 6], refs[4 * len(distances) + 6 :]
    out_hbm, lse_hbm, out_buf, lse_ref, *buffers, worst, run_top, run_acc, sem, out_sems = rest
    rows = out_buf.shape[1]
    all_rows = qx_ref.shape[1]
    heads = all_rows // rows
    k_buf, v_buf, _ = buffers
    block_len, width = k_buf.shape[0] // 2, k_buf.shape[1]
    half_len = block_len // 2
    count = lax.axis_size("seq")
    me = lax.axis_index("seq")
    own_half = lax.rem(lax.axis_index("head"), 2)
    inner = lax.axis_index("inner")
    hi, lo_block, hi_block = blocks_of(sb, me)
    lse_copy = pltpu.make_async_copy(lse_ref, lse_hbm, sem)

    def out_copy(h):
        columns = pl.ds(h * width, width)
        return pltpu.make_async_copy(out_buf.at[:, :, columns], out_hbm.at[:, :, columns], out_sems.at[h])

    def emit(order, h, value, top_row):
        slot = hi if order == HI else 1 - hi
        sums = value[:, width:]
        out_buf[slot, :, h * width : (h + 1) * width] = (value[:, :width] / sums).astype(out_buf.dtype)
        lse_ref[slot, h : h + 1, :] = top_row * (coef * math.log(2.0)) + jnp.log(first_row(sums))
        return sums

    worst[...] = jnp.zeros_like(worst)

    def store(order, row, value):
        group = all_rows // 2 if heads > 1 else all_rows
        if value is None:
            value = acc_ref[order, pl.ds(row, group)]
        for at in range(0, group, rows):
            h = (row + at) // rows
            sums = emit(order, h, value[at : at + rows], top_ref[order, h : h + 1, :])
            worst[...] = jnp.maximum(worst[...], sums)

    visit(coef, distances[-1], parts, sb, qx_ref, acc_ref, buffers, all_rows // 2 if heads > 1 else all_rows, store)
    for h in range(heads):
        out_copy(h).start()
    lse_copy.start()
    for h in range(heads):
        out_copy(h).wait()
    lse_copy.wait()

    @pl.when(jnp.logical_not(jnp.max(worst[...]) < SUM_LIMIT))
    def _():
        def fetch(src, dst):
            copy = pltpu.make_async_copy(src, dst, sem)
            copy.start()
            copy.wait()

        def online(source):
            @pl.loop(0, 4 * heads)
            def _(i):
                h, slot, order = i // 4, lax.rem(i, 4) // 2, lax.rem(i, 2)
                own_block = jnp.where(order == HI, hi_block, lo_block)
                shift = (own_block - sb[2 * source + slot]) * block_len + inner * rows

                @pl.when(shift + rows > 0)
                def _():
                    queries = qx_ref[order, pl.ds(pl.multiple_of(h * rows, rows), rows), pl.ds(0, width)]
                    at = pl.ds(pl.multiple_of(slot * block_len, block_len), block_len)
                    s = score_dot(queries, k_buf[at])
                    row = lax.broadcasted_iota(jnp.int32, s.shape, 0) + shift
                    allowed = lax.broadcasted_iota(jnp.int32, s.shape, 1) <= row
                    s = jnp.where(allowed, s, NEG)
                    before = run_top[order, h]
                    top = jnp.maximum(before, jnp.broadcast_to(jnp.max(s, axis=1, keepdims=True), before.shape))
                    p = jnp.where(allowed, jnp.exp2((s - widen(top, block_len)) * coef), 0.0)
                    run_top[order, h] = top
                    shrink = widen(jnp.exp2((before - top) * coef), 2 * width)
                    fresh = value_dot(p.astype(jnp.bfloat16), with_ones(v_buf[at]))
                    run_acc[order, h] = run_acc[order, h] * shrink + fresh

        run_top[...] = jnp.full_like(run_top, NEG)
        run_acc[...] = jnp.zeros_like(run_acc)
        def rows_of(slot, half):
            return pl.ds(pl.multiple_of((slot * 2 + half) * half_len, half_len), half_len)

        for slot in range(2):
            fetch(every[0].at[slot], k_buf.at[pl.ds(slot * block_len, block_len)])
            fetch(every[1].at[slot], v_buf.at[pl.ds(slot * block_len, block_len)])
        online(me)
        for place, other in enumerate(distances):
            others = every[2 + 4 * place : 6 + 4 * place]
            for value, (own_buf, twin_buf) in enumerate([(k_buf, v_buf), (v_buf, k_buf)]):

                @pl.when(inner == value)
                def _():
                    for turn in range(2):
                        half = own_half if turn == 0 else 1 - own_half
                        for slot in range(2):
                            fetch(others[2 * turn].at[slot], own_buf.at[rows_of(slot, half)])
                            fetch(others[2 * turn + 1].at[slot], twin_buf.at[rows_of(slot, half)])

            online(source_of(me, other, count))
        for h in range(heads):
            for order in (LO, HI):
                emit(order, h, run_acc[order, h], first_row(run_top[order, h]))
            out_copy(h).start()
            out_copy(h).wait()
        lse_copy.start()
        lse_copy.wait()


def body(query_rows, key_rows, value_rows, slot_block):
    _, block_len, width = key_rows.shape
    _, rows, feats = query_rows.shape
    heads = feats // width
    all_rows = heads * rows
    count = lax.axis_size("seq")
    coef = math.log2(math.e) / math.sqrt(width)
    distances = list(range(1, count))

    def along_seq(block, distance):
        if is_power(count):
            route = [(i, i ^ distance) for i in range(count)]
        else:
            route = [(i, (i + distance) % count) for i in range(count)]
        with jax.named_scope("along_seq"):
            return lax.ppermute(block, "seq", route)

    def along_head(block):
        with jax.named_scope("along_head"):
            return lax.ppermute(block, "head", [(i, i ^ 1) for i in range(lax.axis_size("head"))])

    def along_inner(block):
        with jax.named_scope("along_inner"):
            return lax.ppermute(block, "inner", [(0, 1), (1, 0)])

    whole = pl.BlockSpec(memory_space=pltpu.VMEM)
    anywhere = pl.BlockSpec(memory_space=pl.ANY)
    scalars = pl.BlockSpec(memory_space=pltpu.SMEM)
    acc_shape = jax.ShapeDtypeStruct((2, all_rows, 2 * width), jnp.float32)
    qx_shape = jax.ShapeDtypeStruct(acc_shape.shape, jnp.bfloat16)
    top_shape = jax.ShapeDtypeStruct((2, heads, rows), jnp.float32)
    params = pltpu.CompilerParams(vmem_limit_bytes=40 * 1024 * 1024)
    unit = rows * heads * block_len * width * 4
    exps = rows * heads * block_len

    def cost(units, size):
        return pl.CostEstimate(flops=int(2 * units * unit), bytes_accessed=size, transcendentals=int(units * exps))

    in_hbm = [
        pltpu.with_memory_space_constraint(x, pltpu.HBM) for x in (query_rows, key_rows, value_rows, slot_block)
    ]
    half_shape = jax.ShapeDtypeStruct((2, block_len // 2, width), key_rows.dtype)
    piece, q_here, k_here, v_here, sb_here = pl.pallas_call(
        load_kernel,
        in_specs=[anywhere] * 4,
        out_specs=[whole] * 5,
        out_shape=[half_shape, jax.ShapeDtypeStruct((2, all_rows, width), query_rows.dtype)]
        + [jax.ShapeDtypeStruct(x.shape, x.dtype) for x in in_hbm[1:]],
        scratch_shapes=[pltpu.SemaphoreType.DMA((4 + heads,))],
        cost_estimate=pl.CostEstimate(flops=0, bytes_accessed=3_000_000, transcendentals=0),
        compiler_params=params,
        name="load",
    )(*in_hbm)
    arrived, across, beside, beside_across = {}, {}, {}, {}
    for distance in distances:
        if not is_power(count) or is_power(distance):
            arrived[distance] = along_seq(piece, distance)

    qx, acc = pl.pallas_call(
        functools.partial(local_kernel, coef, rows),
        in_specs=[scalars] + [whole] * 3,
        out_specs=[whole] * 2,
        out_shape=[qx_shape, acc_shape],
        cost_estimate=cost(3, 6_000_000),
        scratch_shapes=[pltpu.VMEM((2, width, block_len), key_rows.dtype)],
        compiler_params=params,
        name="local_part",
    )(sb_here, q_here, k_here, v_here)
    kv_buffers = [pltpu.VMEM((2 * block_len, width), jnp.bfloat16)] * 2
    kv_buffers += [pltpu.VMEM((width, 2 * block_len), jnp.bfloat16)]

    def attend(acc, visits, with_tops):
        pieces = [part[d] for d in visits for part in (arrived, beside, across, beside_across)]
        return pl.pallas_call(
            functools.partial(middle_kernel, coef, visits, rows),
            in_specs=[scalars] + [whole] * (2 + len(pieces)),
            out_specs=[whole] * (1 + with_tops),
            out_shape=[acc_shape] + [top_shape] * with_tops,
            scratch_shapes=kv_buffers,
            input_output_aliases={2: 0},
            cost_estimate=cost(2 * len(visits), 7_000_000),
            compiler_params=params,
            name=f"visitors_from_{visits[0]}",
        )(sb_here, qx, acc, *pieces)

    def relay(distance):
        if distance in distances and distance not in arrived:
            near = distance & -distance
            arrived[distance] = along_seq(arrived[distance ^ near], near)

    def spread(distance):
        if distance in distances:
            across[distance] = along_head(arrived[distance])
            beside[distance] = along_inner(arrived[distance])

    last = distances[-1]
    groups = [distances[:2]] + [[d] for d in distances[2:-1]] if count > 3 else [[d] for d in distances[:-1]]
    first, acc = lax.optimization_barrier((dict(arrived), acc))
    arrived.update(first)
    tops = []
    for distance in groups[0]:
        spread(distance)
    for visits in groups:
        ahead = visits[-1] + 1
        relay(ahead)
        tied = lax.optimization_barrier(([across[d] for d in visits], arrived[ahead], acc))
        sides, arrived[ahead], acc = tied
        across.update(zip(visits, sides))
        spread(ahead)
        for distance in visits:
            beside_across[distance] = along_inner(across[distance])
        acc, *tops = attend(acc, visits, int(ahead == last))
    across[last], acc = lax.optimization_barrier((across[last], acc))
    beside_across[last] = along_inner(across[last])

    flat = [part[d] for d in distances for part in (arrived, beside, across, beside_across)]
    attended, log_total = pl.pallas_call(
        functools.partial(last_kernel, coef, distances),
        in_specs=[scalars] + [whole] * 7 + [anywhere] * (2 + len(flat)),
        out_specs=[anywhere, anywhere],
        out_shape=[jax.ShapeDtypeStruct(query_rows.shape, query_rows.dtype), top_shape],
        scratch_shapes=[
            pltpu.VMEM(query_rows.shape, query_rows.dtype),
            pltpu.VMEM(top_shape.shape, jnp.float32),
        ]
        + kv_buffers
        + [
            pltpu.VMEM((rows, width), jnp.float32),
            pltpu.VMEM((2, heads, rows, width), jnp.float32),
            pltpu.VMEM((2, heads, rows, 2 * width), jnp.float32),
            pltpu.SemaphoreType.DMA,
            pltpu.SemaphoreType.DMA((heads,)),
        ],
        cost_estimate=cost(1, 7_000_000),
        compiler_params=params,
        name="last_visitor",
    )(sb_here, qx, acc, *tops, *flat[-4:], in_hbm[1], in_hbm[2], *flat)
    return attended, log_total


def solution(mesh):
    placed = (
        P(("groups", "seq"), "inner", "head"),
        P(("groups", "seq"), None, None),
        P(("groups", "seq"), None, None),
        P(),
    )
    return jax.shard_map(
        body,
        mesh=mesh,
        in_specs=placed,
        out_specs=(P(("groups", "seq"), "inner", "head"), P(("groups", "seq"), "head", "inner")),
        check_vma=False,
    )
```

```python
import functools
import math

import jax
import jax.numpy as jnp
from jax import lax
from jax.experimental import pallas as pl
from jax.experimental.pallas import tpu as pltpu
from jax.sharding import PartitionSpec as P

NEG = -1e30
SUM_LIMIT = 1e36
LO, HI = 0, 1
TILE = 256


def score_dot(q, k):
    return lax.dot_general(q, k, (((1,), (1,)), ((), ())), preferred_element_type=jnp.float32)


def flat_dot(q, k_turned):
    return jnp.dot(q, k_turned, preferred_element_type=jnp.float32)


def value_dot(p, v):
    return jnp.dot(p, v, preferred_element_type=jnp.float32)


def widen(x, width):
    return jnp.concatenate([x] * (width // x.shape[1]), axis=1)


def is_power(count):
    return count & (count - 1) == 0


def source_of(index, distance, count):
    if is_power(count):
        return index ^ distance
    return lax.rem(index - distance + count, count)


def blocks_of(sb, seq_index):
    b0, b1 = sb[2 * seq_index], sb[2 * seq_index + 1]
    return jnp.where(b1 > b0, 1, 0), jnp.minimum(b0, b1), jnp.maximum(b0, b1)


def key_tiles(count):
    return [(start, min(TILE, count - start)) for start in range(0, count, TILE)]


def load_kernel(q_hbm, k_hbm, v_hbm, sb_hbm, piece, q_out, k_out, v_out, sb_out, sems):
    half = piece.shape[1]
    rows, width = q_hbm.shape[1], q_out.shape[2]
    inner = lax.axis_index("inner")
    mine = pl.ds(pl.multiple_of(lax.rem(lax.axis_index("head"), 2) * half, half), half)
    for value, src in enumerate((k_hbm, v_hbm)):

        @pl.when(inner == value)
        def _():
            pltpu.make_async_copy(src.at[:, mine], piece, sems.at[0]).start()

    copies = [pltpu.make_async_copy(k_hbm.at[:, mine], piece, sems.at[0])]
    pairs = [(k_hbm, k_out), (v_hbm, v_out), (sb_hbm, sb_out)]
    for h in range(q_hbm.shape[2] // width):
        pairs.append((q_hbm.at[:, :, pl.ds(h * width, width)], q_out.at[:, pl.ds(h * rows, rows)]))
    for place, (src, dst) in enumerate(pairs):
        copy = pltpu.make_async_copy(src, dst, sems.at[1 + place])
        copy.start()
        copies.append(copy)
    for copy in copies:
        copy.wait()


def weights_of(coef, s, top):
    p = jnp.exp2((s - widen(top, s.shape[1])) * coef)
    sums = functools.reduce(jnp.add, [p[:, at : at + 128] for at in range(0, p.shape[1], 128)])
    return p.astype(jnp.bfloat16), sums


def with_sums(p, sums, v):
    return jnp.concatenate([value_dot(p, v), sums], axis=1)


def in_turn(chunks, score, finish):
    ready = score(*chunks[0])
    for place, chunk in enumerate(chunks):
        now = ready
        if place + 1 < len(chunks):
            ready = score(*chunks[place + 1])
        finish(now, *chunk)


def local_kernel(coef, rows, sb, q_ref, k_ref, v_ref, top_ref, acc_ref, turned):
    _, all_rows, width = q_ref.shape
    block_len = k_ref.shape[1]
    heads = all_rows // rows
    hi, _, _ = blocks_of(sb, lax.axis_index("seq"))
    slots = {HI: hi, LO: 1 - hi}
    tiles = key_tiles(block_len)

    for order in (HI, LO):
        turned[order] = jnp.transpose(k_ref[slots[order]])

    def keys(order, start, size):
        return turned[order, :, start : start + size]

    def values(slot, start, size):
        return v_ref[slot, pl.ds(start, size)]

    def masked(order, start, size):
        row = lax.broadcasted_iota(jnp.int32, (rows, size), 0) + lax.axis_index("inner") * rows
        col = lax.broadcasted_iota(jnp.int32, (rows, size), 1) + start
        bias = jnp.where(col <= row, 0.0, NEG)
        s = flat_dot(q_ref[slots[order]], keys(order, start, size))
        return s + jnp.concatenate([bias] * heads, axis=0)

    def highest(scores):
        parts = [s[:, at : at + width] for s in scores for at in range(0, s.shape[1], width)]
        top = functools.reduce(jnp.maximum, parts)
        return jnp.broadcast_to(jnp.max(top, axis=1, keepdims=True), (all_rows, width))

    def settle(order, scores, top):
        total = None
        for (start, size), s in zip(tiles, scores):
            part = with_sums(*weights_of(coef, s, top), values(slots[order], start, size))
            total = part if total is None else total + part
        acc_ref[order] = total

    diag = [masked(HI, *tile) for tile in tiles]
    top = highest(diag)
    top_ref[HI] = top
    low = [masked(LO, *tile) for tile in tiles]
    settle(HI, diag, top)
    top = highest(low)
    top_ref[LO] = top

    def score(start, size):
        return flat_dot(q_ref[slots[HI]], keys(LO, start, size))

    def finish(s, start, size):
        acc_ref[HI] += with_sums(*weights_of(coef, s, top_ref[HI]), values(slots[LO], start, size))

    settle(LO, low, top)
    in_turn(tiles, score, finish)


def place_pieces(parts, k_buf, v_buf, turned):
    inner = lax.axis_index("inner")
    own_half = lax.rem(lax.axis_index("head"), 2)
    for value, (own_buf, twin_buf) in enumerate([(k_buf, v_buf), (v_buf, k_buf)]):

        @pl.when(inner == value)
        def _():
            for turn in range(2):
                half = own_half if turn == 0 else 1 - own_half
                for piece, buf in zip(parts[2 * turn : 2 * turn + 2], (own_buf, twin_buf)):
                    size = piece.shape[1]
                    for slot in range(2):
                        buf[pl.ds(pl.multiple_of((slot * 2 + half) * size, size), size)] = piece[slot]

    turned[...] = jnp.transpose(k_buf[...])


def visit(coef, distance, parts, sb, q_ref, top_ref, acc_ref, buffers, group, store):
    all_rows = q_ref.shape[1]
    count = lax.axis_size("seq")
    me = lax.axis_index("seq")
    k_buf, v_buf, turned = buffers
    place_pieces(parts, k_buf, v_buf, turned)
    keys_here = k_buf.shape[0] // 2

    hi, _, top_block = blocks_of(sb, me)
    slots = {HI: hi, LO: 1 - hi}
    other_hi, _, other_top = blocks_of(sb, source_of(me, distance, count))
    above = top_block > other_top

    def run(orders, first_key, key_count):
        tiles = key_tiles(key_count)
        totals = {}

        def keys(start, size):
            at = first_key + start
            at = at if isinstance(at, int) else pl.multiple_of(at, 128)
            return turned[:, pl.ds(at, size)]

        def values(start, size):
            return v_buf[pl.ds(first_key + start, size)]

        def score(order, row, start, size):
            return flat_dot(q_ref[slots[order], pl.ds(row, group)], keys(start, size))

        def finish(s, order, row, start, size):
            top = top_ref[order, pl.ds(row, group)]
            part = with_sums(*weights_of(coef, s, top), values(start, size))
            before = acc_ref[order, pl.ds(row, group)] if start == 0 else totals[order, row]
            totals[order, row] = before + part
            if start == tiles[-1][0]:
                store(order, row, totals[order, row])

        chunks = [(order, row, *tile) for row in range(0, all_rows, group) for order in orders for tile in tiles]
        in_turn(chunks, score, finish)

    @pl.when(above)
    def _():
        for row in range(0, all_rows, group):
            store(LO, row, None)
        run((HI,), 0, 2 * keys_here)

    @pl.when(jnp.logical_not(above))
    def _():
        run((HI, LO), pl.multiple_of((1 - other_hi) * keys_here, keys_here), keys_here)


def first_row(x):
    return jnp.transpose(x)[:1]


def middle_kernel(coef, visits, sb, q_ref, top_ref, acc_in, *refs):
    pieces, acc_ref, buffers = refs[: 4 * len(visits)], refs[4 * len(visits)], refs[4 * len(visits) + 1 :]
    all_rows = q_ref.shape[1]

    def store(order, row, value):
        if value is not None:
            acc_ref[order, pl.ds(row, all_rows)] = value

    for place, distance in enumerate(visits):
        parts = pieces[4 * place : 4 * place + 4]
        visit(coef, distance, parts, sb, q_ref, top_ref, acc_ref, buffers, all_rows, store)


def last_kernel(coef, distances, sb, q_ref, top_ref, acc_ref, *refs):
    parts, every, rest = refs[:4], refs[4 : 4 * len(distances) + 6], refs[4 * len(distances) + 6 :]
    out_hbm, lse_hbm, out_buf, lse_ref, *buffers, worst, run_top, run_acc, sem, out_sems = rest
    rows = out_buf.shape[1]
    all_rows = q_ref.shape[1]
    heads = all_rows // rows
    k_buf, v_buf, _ = buffers
    block_len, width = k_buf.shape[0] // 2, k_buf.shape[1]
    half_len = block_len // 2
    count = lax.axis_size("seq")
    me = lax.axis_index("seq")
    own_half = lax.rem(lax.axis_index("head"), 2)
    inner = lax.axis_index("inner")
    hi, lo_block, hi_block = blocks_of(sb, me)
    lse_copy = pltpu.make_async_copy(lse_ref, lse_hbm, sem)

    def out_copy(h):
        columns = pl.ds(h * width, width)
        return pltpu.make_async_copy(out_buf.at[:, :, columns], out_hbm.at[:, :, columns], out_sems.at[h])

    def emit(order, h, value, top):
        slot = hi if order == HI else 1 - hi
        sums = jnp.broadcast_to(jnp.sum(value[:, width:], axis=1, keepdims=True), (rows, width))
        out_buf[slot, :, h * width : (h + 1) * width] = (value[:, :width] / sums).astype(out_buf.dtype)
        lse_ref[slot, h : h + 1, :] = first_row(top * (coef * math.log(2.0)) + jnp.log(sums))
        return sums

    worst[...] = jnp.zeros_like(worst)

    def store(order, row, value):
        group = all_rows // 2 if heads > 1 else all_rows
        if value is None:
            value = acc_ref[order, pl.ds(row, group)]
        for at in range(0, group, rows):
            h = (row + at) // rows
            sums = emit(order, h, value[at : at + rows], top_ref[order, pl.ds(row + at, rows)])
            worst[...] = jnp.maximum(worst[...], sums)

    visit(coef, distances[-1], parts, sb, q_ref, top_ref, acc_ref, buffers, all_rows // 2 if heads > 1 else all_rows, store)
    for h in range(heads):
        out_copy(h).start()
    lse_copy.start()
    for h in range(heads):
        out_copy(h).wait()
    lse_copy.wait()

    @pl.when(jnp.logical_not(jnp.max(worst[...]) < SUM_LIMIT))
    def _():
        def fetch(src, dst):
            copy = pltpu.make_async_copy(src, dst, sem)
            copy.start()
            copy.wait()

        def online(source):
            @pl.loop(0, 4 * heads)
            def _(i):
                h, slot, order = i // 4, lax.rem(i, 4) // 2, lax.rem(i, 2)
                own_block = jnp.where(order == HI, hi_block, lo_block)
                shift = (own_block - sb[2 * source + slot]) * block_len + inner * rows

                @pl.when(shift + rows > 0)
                def _():
                    own_slot = jnp.where(order == HI, hi, 1 - hi)
                    queries = q_ref[own_slot, pl.ds(pl.multiple_of(h * rows, rows), rows)]
                    at = pl.ds(pl.multiple_of(slot * block_len, block_len), block_len)
                    s = score_dot(queries, k_buf[at])
                    row = lax.broadcasted_iota(jnp.int32, s.shape, 0) + shift
                    allowed = lax.broadcasted_iota(jnp.int32, s.shape, 1) <= row
                    s = jnp.where(allowed, s, NEG)
                    before = run_top[order, h]
                    top = jnp.maximum(before, jnp.broadcast_to(jnp.max(s, axis=1, keepdims=True), before.shape))
                    p = jnp.where(allowed, jnp.exp2((s - widen(top, block_len)) * coef), 0.0)
                    run_top[order, h] = top
                    shrink = widen(jnp.exp2((before - top) * coef), 2 * width)
                    lanes = functools.reduce(jnp.add, [p[:, x : x + width] for x in range(0, block_len, width)])
                    fresh = with_sums(p.astype(jnp.bfloat16), lanes, v_buf[at])
                    run_acc[order, h] = run_acc[order, h] * shrink + fresh

        run_top[...] = jnp.full_like(run_top, NEG)
        run_acc[...] = jnp.zeros_like(run_acc)
        def rows_of(slot, half):
            return pl.ds(pl.multiple_of((slot * 2 + half) * half_len, half_len), half_len)

        for slot in range(2):
            fetch(every[0].at[slot], k_buf.at[pl.ds(slot * block_len, block_len)])
            fetch(every[1].at[slot], v_buf.at[pl.ds(slot * block_len, block_len)])
        online(me)
        for place, other in enumerate(distances):
            others = every[2 + 4 * place : 6 + 4 * place]
            for value, (own_buf, twin_buf) in enumerate([(k_buf, v_buf), (v_buf, k_buf)]):

                @pl.when(inner == value)
                def _():
                    for turn in range(2):
                        half = own_half if turn == 0 else 1 - own_half
                        for slot in range(2):
                            fetch(others[2 * turn].at[slot], own_buf.at[rows_of(slot, half)])
                            fetch(others[2 * turn + 1].at[slot], twin_buf.at[rows_of(slot, half)])

            online(source_of(me, other, count))
        for h in range(heads):
            for order in (LO, HI):
                emit(order, h, run_acc[order, h], run_top[order, h])
            out_copy(h).start()
            out_copy(h).wait()
        lse_copy.start()
        lse_copy.wait()


def body(query_rows, key_rows, value_rows, slot_block):
    _, block_len, width = key_rows.shape
    _, rows, feats = query_rows.shape
    heads = feats // width
    all_rows = heads * rows
    count = lax.axis_size("seq")
    coef = math.log2(math.e) / math.sqrt(width)
    distances = list(range(1, count))

    def along_seq(block, distance):
        if is_power(count):
            route = [(i, i ^ distance) for i in range(count)]
        else:
            route = [(i, (i + distance) % count) for i in range(count)]
        with jax.named_scope("along_seq"):
            return lax.ppermute(block, "seq", route)

    def along_head(block):
        with jax.named_scope("along_head"):
            return lax.ppermute(block, "head", [(i, i ^ 1) for i in range(lax.axis_size("head"))])

    def along_inner(block):
        with jax.named_scope("along_inner"):
            return lax.ppermute(block, "inner", [(0, 1), (1, 0)])

    whole = pl.BlockSpec(memory_space=pltpu.VMEM)
    anywhere = pl.BlockSpec(memory_space=pl.ANY)
    scalars = pl.BlockSpec(memory_space=pltpu.SMEM)
    acc_shape = jax.ShapeDtypeStruct((2, all_rows, 2 * width), jnp.float32)
    tops_shape = jax.ShapeDtypeStruct((2, all_rows, width), jnp.float32)
    top_shape = jax.ShapeDtypeStruct((2, heads, rows), jnp.float32)
    params = pltpu.CompilerParams(vmem_limit_bytes=40 * 1024 * 1024)
    unit = rows * heads * block_len * width * 4
    exps = rows * heads * block_len

    def cost(units, size):
        return pl.CostEstimate(flops=int(2 * units * unit), bytes_accessed=size, transcendentals=int(units * exps))

    in_hbm = [
        pltpu.with_memory_space_constraint(x, pltpu.HBM) for x in (query_rows, key_rows, value_rows, slot_block)
    ]
    half_shape = jax.ShapeDtypeStruct((2, block_len // 2, width), key_rows.dtype)
    piece, q_here, k_here, v_here, sb_here = pl.pallas_call(
        load_kernel,
        in_specs=[anywhere] * 4,
        out_specs=[whole] * 5,
        out_shape=[half_shape, jax.ShapeDtypeStruct((2, all_rows, width), query_rows.dtype)]
        + [jax.ShapeDtypeStruct(x.shape, x.dtype) for x in in_hbm[1:]],
        scratch_shapes=[pltpu.SemaphoreType.DMA((4 + heads,))],
        cost_estimate=pl.CostEstimate(flops=0, bytes_accessed=3_000_000, transcendentals=0),
        compiler_params=params,
        name="load",
    )(*in_hbm)
    arrived, across, beside, beside_across = {}, {}, {}, {}
    for distance in reversed(distances):
        if not is_power(count) or is_power(distance):
            arrived[distance] = along_seq(piece, distance)

    tops, acc = pl.pallas_call(
        functools.partial(local_kernel, coef, rows),
        in_specs=[scalars] + [whole] * 3,
        out_specs=[whole] * 2,
        out_shape=[tops_shape, acc_shape],
        cost_estimate=cost(3, 6_000_000),
        scratch_shapes=[pltpu.VMEM((2, width, block_len), key_rows.dtype)],
        compiler_params=params,
        name="local_part",
    )(sb_here, q_here, k_here, v_here)
    kv_buffers = [pltpu.VMEM((2 * block_len, width), jnp.bfloat16)] * 2
    kv_buffers += [pltpu.VMEM((width, 2 * block_len), jnp.bfloat16)]

    def attend(acc, visits):
        pieces = [part[d] for d in visits for part in (arrived, beside, across, beside_across)]
        return pl.pallas_call(
            functools.partial(middle_kernel, coef, visits),
            in_specs=[scalars] + [whole] * (3 + len(pieces)),
            out_specs=whole,
            out_shape=acc_shape,
            scratch_shapes=kv_buffers,
            input_output_aliases={3: 0},
            cost_estimate=cost(2 * len(visits), 7_000_000),
            compiler_params=params,
            name=f"visitors_from_{visits[0]}",
        )(sb_here, q_here, tops, acc, *pieces)

    def relay(distance):
        if distance in distances and distance not in arrived:
            near = distance & -distance
            arrived[distance] = along_seq(arrived[distance ^ near], near)

    def spread(distance):
        if distance in distances:
            across[distance] = along_head(arrived[distance])
            beside[distance] = along_inner(arrived[distance])

    last = distances[-1]
    groups = [distances[:2]] + [[d] for d in distances[2:-1]] if count > 3 else [[d] for d in distances[:-1]]
    for distance in sorted(arrived, reverse=True):
        arrived[distance], acc = lax.optimization_barrier((arrived[distance], acc))
    for distance in groups[0]:
        spread(distance)
    for visits in groups:
        ahead = visits[-1] + 1
        relay(ahead)
        tied = lax.optimization_barrier(([across[d] for d in visits], arrived[ahead], acc))
        sides, arrived[ahead], acc = tied
        across.update(zip(visits, sides))
        spread(ahead)
        for distance in visits:
            beside_across[distance] = along_inner(across[distance])
        acc = attend(acc, visits)
    across[last], acc = lax.optimization_barrier((across[last], acc))
    beside_across[last] = along_inner(across[last])

    flat = [part[d] for d in distances for part in (arrived, beside, across, beside_across)]
    attended, log_total = pl.pallas_call(
        functools.partial(last_kernel, coef, distances),
        in_specs=[scalars] + [whole] * 7 + [anywhere] * (2 + len(flat)),
        out_specs=[anywhere, anywhere],
        out_shape=[jax.ShapeDtypeStruct(query_rows.shape, query_rows.dtype), top_shape],
        scratch_shapes=[
            pltpu.VMEM(query_rows.shape, query_rows.dtype),
            pltpu.VMEM(top_shape.shape, jnp.float32),
        ]
        + kv_buffers
        + [
            pltpu.VMEM((rows, width), jnp.float32),
            pltpu.VMEM((2, heads, rows, width), jnp.float32),
            pltpu.VMEM((2, heads, rows, 2 * width), jnp.float32),
            pltpu.SemaphoreType.DMA,
            pltpu.SemaphoreType.DMA((heads,)),
        ],
        cost_estimate=cost(1, 7_000_000),
        compiler_params=params,
        name="last_visitor",
    )(sb_here, q_here, tops, acc, *flat[-4:], in_hbm[1], in_hbm[2], *flat)
    return attended, log_total


def solution(mesh):
    placed = (
        P(("groups", "seq"), "inner", "head"),
        P(("groups", "seq"), None, None),
        P(("groups", "seq"), None, None),
        P(),
    )
    return jax.shard_map(
        body,
        mesh=mesh,
        in_specs=placed,
        out_specs=(P(("groups", "seq"), "inner", "head"), P(("groups", "seq"), "head", "inner")),
        check_vma=False,
    )
```

```python
import functools
import math

import jax
import jax.numpy as jnp
from jax import lax
from jax.experimental import pallas as pl
from jax.experimental.pallas import tpu as pltpu
from jax.sharding import PartitionSpec as P

NEG = -1e30
SUM_LIMIT = 1e36
LO, HI = 0, 1
TILE = 256
SUBLANES = 8


def score_dot(q, k):
    return lax.dot_general(q, k, (((1,), (1,)), ((), ())), preferred_element_type=jnp.float32)


def value_dot(p, v):
    return jnp.dot(p, v, preferred_element_type=jnp.float32)


def widen(x, width):
    return jnp.concatenate([x] * (width // x.shape[1]), axis=1)


def is_power(count):
    return count & (count - 1) == 0


def source_of(index, distance, count):
    if is_power(count):
        return index ^ distance
    return lax.rem(index - distance + count, count)


def blocks_of(sb, seq_index):
    b0, b1 = sb[2 * seq_index], sb[2 * seq_index + 1]
    return jnp.where(b1 > b0, 1, 0), jnp.minimum(b0, b1), jnp.maximum(b0, b1)


def key_tiles(count):
    return [(start, min(TILE, count - start)) for start in range(0, count, TILE)]


def load_kernel(q_hbm, k_hbm, v_hbm, sb_hbm, piece, q_out, k_out, v_out, sb_out, sems):
    half = piece.shape[1]
    rows, width = q_hbm.shape[1], q_out.shape[2]
    inner = lax.axis_index("inner")
    mine = pl.ds(pl.multiple_of(lax.rem(lax.axis_index("head"), 2) * half, half), half)
    for value, src in enumerate((k_hbm, v_hbm)):

        @pl.when(inner == value)
        def _():
            pltpu.make_async_copy(src.at[:, mine], piece, sems.at[0]).start()

    copies = [pltpu.make_async_copy(k_hbm.at[:, mine], piece, sems.at[0])]
    pairs = [(k_hbm, k_out), (v_hbm, v_out), (sb_hbm, sb_out)]
    for h in range(q_hbm.shape[2] // width):
        pairs.append((q_hbm.at[:, :, pl.ds(h * width, width)], q_out.at[:, pl.ds(h * rows, rows)]))
    for place, (src, dst) in enumerate(pairs):
        copy = pltpu.make_async_copy(src, dst, sems.at[1 + place])
        copy.start()
        copies.append(copy)
    for copy in copies:
        copy.wait()


def weights_of(coef, s, top):
    p = jnp.exp2((s - down(top, s.shape[0])) * coef)
    return p.astype(jnp.bfloat16), folded(jnp.add, p)


def down(x, height):
    return jnp.concatenate([x] * (height // x.shape[0]), axis=0)


def folded(combine, x):
    return functools.reduce(combine, [x[at : at + SUBLANES] for at in range(0, x.shape[0], SUBLANES)])


def with_sums(p, sums, v):
    return jnp.concatenate([value_dot(p, v), sums], axis=1)


def in_turn(chunks, score, finish):
    ready = score(*chunks[0])
    for place, chunk in enumerate(chunks):
        now = ready
        if place + 1 < len(chunks):
            ready = score(*chunks[place + 1])
        finish(now, *chunk)


def local_kernel(coef, rows, sb, q_ref, k_ref, v_ref, turned_q, top_ref, sum_ref, acc_ref, turned_v):
    _, all_rows, width = q_ref.shape
    block_len = k_ref.shape[1]
    hi, _, _ = blocks_of(sb, lax.axis_index("seq"))
    slots = {HI: hi, LO: 1 - hi}
    tiles = key_tiles(block_len)
    for order in (HI, LO):
        turned_q[order] = jnp.transpose(q_ref[slots[order]])
        turned_v[order] = jnp.transpose(v_ref[slots[order]])

    def keys(order, start, size):
        return k_ref[slots[order], pl.ds(start, size)]

    def values(order, start, size):
        return turned_v[order, :, start : start + size]

    def masked(order, start, size):
        lane = lax.broadcasted_iota(jnp.int32, (SUBLANES, all_rows), 1)
        heads_below = sum((lane >= at).astype(jnp.int32) for at in range(rows, all_rows, rows))
        row = lane - heads_below * rows + lax.axis_index("inner") * rows
        key = lax.broadcasted_iota(jnp.int32, (size, all_rows), 0) + start
        s = value_dot(keys(order, start, size), turned_q[order])
        return jnp.where(key <= down(row, size), s, NEG)

    def highest(scores):
        top = functools.reduce(jnp.maximum, [folded(jnp.maximum, s) for s in scores])
        return jnp.broadcast_to(jnp.max(top, axis=0, keepdims=True), top.shape)

    def settle(order, scores, top):
        total, sums = None, None
        for (start, size), s in zip(tiles, scores):
            p, more = weights_of(coef, s, top)
            part = value_dot(values(order, start, size), p)
            total, sums = (part, more) if total is None else (total + part, sums + more)
        acc_ref[order] = total
        sum_ref[order] = sums

    diag = [masked(HI, *tile) for tile in tiles]
    top = highest(diag)
    top_ref[HI] = top
    low = [masked(LO, *tile) for tile in tiles]
    settle(HI, diag, top)
    top = highest(low)
    top_ref[LO] = top

    def score(start, size):
        return value_dot(keys(LO, start, size), turned_q[HI])

    def finish(s, start, size):
        p, more = weights_of(coef, s, top_ref[HI])
        acc_ref[HI] += value_dot(values(LO, start, size), p)
        sum_ref[HI] += more

    settle(LO, low, top)
    in_turn(tiles, score, finish)


def place_pieces(parts, k_buf, v_buf, turned):
    inner = lax.axis_index("inner")
    own_half = lax.rem(lax.axis_index("head"), 2)
    for value, (own_buf, twin_buf) in enumerate([(k_buf, v_buf), (v_buf, k_buf)]):

        @pl.when(inner == value)
        def _():
            for turn in range(2):
                half = own_half if turn == 0 else 1 - own_half
                for piece, buf in zip(parts[2 * turn : 2 * turn + 2], (own_buf, twin_buf)):
                    size = piece.shape[1]
                    for slot in range(2):
                        buf[pl.ds(pl.multiple_of((slot * 2 + half) * size, size), size)] = piece[slot]

    turned[...] = jnp.transpose(v_buf[...])


def visit(coef, distance, parts, sb, turned_q, top_ref, sum_ref, acc_ref, buffers):
    count = lax.axis_size("seq")
    me = lax.axis_index("seq")
    k_buf, v_buf, turned = buffers
    place_pieces(parts, k_buf, v_buf, turned)
    keys_here = k_buf.shape[0] // 2

    _, _, top_block = blocks_of(sb, me)
    other_hi, _, other_top = blocks_of(sb, source_of(me, distance, count))
    above = top_block > other_top

    def run(orders, first_key, key_count):
        tiles = key_tiles(key_count)
        totals = {}

        def at(start, size):
            first = first_key + start
            return pl.ds(first if isinstance(first, int) else pl.multiple_of(first, 128), size)

        def score(order, start, size):
            return value_dot(k_buf[at(start, size)], turned_q[order])

        def finish(s, order, start, size):
            p, sums = weights_of(coef, s, top_ref[order])
            part = value_dot(turned[:, at(start, size)], p)
            before = totals[order] if start else (acc_ref[order], sum_ref[order])
            totals[order] = before[0] + part, before[1] + sums
            if start == tiles[-1][0]:
                acc_ref[order], sum_ref[order] = totals[order]

        in_turn([(order, *tile) for order in orders for tile in tiles], score, finish)

    @pl.when(above)
    def _():
        run((HI,), 0, 2 * keys_here)

    @pl.when(jnp.logical_not(above))
    def _():
        run((HI, LO), pl.multiple_of((1 - other_hi) * keys_here, keys_here), keys_here)


def first_row(x):
    return jnp.transpose(x)[:1]


def middle_kernel(coef, visits, sb, turned_q, top_ref, sum_in, acc_in, *refs):
    pieces, (sum_ref, acc_ref, *buffers) = refs[: 4 * len(visits)], refs[4 * len(visits) :]
    for place, distance in enumerate(visits):
        visit(coef, distance, pieces[4 * place : 4 * place + 4], sb, turned_q, top_ref, sum_ref, acc_ref, buffers)


def last_kernel(coef, distances, sb, q_ref, turned_q, top_ref, sum_ref, acc_ref, *refs):
    parts, every, rest = refs[:4], refs[4 : 4 * len(distances) + 6], refs[4 * len(distances) + 6 :]
    out_hbm, lse_hbm, out_buf, lse_ref, *buffers, run_top, run_acc, sem, out_sems = rest
    rows = out_buf.shape[1]
    all_rows = q_ref.shape[1]
    heads = all_rows // rows
    k_buf, v_buf, _ = buffers
    block_len, width = k_buf.shape[0] // 2, k_buf.shape[1]
    half_len = block_len // 2
    count = lax.axis_size("seq")
    me = lax.axis_index("seq")
    own_half = lax.rem(lax.axis_index("head"), 2)
    inner = lax.axis_index("inner")
    hi, lo_block, hi_block = blocks_of(sb, me)
    lse_copy = pltpu.make_async_copy(lse_ref, lse_hbm, sem)

    def out_copy(h):
        columns = pl.ds(h * width, width)
        return pltpu.make_async_copy(out_buf.at[:, :, columns], out_hbm.at[:, :, columns], out_sems.at[h])

    def emit(order, h, value, top):
        slot = hi if order == HI else 1 - hi
        sums = jnp.broadcast_to(jnp.sum(value[:, width:], axis=1, keepdims=True), (rows, width))
        out_buf[slot, :, h * width : (h + 1) * width] = (value[:, :width] / sums).astype(out_buf.dtype)
        lse_ref[slot, h : h + 1, :] = first_row(top * (coef * math.log(2.0)) + jnp.log(sums))

    visit(coef, distances[-1], parts, sb, turned_q, top_ref, sum_ref, acc_ref, buffers)
    worst = None
    for order in (LO, HI):
        slot = hi if order == HI else 1 - hi
        sums = jnp.sum(sum_ref[order], axis=0, keepdims=True)
        worst = sums if worst is None else jnp.maximum(worst, sums)
        log_total = top_ref[order][:1] * (coef * math.log(2.0)) + jnp.log(sums)
        settled = jnp.transpose(acc_ref[order] * (1.0 / sums)).astype(out_buf.dtype)
        for h in range(heads):
            mine = slice(h * rows, (h + 1) * rows)
            lse_ref[slot, h : h + 1, :] = log_total[:, mine]
            out_buf[slot, :, h * width : (h + 1) * width] = settled[mine]
    for h in range(heads):
        out_copy(h).start()
    lse_copy.start()
    for h in range(heads):
        out_copy(h).wait()
    lse_copy.wait()

    @pl.when(jnp.logical_not(jnp.max(worst) < SUM_LIMIT))
    def _():
        def fetch(src, dst):
            copy = pltpu.make_async_copy(src, dst, sem)
            copy.start()
            copy.wait()

        def online(source):
            @pl.loop(0, 4 * heads)
            def _(i):
                h, slot, order = i // 4, lax.rem(i, 4) // 2, lax.rem(i, 2)
                own_block = jnp.where(order == HI, hi_block, lo_block)
                shift = (own_block - sb[2 * source + slot]) * block_len + inner * rows

                @pl.when(shift + rows > 0)
                def _():
                    own_slot = jnp.where(order == HI, hi, 1 - hi)
                    queries = q_ref[own_slot, pl.ds(pl.multiple_of(h * rows, rows), rows)]
                    at = pl.ds(pl.multiple_of(slot * block_len, block_len), block_len)
                    s = score_dot(queries, k_buf[at])
                    row = lax.broadcasted_iota(jnp.int32, s.shape, 0) + shift
                    allowed = lax.broadcasted_iota(jnp.int32, s.shape, 1) <= row
                    s = jnp.where(allowed, s, NEG)
                    before = run_top[order, h]
                    top = jnp.maximum(before, jnp.broadcast_to(jnp.max(s, axis=1, keepdims=True), before.shape))
                    p = jnp.where(allowed, jnp.exp2((s - widen(top, block_len)) * coef), 0.0)
                    run_top[order, h] = top
                    shrink = widen(jnp.exp2((before - top) * coef), 2 * width)
                    lanes = functools.reduce(jnp.add, [p[:, x : x + width] for x in range(0, block_len, width)])
                    fresh = with_sums(p.astype(jnp.bfloat16), lanes, v_buf[at])
                    run_acc[order, h] = run_acc[order, h] * shrink + fresh

        run_top[...] = jnp.full_like(run_top, NEG)
        run_acc[...] = jnp.zeros_like(run_acc)
        def rows_of(slot, half):
            return pl.ds(pl.multiple_of((slot * 2 + half) * half_len, half_len), half_len)

        for slot in range(2):
            fetch(every[0].at[slot], k_buf.at[pl.ds(slot * block_len, block_len)])
            fetch(every[1].at[slot], v_buf.at[pl.ds(slot * block_len, block_len)])
        online(me)
        for place, other in enumerate(distances):
            others = every[2 + 4 * place : 6 + 4 * place]
            for value, (own_buf, twin_buf) in enumerate([(k_buf, v_buf), (v_buf, k_buf)]):

                @pl.when(inner == value)
                def _():
                    for turn in range(2):
                        half = own_half if turn == 0 else 1 - own_half
                        for slot in range(2):
                            fetch(others[2 * turn].at[slot], own_buf.at[rows_of(slot, half)])
                            fetch(others[2 * turn + 1].at[slot], twin_buf.at[rows_of(slot, half)])

            online(source_of(me, other, count))
        for h in range(heads):
            for order in (LO, HI):
                emit(order, h, run_acc[order, h], run_top[order, h])
            out_copy(h).start()
            out_copy(h).wait()
        lse_copy.start()
        lse_copy.wait()


def body(query_rows, key_rows, value_rows, slot_block):
    _, block_len, width = key_rows.shape
    _, rows, feats = query_rows.shape
    heads = feats // width
    all_rows = heads * rows
    count = lax.axis_size("seq")
    coef = math.log2(math.e) / math.sqrt(width)
    distances = list(range(1, count))

    def along_seq(block, distance):
        if is_power(count):
            route = [(i, i ^ distance) for i in range(count)]
        else:
            route = [(i, (i + distance) % count) for i in range(count)]
        with jax.named_scope("along_seq"):
            return lax.ppermute(block, "seq", route)

    def along_head(block):
        with jax.named_scope("along_head"):
            return lax.ppermute(block, "head", [(i, i ^ 1) for i in range(lax.axis_size("head"))])

    def along_inner(block):
        with jax.named_scope("along_inner"):
            return lax.ppermute(block, "inner", [(0, 1), (1, 0)])

    whole = pl.BlockSpec(memory_space=pltpu.VMEM)
    anywhere = pl.BlockSpec(memory_space=pl.ANY)
    scalars = pl.BlockSpec(memory_space=pltpu.SMEM)
    acc_shape = jax.ShapeDtypeStruct((2, width, all_rows), jnp.float32)
    sum_shape = jax.ShapeDtypeStruct((2, SUBLANES, all_rows), jnp.float32)
    turned_shape = jax.ShapeDtypeStruct(acc_shape.shape, query_rows.dtype)
    top_shape = jax.ShapeDtypeStruct((2, heads, rows), jnp.float32)
    params = pltpu.CompilerParams(vmem_limit_bytes=40 * 1024 * 1024)
    unit = rows * heads * block_len * width * 4
    exps = rows * heads * block_len

    def cost(units, size):
        return pl.CostEstimate(flops=int(2 * units * unit), bytes_accessed=size, transcendentals=int(units * exps))

    in_hbm = [
        pltpu.with_memory_space_constraint(x, pltpu.HBM) for x in (query_rows, key_rows, value_rows, slot_block)
    ]
    half_shape = jax.ShapeDtypeStruct((2, block_len // 2, width), key_rows.dtype)
    piece, q_here, k_here, v_here, sb_here = pl.pallas_call(
        load_kernel,
        in_specs=[anywhere] * 4,
        out_specs=[whole] * 5,
        out_shape=[half_shape, jax.ShapeDtypeStruct((2, all_rows, width), query_rows.dtype)]
        + [jax.ShapeDtypeStruct(x.shape, x.dtype) for x in in_hbm[1:]],
        scratch_shapes=[pltpu.SemaphoreType.DMA((4 + heads,))],
        cost_estimate=pl.CostEstimate(flops=0, bytes_accessed=3_000_000, transcendentals=0),
        compiler_params=params,
        name="load",
    )(*in_hbm)
    arrived, across, beside, beside_across = {}, {}, {}, {}
    for distance in reversed(distances):
        if not is_power(count) or is_power(distance):
            arrived[distance] = along_seq(piece, distance)

    turned, tops, sums, acc = pl.pallas_call(
        functools.partial(local_kernel, coef, rows),
        in_specs=[scalars] + [whole] * 3,
        out_specs=[whole] * 4,
        out_shape=[turned_shape, sum_shape, sum_shape, acc_shape],
        cost_estimate=cost(3, 6_000_000),
        scratch_shapes=[pltpu.VMEM((2, width, block_len), key_rows.dtype)],
        compiler_params=params,
        name="local_part",
    )(sb_here, q_here, k_here, v_here)
    kv_buffers = [pltpu.VMEM((2 * block_len, width), jnp.bfloat16)] * 2
    kv_buffers += [pltpu.VMEM((width, 2 * block_len), jnp.bfloat16)]

    def attend(sums, acc, visits):
        pieces = [part[d] for d in visits for part in (arrived, beside, across, beside_across)]
        return pl.pallas_call(
            functools.partial(middle_kernel, coef, visits),
            in_specs=[scalars] + [whole] * (4 + len(pieces)),
            out_specs=[whole] * 2,
            out_shape=[sum_shape, acc_shape],
            scratch_shapes=kv_buffers,
            input_output_aliases={3: 0, 4: 1},
            cost_estimate=cost(2 * len(visits), 7_000_000),
            compiler_params=params,
            name=f"visitors_from_{visits[0]}",
        )(sb_here, turned, tops, sums, acc, *pieces)

    def relay(distance):
        if distance in distances and distance not in arrived:
            near = distance & -distance
            arrived[distance] = along_seq(arrived[distance ^ near], near)

    def spread(distance):
        if distance in distances:
            across[distance] = along_head(arrived[distance])
            beside[distance] = along_inner(arrived[distance])

    last = distances[-1]
    groups = [distances[:2]] + [[d] for d in distances[2:-1]] if count > 3 else [[d] for d in distances[:-1]]
    for distance in sorted(arrived, reverse=True):
        arrived[distance], acc = lax.optimization_barrier((arrived[distance], acc))
    for distance in groups[0]:
        spread(distance)
    for visits in groups:
        ahead = visits[-1] + 1
        relay(ahead)
        tied = lax.optimization_barrier(([across[d] for d in visits], arrived[ahead], acc))
        sides, arrived[ahead], acc = tied
        across.update(zip(visits, sides))
        spread(ahead)
        for distance in visits:
            beside_across[distance] = along_inner(across[distance])
        sums, acc = attend(sums, acc, visits)
    across[last], acc = lax.optimization_barrier((across[last], acc))
    beside_across[last] = along_inner(across[last])

    flat = [part[d] for d in distances for part in (arrived, beside, across, beside_across)]
    attended, log_total = pl.pallas_call(
        functools.partial(last_kernel, coef, distances),
        in_specs=[scalars] + [whole] * 9 + [anywhere] * (2 + len(flat)),
        out_specs=[anywhere, anywhere],
        out_shape=[jax.ShapeDtypeStruct(query_rows.shape, query_rows.dtype), top_shape],
        scratch_shapes=[
            pltpu.VMEM(query_rows.shape, query_rows.dtype),
            pltpu.VMEM(top_shape.shape, jnp.float32),
        ]
        + kv_buffers
        + [
            pltpu.VMEM((2, heads, rows, width), jnp.float32),
            pltpu.VMEM((2, heads, rows, 2 * width), jnp.float32),
            pltpu.SemaphoreType.DMA,
            pltpu.SemaphoreType.DMA((heads,)),
        ],
        cost_estimate=cost(1, 7_000_000),
        compiler_params=params,
        name="last_visitor",
    )(sb_here, q_here, turned, tops, sums, acc, *flat[-4:], in_hbm[1], in_hbm[2], *flat)
    return attended, log_total


def solution(mesh):
    placed = (
        P(("groups", "seq"), "inner", "head"),
        P(("groups", "seq"), None, None),
        P(("groups", "seq"), None, None),
        P(),
    )
    return jax.shard_map(
        body,
        mesh=mesh,
        in_specs=placed,
        out_specs=(P(("groups", "seq"), "inner", "head"), P(("groups", "seq"), "head", "inner")),
        check_vma=False,
    )
```

```python
import functools
import math

import jax
import jax.numpy as jnp
from jax import lax
from jax.experimental import pallas as pl
from jax.experimental.pallas import tpu as pltpu
from jax.sharding import PartitionSpec as P

NEG = -1e30
SUM_LIMIT = 1e36
LO, HI = 0, 1
TILE = 256
SUBLANES = 8


def score_dot(q, k):
    return lax.dot_general(q, k, (((1,), (1,)), ((), ())), preferred_element_type=jnp.float32)


def value_dot(p, v):
    return jnp.dot(p, v, preferred_element_type=jnp.float32)


def widen(x, width):
    return jnp.concatenate([x] * (width // x.shape[1]), axis=1)


def is_power(count):
    return count & (count - 1) == 0


def source_of(index, distance, count):
    if is_power(count):
        return index ^ distance
    return lax.rem(index - distance + count, count)


def blocks_of(sb, seq_index):
    b0, b1 = sb[2 * seq_index], sb[2 * seq_index + 1]
    return jnp.where(b1 > b0, 1, 0), jnp.minimum(b0, b1), jnp.maximum(b0, b1)


def key_tiles(count):
    return [(start, min(TILE, count - start)) for start in range(0, count, TILE)]


def piece_kernel(k_hbm, v_hbm, sb_hbm, piece, sb_out, sems):
    half = piece.shape[1]
    inner = lax.axis_index("inner")
    mine = pl.ds(pl.multiple_of(lax.rem(lax.axis_index("head"), 2) * half, half), half)
    sb_copy = pltpu.make_async_copy(sb_hbm, sb_out, sems.at[1])
    for value, src in enumerate((k_hbm, v_hbm)):

        @pl.when(inner == value)
        def _():
            pltpu.make_async_copy(src.at[:, mine], piece, sems.at[0]).start()

    sb_copy.start()
    pltpu.make_async_copy(k_hbm.at[:, mine], piece, sems.at[0]).wait()
    sb_copy.wait()


def weights_of(coef, s, top):
    p = jnp.exp2((s - down(top, s.shape[0])) * coef)
    return p.astype(jnp.bfloat16), folded(jnp.add, p)


def down(x, height):
    return jnp.concatenate([x] * (height // x.shape[0]), axis=0)


def folded(combine, x):
    return functools.reduce(combine, [x[at : at + SUBLANES] for at in range(0, x.shape[0], SUBLANES)])


def with_sums(p, sums, v):
    return jnp.concatenate([value_dot(p, v), sums], axis=1)


def in_turn(chunks, score, finish):
    ready = score(*chunks[0])
    for place, chunk in enumerate(chunks):
        now = ready
        if place + 1 < len(chunks):
            ready = score(*chunks[place + 1])
        finish(now, *chunk)


def local_kernel(coef, rows, sb, q_hbm, k_hbm, v_hbm, turned_q, top_ref, sum_ref, acc_ref, q_ref, k_ref, v_ref, turned_v, sems):
    _, all_rows, width = q_ref.shape
    copies = []
    for h in range(all_rows // rows):
        source, target = q_hbm.at[:, :, pl.ds(h * width, width)], q_ref.at[:, pl.ds(h * rows, rows)]
        copies.append(pltpu.make_async_copy(source, target, sems.at[2 + h]))
    copies.append(pltpu.make_async_copy(k_hbm, k_ref, sems.at[0]))
    copies.append(pltpu.make_async_copy(v_hbm, v_ref, sems.at[1]))
    for copy in copies:
        copy.start()
    for copy in copies:
        copy.wait()
    block_len = k_ref.shape[1]
    hi, _, _ = blocks_of(sb, lax.axis_index("seq"))
    slots = {HI: hi, LO: 1 - hi}
    tiles = key_tiles(block_len)
    for order in (HI, LO):
        turned_q[order] = jnp.transpose(q_ref[slots[order]])
        turned_v[order] = jnp.transpose(v_ref[slots[order]])

    def keys(order, start, size):
        return k_ref[slots[order], pl.ds(start, size)]

    def values(order, start, size):
        return turned_v[order, :, start : start + size]

    def masked(order, start, size):
        lane = lax.broadcasted_iota(jnp.int32, (SUBLANES, all_rows), 1)
        heads_below = sum((lane >= at).astype(jnp.int32) for at in range(rows, all_rows, rows))
        row = lane - heads_below * rows + lax.axis_index("inner") * rows
        key = lax.broadcasted_iota(jnp.int32, (size, all_rows), 0) + start
        s = value_dot(keys(order, start, size), turned_q[order])
        return jnp.where(key <= down(row, size), s, NEG)

    def highest(scores):
        top = functools.reduce(jnp.maximum, [folded(jnp.maximum, s) for s in scores])
        return jnp.broadcast_to(jnp.max(top, axis=0, keepdims=True), top.shape)

    def settle(order, scores, top):
        total, sums = None, None
        for (start, size), s in zip(tiles, scores):
            p, more = weights_of(coef, s, top)
            part = value_dot(values(order, start, size), p)
            total, sums = (part, more) if total is None else (total + part, sums + more)
        acc_ref[order] = total
        sum_ref[order] = sums

    diag = [masked(HI, *tile) for tile in tiles]
    top = highest(diag)
    top_ref[HI] = top
    low = [masked(LO, *tile) for tile in tiles]
    settle(HI, diag, top)
    top = highest(low)
    top_ref[LO] = top

    def score(start, size):
        return value_dot(keys(LO, start, size), turned_q[HI])

    def finish(s, start, size):
        p, more = weights_of(coef, s, top_ref[HI])
        acc_ref[HI] += value_dot(values(LO, start, size), p)
        sum_ref[HI] += more

    settle(LO, low, top)
    in_turn(tiles, score, finish)


def visit_chunks(distance, own, twin, sb, k_buf, v_buf, turned):
    inner = lax.axis_index("inner")
    for value, (own_buf, twin_buf) in enumerate([(k_buf, v_buf), (v_buf, k_buf)]):

        @pl.when(inner == value)
        def _():
            own_buf[...] = own[...]
            twin_buf[...] = twin[...]

    for slot in range(2):
        turned[slot] = jnp.transpose(v_buf[slot])
    me = lax.axis_index("seq")
    _, _, top_block = blocks_of(sb, me)
    other_hi, _, other_top = blocks_of(sb, source_of(me, distance, lax.axis_size("seq")))
    above = top_block > other_top
    first = (HI, jnp.where(above, 0, 1 - other_hi))
    return first, (jnp.where(above, HI, LO), jnp.where(above, 1, 1 - other_hi))


def attend(coef, visits, sb, turned_q, top_ref, sum_ref, acc_ref, buffers, done=None):
    chunks, ends = [], []
    laid_out = [visit_chunks(*visit, sb, *buffers[3 * i : 3 * i + 3]) for i, visit in enumerate(visits)]
    for place, pairs in enumerate(laid_out):
        k_buf, _, turned = buffers[3 * place : 3 * place + 3]
        tiles = key_tiles(k_buf.shape[1])
        for order, slot in pairs:
            for tile in tiles:
                chunks.append((len(ends), order, slot, k_buf, turned, *tile))
            ends.append(tiles[-1][0])
    totals = {}

    def score(place, order, slot, k_buf, turned, start, size):
        return value_dot(k_buf[slot, pl.ds(start, size)], turned_q[order])

    def finish(s, place, order, slot, k_buf, turned, start, size):
        p, sums = weights_of(coef, s, top_ref[order])
        part = value_dot(turned[slot, :, pl.ds(start, size)], p)
        if start:
            part, sums = totals[place][0] + part, totals[place][1] + sums
        totals[place] = part, sums
        if start == ends[place]:
            acc_ref[order] += part
            sum_ref[order] += sums
            if done is not None:
                done(place, laid_out[-1][1][0])

    in_turn(chunks, score, finish)


def first_row(x):
    return jnp.transpose(x)[:1]


def middle_kernel(coef, distances, sb, turned_q, top_ref, sum_in, acc_in, *refs):
    count = len(distances)
    visits = [(d, refs[2 * i], refs[2 * i + 1]) for i, d in enumerate(distances)]
    sum_ref, acc_ref, *buffers = refs[2 * count :]
    attend(coef, visits, sb, turned_q, top_ref, sum_ref, acc_ref, buffers)


def last_kernel(coef, distances, sb, turned_q, top_ref, sum_ref, acc_ref, own, twin, *refs):
    every, rest = refs[: 4 * len(distances) + 3], refs[4 * len(distances) + 3 :]
    out_hbm, lse_hbm, out_buf, lse_ref, *buffers, worst, k_buf, v_buf, run_top, run_acc, sem, out_sems = rest
    _, rows, feats = out_buf.shape
    width = k_buf.shape[1]
    block_len, heads = k_buf.shape[0] // 2, feats // width
    half_len = block_len // 2
    count = lax.axis_size("seq")
    me = lax.axis_index("seq")
    own_half = lax.rem(lax.axis_index("head"), 2)
    inner = lax.axis_index("inner")
    hi, lo_block, hi_block = blocks_of(sb, me)
    lse_copy = pltpu.make_async_copy(lse_ref, lse_hbm, sem)

    def out_copy(slot):
        return pltpu.make_async_copy(out_buf.at[slot], out_hbm.at[slot], out_sems.at[slot])

    def emit(order, h, value, top):
        slot = hi if order == HI else 1 - hi
        sums = jnp.broadcast_to(jnp.sum(value[:, width:], axis=1, keepdims=True), (rows, width))
        out_buf[slot, :, h * width : (h + 1) * width] = (value[:, :width] / sums).astype(out_buf.dtype)
        lse_ref[slot, h : h + 1, :] = first_row(top * (coef * math.log(2.0)) + jnp.log(sums))

    def done(place, last_order):
        order = 1 - last_order if place == 0 else last_order
        slot = jnp.where(order == HI, hi, 1 - hi)
        sums = jnp.sum(sum_ref[order], axis=0, keepdims=True)
        log_total = top_ref[order][:1] * (coef * math.log(2.0)) + jnp.log(sums)
        settled = jnp.transpose((acc_ref[order] * (1.0 / sums)).astype(out_buf.dtype))
        for h in range(heads):
            mine = slice(h * rows, (h + 1) * rows)
            lse_ref[slot, h : h + 1, :] = log_total[:, mine]
            out_buf[slot, :, h * width : (h + 1) * width] = settled[mine]
        worst[place : place + 1] = sums
        out_copy(slot).start()

    attend(coef, [(distances[-1], own, twin)], sb, turned_q, top_ref, sum_ref, acc_ref, buffers, done)
    lse_copy.start()
    for slot in range(2):
        out_copy(slot).wait()
    lse_copy.wait()

    @pl.when(jnp.logical_not(jnp.max(worst[...]) < SUM_LIMIT))
    def _():
        def fetch(src, dst):
            copy = pltpu.make_async_copy(src, dst, sem)
            copy.start()
            copy.wait()

        def online(source):
            @pl.loop(0, 4 * heads)
            def _(i):
                h, slot, order = i // 4, lax.rem(i, 4) // 2, lax.rem(i, 2)
                own_block = jnp.where(order == HI, hi_block, lo_block)
                shift = (own_block - sb[2 * source + slot]) * block_len + inner * rows

                @pl.when(shift + rows > 0)
                def _():
                    own_slot = jnp.where(order == HI, hi, 1 - hi)
                    queries = out_buf[own_slot, :, pl.ds(pl.multiple_of(h * width, width), width)]
                    at = pl.ds(pl.multiple_of(slot * block_len, block_len), block_len)
                    s = score_dot(queries, k_buf[at])
                    row = lax.broadcasted_iota(jnp.int32, s.shape, 0) + shift
                    allowed = lax.broadcasted_iota(jnp.int32, s.shape, 1) <= row
                    s = jnp.where(allowed, s, NEG)
                    before = run_top[order, h]
                    top = jnp.maximum(before, jnp.broadcast_to(jnp.max(s, axis=1, keepdims=True), before.shape))
                    p = jnp.where(allowed, jnp.exp2((s - widen(top, block_len)) * coef), 0.0)
                    run_top[order, h] = top
                    shrink = widen(jnp.exp2((before - top) * coef), 2 * width)
                    lanes = functools.reduce(jnp.add, [p[:, x : x + width] for x in range(0, block_len, width)])
                    fresh = with_sums(p.astype(jnp.bfloat16), lanes, v_buf[at])
                    run_acc[order, h] = run_acc[order, h] * shrink + fresh

        run_top[...] = jnp.full_like(run_top, NEG)
        run_acc[...] = jnp.zeros_like(run_acc)
        def rows_of(slot, half):
            return pl.ds(pl.multiple_of((slot * 2 + half) * half_len, half_len), half_len)

        fetch(every[2], out_buf)
        for slot in range(2):
            fetch(every[0].at[slot], k_buf.at[pl.ds(slot * block_len, block_len)])
            fetch(every[1].at[slot], v_buf.at[pl.ds(slot * block_len, block_len)])
        online(me)
        for place, other in enumerate(distances):
            others = every[3 + 4 * place : 7 + 4 * place]
            for value, (own_buf, twin_buf) in enumerate([(k_buf, v_buf), (v_buf, k_buf)]):

                @pl.when(inner == value)
                def _():
                    for turn in range(2):
                        half = own_half if turn == 0 else 1 - own_half
                        for slot in range(2):
                            fetch(others[2 * turn].at[slot], own_buf.at[rows_of(slot, half)])
                            fetch(others[2 * turn + 1].at[slot], twin_buf.at[rows_of(slot, half)])

            online(source_of(me, other, count))
        for h in range(heads):
            for order in (LO, HI):
                emit(order, h, run_acc[order, h], run_top[order, h])
        for copy in (lse_copy, out_copy(0), out_copy(1)):
            copy.start()
        for copy in (lse_copy, out_copy(0), out_copy(1)):
            copy.wait()


def body(query_rows, key_rows, value_rows, slot_block):
    _, block_len, width = key_rows.shape
    _, rows, feats = query_rows.shape
    heads = feats // width
    all_rows = heads * rows
    count = lax.axis_size("seq")
    coef = math.log2(math.e) / math.sqrt(width)
    distances = list(range(1, count))

    def along_seq(block, distance):
        if is_power(count):
            route = [(i, i ^ distance) for i in range(count)]
        else:
            route = [(i, (i + distance) % count) for i in range(count)]
        with jax.named_scope("along_seq"):
            return lax.ppermute(block, "seq", route)

    def along_head(block):
        with jax.named_scope("along_head"):
            return lax.ppermute(block, "head", [(i, i ^ 1) for i in range(lax.axis_size("head"))])

    def along_inner(block):
        with jax.named_scope("along_inner"):
            return lax.ppermute(block, "inner", [(0, 1), (1, 0)])

    whole = pl.BlockSpec(memory_space=pltpu.VMEM)
    anywhere = pl.BlockSpec(memory_space=pl.ANY)
    scalars = pl.BlockSpec(memory_space=pltpu.SMEM)
    acc_shape = jax.ShapeDtypeStruct((2, width, all_rows), jnp.float32)
    sum_shape = jax.ShapeDtypeStruct((2, SUBLANES, all_rows), jnp.float32)
    turned_shape = jax.ShapeDtypeStruct(acc_shape.shape, query_rows.dtype)
    top_shape = jax.ShapeDtypeStruct((2, heads, rows), jnp.float32)
    params = pltpu.CompilerParams(vmem_limit_bytes=40 * 1024 * 1024)
    unit = rows * heads * block_len * width * 4
    exps = rows * heads * block_len

    def cost(units, size):
        return pl.CostEstimate(flops=int(2 * units * unit), bytes_accessed=size, transcendentals=int(units * exps))

    in_hbm = [
        pltpu.with_memory_space_constraint(x, pltpu.HBM) for x in (query_rows, key_rows, value_rows, slot_block)
    ]
    half_shape = jax.ShapeDtypeStruct((2, block_len // 2, width), key_rows.dtype)
    piece, sb_here = pl.pallas_call(
        piece_kernel,
        in_specs=[anywhere] * 3,
        out_specs=[whole] * 2,
        out_shape=[half_shape, jax.ShapeDtypeStruct(slot_block.shape, slot_block.dtype)],
        scratch_shapes=[pltpu.SemaphoreType.DMA((2,))],
        cost_estimate=pl.CostEstimate(flops=0, bytes_accessed=400_000, transcendentals=0),
        compiler_params=params,
        name="pick_piece",
    )(*in_hbm[1:])
    arrived, across, beside, beside_across = {}, {}, {}, {}
    for distance in reversed(distances):
        if not is_power(count) or is_power(distance):
            arrived[distance] = along_seq(piece, distance)

    turned, tops, sums, acc = pl.pallas_call(
        functools.partial(local_kernel, coef, rows),
        in_specs=[scalars] + [anywhere] * 3,
        out_specs=[whole] * 4,
        out_shape=[turned_shape, sum_shape, sum_shape, acc_shape],
        cost_estimate=cost(3, 6_000_000),
        scratch_shapes=[
            pltpu.VMEM((2, all_rows, width), query_rows.dtype),
            pltpu.VMEM(key_rows.shape, key_rows.dtype),
            pltpu.VMEM(key_rows.shape, key_rows.dtype),
            pltpu.VMEM((2, width, block_len), key_rows.dtype),
            pltpu.SemaphoreType.DMA((2 + heads,)),
        ],
        compiler_params=params,
        name="local_part",
    )(sb_here, *in_hbm[:3])
    half_buffers = [
        pltpu.VMEM(half_shape.shape, half_shape.dtype),
        pltpu.VMEM(half_shape.shape, half_shape.dtype),
        pltpu.VMEM((2, width, block_len // 2), half_shape.dtype),
    ]

    def near_half(distance):
        return distance, arrived[distance], beside[distance]

    def far_half(distance):
        return distance, across[distance], beside_across[distance]

    def attended_with(sums, acc, visits):
        return pl.pallas_call(
            functools.partial(middle_kernel, coef, [visit[0] for visit in visits]),
            in_specs=[scalars] + [whole] * (4 + 2 * len(visits)),
            out_specs=[whole] * 2,
            out_shape=[sum_shape, acc_shape],
            scratch_shapes=half_buffers * len(visits),
            input_output_aliases={3: 0, 4: 1},
            cost_estimate=cost(len(visits), 4_000_000),
            compiler_params=params,
            name="visits_of_" + "_".join(str(visit[0]) for visit in visits),
        )(sb_here, turned, tops, sums, acc, *(part for visit in visits for part in visit[1:]))

    def relay(distance):
        if distance in distances and distance not in arrived:
            near = distance & -distance
            arrived[distance] = along_seq(arrived[distance ^ near], near)

    def spread(distance):
        if distance in distances:
            across[distance] = along_head(arrived[distance])
            beside[distance] = along_inner(arrived[distance])

    last = distances[-1]
    for distance in sorted(arrived, reverse=True):
        arrived[distance], acc = lax.optimization_barrier((arrived[distance], acc))
    waiting = distances[:2]
    for distance in waiting:
        spread(distance)
    relay(3)
    sums, acc = attended_with(sums, acc, [near_half(d) for d in waiting])
    for ahead in distances[2:]:
        relay(ahead)
        arrived[ahead], acc = lax.optimization_barrier((arrived[ahead], acc))
        spread(ahead)
        for distance in waiting:
            across[distance], acc = lax.optimization_barrier((across[distance], acc))
            beside_across[distance] = along_inner(across[distance])
        sums, acc = attended_with(sums, acc, [far_half(d) for d in waiting] + [near_half(ahead)])
        waiting = [ahead]
    across[last], acc = lax.optimization_barrier((across[last], acc))
    beside_across[last] = along_inner(across[last])

    flat = [part[d] for d in distances for part in (arrived, beside, across, beside_across)]
    attended, log_total = pl.pallas_call(
        functools.partial(last_kernel, coef, distances),
        in_specs=[scalars] + [whole] * 6 + [anywhere] * (3 + len(flat)),
        out_specs=[anywhere, anywhere],
        out_shape=[jax.ShapeDtypeStruct(query_rows.shape, query_rows.dtype), top_shape],
        scratch_shapes=[
            pltpu.VMEM(query_rows.shape, query_rows.dtype),
            pltpu.VMEM(top_shape.shape, jnp.float32),
        ]
        + half_buffers
        + [
            pltpu.VMEM((2, all_rows), jnp.float32),
            pltpu.VMEM((2 * block_len, width), key_rows.dtype),
            pltpu.VMEM((2 * block_len, width), key_rows.dtype),
            pltpu.VMEM((2, heads, rows, width), jnp.float32),
            pltpu.VMEM((2, heads, rows, 2 * width), jnp.float32),
            pltpu.SemaphoreType.DMA,
            pltpu.SemaphoreType.DMA((2,)),
        ],
        cost_estimate=cost(1, 7_000_000),
        compiler_params=params,
        name="last_visitor",
    )(sb_here, turned, tops, sums, acc, *far_half(last)[1:], in_hbm[1], in_hbm[2], in_hbm[0], *flat)
    return attended, log_total


def solution(mesh):
    placed = (
        P(("groups", "seq"), "inner", "head"),
        P(("groups", "seq"), None, None),
        P(("groups", "seq"), None, None),
        P(),
    )
    return jax.shard_map(
        body,
        mesh=mesh,
        in_specs=placed,
        out_specs=(P(("groups", "seq"), "inner", "head"), P(("groups", "seq"), "head", "inner")),
        check_vma=False,
    )
```

```python
import functools
import math

import jax
import jax.numpy as jnp
from jax import lax
from jax.experimental import pallas as pl
from jax.experimental.pallas import tpu as pltpu
from jax.sharding import PartitionSpec as P

NEG = -1e30
SUM_LIMIT = 1e36
LO, HI = 0, 1
TILE = 256
SUBLANES = 8


def score_dot(q, k):
    return lax.dot_general(q, k, (((1,), (1,)), ((), ())), preferred_element_type=jnp.float32)


def value_dot(p, v):
    return jnp.dot(p, v, preferred_element_type=jnp.float32)


def widen(x, width):
    return jnp.concatenate([x] * (width // x.shape[1]), axis=1)


def is_power(count):
    return count & (count - 1) == 0


def source_of(index, distance, count):
    if is_power(count):
        return index ^ distance
    return lax.rem(index - distance + count, count)


def blocks_of(sb, seq_index):
    b0, b1 = sb[2 * seq_index], sb[2 * seq_index + 1]
    return jnp.where(b1 > b0, 1, 0), jnp.minimum(b0, b1), jnp.maximum(b0, b1)


def key_tiles(count):
    return [(start, min(TILE, count - start)) for start in range(0, count, TILE)]


def piece_kernel(k_hbm, v_hbm, sb_hbm, piece, sb_out, sems):
    half = piece.shape[1]
    inner = lax.axis_index("inner")
    mine = pl.ds(pl.multiple_of(lax.rem(lax.axis_index("head"), 2) * half, half), half)
    sb_copy = pltpu.make_async_copy(sb_hbm, sb_out, sems.at[1])
    for value, src in enumerate((k_hbm, v_hbm)):

        @pl.when(inner == value)
        def _():
            pltpu.make_async_copy(src.at[:, mine], piece, sems.at[0]).start()

    sb_copy.start()
    pltpu.make_async_copy(k_hbm.at[:, mine], piece, sems.at[0]).wait()
    sb_copy.wait()


def weights_of(coef, s):
    p = jnp.exp2(s * coef)
    return p.astype(jnp.bfloat16), folded(jnp.add, p)


def with_ones(x):
    return jnp.concatenate([x, jnp.ones_like(x)], axis=1)


def minus_rows(top, height):
    high = top.astype(jnp.bfloat16).astype(jnp.float32)
    middle = (top - high).astype(jnp.bfloat16).astype(jnp.float32)
    low = top - high - middle
    row = lax.broadcasted_iota(jnp.int32, top.shape, 0)
    picked = jnp.where(row == 0, high, jnp.where(row == 1, middle, jnp.where(row == 2, low, 0.0)))
    zeros = jnp.zeros((height - top.shape[0], top.shape[1]), jnp.float32)
    return jnp.concatenate([-picked, zeros], axis=0).astype(jnp.bfloat16)


def down(x, height):
    return jnp.concatenate([x] * (height // x.shape[0]), axis=0)


def folded(combine, x):
    return functools.reduce(combine, [x[at : at + SUBLANES] for at in range(0, x.shape[0], SUBLANES)])


def with_sums(p, sums, v):
    return jnp.concatenate([value_dot(p, v), sums], axis=1)


def in_turn(chunks, score, finish):
    ready = score(*chunks[0])
    for place, chunk in enumerate(chunks):
        now = ready
        if place + 1 < len(chunks):
            ready = score(*chunks[place + 1])
        finish(now, *chunk)


def diagonal_kernel(coef, rows, sb, q_hbm, k_hbm, v_hbm, turned_q, top_ref, sum_ref, acc_ref, k_ref, turned_v, q_ref, v_ref, sems):
    _, all_rows, width = q_ref.shape
    copies = []
    for h in range(all_rows // rows):
        source, target = q_hbm.at[:, :, pl.ds(h * width, width)], q_ref.at[:, pl.ds(h * rows, rows)]
        copies.append(pltpu.make_async_copy(source, target, sems.at[2 + h]))
    copies.append(pltpu.make_async_copy(k_hbm, k_ref, sems.at[0]))
    copies.append(pltpu.make_async_copy(v_hbm, v_ref, sems.at[1]))
    for copy in copies:
        copy.start()
    for copy in copies:
        copy.wait()
    block_len = k_ref.shape[1]
    hi, _, _ = blocks_of(sb, lax.axis_index("seq"))
    slots = {HI: hi, LO: 1 - hi}
    tiles = key_tiles(block_len)
    for order in (HI, LO):
        turned_q[order, pl.ds(0, width)] = jnp.transpose(q_ref[slots[order]])
        turned_v[order] = jnp.transpose(v_ref[slots[order]])

    def keys(order, start, size):
        return k_ref[slots[order], pl.ds(start, size)]

    def values(order, start, size):
        return turned_v[order, :, start : start + size]

    def masked(order, start, size):
        lane = lax.broadcasted_iota(jnp.int32, (SUBLANES, all_rows), 1)
        heads_below = sum((lane >= at).astype(jnp.int32) for at in range(rows, all_rows, rows))
        row = lane - heads_below * rows + lax.axis_index("inner") * rows
        key = lax.broadcasted_iota(jnp.int32, (size, all_rows), 0) + start
        s = value_dot(keys(order, start, size), turned_q[order, pl.ds(0, width)])
        return jnp.where(key <= down(row, size), s, NEG)

    def highest(scores):
        top = functools.reduce(jnp.maximum, [folded(jnp.maximum, s) for s in scores])
        return jnp.broadcast_to(jnp.max(top, axis=0, keepdims=True), top.shape)

    def settle(order, scores, top):
        total, sums = None, None
        for (start, size), s in zip(tiles, scores):
            p, more = weights_of(coef, s - down(top, size))
            part = value_dot(values(order, start, size), p)
            total, sums = (part, more) if total is None else (total + part, sums + more)
        acc_ref[order] = total
        sum_ref[order] = sums

    def extend(order, scores):
        top = highest(scores)
        top_ref[order] = top
        turned_q[order, pl.ds(width, width)] = minus_rows(top, width)
        return top

    diag = [masked(HI, *tile) for tile in tiles]
    top = extend(HI, diag)
    low = [masked(LO, *tile) for tile in tiles]
    settle(HI, diag, top)
    settle(LO, low, extend(LO, low))


def past_kernel(coef, sb, turned_q, sum_in, acc_in, k_ref, turned_v, sum_ref, acc_ref):
    hi, _, _ = blocks_of(sb, lax.axis_index("seq"))
    tiles = key_tiles(k_ref.shape[1])
    totals = []

    def score(start, size):
        return value_dot(with_ones(k_ref[1 - hi, pl.ds(start, size)]), turned_q[HI])

    def finish(s, start, size):
        p, sums = weights_of(coef, s)
        totals.append((value_dot(turned_v[LO, :, pl.ds(start, size)], p), sums))

    in_turn(tiles, score, finish)
    acc_ref[HI] += functools.reduce(jnp.add, [part for part, _ in totals])
    sum_ref[HI] += functools.reduce(jnp.add, [sums for _, sums in totals])


def visit_chunks(distance, own, twin, sb, k_buf, v_buf, turned):
    inner = lax.axis_index("inner")
    for value, (own_buf, twin_buf) in enumerate([(k_buf, v_buf), (v_buf, k_buf)]):

        @pl.when(inner == value)
        def _():
            own_buf[...] = own[...]
            twin_buf[...] = twin[...]

    for slot in range(2):
        turned[slot] = jnp.transpose(v_buf[slot])
    me = lax.axis_index("seq")
    _, _, top_block = blocks_of(sb, me)
    other_hi, _, other_top = blocks_of(sb, source_of(me, distance, lax.axis_size("seq")))
    above = top_block > other_top
    first = (HI, jnp.where(above, 0, 1 - other_hi))
    return first, (jnp.where(above, HI, LO), jnp.where(above, 1, 1 - other_hi))


def attend(coef, visits, sb, turned_q, sum_ref, acc_ref, buffers, done=None):
    chunks, ends = [], []
    laid_out = [visit_chunks(*visit, sb, *buffers[3 * i : 3 * i + 3]) for i, visit in enumerate(visits)]
    for place, pairs in enumerate(laid_out):
        k_buf, _, turned = buffers[3 * place : 3 * place + 3]
        tiles = key_tiles(k_buf.shape[1])
        for order, slot in pairs:
            for tile in tiles:
                chunks.append((len(ends), order, slot, k_buf, turned, *tile))
            ends.append(tiles[-1][0])
    totals = {}

    def score(place, order, slot, k_buf, turned, start, size):
        return value_dot(with_ones(k_buf[slot, pl.ds(start, size)]), turned_q[order])

    def finish(s, place, order, slot, k_buf, turned, start, size):
        p, sums = weights_of(coef, s)
        part = value_dot(turned[slot, :, pl.ds(start, size)], p)
        if start:
            part, sums = totals[place][0] + part, totals[place][1] + sums
        totals[place] = part, sums
        if start == ends[place]:
            acc_ref[order] += part
            sum_ref[order] += sums
            if done is not None:
                done(place, laid_out[-1][1][0])

    in_turn(chunks, score, finish)


def first_row(x):
    return jnp.transpose(x)[:1]


def middle_kernel(coef, distances, sb, turned_q, sum_in, acc_in, *refs):
    count = len(distances)
    visits = [(d, refs[2 * i], refs[2 * i + 1]) for i, d in enumerate(distances)]
    sum_ref, acc_ref, *buffers = refs[2 * count :]
    attend(coef, visits, sb, turned_q, sum_ref, acc_ref, buffers)


def last_kernel(coef, distances, sb, turned_q, top_ref, sum_ref, acc_ref, own, twin, *refs):
    every, rest = refs[: 4 * len(distances) + 3], refs[4 * len(distances) + 3 :]
    out_hbm, lse_hbm, out_buf, lse_ref, *buffers, worst, k_buf, v_buf, run_top, run_acc, sem, out_sems = rest
    _, rows, feats = out_buf.shape
    width = k_buf.shape[1]
    block_len, heads = k_buf.shape[0] // 2, feats // width
    half_len = block_len // 2
    count = lax.axis_size("seq")
    me = lax.axis_index("seq")
    own_half = lax.rem(lax.axis_index("head"), 2)
    inner = lax.axis_index("inner")
    hi, lo_block, hi_block = blocks_of(sb, me)
    lse_copy = pltpu.make_async_copy(lse_ref, lse_hbm, sem)

    def out_copy(slot):
        return pltpu.make_async_copy(out_buf.at[slot], out_hbm.at[slot], out_sems.at[slot])

    def emit(order, h, value, top):
        slot = hi if order == HI else 1 - hi
        sums = jnp.broadcast_to(jnp.sum(value[:, width:], axis=1, keepdims=True), (rows, width))
        out_buf[slot, :, h * width : (h + 1) * width] = (value[:, :width] / sums).astype(out_buf.dtype)
        lse_ref[slot, h : h + 1, :] = first_row(top * (coef * math.log(2.0)) + jnp.log(sums))

    def done(place, last_order):
        order = 1 - last_order if place == 0 else last_order
        slot = jnp.where(order == HI, hi, 1 - hi)
        sums = jnp.sum(sum_ref[order], axis=0, keepdims=True)
        log_total = top_ref[order][:1] * (coef * math.log(2.0)) + jnp.log(sums)
        settled = jnp.transpose((acc_ref[order] * (1.0 / sums)).astype(out_buf.dtype))
        for h in range(heads):
            mine = slice(h * rows, (h + 1) * rows)
            lse_ref[slot, h : h + 1, :] = log_total[:, mine]
            out_buf[slot, :, h * width : (h + 1) * width] = settled[mine]
        worst[place : place + 1] = sums
        out_copy(slot).start()

    attend(coef, [(distances[-1], own, twin)], sb, turned_q, sum_ref, acc_ref, buffers, done)
    fits = jnp.max(worst[...]) < SUM_LIMIT
    lse_copy.start()
    for slot in range(2):
        out_copy(slot).wait()
    lse_copy.wait()

    @pl.when(jnp.logical_not(fits))
    def _():
        def fetch(src, dst):
            copy = pltpu.make_async_copy(src, dst, sem)
            copy.start()
            copy.wait()

        def online(source):
            @pl.loop(0, 4 * heads)
            def _(i):
                h, slot, order = i // 4, lax.rem(i, 4) // 2, lax.rem(i, 2)
                own_block = jnp.where(order == HI, hi_block, lo_block)
                shift = (own_block - sb[2 * source + slot]) * block_len + inner * rows

                @pl.when(shift + rows > 0)
                def _():
                    own_slot = jnp.where(order == HI, hi, 1 - hi)
                    queries = out_buf[own_slot, :, pl.ds(pl.multiple_of(h * width, width), width)]
                    at = pl.ds(pl.multiple_of(slot * block_len, block_len), block_len)
                    s = score_dot(queries, k_buf[at])
                    row = lax.broadcasted_iota(jnp.int32, s.shape, 0) + shift
                    allowed = lax.broadcasted_iota(jnp.int32, s.shape, 1) <= row
                    s = jnp.where(allowed, s, NEG)
                    before = run_top[order, h]
                    top = jnp.maximum(before, jnp.broadcast_to(jnp.max(s, axis=1, keepdims=True), before.shape))
                    p = jnp.where(allowed, jnp.exp2((s - widen(top, block_len)) * coef), 0.0)
                    run_top[order, h] = top
                    shrink = widen(jnp.exp2((before - top) * coef), 2 * width)
                    lanes = functools.reduce(jnp.add, [p[:, x : x + width] for x in range(0, block_len, width)])
                    fresh = with_sums(p.astype(jnp.bfloat16), lanes, v_buf[at])
                    run_acc[order, h] = run_acc[order, h] * shrink + fresh

        run_top[...] = jnp.full_like(run_top, NEG)
        run_acc[...] = jnp.zeros_like(run_acc)
        def rows_of(slot, half):
            return pl.ds(pl.multiple_of((slot * 2 + half) * half_len, half_len), half_len)

        fetch(every[2], out_buf)
        for slot in range(2):
            fetch(every[0].at[slot], k_buf.at[pl.ds(slot * block_len, block_len)])
            fetch(every[1].at[slot], v_buf.at[pl.ds(slot * block_len, block_len)])
        online(me)
        for place, other in enumerate(distances):
            others = every[3 + 4 * place : 7 + 4 * place]
            for value, (own_buf, twin_buf) in enumerate([(k_buf, v_buf), (v_buf, k_buf)]):

                @pl.when(inner == value)
                def _():
                    for turn in range(2):
                        half = own_half if turn == 0 else 1 - own_half
                        for slot in range(2):
                            fetch(others[2 * turn].at[slot], own_buf.at[rows_of(slot, half)])
                            fetch(others[2 * turn + 1].at[slot], twin_buf.at[rows_of(slot, half)])

            online(source_of(me, other, count))
        for h in range(heads):
            for order in (LO, HI):
                emit(order, h, run_acc[order, h], run_top[order, h])
        for copy in (lse_copy, out_copy(0), out_copy(1)):
            copy.start()
        for copy in (lse_copy, out_copy(0), out_copy(1)):
            copy.wait()


def body(query_rows, key_rows, value_rows, slot_block):
    _, block_len, width = key_rows.shape
    _, rows, feats = query_rows.shape
    heads = feats // width
    all_rows = heads * rows
    count = lax.axis_size("seq")
    coef = math.log2(math.e) / math.sqrt(width)
    distances = list(range(1, count))

    def along_seq(block, distance):
        if is_power(count):
            route = [(i, i ^ distance) for i in range(count)]
        else:
            route = [(i, (i + distance) % count) for i in range(count)]
        with jax.named_scope("along_seq"):
            return lax.ppermute(block, "seq", route)

    def along_head(block):
        with jax.named_scope("along_head"):
            return lax.ppermute(block, "head", [(i, i ^ 1) for i in range(lax.axis_size("head"))])

    def along_inner(block):
        with jax.named_scope("along_inner"):
            return lax.ppermute(block, "inner", [(0, 1), (1, 0)])

    whole = pl.BlockSpec(memory_space=pltpu.VMEM)
    anywhere = pl.BlockSpec(memory_space=pl.ANY)
    scalars = pl.BlockSpec(memory_space=pltpu.SMEM)
    acc_shape = jax.ShapeDtypeStruct((2, width, all_rows), jnp.float32)
    sum_shape = jax.ShapeDtypeStruct((2, SUBLANES, all_rows), jnp.float32)
    turned_shape = jax.ShapeDtypeStruct((2, 2 * width, all_rows), query_rows.dtype)
    top_shape = jax.ShapeDtypeStruct((2, heads, rows), jnp.float32)
    params = pltpu.CompilerParams(vmem_limit_bytes=40 * 1024 * 1024)
    unit = rows * heads * block_len * width * 4
    exps = rows * heads * block_len

    def cost(units, size):
        return pl.CostEstimate(flops=int(2 * units * unit), bytes_accessed=size, transcendentals=int(units * exps))

    in_hbm = [
        pltpu.with_memory_space_constraint(x, pltpu.HBM) for x in (query_rows, key_rows, value_rows, slot_block)
    ]
    half_shape = jax.ShapeDtypeStruct((2, block_len // 2, width), key_rows.dtype)
    piece, sb_here = pl.pallas_call(
        piece_kernel,
        in_specs=[anywhere] * 3,
        out_specs=[whole] * 2,
        out_shape=[half_shape, jax.ShapeDtypeStruct(slot_block.shape, slot_block.dtype)],
        scratch_shapes=[pltpu.SemaphoreType.DMA((2,))],
        cost_estimate=pl.CostEstimate(flops=0, bytes_accessed=400_000, transcendentals=0),
        compiler_params=params,
        name="pick_piece",
    )(*in_hbm[1:])
    arrived, across, beside, beside_across = {}, {}, {}, {}
    for distance in reversed(distances):
        if not is_power(count) or is_power(distance):
            arrived[distance] = along_seq(piece, distance)

    turned_kv = jax.ShapeDtypeStruct((2, width, block_len), key_rows.dtype)
    turned, tops, sums, acc, k_here, v_turned = pl.pallas_call(
        functools.partial(diagonal_kernel, coef, rows),
        in_specs=[scalars] + [anywhere] * 3,
        out_specs=[whole] * 6,
        out_shape=[turned_shape, sum_shape, sum_shape, acc_shape]
        + [jax.ShapeDtypeStruct(key_rows.shape, key_rows.dtype), turned_kv],
        scratch_shapes=[
            pltpu.VMEM((2, all_rows, width), query_rows.dtype),
            pltpu.VMEM(key_rows.shape, key_rows.dtype),
            pltpu.SemaphoreType.DMA((2 + heads,)),
        ],
        cost_estimate=cost(2, 6_000_000),
        compiler_params=params,
        name="diagonal",
    )(sb_here, *in_hbm[:3])
    half_buffers = [
        pltpu.VMEM(half_shape.shape, half_shape.dtype),
        pltpu.VMEM(half_shape.shape, half_shape.dtype),
        pltpu.VMEM((2, width, block_len // 2), half_shape.dtype),
    ]

    def near_half(distance):
        return distance, arrived[distance], beside[distance]

    def far_half(distance):
        return distance, across[distance], beside_across[distance]

    def attended_with(sums, acc, visits):
        return pl.pallas_call(
            functools.partial(middle_kernel, coef, [visit[0] for visit in visits]),
            in_specs=[scalars] + [whole] * (3 + 2 * len(visits)),
            out_specs=[whole] * 2,
            out_shape=[sum_shape, acc_shape],
            scratch_shapes=half_buffers * len(visits),
            input_output_aliases={2: 0, 3: 1},
            cost_estimate=cost(len(visits), 4_000_000),
            compiler_params=params,
            name="visits_of_" + "_".join(str(visit[0]) for visit in visits),
        )(sb_here, turned, sums, acc, *(part for visit in visits for part in visit[1:]))

    def relay(distance):
        if distance in distances and distance not in arrived:
            near = distance & -distance
            arrived[distance] = along_seq(arrived[distance ^ near], near)

    def spread(distance):
        if distance in distances:
            across[distance] = along_head(arrived[distance])
            beside[distance] = along_inner(arrived[distance])

    last = distances[-1]
    for distance in sorted(arrived, reverse=True):
        arrived[distance], acc = lax.optimization_barrier((arrived[distance], acc))
    waiting = distances[:2]
    for distance in waiting:
        spread(distance)
    relay(3)
    sums, acc = pl.pallas_call(
        functools.partial(past_kernel, coef),
        in_specs=[scalars] + [whole] * 5,
        out_specs=[whole] * 2,
        out_shape=[sum_shape, acc_shape],
        input_output_aliases={2: 0, 3: 1},
        cost_estimate=cost(1, 4_000_000),
        compiler_params=params,
        name="past",
    )(sb_here, turned, sums, acc, k_here, v_turned)
    sums, acc = attended_with(sums, acc, [near_half(d) for d in waiting])
    for ahead in distances[2:]:
        relay(ahead)
        arrived[ahead], acc = lax.optimization_barrier((arrived[ahead], acc))
        spread(ahead)
        for distance in waiting:
            across[distance], acc = lax.optimization_barrier((across[distance], acc))
            beside_across[distance] = along_inner(across[distance])
        sums, acc = attended_with(sums, acc, [far_half(d) for d in waiting] + [near_half(ahead)])
        waiting = [ahead]
    across[last], acc = lax.optimization_barrier((across[last], acc))
    beside_across[last] = along_inner(across[last])

    flat = [part[d] for d in distances for part in (arrived, beside, across, beside_across)]
    attended, log_total = pl.pallas_call(
        functools.partial(last_kernel, coef, distances),
        in_specs=[scalars] + [whole] * 6 + [anywhere] * (3 + len(flat)),
        out_specs=[anywhere, anywhere],
        out_shape=[jax.ShapeDtypeStruct(query_rows.shape, query_rows.dtype), top_shape],
        scratch_shapes=[
            pltpu.VMEM(query_rows.shape, query_rows.dtype),
            pltpu.VMEM(top_shape.shape, jnp.float32),
        ]
        + half_buffers
        + [
            pltpu.VMEM((2, all_rows), jnp.float32),
            pltpu.VMEM((2 * block_len, width), key_rows.dtype),
            pltpu.VMEM((2 * block_len, width), key_rows.dtype),
            pltpu.VMEM((2, heads, rows, width), jnp.float32),
            pltpu.VMEM((2, heads, rows, 2 * width), jnp.float32),
            pltpu.SemaphoreType.DMA,
            pltpu.SemaphoreType.DMA((2,)),
        ],
        cost_estimate=cost(1, 7_000_000),
        compiler_params=params,
        name="last_visitor",
    )(sb_here, turned, tops, sums, acc, *far_half(last)[1:], in_hbm[1], in_hbm[2], in_hbm[0], *flat)
    return attended, log_total


def solution(mesh):
    placed = (
        P(("groups", "seq"), "inner", "head"),
        P(("groups", "seq"), None, None),
        P(("groups", "seq"), None, None),
        P(),
    )
    return jax.shard_map(
        body,
        mesh=mesh,
        in_specs=placed,
        out_specs=(P(("groups", "seq"), "inner", "head"), P(("groups", "seq"), "head", "inner")),
        check_vma=False,
    )
```

```python
import functools
import math

import jax
import jax.numpy as jnp
from jax import lax
from jax.experimental import pallas as pl
from jax.experimental.pallas import tpu as pltpu
from jax.sharding import PartitionSpec as P

NEG = -1e30
SUM_LIMIT = 1e36
LO, HI = 0, 1
TILE = 256
SUBLANES = 8


def score_dot(q, k):
    return lax.dot_general(q, k, (((1,), (1,)), ((), ())), preferred_element_type=jnp.float32)


def value_dot(p, v):
    return jnp.dot(p, v, preferred_element_type=jnp.float32)


def widen(x, width):
    return jnp.concatenate([x] * (width // x.shape[1]), axis=1)


def is_power(count):
    return count & (count - 1) == 0


def source_of(index, distance, count):
    if is_power(count):
        return index ^ distance
    return lax.rem(index - distance + count, count)


def blocks_of(sb, seq_index):
    b0, b1 = sb[2 * seq_index], sb[2 * seq_index + 1]
    return jnp.where(b1 > b0, 1, 0), jnp.minimum(b0, b1), jnp.maximum(b0, b1)


def key_tiles(count):
    return [(start, min(TILE, count - start)) for start in range(0, count, TILE)]


def piece_kernel(k_hbm, v_hbm, sb_hbm, piece, sb_out, sems):
    half = piece.shape[1]
    inner = lax.axis_index("inner")
    mine = pl.ds(pl.multiple_of(lax.rem(lax.axis_index("head"), 2) * half, half), half)
    sb_copy = pltpu.make_async_copy(sb_hbm, sb_out, sems.at[1])
    for value, src in enumerate((k_hbm, v_hbm)):

        @pl.when(inner == value)
        def _():
            pltpu.make_async_copy(src.at[:, mine], piece, sems.at[0]).start()

    sb_copy.start()
    pltpu.make_async_copy(k_hbm.at[:, mine], piece, sems.at[0]).wait()
    sb_copy.wait()


def weights_of(coef, s):
    p = jnp.exp2(s * coef)
    return p.astype(jnp.bfloat16), folded(jnp.add, p)


def with_ones(x):
    return jnp.concatenate([x, jnp.ones_like(x)], axis=1)


def minus_rows(top, height):
    high = top.astype(jnp.bfloat16).astype(jnp.float32)
    middle = (top - high).astype(jnp.bfloat16).astype(jnp.float32)
    low = top - high - middle
    row = lax.broadcasted_iota(jnp.int32, top.shape, 0)
    picked = jnp.where(row == 0, high, jnp.where(row == 1, middle, jnp.where(row == 2, low, 0.0)))
    zeros = jnp.zeros((height - top.shape[0], top.shape[1]), jnp.float32)
    return jnp.concatenate([-picked, zeros], axis=0).astype(jnp.bfloat16)


def down(x, height):
    return jnp.concatenate([x] * (height // x.shape[0]), axis=0)


def folded(combine, x):
    return functools.reduce(combine, [x[at : at + SUBLANES] for at in range(0, x.shape[0], SUBLANES)])


def with_sums(p, sums, v):
    return jnp.concatenate([value_dot(p, v), sums], axis=1)


def in_turn(chunks, score, finish):
    ready = score(*chunks[0])
    for place, chunk in enumerate(chunks):
        now = ready
        if place + 1 < len(chunks):
            ready = score(*chunks[place + 1])
        finish(now, *chunk)


def diagonal_kernel(coef, rows, sb, q_hbm, k_hbm, v_hbm, turned_q, top_ref, sum_ref, acc_ref, k_ref, turned_v, q_ref, v_ref, sems):
    _, all_rows, width = q_ref.shape
    copies = []
    for h in range(all_rows // rows):
        source, target = q_hbm.at[:, :, pl.ds(h * width, width)], q_ref.at[:, pl.ds(h * rows, rows)]
        copies.append(pltpu.make_async_copy(source, target, sems.at[2 + h]))
    copies.append(pltpu.make_async_copy(k_hbm, k_ref, sems.at[0]))
    copies.append(pltpu.make_async_copy(v_hbm, v_ref, sems.at[1]))
    for copy in copies:
        copy.start()
    for copy in copies:
        copy.wait()
    block_len = k_ref.shape[1]
    hi, _, _ = blocks_of(sb, lax.axis_index("seq"))
    slots = {HI: hi, LO: 1 - hi}
    tiles = key_tiles(block_len)
    for order in (HI, LO):
        turned_q[order, pl.ds(0, width)] = jnp.transpose(q_ref[slots[order]])
        turned_v[order] = jnp.transpose(v_ref[slots[order]])

    def keys(order, start, size):
        return k_ref[slots[order], pl.ds(start, size)]

    def values(order, start, size):
        return turned_v[order, :, start : start + size]

    def masked(order, start, size):
        lane = lax.broadcasted_iota(jnp.int32, (SUBLANES, all_rows), 1)
        heads_below = sum((lane >= at).astype(jnp.int32) for at in range(rows, all_rows, rows))
        row = lane - heads_below * rows + lax.axis_index("inner") * rows
        key = lax.broadcasted_iota(jnp.int32, (size, all_rows), 0) + start
        s = value_dot(keys(order, start, size), turned_q[order, pl.ds(0, width)])
        return jnp.where(key <= down(row, size), s, NEG)

    def highest(scores):
        top = functools.reduce(jnp.maximum, [folded(jnp.maximum, s) for s in scores])
        return jnp.broadcast_to(jnp.max(top, axis=0, keepdims=True), top.shape)

    def settle(order, scores, top):
        total, sums = None, None
        for (start, size), s in zip(tiles, scores):
            p, more = weights_of(coef, s - down(top, size))
            part = value_dot(values(order, start, size), p)
            total, sums = (part, more) if total is None else (total + part, sums + more)
        acc_ref[order] = total
        sum_ref[order] = sums

    def extend(order, scores):
        top = highest(scores)
        top_ref[order] = top
        turned_q[order, pl.ds(width, width)] = minus_rows(top, width)
        return top

    diag = [masked(HI, *tile) for tile in tiles]
    top = extend(HI, diag)
    low = [masked(LO, *tile) for tile in tiles]
    settle(HI, diag, top)
    settle(LO, low, extend(LO, low))


def past_kernel(coef, sb, turned_q, sum_in, acc_in, k_ref, turned_v, sum_ref, acc_ref):
    hi, _, _ = blocks_of(sb, lax.axis_index("seq"))
    tiles = key_tiles(k_ref.shape[1])
    totals = []

    def score(start, size):
        return value_dot(with_ones(k_ref[1 - hi, pl.ds(start, size)]), turned_q[HI])

    def finish(s, start, size):
        p, sums = weights_of(coef, s)
        totals.append((value_dot(turned_v[LO, :, pl.ds(start, size)], p), sums))

    in_turn(tiles, score, finish)
    acc_ref[HI] += functools.reduce(jnp.add, [part for part, _ in totals])
    sum_ref[HI] += functools.reduce(jnp.add, [sums for _, sums in totals])


def visit_chunks(distance, own, twin, sb, k_buf, v_buf, turned):
    inner = lax.axis_index("inner")
    for value, (own_buf, twin_buf) in enumerate([(k_buf, v_buf), (v_buf, k_buf)]):

        @pl.when(inner == value)
        def _():
            own_buf[...] = own[...]
            twin_buf[...] = twin[...]

    for slot in range(2):
        turned[slot] = jnp.transpose(v_buf[slot])
    me = lax.axis_index("seq")
    _, _, top_block = blocks_of(sb, me)
    other_hi, _, other_top = blocks_of(sb, source_of(me, distance, lax.axis_size("seq")))
    above = top_block > other_top
    first = (HI, jnp.where(above, 0, 1 - other_hi))
    return first, (jnp.where(above, HI, LO), jnp.where(above, 1, 1 - other_hi))


def attend(coef, visits, sb, turned_q, sum_ref, acc_ref, buffers, done=None):
    chunks, ends = [], []
    laid_out = [visit_chunks(*visit, sb, *buffers[3 * i : 3 * i + 3]) for i, visit in enumerate(visits)]
    for place, pairs in enumerate(laid_out):
        k_buf, _, turned = buffers[3 * place : 3 * place + 3]
        tiles = key_tiles(k_buf.shape[1])
        for order, slot in pairs:
            for tile in tiles:
                chunks.append((len(ends), order, slot, k_buf, turned, *tile))
            ends.append(tiles[-1][0])
    totals = {}

    def score(place, order, slot, k_buf, turned, start, size):
        return value_dot(with_ones(k_buf[slot, pl.ds(start, size)]), turned_q[order])

    def finish(s, place, order, slot, k_buf, turned, start, size):
        p, sums = weights_of(coef, s)
        part = value_dot(turned[slot, :, pl.ds(start, size)], p)
        if start:
            part, sums = totals[place][0] + part, totals[place][1] + sums
        totals[place] = part, sums
        if start == ends[place]:
            acc_ref[order] += part
            sum_ref[order] += sums
            if done is not None:
                done(place - len(ends), laid_out[-1][1][0])

    in_turn(chunks, score, finish)


def first_row(x):
    return jnp.transpose(x)[:1]


def middle_kernel(coef, distances, sb, turned_q, sum_in, acc_in, *refs):
    count = len(distances)
    visits = [(d, refs[2 * i], refs[2 * i + 1]) for i, d in enumerate(distances)]
    sum_ref, acc_ref, *buffers = refs[2 * count :]
    attend(coef, visits, sb, turned_q, sum_ref, acc_ref, buffers)


def last_kernel(coef, distances, final, sb, turned_q, top_ref, sum_ref, acc_ref, *refs):
    visits = [(d, refs[2 * i], refs[2 * i + 1]) for i, d in enumerate(final)]
    refs = refs[2 * len(final) :]
    every, rest = refs[: 4 * len(distances) + 3], refs[4 * len(distances) + 3 :]
    out_hbm, lse_hbm, out_buf, lse_ref, *buffers, worst, k_buf, v_buf, run_top, run_acc, sem, out_sems = rest
    _, rows, feats = out_buf.shape
    width = k_buf.shape[1]
    block_len, heads = k_buf.shape[0] // 2, feats // width
    half_len = block_len // 2
    count = lax.axis_size("seq")
    me = lax.axis_index("seq")
    own_half = lax.rem(lax.axis_index("head"), 2)
    inner = lax.axis_index("inner")
    hi, lo_block, hi_block = blocks_of(sb, me)
    lse_copy = pltpu.make_async_copy(lse_ref, lse_hbm, sem)

    def out_copy(slot):
        return pltpu.make_async_copy(out_buf.at[slot], out_hbm.at[slot], out_sems.at[slot])

    def emit(order, h, value, top):
        slot = hi if order == HI else 1 - hi
        sums = jnp.broadcast_to(jnp.sum(value[:, width:], axis=1, keepdims=True), (rows, width))
        out_buf[slot, :, h * width : (h + 1) * width] = (value[:, :width] / sums).astype(out_buf.dtype)
        lse_ref[slot, h : h + 1, :] = first_row(top * (coef * math.log(2.0)) + jnp.log(sums))

    def done(place, last_order):
        if place < -2:
            return
        order = 1 - last_order if place == -2 else last_order
        slot = jnp.where(order == HI, hi, 1 - hi)
        sums = jnp.sum(sum_ref[order], axis=0, keepdims=True)
        log_total = top_ref[order][:1] * (coef * math.log(2.0)) + jnp.log(sums)
        settled = jnp.transpose((acc_ref[order] * (1.0 / sums)).astype(out_buf.dtype))
        for h in range(heads):
            mine = slice(h * rows, (h + 1) * rows)
            lse_ref[slot, h : h + 1, :] = log_total[:, mine]
            out_buf[slot, :, h * width : (h + 1) * width] = settled[mine]
        worst[place + 2 : place + 3] = sums
        out_copy(slot).start()

    attend(coef, visits, sb, turned_q, sum_ref, acc_ref, buffers, done)
    fits = jnp.max(worst[...]) < SUM_LIMIT
    lse_copy.start()
    for slot in range(2):
        out_copy(slot).wait()
    lse_copy.wait()

    @pl.when(jnp.logical_not(fits))
    def _():
        def fetch(src, dst):
            copy = pltpu.make_async_copy(src, dst, sem)
            copy.start()
            copy.wait()

        def online(source):
            @pl.loop(0, 4 * heads)
            def _(i):
                h, slot, order = i // 4, lax.rem(i, 4) // 2, lax.rem(i, 2)
                own_block = jnp.where(order == HI, hi_block, lo_block)
                shift = (own_block - sb[2 * source + slot]) * block_len + inner * rows

                @pl.when(shift + rows > 0)
                def _():
                    own_slot = jnp.where(order == HI, hi, 1 - hi)
                    queries = out_buf[own_slot, :, pl.ds(pl.multiple_of(h * width, width), width)]
                    at = pl.ds(pl.multiple_of(slot * block_len, block_len), block_len)
                    s = score_dot(queries, k_buf[at])
                    row = lax.broadcasted_iota(jnp.int32, s.shape, 0) + shift
                    allowed = lax.broadcasted_iota(jnp.int32, s.shape, 1) <= row
                    s = jnp.where(allowed, s, NEG)
                    before = run_top[order, h]
                    top = jnp.maximum(before, jnp.broadcast_to(jnp.max(s, axis=1, keepdims=True), before.shape))
                    p = jnp.where(allowed, jnp.exp2((s - widen(top, block_len)) * coef), 0.0)
                    run_top[order, h] = top
                    shrink = widen(jnp.exp2((before - top) * coef), 2 * width)
                    lanes = functools.reduce(jnp.add, [p[:, x : x + width] for x in range(0, block_len, width)])
                    fresh = with_sums(p.astype(jnp.bfloat16), lanes, v_buf[at])
                    run_acc[order, h] = run_acc[order, h] * shrink + fresh

        run_top[...] = jnp.full_like(run_top, NEG)
        run_acc[...] = jnp.zeros_like(run_acc)
        def rows_of(slot, half):
            return pl.ds(pl.multiple_of((slot * 2 + half) * half_len, half_len), half_len)

        fetch(every[2], out_buf)
        for slot in range(2):
            fetch(every[0].at[slot], k_buf.at[pl.ds(slot * block_len, block_len)])
            fetch(every[1].at[slot], v_buf.at[pl.ds(slot * block_len, block_len)])
        online(me)
        for place, other in enumerate(distances):
            others = every[3 + 4 * place : 7 + 4 * place]
            for value, (own_buf, twin_buf) in enumerate([(k_buf, v_buf), (v_buf, k_buf)]):

                @pl.when(inner == value)
                def _():
                    for turn in range(2):
                        half = own_half if turn == 0 else 1 - own_half
                        for slot in range(2):
                            fetch(others[2 * turn].at[slot], own_buf.at[rows_of(slot, half)])
                            fetch(others[2 * turn + 1].at[slot], twin_buf.at[rows_of(slot, half)])

            online(source_of(me, other, count))
        for h in range(heads):
            for order in (LO, HI):
                emit(order, h, run_acc[order, h], run_top[order, h])
        for copy in (lse_copy, out_copy(0), out_copy(1)):
            copy.start()
        for copy in (lse_copy, out_copy(0), out_copy(1)):
            copy.wait()


def body(query_rows, key_rows, value_rows, slot_block):
    _, block_len, width = key_rows.shape
    _, rows, feats = query_rows.shape
    heads = feats // width
    all_rows = heads * rows
    count = lax.axis_size("seq")
    coef = math.log2(math.e) / math.sqrt(width)
    distances = list(range(1, count))

    def along_seq(block, distance):
        if is_power(count):
            route = [(i, i ^ distance) for i in range(count)]
        else:
            route = [(i, (i + distance) % count) for i in range(count)]
        with jax.named_scope("along_seq"):
            return lax.ppermute(block, "seq", route)

    def along_head(block):
        with jax.named_scope("along_head"):
            return lax.ppermute(block, "head", [(i, i ^ 1) for i in range(lax.axis_size("head"))])

    def along_inner(block):
        with jax.named_scope("along_inner"):
            return lax.ppermute(block, "inner", [(0, 1), (1, 0)])

    whole = pl.BlockSpec(memory_space=pltpu.VMEM)
    anywhere = pl.BlockSpec(memory_space=pl.ANY)
    scalars = pl.BlockSpec(memory_space=pltpu.SMEM)
    acc_shape = jax.ShapeDtypeStruct((2, width, all_rows), jnp.float32)
    sum_shape = jax.ShapeDtypeStruct((2, SUBLANES, all_rows), jnp.float32)
    turned_shape = jax.ShapeDtypeStruct((2, 2 * width, all_rows), query_rows.dtype)
    top_shape = jax.ShapeDtypeStruct((2, heads, rows), jnp.float32)
    params = pltpu.CompilerParams(vmem_limit_bytes=40 * 1024 * 1024)
    unit = rows * heads * block_len * width * 4
    exps = rows * heads * block_len

    def cost(units, size):
        return pl.CostEstimate(flops=int(2 * units * unit), bytes_accessed=size, transcendentals=int(units * exps))

    in_hbm = [
        pltpu.with_memory_space_constraint(x, pltpu.HBM) for x in (query_rows, key_rows, value_rows, slot_block)
    ]
    half_shape = jax.ShapeDtypeStruct((2, block_len // 2, width), key_rows.dtype)
    piece, sb_here = pl.pallas_call(
        piece_kernel,
        in_specs=[anywhere] * 3,
        out_specs=[whole] * 2,
        out_shape=[half_shape, jax.ShapeDtypeStruct(slot_block.shape, slot_block.dtype)],
        scratch_shapes=[pltpu.SemaphoreType.DMA((2,))],
        cost_estimate=pl.CostEstimate(flops=0, bytes_accessed=400_000, transcendentals=0),
        compiler_params=params,
        name="pick_piece",
    )(*in_hbm[1:])
    arrived, across, beside, beside_across = {}, {}, {}, {}
    for distance in reversed(distances):
        if not is_power(count) or is_power(distance):
            arrived[distance] = along_seq(piece, distance)

    turned_kv = jax.ShapeDtypeStruct((2, width, block_len), key_rows.dtype)
    turned, tops, sums, acc, k_here, v_turned = pl.pallas_call(
        functools.partial(diagonal_kernel, coef, rows),
        in_specs=[scalars] + [anywhere] * 3,
        out_specs=[whole] * 6,
        out_shape=[turned_shape, sum_shape, sum_shape, acc_shape]
        + [jax.ShapeDtypeStruct(key_rows.shape, key_rows.dtype), turned_kv],
        scratch_shapes=[
            pltpu.VMEM((2, all_rows, width), query_rows.dtype),
            pltpu.VMEM(key_rows.shape, key_rows.dtype),
            pltpu.SemaphoreType.DMA((2 + heads,)),
        ],
        cost_estimate=cost(2, 6_000_000),
        compiler_params=params,
        name="diagonal",
    )(sb_here, *in_hbm[:3])
    half_buffers = [
        pltpu.VMEM(half_shape.shape, half_shape.dtype),
        pltpu.VMEM(half_shape.shape, half_shape.dtype),
        pltpu.VMEM((2, width, block_len // 2), half_shape.dtype),
    ]

    def near_half(distance):
        return distance, arrived[distance], beside[distance]

    def far_half(distance):
        return distance, across[distance], beside_across[distance]

    def attended_with(sums, acc, visits):
        return pl.pallas_call(
            functools.partial(middle_kernel, coef, [visit[0] for visit in visits]),
            in_specs=[scalars] + [whole] * (3 + 2 * len(visits)),
            out_specs=[whole] * 2,
            out_shape=[sum_shape, acc_shape],
            scratch_shapes=half_buffers * len(visits),
            input_output_aliases={2: 0, 3: 1},
            cost_estimate=cost(len(visits), 4_000_000),
            compiler_params=params,
            name="visits_of_" + "_".join(str(visit[0]) for visit in visits),
        )(sb_here, turned, sums, acc, *(part for visit in visits for part in visit[1:]))

    def relay(distance):
        if distance in distances and distance not in arrived:
            near = distance & -distance
            arrived[distance] = along_seq(arrived[distance ^ near], near)

    def spread(distance):
        if distance in distances:
            across[distance] = along_head(arrived[distance])
            beside[distance] = along_inner(arrived[distance])

    def settle(distance):
        nonlocal acc
        across[distance], acc = lax.optimization_barrier((across[distance], acc))
        beside_across[distance] = along_inner(across[distance])

    last = distances[-1]
    for distance in sorted(arrived, reverse=True):
        arrived[distance], acc = lax.optimization_barrier((arrived[distance], acc))
    waiting = distances[:2]
    for distance in waiting:
        beside[distance] = along_inner(arrived[distance])
    across[1] = along_head(arrived[1])
    relay(3)
    sums, acc = pl.pallas_call(
        functools.partial(past_kernel, coef),
        in_specs=[scalars] + [whole] * 5,
        out_specs=[whole] * 2,
        out_shape=[sum_shape, acc_shape],
        input_output_aliases={2: 0, 3: 1},
        cost_estimate=cost(1, 4_000_000),
        compiler_params=params,
        name="past",
    )(sb_here, turned, sums, acc, k_here, v_turned)
    arrived[2], acc = lax.optimization_barrier((arrived[2], acc))
    across[2] = along_head(arrived[2])
    sums, acc = attended_with(sums, acc, [near_half(d) for d in waiting])
    for ahead in distances[2:]:
        relay(ahead)
        arrived[ahead], acc = lax.optimization_barrier((arrived[ahead], acc))
        spread(ahead)
        settle(ahead - 2)
        across[ahead - 1], acc = lax.optimization_barrier((across[ahead - 1], acc))
        sums, acc = attended_with(sums, acc, [far_half(ahead - 2), near_half(ahead)])
    final = distances[-2:]
    for distance in final:
        settle(distance)

    flat = [part[d] for d in distances for part in (arrived, beside, across, beside_across)]
    attended, log_total = pl.pallas_call(
        functools.partial(last_kernel, coef, distances, final),
        in_specs=[scalars] + [whole] * (4 + 2 * len(final)) + [anywhere] * (3 + len(flat)),
        out_specs=[anywhere, anywhere],
        out_shape=[jax.ShapeDtypeStruct(query_rows.shape, query_rows.dtype), top_shape],
        scratch_shapes=[
            pltpu.VMEM(query_rows.shape, query_rows.dtype),
            pltpu.VMEM(top_shape.shape, jnp.float32),
        ]
        + half_buffers * len(final)
        + [
            pltpu.VMEM((2, all_rows), jnp.float32),
            pltpu.VMEM((2 * block_len, width), key_rows.dtype),
            pltpu.VMEM((2 * block_len, width), key_rows.dtype),
            pltpu.VMEM((2, heads, rows, width), jnp.float32),
            pltpu.VMEM((2, heads, rows, 2 * width), jnp.float32),
            pltpu.SemaphoreType.DMA,
            pltpu.SemaphoreType.DMA((2,)),
        ],
        cost_estimate=cost(1, 7_000_000),
        compiler_params=params,
        name="last_visitor",
    )(sb_here, turned, tops, sums, acc, *(part for d in final for part in far_half(d)[1:]), in_hbm[1], in_hbm[2], in_hbm[0], *flat)
    return attended, log_total


def solution(mesh):
    placed = (
        P(("groups", "seq"), "inner", "head"),
        P(("groups", "seq"), None, None),
        P(("groups", "seq"), None, None),
        P(),
    )
    return jax.shard_map(
        body,
        mesh=mesh,
        in_specs=placed,
        out_specs=(P(("groups", "seq"), "inner", "head"), P(("groups", "seq"), "head", "inner")),
        check_vma=False,
    )
```

```python
import functools
import math

import jax
import jax.numpy as jnp
from jax import lax
from jax.experimental import pallas as pl
from jax.experimental.pallas import tpu as pltpu
from jax.sharding import PartitionSpec as P

NEG = -1e30
SUM_LIMIT = 1e36
LO, HI = 0, 1
TILE = 256
SUBLANES = 8


def score_dot(q, k):
    return lax.dot_general(q, k, (((1,), (1,)), ((), ())), preferred_element_type=jnp.float32)


def value_dot(p, v):
    return jnp.dot(p, v, preferred_element_type=jnp.float32)


def widen(x, width):
    return jnp.concatenate([x] * (width // x.shape[1]), axis=1)


def is_power(count):
    return count & (count - 1) == 0


def source_of(index, distance, count):
    if is_power(count):
        return index ^ distance
    return lax.rem(index - distance + count, count)


def blocks_of(sb, seq_index):
    b0, b1 = sb[2 * seq_index], sb[2 * seq_index + 1]
    return jnp.where(b1 > b0, 1, 0), jnp.minimum(b0, b1), jnp.maximum(b0, b1)


def key_tiles(count):
    return [(start, min(TILE, count - start)) for start in range(0, count, TILE)]


def piece_kernel(k_hbm, v_hbm, sb_hbm, piece, sb_out, sems):
    half = piece.shape[1]
    inner = lax.axis_index("inner")
    mine = pl.ds(pl.multiple_of(lax.rem(lax.axis_index("head"), 2) * half, half), half)
    sb_copy = pltpu.make_async_copy(sb_hbm, sb_out, sems.at[1])
    for value, src in enumerate((k_hbm, v_hbm)):

        @pl.when(inner == value)
        def _():
            pltpu.make_async_copy(src.at[:, mine], piece, sems.at[0]).start()

    sb_copy.start()
    pltpu.make_async_copy(k_hbm.at[:, mine], piece, sems.at[0]).wait()
    sb_copy.wait()


def weights_of(coef, s):
    p = jnp.exp2(s * coef)
    return p.astype(jnp.bfloat16), folded(jnp.add, p)


def with_ones(x):
    return jnp.concatenate([x, jnp.ones_like(x)], axis=1)


def minus_rows(top, height):
    high = top.astype(jnp.bfloat16).astype(jnp.float32)
    middle = (top - high).astype(jnp.bfloat16).astype(jnp.float32)
    low = top - high - middle
    row = lax.broadcasted_iota(jnp.int32, top.shape, 0)
    picked = jnp.where(row == 0, high, jnp.where(row == 1, middle, jnp.where(row == 2, low, 0.0)))
    zeros = jnp.zeros((height - top.shape[0], top.shape[1]), jnp.float32)
    return jnp.concatenate([-picked, zeros], axis=0).astype(jnp.bfloat16)


def down(x, height):
    return jnp.concatenate([x] * (height // x.shape[0]), axis=0)


def folded(combine, x):
    return functools.reduce(combine, [x[at : at + SUBLANES] for at in range(0, x.shape[0], SUBLANES)])


def with_sums(p, sums, v):
    return jnp.concatenate([value_dot(p, v), sums], axis=1)


def in_turn(chunks, score, finish):
    ready = score(*chunks[0])
    for place, chunk in enumerate(chunks):
        now = ready
        if place + 1 < len(chunks):
            ready = score(*chunks[place + 1])
        finish(now, *chunk)


def local_kernel(coef, rows, sb, q_hbm, k_hbm, v_hbm, turned_q, top_ref, sum_ref, acc_ref, k_ref, turned_v, q_ref, v_ref, sems):
    _, all_rows, width = q_ref.shape
    copies = []
    for h in range(all_rows // rows):
        source, target = q_hbm.at[:, :, pl.ds(h * width, width)], q_ref.at[:, pl.ds(h * rows, rows)]
        copies.append(pltpu.make_async_copy(source, target, sems.at[2 + h]))
    copies.append(pltpu.make_async_copy(k_hbm, k_ref, sems.at[0]))
    copies.append(pltpu.make_async_copy(v_hbm, v_ref, sems.at[1]))
    for copy in copies:
        copy.start()
    for copy in copies:
        copy.wait()
    block_len = k_ref.shape[1]
    hi, _, _ = blocks_of(sb, lax.axis_index("seq"))
    slots = {HI: hi, LO: 1 - hi}
    tiles = key_tiles(block_len)
    for order in (HI, LO):
        turned_q[order, pl.ds(0, width)] = jnp.transpose(q_ref[slots[order]])
        turned_v[order] = jnp.transpose(v_ref[slots[order]])

    def keys(order, start, size):
        return k_ref[slots[order], pl.ds(start, size)]

    def values(order, start, size):
        return turned_v[order, :, start : start + size]

    def masked(order, start, size):
        lane = lax.broadcasted_iota(jnp.int32, (SUBLANES, all_rows), 1)
        heads_below = sum((lane >= at).astype(jnp.int32) for at in range(rows, all_rows, rows))
        row = lane - heads_below * rows + lax.axis_index("inner") * rows
        key = lax.broadcasted_iota(jnp.int32, (size, all_rows), 0) + start
        s = value_dot(keys(order, start, size), turned_q[order, pl.ds(0, width)])
        return jnp.where(key <= down(row, size), s, NEG)

    def highest(scores):
        top = functools.reduce(jnp.maximum, [folded(jnp.maximum, s) for s in scores])
        return jnp.broadcast_to(jnp.max(top, axis=0, keepdims=True), top.shape)

    def settle(order, scores, top):
        total, sums = None, None
        for (start, size), s in zip(tiles, scores):
            p, more = weights_of(coef, s - down(top, size))
            part = value_dot(values(order, start, size), p)
            total, sums = (part, more) if total is None else (total + part, sums + more)
        acc_ref[order] = total
        sum_ref[order] = sums

    def extend(order, scores):
        top = highest(scores)
        top_ref[order] = top
        turned_q[order, pl.ds(width, width)] = minus_rows(top, width)
        return top

    diag = [masked(HI, *tile) for tile in tiles]
    top = extend(HI, diag)
    low = [masked(LO, *tile) for tile in tiles]
    settle(HI, diag, top)
    low_top = extend(LO, low)

    def score(start, size):
        return value_dot(with_ones(keys(LO, start, size)), turned_q[HI])

    def finish(s, start, size):
        p, sums = weights_of(coef, s)
        acc_ref[HI] += value_dot(values(LO, start, size), p)
        sum_ref[HI] += sums

    settle(LO, low, low_top)
    in_turn(tiles, score, finish)


def visit_chunks(distance, own, twin, sb, k_buf, v_buf, turned):
    inner = lax.axis_index("inner")
    for value, (own_buf, twin_buf) in enumerate([(k_buf, v_buf), (v_buf, k_buf)]):

        @pl.when(inner == value)
        def _():
            own_buf[...] = own[...]
            twin_buf[...] = twin[...]

    for slot in range(2):
        turned[slot] = jnp.transpose(v_buf[slot])
    me = lax.axis_index("seq")
    _, _, top_block = blocks_of(sb, me)
    other_hi, _, other_top = blocks_of(sb, source_of(me, distance, lax.axis_size("seq")))
    above = top_block > other_top
    first = (HI, jnp.where(above, 0, 1 - other_hi))
    return first, (jnp.where(above, HI, LO), jnp.where(above, 1, 1 - other_hi))


def attend(coef, visits, sb, turned_q, sum_ref, acc_ref, buffers, done=None):
    chunks, ends = [], []
    laid_out = [visit_chunks(*visit, sb, *buffers[3 * i : 3 * i + 3]) for i, visit in enumerate(visits)]
    for place, pairs in enumerate(laid_out):
        k_buf, _, turned = buffers[3 * place : 3 * place + 3]
        tiles = key_tiles(k_buf.shape[1])
        for order, slot in pairs:
            for tile in tiles:
                chunks.append((len(ends), order, slot, k_buf, turned, *tile))
            ends.append(tiles[-1][0])
    totals = {}

    def score(place, order, slot, k_buf, turned, start, size):
        return value_dot(with_ones(k_buf[slot, pl.ds(start, size)]), turned_q[order])

    def finish(s, place, order, slot, k_buf, turned, start, size):
        p, sums = weights_of(coef, s)
        part = value_dot(turned[slot, :, pl.ds(start, size)], p)
        if start:
            part, sums = totals[place][0] + part, totals[place][1] + sums
        totals[place] = part, sums
        if start == ends[place]:
            acc_ref[order] += part
            sum_ref[order] += sums
            if done is not None:
                done(place - len(ends), laid_out[-1][1][0])

    in_turn(chunks, score, finish)


def first_row(x):
    return jnp.transpose(x)[:1]


def middle_kernel(coef, distances, sb, turned_q, sum_in, acc_in, *refs):
    count = len(distances)
    visits = [(d, refs[2 * i], refs[2 * i + 1]) for i, d in enumerate(distances)]
    sum_ref, acc_ref, *buffers = refs[2 * count :]
    attend(coef, visits, sb, turned_q, sum_ref, acc_ref, buffers)


def last_kernel(coef, distances, final, sb, turned_q, top_ref, sum_ref, acc_ref, *refs):
    visits = [(d, refs[2 * i], refs[2 * i + 1]) for i, d in enumerate(final)]
    refs = refs[2 * len(final) :]
    every, rest = refs[: 4 * len(distances) + 3], refs[4 * len(distances) + 3 :]
    out_hbm, lse_hbm, out_buf, lse_ref, *buffers, worst, k_buf, v_buf, run_top, run_acc, sem, out_sems = rest
    _, rows, feats = out_buf.shape
    width = k_buf.shape[1]
    block_len, heads = k_buf.shape[0] // 2, feats // width
    half_len = block_len // 2
    count = lax.axis_size("seq")
    me = lax.axis_index("seq")
    own_half = lax.rem(lax.axis_index("head"), 2)
    inner = lax.axis_index("inner")
    hi, lo_block, hi_block = blocks_of(sb, me)
    lse_copy = pltpu.make_async_copy(lse_ref, lse_hbm, sem)

    def out_copy(slot):
        return pltpu.make_async_copy(out_buf.at[slot], out_hbm.at[slot], out_sems.at[slot])

    def emit(order, h, value, top):
        slot = hi if order == HI else 1 - hi
        sums = jnp.broadcast_to(jnp.sum(value[:, width:], axis=1, keepdims=True), (rows, width))
        out_buf[slot, :, h * width : (h + 1) * width] = (value[:, :width] / sums).astype(out_buf.dtype)
        lse_ref[slot, h : h + 1, :] = first_row(top * (coef * math.log(2.0)) + jnp.log(sums))

    def done(place, last_order):
        if place < -2:
            return
        order = 1 - last_order if place == -2 else last_order
        slot = jnp.where(order == HI, hi, 1 - hi)
        sums = jnp.sum(sum_ref[order], axis=0, keepdims=True)
        log_total = top_ref[order][:1] * (coef * math.log(2.0)) + jnp.log(sums)
        settled = jnp.transpose((acc_ref[order] * (1.0 / sums)).astype(out_buf.dtype))
        for h in range(heads):
            mine = slice(h * rows, (h + 1) * rows)
            lse_ref[slot, h : h + 1, :] = log_total[:, mine]
            out_buf[slot, :, h * width : (h + 1) * width] = settled[mine]
        worst[place + 2 : place + 3] = sums
        out_copy(slot).start()

    attend(coef, visits, sb, turned_q, sum_ref, acc_ref, buffers, done)
    fits = jnp.max(worst[...]) < SUM_LIMIT
    lse_copy.start()
    for slot in range(2):
        out_copy(slot).wait()
    lse_copy.wait()

    @pl.when(jnp.logical_not(fits))
    def _():
        def fetch(src, dst):
            copy = pltpu.make_async_copy(src, dst, sem)
            copy.start()
            copy.wait()

        def online(source):
            @pl.loop(0, 4 * heads)
            def _(i):
                h, slot, order = i // 4, lax.rem(i, 4) // 2, lax.rem(i, 2)
                own_block = jnp.where(order == HI, hi_block, lo_block)
                shift = (own_block - sb[2 * source + slot]) * block_len + inner * rows

                @pl.when(shift + rows > 0)
                def _():
                    own_slot = jnp.where(order == HI, hi, 1 - hi)
                    queries = out_buf[own_slot, :, pl.ds(pl.multiple_of(h * width, width), width)]
                    at = pl.ds(pl.multiple_of(slot * block_len, block_len), block_len)
                    s = score_dot(queries, k_buf[at])
                    row = lax.broadcasted_iota(jnp.int32, s.shape, 0) + shift
                    allowed = lax.broadcasted_iota(jnp.int32, s.shape, 1) <= row
                    s = jnp.where(allowed, s, NEG)
                    before = run_top[order, h]
                    top = jnp.maximum(before, jnp.broadcast_to(jnp.max(s, axis=1, keepdims=True), before.shape))
                    p = jnp.where(allowed, jnp.exp2((s - widen(top, block_len)) * coef), 0.0)
                    run_top[order, h] = top
                    shrink = widen(jnp.exp2((before - top) * coef), 2 * width)
                    lanes = functools.reduce(jnp.add, [p[:, x : x + width] for x in range(0, block_len, width)])
                    fresh = with_sums(p.astype(jnp.bfloat16), lanes, v_buf[at])
                    run_acc[order, h] = run_acc[order, h] * shrink + fresh

        run_top[...] = jnp.full_like(run_top, NEG)
        run_acc[...] = jnp.zeros_like(run_acc)
        def rows_of(slot, half):
            return pl.ds(pl.multiple_of((slot * 2 + half) * half_len, half_len), half_len)

        fetch(every[2], out_buf)
        for slot in range(2):
            fetch(every[0].at[slot], k_buf.at[pl.ds(slot * block_len, block_len)])
            fetch(every[1].at[slot], v_buf.at[pl.ds(slot * block_len, block_len)])
        online(me)
        for place, other in enumerate(distances):
            others = every[3 + 4 * place : 7 + 4 * place]
            for value, (own_buf, twin_buf) in enumerate([(k_buf, v_buf), (v_buf, k_buf)]):

                @pl.when(inner == value)
                def _():
                    for turn in range(2):
                        half = own_half if turn == 0 else 1 - own_half
                        for slot in range(2):
                            fetch(others[2 * turn].at[slot], own_buf.at[rows_of(slot, half)])
                            fetch(others[2 * turn + 1].at[slot], twin_buf.at[rows_of(slot, half)])

            online(source_of(me, other, count))
        for h in range(heads):
            for order in (LO, HI):
                emit(order, h, run_acc[order, h], run_top[order, h])
        for copy in (lse_copy, out_copy(0), out_copy(1)):
            copy.start()
        for copy in (lse_copy, out_copy(0), out_copy(1)):
            copy.wait()


def body(query_rows, key_rows, value_rows, slot_block):
    _, block_len, width = key_rows.shape
    _, rows, feats = query_rows.shape
    heads = feats // width
    all_rows = heads * rows
    count = lax.axis_size("seq")
    coef = math.log2(math.e) / math.sqrt(width)
    distances = list(range(1, count))

    def along_seq(block, distance):
        if is_power(count):
            route = [(i, i ^ distance) for i in range(count)]
        else:
            route = [(i, (i + distance) % count) for i in range(count)]
        with jax.named_scope("along_seq"):
            return lax.ppermute(block, "seq", route)

    def along_head(block):
        with jax.named_scope("along_head"):
            return lax.ppermute(block, "head", [(i, i ^ 1) for i in range(lax.axis_size("head"))])

    def along_inner(block):
        with jax.named_scope("along_inner"):
            return lax.ppermute(block, "inner", [(0, 1), (1, 0)])

    whole = pl.BlockSpec(memory_space=pltpu.VMEM)
    anywhere = pl.BlockSpec(memory_space=pl.ANY)
    scalars = pl.BlockSpec(memory_space=pltpu.SMEM)
    acc_shape = jax.ShapeDtypeStruct((2, width, all_rows), jnp.float32)
    sum_shape = jax.ShapeDtypeStruct((2, SUBLANES, all_rows), jnp.float32)
    turned_shape = jax.ShapeDtypeStruct((2, 2 * width, all_rows), query_rows.dtype)
    top_shape = jax.ShapeDtypeStruct((2, heads, rows), jnp.float32)
    params = pltpu.CompilerParams(vmem_limit_bytes=40 * 1024 * 1024)
    unit = rows * heads * block_len * width * 4
    exps = rows * heads * block_len

    def cost(units, size):
        return pl.CostEstimate(flops=int(2 * units * unit), bytes_accessed=size, transcendentals=int(units * exps))

    in_hbm = [
        pltpu.with_memory_space_constraint(x, pltpu.HBM) for x in (query_rows, key_rows, value_rows, slot_block)
    ]
    half_shape = jax.ShapeDtypeStruct((2, block_len // 2, width), key_rows.dtype)
    piece, sb_here = pl.pallas_call(
        piece_kernel,
        in_specs=[anywhere] * 3,
        out_specs=[whole] * 2,
        out_shape=[half_shape, jax.ShapeDtypeStruct(slot_block.shape, slot_block.dtype)],
        scratch_shapes=[pltpu.SemaphoreType.DMA((2,))],
        cost_estimate=pl.CostEstimate(flops=0, bytes_accessed=400_000, transcendentals=0),
        compiler_params=params,
        name="pick_piece",
    )(*in_hbm[1:])
    arrived, across, beside, beside_across = {}, {}, {}, {}
    for distance in reversed(distances):
        if not is_power(count) or is_power(distance):
            arrived[distance] = along_seq(piece, distance)

    turned, tops, sums, acc = pl.pallas_call(
        functools.partial(local_kernel, coef, rows),
        in_specs=[scalars] + [anywhere] * 3,
        out_specs=[whole] * 4,
        out_shape=[turned_shape, sum_shape, sum_shape, acc_shape],
        scratch_shapes=[
            pltpu.VMEM(key_rows.shape, key_rows.dtype),
            pltpu.VMEM((2, width, block_len), key_rows.dtype),
            pltpu.VMEM((2, all_rows, width), query_rows.dtype),
            pltpu.VMEM(key_rows.shape, key_rows.dtype),
            pltpu.SemaphoreType.DMA((2 + heads,)),
        ],
        cost_estimate=cost(3, 6_000_000),
        compiler_params=params,
        name="local_part",
    )(sb_here, *in_hbm[:3])
    half_buffers = [
        pltpu.VMEM(half_shape.shape, half_shape.dtype),
        pltpu.VMEM(half_shape.shape, half_shape.dtype),
        pltpu.VMEM((2, width, block_len // 2), half_shape.dtype),
    ]

    def near_half(distance):
        return distance, arrived[distance], beside[distance]

    def far_half(distance):
        return distance, across[distance], beside_across[distance]

    def attended_with(sums, acc, visits):
        return pl.pallas_call(
            functools.partial(middle_kernel, coef, [visit[0] for visit in visits]),
            in_specs=[scalars] + [whole] * (3 + 2 * len(visits)),
            out_specs=[whole] * 2,
            out_shape=[sum_shape, acc_shape],
            scratch_shapes=half_buffers * len(visits),
            input_output_aliases={2: 0, 3: 1},
            cost_estimate=cost(len(visits), 4_000_000),
            compiler_params=params,
            name="visits_of_" + "_".join(str(visit[0]) for visit in visits),
        )(sb_here, turned, sums, acc, *(part for visit in visits for part in visit[1:]))

    def relay(distance):
        if distance in distances and distance not in arrived:
            near = distance & -distance
            arrived[distance] = along_seq(arrived[distance ^ near], near)

    def spread(distance):
        if distance in distances:
            across[distance] = along_head(arrived[distance])
            beside[distance] = along_inner(arrived[distance])

    def settle(distance):
        nonlocal acc
        across[distance], acc = lax.optimization_barrier((across[distance], acc))
        beside_across[distance] = along_inner(across[distance])

    last = distances[-1]
    for distance in sorted(arrived, reverse=True):
        arrived[distance], acc = lax.optimization_barrier((arrived[distance], acc))
    waiting = distances[:2]
    for distance in waiting:
        beside[distance] = along_inner(arrived[distance])
    across[1] = along_head(arrived[1])
    relay(3)
    across[2] = along_head(arrived[2])
    sums, acc = attended_with(sums, acc, [near_half(d) for d in waiting])
    for ahead in distances[2:]:
        relay(ahead)
        arrived[ahead], acc = lax.optimization_barrier((arrived[ahead], acc))
        spread(ahead)
        settle(ahead - 2)
        across[ahead - 1], acc = lax.optimization_barrier((across[ahead - 1], acc))
        sums, acc = attended_with(sums, acc, [far_half(ahead - 2), near_half(ahead)])
    across[last], acc = lax.optimization_barrier((across[last], acc))
    for distance in distances[-2:]:
        beside_across[distance] = along_inner(across[distance])
    sums, acc = attended_with(sums, acc, [far_half(last - 1)])
    final = [last]

    flat = [part[d] for d in distances for part in (arrived, beside, across, beside_across)]
    attended, log_total = pl.pallas_call(
        functools.partial(last_kernel, coef, distances, final),
        in_specs=[scalars] + [whole] * (4 + 2 * len(final)) + [anywhere] * (3 + len(flat)),
        out_specs=[anywhere, anywhere],
        out_shape=[jax.ShapeDtypeStruct(query_rows.shape, query_rows.dtype), top_shape],
        scratch_shapes=[
            pltpu.VMEM(query_rows.shape, query_rows.dtype),
            pltpu.VMEM(top_shape.shape, jnp.float32),
        ]
        + half_buffers * len(final)
        + [
            pltpu.VMEM((2, all_rows), jnp.float32),
            pltpu.VMEM((2 * block_len, width), key_rows.dtype),
            pltpu.VMEM((2 * block_len, width), key_rows.dtype),
            pltpu.VMEM((2, heads, rows, width), jnp.float32),
            pltpu.VMEM((2, heads, rows, 2 * width), jnp.float32),
            pltpu.SemaphoreType.DMA,
            pltpu.SemaphoreType.DMA((2,)),
        ],
        cost_estimate=cost(1, 7_000_000),
        compiler_params=params,
        name="last_visitor",
    )(sb_here, turned, tops, sums, acc, *(part for d in final for part in far_half(d)[1:]), in_hbm[1], in_hbm[2], in_hbm[0], *flat)
    return attended, log_total


def solution(mesh):
    placed = (
        P(("groups", "seq"), "inner", "head"),
        P(("groups", "seq"), None, None),
        P(("groups", "seq"), None, None),
        P(),
    )
    return jax.shard_map(
        body,
        mesh=mesh,
        in_specs=placed,
        out_specs=(P(("groups", "seq"), "inner", "head"), P(("groups", "seq"), "head", "inner")),
        check_vma=False,
    )
```

```python
import functools
import math

import jax
import jax.numpy as jnp
from jax import lax
from jax.experimental import pallas as pl
from jax.experimental.pallas import tpu as pltpu
from jax.sharding import PartitionSpec as P

NEG = -1e30
SUM_LIMIT = 1e36
LO, HI = 0, 1
TILE = 256
SUBLANES = 8


def score_dot(q, k):
    return lax.dot_general(q, k, (((1,), (1,)), ((), ())), preferred_element_type=jnp.float32)


def value_dot(p, v):
    return jnp.dot(p, v, preferred_element_type=jnp.float32)


def widen(x, width):
    return jnp.concatenate([x] * (width // x.shape[1]), axis=1)


def is_power(count):
    return count & (count - 1) == 0


def source_of(index, distance, count):
    if is_power(count):
        return index ^ distance
    return lax.rem(index - distance + count, count)


def blocks_of(sb, seq_index):
    b0, b1 = sb[2 * seq_index], sb[2 * seq_index + 1]
    return jnp.where(b1 > b0, 1, 0), jnp.minimum(b0, b1), jnp.maximum(b0, b1)


def key_tiles(count):
    return [(start, min(TILE, count - start)) for start in range(0, count, TILE)]


def piece_kernel(k_hbm, v_hbm, sb_hbm, piece, far_piece, sb_out, sems):
    half = piece.shape[1]
    inner = lax.axis_index("inner")
    own_half = lax.rem(lax.axis_index("head"), 2)

    def copies(src):
        found = []
        for place, (part, target) in enumerate([(own_half, piece), (1 - own_half, far_piece)]):
            rows = pl.ds(pl.multiple_of(part * half, half), half)
            found.append(pltpu.make_async_copy(src.at[:, rows], target, sems.at[place]))
        return found

    for value, src in enumerate((k_hbm, v_hbm)):

        @pl.when(inner == value)
        def _():
            for copy in copies(src):
                copy.start()

    sb_copy = pltpu.make_async_copy(sb_hbm, sb_out, sems.at[2])
    sb_copy.start()
    for copy in copies(k_hbm):
        copy.wait()
    sb_copy.wait()


def weights_of(coef, s):
    p = jnp.exp2(s * coef)
    return p.astype(jnp.bfloat16), folded(jnp.add, p)


def with_ones(x):
    return jnp.concatenate([x, jnp.ones_like(x)], axis=1)


def minus_rows(top, height):
    high = top.astype(jnp.bfloat16).astype(jnp.float32)
    middle = (top - high).astype(jnp.bfloat16).astype(jnp.float32)
    low = top - high - middle
    row = lax.broadcasted_iota(jnp.int32, top.shape, 0)
    picked = jnp.where(row == 0, high, jnp.where(row == 1, middle, jnp.where(row == 2, low, 0.0)))
    zeros = jnp.zeros((height - top.shape[0], top.shape[1]), jnp.float32)
    return jnp.concatenate([-picked, zeros], axis=0).astype(jnp.bfloat16)


def down(x, height):
    return jnp.concatenate([x] * (height // x.shape[0]), axis=0)


def folded(combine, x):
    return functools.reduce(combine, [x[at : at + SUBLANES] for at in range(0, x.shape[0], SUBLANES)])


def with_sums(p, sums, v):
    return jnp.concatenate([value_dot(p, v), sums], axis=1)


def in_turn(chunks, score, finish):
    ready = score(*chunks[0])
    for place, chunk in enumerate(chunks):
        now = ready
        if place + 1 < len(chunks):
            ready = score(*chunks[place + 1])
        finish(now, *chunk)


def local_kernel(coef, rows, sb, q_hbm, k_hbm, v_hbm, turned_q, top_ref, sum_ref, acc_ref, k_ref, turned_v, q_ref, v_ref, sems):
    _, all_rows, width = q_ref.shape
    copies = []
    for h in range(all_rows // rows):
        source, target = q_hbm.at[:, :, pl.ds(h * width, width)], q_ref.at[:, pl.ds(h * rows, rows)]
        copies.append(pltpu.make_async_copy(source, target, sems.at[2 + h]))
    copies.append(pltpu.make_async_copy(k_hbm, k_ref, sems.at[0]))
    copies.append(pltpu.make_async_copy(v_hbm, v_ref, sems.at[1]))
    for copy in copies:
        copy.start()
    for copy in copies:
        copy.wait()
    block_len = k_ref.shape[1]
    hi, _, _ = blocks_of(sb, lax.axis_index("seq"))
    slots = {HI: hi, LO: 1 - hi}
    tiles = key_tiles(block_len)
    for order in (HI, LO):
        turned_q[order, pl.ds(0, width)] = jnp.transpose(q_ref[slots[order]])
        turned_v[order] = jnp.transpose(v_ref[slots[order]])

    def keys(order, start, size):
        return k_ref[slots[order], pl.ds(start, size)]

    def values(order, start, size):
        return turned_v[order, :, start : start + size]

    def masked(order, start, size):
        lane = lax.broadcasted_iota(jnp.int32, (SUBLANES, all_rows), 1)
        heads_below = sum((lane >= at).astype(jnp.int32) for at in range(rows, all_rows, rows))
        row = lane - heads_below * rows + lax.axis_index("inner") * rows
        key = lax.broadcasted_iota(jnp.int32, (size, all_rows), 0) + start
        s = value_dot(keys(order, start, size), turned_q[order, pl.ds(0, width)])
        return jnp.where(key <= down(row, size), s, NEG)

    def highest(scores):
        top = functools.reduce(jnp.maximum, [folded(jnp.maximum, s) for s in scores])
        return jnp.broadcast_to(jnp.max(top, axis=0, keepdims=True), top.shape)

    def settle(order, scores, top):
        total, sums = None, None
        for (start, size), s in zip(tiles, scores):
            p, more = weights_of(coef, s - down(top, size))
            part = value_dot(values(order, start, size), p)
            total, sums = (part, more) if total is None else (total + part, sums + more)
        acc_ref[order] = total
        sum_ref[order] = sums

    def extend(order, scores):
        top = highest(scores)
        top_ref[order] = top
        turned_q[order, pl.ds(width, width)] = minus_rows(top, width)
        return top

    diag = [masked(HI, *tile) for tile in tiles]
    top = extend(HI, diag)
    low = [masked(LO, *tile) for tile in tiles]
    settle(HI, diag, top)
    low_top = extend(LO, low)

    def score(start, size):
        return value_dot(with_ones(keys(LO, start, size)), turned_q[HI])

    def finish(s, start, size):
        p, sums = weights_of(coef, s)
        acc_ref[HI] += value_dot(values(LO, start, size), p)
        sum_ref[HI] += sums

    settle(LO, low, low_top)
    in_turn(tiles, score, finish)


def visit_chunks(distance, own, twin, sb, k_buf, v_buf, turned):
    inner = lax.axis_index("inner")
    for value, (own_buf, twin_buf) in enumerate([(k_buf, v_buf), (v_buf, k_buf)]):

        @pl.when(inner == value)
        def _():
            own_buf[...] = own[...]
            twin_buf[...] = twin[...]

    for slot in range(2):
        turned[slot] = jnp.transpose(v_buf[slot])
    me = lax.axis_index("seq")
    _, _, top_block = blocks_of(sb, me)
    other_hi, _, other_top = blocks_of(sb, source_of(me, distance, lax.axis_size("seq")))
    above = top_block > other_top
    first = (HI, jnp.where(above, 0, 1 - other_hi))
    return first, (jnp.where(above, HI, LO), jnp.where(above, 1, 1 - other_hi))


def attend(coef, visits, sb, turned_q, sum_ref, acc_ref, buffers, done=None):
    chunks, ends = [], []
    laid_out = [visit_chunks(*visit, sb, *buffers[3 * i : 3 * i + 3]) for i, visit in enumerate(visits)]
    for place, pairs in enumerate(laid_out):
        k_buf, _, turned = buffers[3 * place : 3 * place + 3]
        tiles = key_tiles(k_buf.shape[1])
        for order, slot in pairs:
            for tile in tiles:
                chunks.append((len(ends), order, slot, k_buf, turned, *tile))
            ends.append(tiles[-1][0])
    totals = {}

    def score(place, order, slot, k_buf, turned, start, size):
        return value_dot(with_ones(k_buf[slot, pl.ds(start, size)]), turned_q[order])

    def finish(s, place, order, slot, k_buf, turned, start, size):
        p, sums = weights_of(coef, s)
        part = value_dot(turned[slot, :, pl.ds(start, size)], p)
        if start:
            part, sums = totals[place][0] + part, totals[place][1] + sums
        totals[place] = part, sums
        if start == ends[place]:
            acc_ref[order] += part
            sum_ref[order] += sums
            if done is not None:
                done(place - len(ends), laid_out[-1][1][0])

    in_turn(chunks, score, finish)


def first_row(x):
    return jnp.transpose(x)[:1]


def middle_kernel(coef, distances, sb, turned_q, sum_in, acc_in, *refs):
    count = len(distances)
    visits = [(d, refs[2 * i], refs[2 * i + 1]) for i, d in enumerate(distances)]
    sum_ref, acc_ref, *buffers = refs[2 * count :]
    attend(coef, visits, sb, turned_q, sum_ref, acc_ref, buffers)


def last_kernel(coef, distances, final, sb, turned_q, top_ref, sum_ref, acc_ref, *refs):
    visits = [(d, refs[2 * i], refs[2 * i + 1]) for i, d in enumerate(final)]
    refs = refs[2 * len(final) :]
    every, rest = refs[: 4 * len(distances) + 3], refs[4 * len(distances) + 3 :]
    out_hbm, lse_hbm, out_buf, lse_ref, *buffers, worst, k_buf, v_buf, run_top, run_acc, sem, out_sems = rest
    _, rows, feats = out_buf.shape
    width = k_buf.shape[1]
    block_len, heads = k_buf.shape[0] // 2, feats // width
    half_len = block_len // 2
    count = lax.axis_size("seq")
    me = lax.axis_index("seq")
    own_half = lax.rem(lax.axis_index("head"), 2)
    inner = lax.axis_index("inner")
    hi, lo_block, hi_block = blocks_of(sb, me)
    lse_copy = pltpu.make_async_copy(lse_ref, lse_hbm, sem)

    def out_copy(slot):
        return pltpu.make_async_copy(out_buf.at[slot], out_hbm.at[slot], out_sems.at[slot])

    def emit(order, h, value, top):
        slot = hi if order == HI else 1 - hi
        sums = jnp.broadcast_to(jnp.sum(value[:, width:], axis=1, keepdims=True), (rows, width))
        out_buf[slot, :, h * width : (h + 1) * width] = (value[:, :width] / sums).astype(out_buf.dtype)
        lse_ref[slot, h : h + 1, :] = first_row(top * (coef * math.log(2.0)) + jnp.log(sums))

    def done(place, last_order):
        if place < -2:
            return
        order = 1 - last_order if place == -2 else last_order
        slot = jnp.where(order == HI, hi, 1 - hi)
        sums = jnp.sum(sum_ref[order], axis=0, keepdims=True)
        log_total = top_ref[order][:1] * (coef * math.log(2.0)) + jnp.log(sums)
        settled = jnp.transpose((acc_ref[order] * (1.0 / sums)).astype(out_buf.dtype))
        for h in range(heads):
            mine = slice(h * rows, (h + 1) * rows)
            lse_ref[slot, h : h + 1, :] = log_total[:, mine]
            out_buf[slot, :, h * width : (h + 1) * width] = settled[mine]
        worst[place + 2 : place + 3] = sums
        out_copy(slot).start()

    attend(coef, visits, sb, turned_q, sum_ref, acc_ref, buffers, done)
    fits = jnp.max(worst[...]) < SUM_LIMIT
    lse_copy.start()
    for slot in range(2):
        out_copy(slot).wait()
    lse_copy.wait()

    @pl.when(jnp.logical_not(fits))
    def _():
        def fetch(src, dst):
            copy = pltpu.make_async_copy(src, dst, sem)
            copy.start()
            copy.wait()

        def online(source):
            @pl.loop(0, 4 * heads)
            def _(i):
                h, slot, order = i // 4, lax.rem(i, 4) // 2, lax.rem(i, 2)
                own_block = jnp.where(order == HI, hi_block, lo_block)
                shift = (own_block - sb[2 * source + slot]) * block_len + inner * rows

                @pl.when(shift + rows > 0)
                def _():
                    own_slot = jnp.where(order == HI, hi, 1 - hi)
                    queries = out_buf[own_slot, :, pl.ds(pl.multiple_of(h * width, width), width)]
                    at = pl.ds(pl.multiple_of(slot * block_len, block_len), block_len)
                    s = score_dot(queries, k_buf[at])
                    row = lax.broadcasted_iota(jnp.int32, s.shape, 0) + shift
                    allowed = lax.broadcasted_iota(jnp.int32, s.shape, 1) <= row
                    s = jnp.where(allowed, s, NEG)
                    before = run_top[order, h]
                    top = jnp.maximum(before, jnp.broadcast_to(jnp.max(s, axis=1, keepdims=True), before.shape))
                    p = jnp.where(allowed, jnp.exp2((s - widen(top, block_len)) * coef), 0.0)
                    run_top[order, h] = top
                    shrink = widen(jnp.exp2((before - top) * coef), 2 * width)
                    lanes = functools.reduce(jnp.add, [p[:, x : x + width] for x in range(0, block_len, width)])
                    fresh = with_sums(p.astype(jnp.bfloat16), lanes, v_buf[at])
                    run_acc[order, h] = run_acc[order, h] * shrink + fresh

        run_top[...] = jnp.full_like(run_top, NEG)
        run_acc[...] = jnp.zeros_like(run_acc)
        def rows_of(slot, half):
            return pl.ds(pl.multiple_of((slot * 2 + half) * half_len, half_len), half_len)

        fetch(every[2], out_buf)
        for slot in range(2):
            fetch(every[0].at[slot], k_buf.at[pl.ds(slot * block_len, block_len)])
            fetch(every[1].at[slot], v_buf.at[pl.ds(slot * block_len, block_len)])
        online(me)
        for place, other in enumerate(distances):
            others = every[3 + 4 * place : 7 + 4 * place]
            for value, (own_buf, twin_buf) in enumerate([(k_buf, v_buf), (v_buf, k_buf)]):

                @pl.when(inner == value)
                def _():
                    for turn in range(2):
                        half = own_half if turn == 0 else 1 - own_half
                        for slot in range(2):
                            fetch(others[2 * turn].at[slot], own_buf.at[rows_of(slot, half)])
                            fetch(others[2 * turn + 1].at[slot], twin_buf.at[rows_of(slot, half)])

            online(source_of(me, other, count))
        for h in range(heads):
            for order in (LO, HI):
                emit(order, h, run_acc[order, h], run_top[order, h])
        for copy in (lse_copy, out_copy(0), out_copy(1)):
            copy.start()
        for copy in (lse_copy, out_copy(0), out_copy(1)):
            copy.wait()


def body(query_rows, key_rows, value_rows, slot_block):
    _, block_len, width = key_rows.shape
    _, rows, feats = query_rows.shape
    heads = feats // width
    all_rows = heads * rows
    count = lax.axis_size("seq")
    coef = math.log2(math.e) / math.sqrt(width)
    distances = list(range(1, count))

    def along_seq(block, distance):
        if is_power(count):
            route = [(i, i ^ distance) for i in range(count)]
        else:
            route = [(i, (i + distance) % count) for i in range(count)]
        with jax.named_scope("along_seq"):
            return lax.ppermute(block, "seq", route)

    def along_head(block):
        with jax.named_scope("along_head"):
            return lax.ppermute(block, "head", [(i, i ^ 1) for i in range(lax.axis_size("head"))])

    def along_inner(block):
        with jax.named_scope("along_inner"):
            return lax.ppermute(block, "inner", [(0, 1), (1, 0)])

    whole = pl.BlockSpec(memory_space=pltpu.VMEM)
    anywhere = pl.BlockSpec(memory_space=pl.ANY)
    scalars = pl.BlockSpec(memory_space=pltpu.SMEM)
    acc_shape = jax.ShapeDtypeStruct((2, width, all_rows), jnp.float32)
    sum_shape = jax.ShapeDtypeStruct((2, SUBLANES, all_rows), jnp.float32)
    turned_shape = jax.ShapeDtypeStruct((2, 2 * width, all_rows), query_rows.dtype)
    top_shape = jax.ShapeDtypeStruct((2, heads, rows), jnp.float32)
    params = pltpu.CompilerParams(vmem_limit_bytes=40 * 1024 * 1024)
    unit = rows * heads * block_len * width * 4
    exps = rows * heads * block_len

    def cost(units, size):
        return pl.CostEstimate(flops=int(2 * units * unit), bytes_accessed=size, transcendentals=int(units * exps))

    in_hbm = [
        pltpu.with_memory_space_constraint(x, pltpu.HBM) for x in (query_rows, key_rows, value_rows, slot_block)
    ]
    half_shape = jax.ShapeDtypeStruct((2, block_len // 2, width), key_rows.dtype)
    piece, far_piece, sb_here = pl.pallas_call(
        piece_kernel,
        in_specs=[anywhere] * 3,
        out_specs=[whole] * 3,
        out_shape=[half_shape, half_shape, jax.ShapeDtypeStruct(slot_block.shape, slot_block.dtype)],
        scratch_shapes=[pltpu.SemaphoreType.DMA((3,))],
        cost_estimate=pl.CostEstimate(flops=0, bytes_accessed=400_000, transcendentals=0),
        compiler_params=params,
        name="pick_piece",
    )(*in_hbm[1:])
    arrived, across, beside, beside_across = {}, {}, {}, {}
    for distance in reversed(distances):
        if not is_power(count) or is_power(distance):
            arrived[distance] = along_seq(piece, distance)

    turned, tops, sums, acc = pl.pallas_call(
        functools.partial(local_kernel, coef, rows),
        in_specs=[scalars] + [anywhere] * 3,
        out_specs=[whole] * 4,
        out_shape=[turned_shape, sum_shape, sum_shape, acc_shape],
        scratch_shapes=[
            pltpu.VMEM(key_rows.shape, key_rows.dtype),
            pltpu.VMEM((2, width, block_len), key_rows.dtype),
            pltpu.VMEM((2, all_rows, width), query_rows.dtype),
            pltpu.VMEM(key_rows.shape, key_rows.dtype),
            pltpu.SemaphoreType.DMA((2 + heads,)),
        ],
        cost_estimate=cost(3, 6_000_000),
        compiler_params=params,
        name="local_part",
    )(sb_here, *in_hbm[:3])
    half_buffers = [
        pltpu.VMEM(half_shape.shape, half_shape.dtype),
        pltpu.VMEM(half_shape.shape, half_shape.dtype),
        pltpu.VMEM((2, width, block_len // 2), half_shape.dtype),
    ]

    def near_half(distance):
        return distance, arrived[distance], beside[distance]

    def far_half(distance):
        return distance, across[distance], beside_across[distance]

    def attended_with(sums, acc, visits):
        return pl.pallas_call(
            functools.partial(middle_kernel, coef, [visit[0] for visit in visits]),
            in_specs=[scalars] + [whole] * (3 + 2 * len(visits)),
            out_specs=[whole] * 2,
            out_shape=[sum_shape, acc_shape],
            scratch_shapes=half_buffers * len(visits),
            input_output_aliases={2: 0, 3: 1},
            cost_estimate=cost(len(visits), 4_000_000),
            compiler_params=params,
            name="visits_of_" + "_".join(str(visit[0]) for visit in visits),
        )(sb_here, turned, sums, acc, *(part for visit in visits for part in visit[1:]))

    def relay(distance):
        if distance in distances and distance not in arrived:
            near = distance & -distance
            arrived[distance] = along_seq(arrived[distance ^ near], near)

    def spread(distance):
        if distance in distances:
            across[distance] = along_head(arrived[distance])
            beside[distance] = along_inner(arrived[distance])

    def settle(distance):
        nonlocal acc
        across[distance], acc = lax.optimization_barrier((across[distance], acc))
        beside_across[distance] = along_inner(across[distance])

    last = distances[-1]
    ready = sorted(arrived, reverse=True)
    *first, acc = lax.optimization_barrier((*(arrived[d] for d in ready), acc))
    arrived.update(zip(ready, first))

    def meet(distance):
        nonlocal acc
        arrived[distance], acc = lax.optimization_barrier((arrived[distance], acc))

    relay(3)
    across[2] = along_head(arrived[2])
    for distance in (1, 2):
        beside[distance] = along_inner(arrived[distance])
    sums, acc = attended_with(sums, acc, [near_half(1), near_half(2)])
    for ahead in distances[2:]:
        relay(ahead)
        meet(ahead)
        spread(ahead)
        if ahead == 3:
            far_piece, acc = lax.optimization_barrier((far_piece, acc))
            across[1] = along_seq(far_piece, 1)
        settle(ahead - 1)
        sums, acc = attended_with(sums, acc, [far_half(ahead - 1), near_half(ahead)])
    tied = (across[last], across[1], acc)
    across[last], across[1], acc = lax.optimization_barrier(tied)
    for distance in (1, last):
        beside_across[distance] = along_inner(across[distance])
    sums, acc = attended_with(sums, acc, [far_half(1)])
    final = [last]

    flat = [part[d] for d in distances for part in (arrived, beside, across, beside_across)]
    attended, log_total = pl.pallas_call(
        functools.partial(last_kernel, coef, distances, final),
        in_specs=[scalars] + [whole] * (4 + 2 * len(final)) + [anywhere] * (3 + len(flat)),
        out_specs=[anywhere, anywhere],
        out_shape=[jax.ShapeDtypeStruct(query_rows.shape, query_rows.dtype), top_shape],
        scratch_shapes=[
            pltpu.VMEM(query_rows.shape, query_rows.dtype),
            pltpu.VMEM(top_shape.shape, jnp.float32),
        ]
        + half_buffers * len(final)
        + [
            pltpu.VMEM((2, all_rows), jnp.float32),
            pltpu.VMEM((2 * block_len, width), key_rows.dtype),
            pltpu.VMEM((2 * block_len, width), key_rows.dtype),
            pltpu.VMEM((2, heads, rows, width), jnp.float32),
            pltpu.VMEM((2, heads, rows, 2 * width), jnp.float32),
            pltpu.SemaphoreType.DMA,
            pltpu.SemaphoreType.DMA((2,)),
        ],
        cost_estimate=cost(1, 7_000_000),
        compiler_params=params,
        name="last_visitor",
    )(sb_here, turned, tops, sums, acc, *(part for d in final for part in far_half(d)[1:]), in_hbm[1], in_hbm[2], in_hbm[0], *flat)
    return attended, log_total


def solution(mesh):
    placed = (
        P(("groups", "seq"), "inner", "head"),
        P(("groups", "seq"), None, None),
        P(("groups", "seq"), None, None),
        P(),
    )
    return jax.shard_map(
        body,
        mesh=mesh,
        in_specs=placed,
        out_specs=(P(("groups", "seq"), "inner", "head"), P(("groups", "seq"), "head", "inner")),
        check_vma=False,
    )
```

```python
import functools
import math

import jax
import jax.numpy as jnp
from jax import lax
from jax.experimental import pallas as pl
from jax.experimental.pallas import tpu as pltpu
from jax.sharding import PartitionSpec as P

NEG = -1e30
SUM_LIMIT = 1e36
LO, HI = 0, 1
TILE = 256
SUBLANES = 8


def score_dot(q, k):
    return lax.dot_general(q, k, (((1,), (1,)), ((), ())), preferred_element_type=jnp.float32)


def value_dot(p, v):
    return jnp.dot(p, v, preferred_element_type=jnp.float32)


def widen(x, width):
    return jnp.concatenate([x] * (width // x.shape[1]), axis=1)


def is_power(count):
    return count & (count - 1) == 0


def source_of(index, distance, count):
    if is_power(count):
        return index ^ distance
    return lax.rem(index - distance + count, count)


def blocks_of(sb, seq_index):
    b0, b1 = sb[2 * seq_index], sb[2 * seq_index + 1]
    return jnp.where(b1 > b0, 1, 0), jnp.minimum(b0, b1), jnp.maximum(b0, b1)


def key_tiles(count):
    return [(start, min(TILE, count - start)) for start in range(0, count, TILE)]


def piece_kernel(k_hbm, v_hbm, sb_hbm, piece, sb_out, sems):
    half = piece.shape[1]
    inner = lax.axis_index("inner")
    mine = pl.ds(pl.multiple_of(lax.rem(lax.axis_index("head"), 2) * half, half), half)
    sb_copy = pltpu.make_async_copy(sb_hbm, sb_out, sems.at[1])
    for value, src in enumerate((k_hbm, v_hbm)):

        @pl.when(inner == value)
        def _():
            pltpu.make_async_copy(src.at[:, mine], piece, sems.at[0]).start()

    sb_copy.start()
    pltpu.make_async_copy(k_hbm.at[:, mine], piece, sems.at[0]).wait()
    sb_copy.wait()


def weights_of(coef, s):
    p = jnp.exp2(s * coef)
    return p.astype(jnp.bfloat16), folded(jnp.add, p)


def with_ones(x):
    return jnp.concatenate([x, jnp.ones_like(x)], axis=1)


def minus_rows(top, height):
    high = top.astype(jnp.bfloat16).astype(jnp.float32)
    middle = (top - high).astype(jnp.bfloat16).astype(jnp.float32)
    low = top - high - middle
    row = lax.broadcasted_iota(jnp.int32, top.shape, 0)
    picked = jnp.where(row == 0, high, jnp.where(row == 1, middle, jnp.where(row == 2, low, 0.0)))
    zeros = jnp.zeros((height - top.shape[0], top.shape[1]), jnp.float32)
    return jnp.concatenate([-picked, zeros], axis=0).astype(jnp.bfloat16)


def down(x, height):
    return jnp.concatenate([x] * (height // x.shape[0]), axis=0)


def folded(combine, x):
    return functools.reduce(combine, [x[at : at + SUBLANES] for at in range(0, x.shape[0], SUBLANES)])


def with_sums(p, sums, v):
    return jnp.concatenate([value_dot(p, v), sums], axis=1)


def in_turn(chunks, score, finish):
    ready = score(*chunks[0])
    for place, chunk in enumerate(chunks):
        now = ready
        if place + 1 < len(chunks):
            ready = score(*chunks[place + 1])
        finish(now, *chunk)


def local_kernel(coef, rows, sb, q_hbm, k_hbm, v_hbm, turned_q, top_ref, sum_ref, acc_ref, notes, k_ref, turned_v, q_ref, v_ref, sems):
    _, all_rows, width = q_ref.shape
    copies = []
    for h in range(all_rows // rows):
        source, target = q_hbm.at[:, :, pl.ds(h * width, width)], q_ref.at[:, pl.ds(h * rows, rows)]
        copies.append(pltpu.make_async_copy(source, target, sems.at[2 + h]))
    copies.append(pltpu.make_async_copy(k_hbm, k_ref, sems.at[0]))
    copies.append(pltpu.make_async_copy(v_hbm, v_ref, sems.at[1]))
    for copy in copies:
        copy.start()
    for copy in copies:
        copy.wait()
    block_len = k_ref.shape[1]
    hi, _, _ = blocks_of(sb, lax.axis_index("seq"))
    slots = {HI: hi, LO: 1 - hi}
    tiles = key_tiles(block_len)
    me, count = lax.axis_index("seq"), lax.axis_size("seq")
    notes[0] = jnp.full(notes.shape[1:], hi, jnp.int32).astype(jnp.float32)
    for distance in range(1, count):
        notes[distance] = jnp.full(notes.shape[1:], visit_code(sb, me, distance, count), jnp.int32).astype(jnp.float32)
    for order in (HI, LO):
        turned_q[order, pl.ds(0, width)] = jnp.transpose(q_ref[slots[order]])
        turned_v[order] = jnp.transpose(v_ref[slots[order]])

    def keys(order, start, size):
        return k_ref[slots[order], pl.ds(start, size)]

    def values(order, start, size):
        return turned_v[order, :, start : start + size]

    def masked(order, start, size):
        lane = lax.broadcasted_iota(jnp.int32, (SUBLANES, all_rows), 1)
        heads_below = sum((lane >= at).astype(jnp.int32) for at in range(rows, all_rows, rows))
        row = lane - heads_below * rows + lax.axis_index("inner") * rows
        key = lax.broadcasted_iota(jnp.int32, (size, all_rows), 0) + start
        s = value_dot(keys(order, start, size), turned_q[order, pl.ds(0, width)])
        return jnp.where(key <= down(row, size), s, NEG)

    def highest(scores):
        top = functools.reduce(jnp.maximum, [folded(jnp.maximum, s) for s in scores])
        return jnp.broadcast_to(jnp.max(top, axis=0, keepdims=True), top.shape)

    def settle(order, scores, top):
        total, sums = None, None
        for (start, size), s in zip(tiles, scores):
            p, more = weights_of(coef, s - down(top, size))
            part = value_dot(values(order, start, size), p)
            total, sums = (part, more) if total is None else (total + part, sums + more)
        acc_ref[order] = total
        sum_ref[order] = sums

    def extend(order, scores):
        top = highest(scores)
        top_ref[order] = top
        turned_q[order, pl.ds(width, width)] = minus_rows(top, width)
        return top

    diag = [masked(HI, *tile) for tile in tiles]
    top = extend(HI, diag)
    low = [masked(LO, *tile) for tile in tiles]
    settle(HI, diag, top)
    low_top = extend(LO, low)

    def score(start, size):
        return value_dot(with_ones(keys(LO, start, size)), turned_q[HI])

    def finish(s, start, size):
        p, sums = weights_of(coef, s)
        acc_ref[HI] += value_dot(values(LO, start, size), p)
        sum_ref[HI] += sums

    settle(LO, low, low_top)
    in_turn(tiles, score, finish)


def visit_code(sb, me, distance, count):
    _, _, top_block = blocks_of(sb, me)
    other_hi, _, other_top = blocks_of(sb, source_of(me, distance, count))
    above = top_block > other_top
    other_lo = 1 - other_hi
    return other_lo + 2 * jnp.where(above, other_hi, other_lo) + 4 * jnp.where(above, HI, LO)


def noted(notes, place):
    return jnp.max(notes[place]).astype(jnp.int32)


def visit_chunks(distance, own, twin, notes, k_buf, v_buf, turned):
    code = noted(notes, distance)
    inner = lax.axis_index("inner")
    for value, (own_buf, twin_buf) in enumerate([(k_buf, v_buf), (v_buf, k_buf)]):

        @pl.when(inner == value)
        def _():
            own_buf[...] = own[...]
            twin_buf[...] = twin[...]

    for slot in range(2):
        turned[slot] = jnp.transpose(v_buf[slot])
    return (HI, code & 1), (code >> 2, (code >> 1) & 1)


def attend(coef, visits, notes, turned_q, sum_ref, acc_ref, buffers, done=None):
    chunks, ends = [], []
    laid_out = [visit_chunks(*visit, notes, *buffers[3 * i : 3 * i + 3]) for i, visit in enumerate(visits)]
    for place, pairs in enumerate(laid_out):
        k_buf, _, turned = buffers[3 * place : 3 * place + 3]
        tiles = key_tiles(k_buf.shape[1])
        for order, slot in pairs:
            for tile in tiles:
                chunks.append((len(ends), order, slot, k_buf, turned, *tile))
            ends.append(tiles[-1][0])
    totals = {}

    def score(place, order, slot, k_buf, turned, start, size):
        return value_dot(with_ones(k_buf[slot, pl.ds(start, size)]), turned_q[order])

    def finish(s, place, order, slot, k_buf, turned, start, size):
        p, sums = weights_of(coef, s)
        part = value_dot(turned[slot, :, pl.ds(start, size)], p)
        if start:
            part, sums = totals[place][0] + part, totals[place][1] + sums
        totals[place] = part, sums
        if start == ends[place]:
            acc_ref[order] += part
            sum_ref[order] += sums
            if done is not None:
                done(place - len(ends), laid_out[-1][1][0])

    in_turn(chunks, score, finish)


def first_row(x):
    return jnp.transpose(x)[:1]


def middle_kernel(coef, distances, notes, turned_q, sum_in, acc_in, *refs):
    count = len(distances)
    visits = [(d, refs[2 * i], refs[2 * i + 1]) for i, d in enumerate(distances)]
    sum_ref, acc_ref, *buffers = refs[2 * count :]
    attend(coef, visits, notes, turned_q, sum_ref, acc_ref, buffers)


def last_kernel(coef, distances, final, sb_ref, notes, turned_q, top_ref, sum_ref, acc_ref, *refs):
    visits = [(d, refs[2 * i], refs[2 * i + 1]) for i, d in enumerate(final)]
    refs = refs[2 * len(final) :]
    every, rest = refs[: 4 * len(distances) + 3], refs[4 * len(distances) + 3 :]
    out_hbm, lse_hbm, out_buf, lse_ref, *buffers, worst, k_buf, v_buf, run_top, run_acc, sb, sem, out_sems = rest
    _, rows, feats = out_buf.shape
    width = k_buf.shape[1]
    block_len, heads = k_buf.shape[0] // 2, feats // width
    half_len = block_len // 2
    count = lax.axis_size("seq")
    me = lax.axis_index("seq")
    own_half = lax.rem(lax.axis_index("head"), 2)
    inner = lax.axis_index("inner")
    hi = noted(notes, 0)
    lse_copy = pltpu.make_async_copy(lse_ref, lse_hbm, sem)

    def out_copy(slot):
        return pltpu.make_async_copy(out_buf.at[slot], out_hbm.at[slot], out_sems.at[slot])

    def emit(order, h, value, top):
        slot = hi if order == HI else 1 - hi
        sums = jnp.broadcast_to(jnp.sum(value[:, width:], axis=1, keepdims=True), (rows, width))
        out_buf[slot, :, h * width : (h + 1) * width] = (value[:, :width] / sums).astype(out_buf.dtype)
        lse_ref[slot, h : h + 1, :] = first_row(top * (coef * math.log(2.0)) + jnp.log(sums))

    def done(place, last_order):
        if place < -2:
            return
        order = 1 - last_order if place == -2 else last_order
        slot = jnp.where(order == HI, hi, 1 - hi)
        sums = jnp.sum(sum_ref[order], axis=0, keepdims=True)
        log_total = top_ref[order][:1] * (coef * math.log(2.0)) + jnp.log(sums)
        settled = jnp.transpose((acc_ref[order] * (1.0 / sums)).astype(out_buf.dtype))
        for h in range(heads):
            mine = slice(h * rows, (h + 1) * rows)
            lse_ref[slot, h : h + 1, :] = log_total[:, mine]
            out_buf[slot, :, h * width : (h + 1) * width] = settled[mine]
        worst[place + 2 : place + 3] = sums
        out_copy(slot).start()

    attend(coef, visits, notes, turned_q, sum_ref, acc_ref, buffers, done)
    fits = jnp.max(worst[...]) < SUM_LIMIT
    lse_copy.start()
    for slot in range(2):
        out_copy(slot).wait()
    lse_copy.wait()

    @pl.when(jnp.logical_not(fits))
    def _():
        def fetch(src, dst):
            copy = pltpu.make_async_copy(src, dst, sem)
            copy.start()
            copy.wait()

        fetch(sb_ref, sb)
        _, lo_block, hi_block = blocks_of(sb, me)

        def online(source):
            @pl.loop(0, 4 * heads)
            def _(i):
                h, slot, order = i // 4, lax.rem(i, 4) // 2, lax.rem(i, 2)
                own_block = jnp.where(order == HI, hi_block, lo_block)
                shift = (own_block - sb[2 * source + slot]) * block_len + inner * rows

                @pl.when(shift + rows > 0)
                def _():
                    own_slot = jnp.where(order == HI, hi, 1 - hi)
                    queries = out_buf[own_slot, :, pl.ds(pl.multiple_of(h * width, width), width)]
                    at = pl.ds(pl.multiple_of(slot * block_len, block_len), block_len)
                    s = score_dot(queries, k_buf[at])
                    row = lax.broadcasted_iota(jnp.int32, s.shape, 0) + shift
                    allowed = lax.broadcasted_iota(jnp.int32, s.shape, 1) <= row
                    s = jnp.where(allowed, s, NEG)
                    before = run_top[order, h]
                    top = jnp.maximum(before, jnp.broadcast_to(jnp.max(s, axis=1, keepdims=True), before.shape))
                    p = jnp.where(allowed, jnp.exp2((s - widen(top, block_len)) * coef), 0.0)
                    run_top[order, h] = top
                    shrink = widen(jnp.exp2((before - top) * coef), 2 * width)
                    lanes = functools.reduce(jnp.add, [p[:, x : x + width] for x in range(0, block_len, width)])
                    fresh = with_sums(p.astype(jnp.bfloat16), lanes, v_buf[at])
                    run_acc[order, h] = run_acc[order, h] * shrink + fresh

        run_top[...] = jnp.full_like(run_top, NEG)
        run_acc[...] = jnp.zeros_like(run_acc)
        def rows_of(slot, half):
            return pl.ds(pl.multiple_of((slot * 2 + half) * half_len, half_len), half_len)

        fetch(every[2], out_buf)
        for slot in range(2):
            fetch(every[0].at[slot], k_buf.at[pl.ds(slot * block_len, block_len)])
            fetch(every[1].at[slot], v_buf.at[pl.ds(slot * block_len, block_len)])
        online(me)
        for place, other in enumerate(distances):
            others = every[3 + 4 * place : 7 + 4 * place]
            for value, (own_buf, twin_buf) in enumerate([(k_buf, v_buf), (v_buf, k_buf)]):

                @pl.when(inner == value)
                def _():
                    for turn in range(2):
                        half = own_half if turn == 0 else 1 - own_half
                        for slot in range(2):
                            fetch(others[2 * turn].at[slot], own_buf.at[rows_of(slot, half)])
                            fetch(others[2 * turn + 1].at[slot], twin_buf.at[rows_of(slot, half)])

            online(source_of(me, other, count))
        for h in range(heads):
            for order in (LO, HI):
                emit(order, h, run_acc[order, h], run_top[order, h])
        for copy in (lse_copy, out_copy(0), out_copy(1)):
            copy.start()
        for copy in (lse_copy, out_copy(0), out_copy(1)):
            copy.wait()


def body(query_rows, key_rows, value_rows, slot_block):
    _, block_len, width = key_rows.shape
    _, rows, feats = query_rows.shape
    heads = feats // width
    all_rows = heads * rows
    count = lax.axis_size("seq")
    coef = math.log2(math.e) / math.sqrt(width)
    distances = list(range(1, count))

    def along_seq(block, distance):
        if is_power(count):
            route = [(i, i ^ distance) for i in range(count)]
        else:
            route = [(i, (i + distance) % count) for i in range(count)]
        with jax.named_scope("along_seq"):
            return lax.ppermute(block, "seq", route)

    def along_head(block):
        with jax.named_scope("along_head"):
            return lax.ppermute(block, "head", [(i, i ^ 1) for i in range(lax.axis_size("head"))])

    def along_inner(block):
        with jax.named_scope("along_inner"):
            return lax.ppermute(block, "inner", [(0, 1), (1, 0)])

    whole = pl.BlockSpec(memory_space=pltpu.VMEM)
    anywhere = pl.BlockSpec(memory_space=pl.ANY)
    scalars = pl.BlockSpec(memory_space=pltpu.SMEM)
    acc_shape = jax.ShapeDtypeStruct((2, width, all_rows), jnp.float32)
    sum_shape = jax.ShapeDtypeStruct((2, SUBLANES, all_rows), jnp.float32)
    turned_shape = jax.ShapeDtypeStruct((2, 2 * width, all_rows), query_rows.dtype)
    top_shape = jax.ShapeDtypeStruct((2, heads, rows), jnp.float32)
    params = pltpu.CompilerParams(vmem_limit_bytes=40 * 1024 * 1024)
    unit = rows * heads * block_len * width * 4
    exps = rows * heads * block_len

    def cost(units, size):
        return pl.CostEstimate(flops=int(2 * units * unit), bytes_accessed=size, transcendentals=int(units * exps))

    in_hbm = [
        pltpu.with_memory_space_constraint(x, pltpu.HBM) for x in (query_rows, key_rows, value_rows, slot_block)
    ]
    half_shape = jax.ShapeDtypeStruct((2, block_len // 2, width), key_rows.dtype)
    piece, sb_here = pl.pallas_call(
        piece_kernel,
        in_specs=[anywhere] * 3,
        out_specs=[whole] * 2,
        out_shape=[half_shape, jax.ShapeDtypeStruct(slot_block.shape, slot_block.dtype)],
        scratch_shapes=[pltpu.SemaphoreType.DMA((2,))],
        cost_estimate=pl.CostEstimate(flops=0, bytes_accessed=400_000, transcendentals=0),
        compiler_params=params,
        name="pick_piece",
    )(*in_hbm[1:])
    arrived, across, beside, beside_across = {}, {}, {}, {}
    for distance in reversed(distances):
        if not is_power(count) or is_power(distance):
            arrived[distance] = along_seq(piece, distance)

    notes_shape = jax.ShapeDtypeStruct((count, SUBLANES, 128), jnp.float32)
    turned, tops, sums, acc, notes = pl.pallas_call(
        functools.partial(local_kernel, coef, rows),
        in_specs=[scalars] + [anywhere] * 3,
        out_specs=[whole] * 5,
        out_shape=[turned_shape, sum_shape, sum_shape, acc_shape, notes_shape],
        scratch_shapes=[
            pltpu.VMEM(key_rows.shape, key_rows.dtype),
            pltpu.VMEM((2, width, block_len), key_rows.dtype),
            pltpu.VMEM((2, all_rows, width), query_rows.dtype),
            pltpu.VMEM(key_rows.shape, key_rows.dtype),
            pltpu.SemaphoreType.DMA((2 + heads,)),
        ],
        cost_estimate=cost(3, 6_000_000),
        compiler_params=params,
        name="local_part",
    )(sb_here, *in_hbm[:3])
    half_buffers = [
        pltpu.VMEM(half_shape.shape, half_shape.dtype),
        pltpu.VMEM(half_shape.shape, half_shape.dtype),
        pltpu.VMEM((2, width, block_len // 2), half_shape.dtype),
    ]

    def near_half(distance):
        return distance, arrived[distance], beside[distance]

    def far_half(distance):
        return distance, across[distance], beside_across[distance]

    def attended_with(sums, acc, visits):
        return pl.pallas_call(
            functools.partial(middle_kernel, coef, [visit[0] for visit in visits]),
            in_specs=[whole] * (4 + 2 * len(visits)),
            out_specs=[whole] * 2,
            out_shape=[sum_shape, acc_shape],
            scratch_shapes=half_buffers * len(visits),
            input_output_aliases={2: 0, 3: 1},
            cost_estimate=cost(len(visits), 4_000_000),
            compiler_params=params,
            name="visits_of_" + "_".join(str(visit[0]) for visit in visits),
        )(notes, turned, sums, acc, *(part for visit in visits for part in visit[1:]))

    def relay(distance):
        if distance in distances and distance not in arrived:
            near = distance & -distance
            arrived[distance] = along_seq(arrived[distance ^ near], near)

    def spread(distance):
        if distance in distances:
            across[distance] = along_head(arrived[distance])
            beside[distance] = along_inner(arrived[distance])

    def settle(distance):
        nonlocal acc
        across[distance], acc = lax.optimization_barrier((across[distance], acc))
        beside_across[distance] = along_inner(across[distance])

    last = distances[-1]
    for distance in sorted(arrived, reverse=True):
        arrived[distance], acc = lax.optimization_barrier((arrived[distance], acc))
    waiting = distances[:2]
    for distance in waiting:
        beside[distance] = along_inner(arrived[distance])
    across[1] = along_head(arrived[1])
    relay(3)
    across[2] = along_head(arrived[2])
    sums, acc = attended_with(sums, acc, [near_half(d) for d in waiting])
    for ahead in distances[2:]:
        relay(ahead)
        settle(ahead - 2)
        arrived[ahead], acc = lax.optimization_barrier((arrived[ahead], acc))
        spread(ahead)
        across[ahead - 1], acc = lax.optimization_barrier((across[ahead - 1], acc))
        sums, acc = attended_with(sums, acc, [far_half(ahead - 2), near_half(ahead)])
    across[last], acc = lax.optimization_barrier((across[last], acc))
    for distance in distances[-2:]:
        beside_across[distance] = along_inner(across[distance])
    sums, acc = attended_with(sums, acc, [far_half(last - 1)])
    final = [last]

    flat = [part[d] for d in distances for part in (arrived, beside, across, beside_across)]
    attended, log_total = pl.pallas_call(
        functools.partial(last_kernel, coef, distances, final),
        in_specs=[anywhere] + [whole] * (5 + 2 * len(final)) + [anywhere] * (3 + len(flat)),
        out_specs=[anywhere, anywhere],
        out_shape=[jax.ShapeDtypeStruct(query_rows.shape, query_rows.dtype), top_shape],
        scratch_shapes=[
            pltpu.VMEM(query_rows.shape, query_rows.dtype),
            pltpu.VMEM(top_shape.shape, jnp.float32),
        ]
        + half_buffers * len(final)
        + [
            pltpu.VMEM((2, all_rows), jnp.float32),
            pltpu.VMEM((2 * block_len, width), key_rows.dtype),
            pltpu.VMEM((2 * block_len, width), key_rows.dtype),
            pltpu.VMEM((2, heads, rows, width), jnp.float32),
            pltpu.VMEM((2, heads, rows, 2 * width), jnp.float32),
            pltpu.SMEM(slot_block.shape, slot_block.dtype),
            pltpu.SemaphoreType.DMA,
            pltpu.SemaphoreType.DMA((2,)),
        ],
        cost_estimate=cost(1, 7_000_000),
        compiler_params=params,
        name="last_visitor",
    )(sb_here, notes, turned, tops, sums, acc, *(part for d in final for part in far_half(d)[1:]), in_hbm[1], in_hbm[2], in_hbm[0], *flat)
    return attended, log_total


def solution(mesh):
    placed = (
        P(("groups", "seq"), "inner", "head"),
        P(("groups", "seq"), None, None),
        P(("groups", "seq"), None, None),
        P(),
    )
    return jax.shard_map(
        body,
        mesh=mesh,
        in_specs=placed,
        out_specs=(P(("groups", "seq"), "inner", "head"), P(("groups", "seq"), "head", "inner")),
        check_vma=False,
    )
```

```python
import functools
import math

import jax
import jax.numpy as jnp
from jax import lax
from jax.experimental import pallas as pl
from jax.experimental.pallas import tpu as pltpu
from jax.sharding import PartitionSpec as P

NEG = -1e30
SUM_LIMIT = 1e36
LO, HI = 0, 1
TILE = 256
SUBLANES = 8


def score_dot(q, k):
    return lax.dot_general(q, k, (((1,), (1,)), ((), ())), preferred_element_type=jnp.float32)


def value_dot(p, v):
    return jnp.dot(p, v, preferred_element_type=jnp.float32)


def widen(x, width):
    return jnp.concatenate([x] * (width // x.shape[1]), axis=1)


def is_power(count):
    return count & (count - 1) == 0


def source_of(index, distance, count):
    if is_power(count):
        return index ^ distance
    return lax.rem(index - distance + count, count)


def blocks_of(sb, seq_index):
    b0, b1 = sb[2 * seq_index], sb[2 * seq_index + 1]
    return jnp.where(b1 > b0, 1, 0), jnp.minimum(b0, b1), jnp.maximum(b0, b1)


def key_tiles(count):
    return [(start, min(TILE, count - start)) for start in range(0, count, TILE)]


def piece_kernel(k_hbm, v_hbm, piece, sem):
    half = piece.shape[1]
    inner = lax.axis_index("inner")
    mine = pl.ds(pl.multiple_of(lax.rem(lax.axis_index("head"), 2) * half, half), half)
    for value, src in enumerate((k_hbm, v_hbm)):

        @pl.when(inner == value)
        def _():
            pltpu.make_async_copy(src.at[:, mine], piece, sem).start()

    pltpu.make_async_copy(k_hbm.at[:, mine], piece, sem).wait()


def weights_of(coef, s):
    p = jnp.exp2(s * coef)
    return p.astype(jnp.bfloat16), folded(jnp.add, p)


def with_ones(x):
    return jnp.concatenate([x, jnp.ones_like(x)], axis=1)


def minus_rows(top, height):
    high = top.astype(jnp.bfloat16).astype(jnp.float32)
    middle = (top - high).astype(jnp.bfloat16).astype(jnp.float32)
    low = top - high - middle
    row = lax.broadcasted_iota(jnp.int32, top.shape, 0)
    picked = jnp.where(row == 0, high, jnp.where(row == 1, middle, jnp.where(row == 2, low, 0.0)))
    zeros = jnp.zeros((height - top.shape[0], top.shape[1]), jnp.float32)
    return jnp.concatenate([-picked, zeros], axis=0).astype(jnp.bfloat16)


def down(x, height):
    return jnp.concatenate([x] * (height // x.shape[0]), axis=0)


def folded(combine, x):
    return functools.reduce(combine, [x[at : at + SUBLANES] for at in range(0, x.shape[0], SUBLANES)])


def with_sums(p, sums, v):
    return jnp.concatenate([value_dot(p, v), sums], axis=1)


def in_turn(chunks, score, finish):
    ready = score(*chunks[0])
    for place, chunk in enumerate(chunks):
        now = ready
        if place + 1 < len(chunks):
            ready = score(*chunks[place + 1])
        finish(now, *chunk)


def local_kernel(coef, rows, sb, q_hbm, k_hbm, v_hbm, turned_q, top_ref, sum_ref, acc_ref, notes, k_ref, turned_v, q_ref, v_ref, sems):
    _, all_rows, width = q_ref.shape
    copies = []
    for h in range(all_rows // rows):
        source, target = q_hbm.at[:, :, pl.ds(h * width, width)], q_ref.at[:, pl.ds(h * rows, rows)]
        copies.append(pltpu.make_async_copy(source, target, sems.at[2 + h]))
    copies.append(pltpu.make_async_copy(k_hbm, k_ref, sems.at[0]))
    copies.append(pltpu.make_async_copy(v_hbm, v_ref, sems.at[1]))
    for copy in copies:
        copy.start()
    for copy in copies:
        copy.wait()
    block_len = k_ref.shape[1]
    hi, _, _ = blocks_of(sb, lax.axis_index("seq"))
    slots = {HI: hi, LO: 1 - hi}
    tiles = key_tiles(block_len)
    me, count = lax.axis_index("seq"), lax.axis_size("seq")
    notes[0] = jnp.full(notes.shape[1:], hi, jnp.int32).astype(jnp.float32)
    for distance in range(1, count):
        notes[distance] = jnp.full(notes.shape[1:], visit_code(sb, me, distance, count), jnp.int32).astype(jnp.float32)
    for order in (HI, LO):
        turned_q[order, pl.ds(0, width)] = jnp.transpose(q_ref[slots[order]])
        turned_v[order] = jnp.transpose(v_ref[slots[order]])

    def keys(order, start, size):
        return k_ref[slots[order], pl.ds(start, size)]

    def values(order, start, size):
        return turned_v[order, :, start : start + size]

    def masked(order, start, size):
        lane = lax.broadcasted_iota(jnp.int32, (SUBLANES, all_rows), 1)
        heads_below = sum((lane >= at).astype(jnp.int32) for at in range(rows, all_rows, rows))
        row = lane - heads_below * rows + lax.axis_index("inner") * rows
        key = lax.broadcasted_iota(jnp.int32, (size, all_rows), 0) + start
        s = value_dot(keys(order, start, size), turned_q[order, pl.ds(0, width)])
        return jnp.where(key <= down(row, size), s, NEG)

    def highest(scores):
        top = functools.reduce(jnp.maximum, [folded(jnp.maximum, s) for s in scores])
        return jnp.broadcast_to(jnp.max(top, axis=0, keepdims=True), top.shape)

    def settle(order, scores, top):
        total, sums = None, None
        for (start, size), s in zip(tiles, scores):
            p, more = weights_of(coef, s - down(top, size))
            part = value_dot(values(order, start, size), p)
            total, sums = (part, more) if total is None else (total + part, sums + more)
        acc_ref[order] = total
        sum_ref[order] = sums

    def extend(order, scores):
        top = highest(scores)
        top_ref[order] = top
        turned_q[order, pl.ds(width, width)] = minus_rows(top, width)
        return top

    diag = [masked(HI, *tile) for tile in tiles]
    top = extend(HI, diag)
    low = [masked(LO, *tile) for tile in tiles]
    settle(HI, diag, top)
    low_top = extend(LO, low)

    def score(start, size):
        return value_dot(with_ones(keys(LO, start, size)), turned_q[HI])

    def finish(s, start, size):
        p, sums = weights_of(coef, s)
        acc_ref[HI] += value_dot(values(LO, start, size), p)
        sum_ref[HI] += sums

    settle(LO, low, low_top)
    in_turn(tiles, score, finish)


def visit_code(sb, me, distance, count):
    _, _, top_block = blocks_of(sb, me)
    other_hi, _, other_top = blocks_of(sb, source_of(me, distance, count))
    above = top_block > other_top
    other_lo = 1 - other_hi
    return other_lo + 2 * jnp.where(above, other_hi, other_lo) + 4 * jnp.where(above, HI, LO)


def noted(notes, place):
    return jnp.max(notes[place]).astype(jnp.int32)


def visit_chunks(distance, own, twin, notes, k_buf, v_buf, turned):
    code = noted(notes, distance)
    inner = lax.axis_index("inner")
    for value, (own_buf, twin_buf) in enumerate([(k_buf, v_buf), (v_buf, k_buf)]):

        @pl.when(inner == value)
        def _():
            own_buf[...] = own[...]
            twin_buf[...] = twin[...]

    for slot in range(2):
        turned[slot] = jnp.transpose(v_buf[slot])
    return (HI, code & 1), (code >> 2, (code >> 1) & 1)


def attend(coef, visits, notes, turned_q, sum_ref, acc_ref, buffers, done=None):
    chunks, ends = [], []
    laid_out = [visit_chunks(*visit, notes, *buffers[3 * i : 3 * i + 3]) for i, visit in enumerate(visits)]
    for place, pairs in enumerate(laid_out):
        k_buf, _, turned = buffers[3 * place : 3 * place + 3]
        tiles = key_tiles(k_buf.shape[1])
        for order, slot in pairs:
            for tile in tiles if ends else tiles[::-1]:
                chunks.append((len(ends), order, slot, k_buf, turned, *tile))
            ends.append(len(chunks) - 1)
    totals, seen = {}, []

    def score(place, order, slot, k_buf, turned, start, size):
        return value_dot(with_ones(k_buf[slot, pl.ds(start, size)]), turned_q[order])

    def finish(s, place, order, slot, k_buf, turned, start, size):
        p, sums = weights_of(coef, s)
        part = value_dot(turned[slot, :, pl.ds(start, size)], p)
        if place in totals:
            part, sums = totals[place][0] + part, totals[place][1] + sums
        totals[place] = part, sums
        seen.append(place)
        if len(seen) - 1 == ends[place]:
            acc_ref[order] += part
            sum_ref[order] += sums
            if done is not None:
                done(place - len(ends), laid_out[-1][1][0])

    in_turn(chunks, score, finish)


def first_row(x):
    return jnp.transpose(x)[:1]


def middle_kernel(coef, distances, notes, turned_q, sum_in, acc_in, *refs):
    count = len(distances)
    visits = [(d, refs[2 * i], refs[2 * i + 1]) for i, d in enumerate(distances)]
    sum_ref, acc_ref, *buffers = refs[2 * count :]
    attend(coef, visits, notes, turned_q, sum_ref, acc_ref, buffers)


def last_kernel(coef, distances, final, sb_ref, notes, turned_q, top_ref, sum_ref, acc_ref, *refs):
    visits = [(d, refs[2 * i], refs[2 * i + 1]) for i, d in enumerate(final)]
    refs = refs[2 * len(final) :]
    every, rest = refs[: 4 * len(distances) + 3], refs[4 * len(distances) + 3 :]
    out_hbm, lse_hbm, out_buf, lse_ref, *buffers, worst, k_buf, v_buf, run_top, run_acc, sb, sem, out_sems = rest
    _, rows, feats = out_buf.shape
    width = k_buf.shape[1]
    block_len, heads = k_buf.shape[0] // 2, feats // width
    half_len = block_len // 2
    count = lax.axis_size("seq")
    me = lax.axis_index("seq")
    own_half = lax.rem(lax.axis_index("head"), 2)
    inner = lax.axis_index("inner")
    hi = noted(notes, 0)
    lse_copy = pltpu.make_async_copy(lse_ref, lse_hbm, sem)

    def out_copy(slot):
        return pltpu.make_async_copy(out_buf.at[slot], out_hbm.at[slot], out_sems.at[slot])

    def emit(order, h, value, top):
        slot = hi if order == HI else 1 - hi
        sums = jnp.broadcast_to(jnp.sum(value[:, width:], axis=1, keepdims=True), (rows, width))
        out_buf[slot, :, h * width : (h + 1) * width] = (value[:, :width] / sums).astype(out_buf.dtype)
        lse_ref[slot, h : h + 1, :] = first_row(top * (coef * math.log(2.0)) + jnp.log(sums))

    def done(place, last_order):
        if place < -2:
            return
        order = 1 - last_order if place == -2 else last_order
        slot = jnp.where(order == HI, hi, 1 - hi)
        sums = jnp.sum(sum_ref[order], axis=0, keepdims=True)
        log_total = top_ref[order][:1] * (coef * math.log(2.0)) + jnp.log(sums)
        settled = jnp.transpose((acc_ref[order] * (1.0 / sums)).astype(out_buf.dtype))
        for h in range(heads):
            mine = slice(h * rows, (h + 1) * rows)
            lse_ref[slot, h : h + 1, :] = log_total[:, mine]
            out_buf[slot, :, h * width : (h + 1) * width] = settled[mine]
        worst[place + 2 : place + 3] = sums
        out_copy(slot).start()

    attend(coef, visits, notes, turned_q, sum_ref, acc_ref, buffers, done)
    fits = jnp.max(worst[...]) < SUM_LIMIT
    lse_copy.start()
    for slot in range(2):
        out_copy(slot).wait()
    lse_copy.wait()

    @pl.when(jnp.logical_not(fits))
    def _():
        def fetch(src, dst):
            copy = pltpu.make_async_copy(src, dst, sem)
            copy.start()
            copy.wait()

        fetch(sb_ref, sb)
        _, lo_block, hi_block = blocks_of(sb, me)

        def online(source):
            @pl.loop(0, 4 * heads)
            def _(i):
                h, slot, order = i // 4, lax.rem(i, 4) // 2, lax.rem(i, 2)
                own_block = jnp.where(order == HI, hi_block, lo_block)
                shift = (own_block - sb[2 * source + slot]) * block_len + inner * rows

                @pl.when(shift + rows > 0)
                def _():
                    own_slot = jnp.where(order == HI, hi, 1 - hi)
                    queries = out_buf[own_slot, :, pl.ds(pl.multiple_of(h * width, width), width)]
                    at = pl.ds(pl.multiple_of(slot * block_len, block_len), block_len)
                    s = score_dot(queries, k_buf[at])
                    row = lax.broadcasted_iota(jnp.int32, s.shape, 0) + shift
                    allowed = lax.broadcasted_iota(jnp.int32, s.shape, 1) <= row
                    s = jnp.where(allowed, s, NEG)
                    before = run_top[order, h]
                    top = jnp.maximum(before, jnp.broadcast_to(jnp.max(s, axis=1, keepdims=True), before.shape))
                    p = jnp.where(allowed, jnp.exp2((s - widen(top, block_len)) * coef), 0.0)
                    run_top[order, h] = top
                    shrink = widen(jnp.exp2((before - top) * coef), 2 * width)
                    lanes = functools.reduce(jnp.add, [p[:, x : x + width] for x in range(0, block_len, width)])
                    fresh = with_sums(p.astype(jnp.bfloat16), lanes, v_buf[at])
                    run_acc[order, h] = run_acc[order, h] * shrink + fresh

        run_top[...] = jnp.full_like(run_top, NEG)
        run_acc[...] = jnp.zeros_like(run_acc)
        def rows_of(slot, half):
            return pl.ds(pl.multiple_of((slot * 2 + half) * half_len, half_len), half_len)

        fetch(every[2], out_buf)
        for slot in range(2):
            fetch(every[0].at[slot], k_buf.at[pl.ds(slot * block_len, block_len)])
            fetch(every[1].at[slot], v_buf.at[pl.ds(slot * block_len, block_len)])
        online(me)
        for place, other in enumerate(distances):
            others = every[3 + 4 * place : 7 + 4 * place]
            for value, (own_buf, twin_buf) in enumerate([(k_buf, v_buf), (v_buf, k_buf)]):

                @pl.when(inner == value)
                def _():
                    for turn in range(2):
                        half = own_half if turn == 0 else 1 - own_half
                        for slot in range(2):
                            fetch(others[2 * turn].at[slot], own_buf.at[rows_of(slot, half)])
                            fetch(others[2 * turn + 1].at[slot], twin_buf.at[rows_of(slot, half)])

            online(source_of(me, other, count))
        for h in range(heads):
            for order in (LO, HI):
                emit(order, h, run_acc[order, h], run_top[order, h])
        for copy in (lse_copy, out_copy(0), out_copy(1)):
            copy.start()
        for copy in (lse_copy, out_copy(0), out_copy(1)):
            copy.wait()


def body(query_rows, key_rows, value_rows, slot_block):
    _, block_len, width = key_rows.shape
    _, rows, feats = query_rows.shape
    heads = feats // width
    all_rows = heads * rows
    count = lax.axis_size("seq")
    coef = math.log2(math.e) / math.sqrt(width)
    distances = list(range(1, count))

    def along_seq(block, distance):
        if is_power(count):
            route = [(i, i ^ distance) for i in range(count)]
        else:
            route = [(i, (i + distance) % count) for i in range(count)]
        with jax.named_scope("along_seq"):
            return lax.ppermute(block, "seq", route)

    def along_head(block):
        with jax.named_scope("along_head"):
            return lax.ppermute(block, "head", [(i, i ^ 1) for i in range(lax.axis_size("head"))])

    def along_inner(block):
        with jax.named_scope("along_inner"):
            return lax.ppermute(block, "inner", [(0, 1), (1, 0)])

    whole = pl.BlockSpec(memory_space=pltpu.VMEM)
    anywhere = pl.BlockSpec(memory_space=pl.ANY)
    scalars = pl.BlockSpec(memory_space=pltpu.SMEM)
    acc_shape = jax.ShapeDtypeStruct((2, width, all_rows), jnp.float32)
    sum_shape = jax.ShapeDtypeStruct((2, SUBLANES, all_rows), jnp.float32)
    turned_shape = jax.ShapeDtypeStruct((2, 2 * width, all_rows), query_rows.dtype)
    top_shape = jax.ShapeDtypeStruct((2, heads, rows), jnp.float32)
    params = pltpu.CompilerParams(vmem_limit_bytes=40 * 1024 * 1024)
    unit = rows * heads * block_len * width * 4
    exps = rows * heads * block_len

    def cost(units, size):
        return pl.CostEstimate(flops=int(2 * units * unit), bytes_accessed=size, transcendentals=int(units * exps))

    in_hbm = [
        pltpu.with_memory_space_constraint(x, pltpu.HBM) for x in (query_rows, key_rows, value_rows, slot_block)
    ]
    half_shape = jax.ShapeDtypeStruct((2, block_len // 2, width), key_rows.dtype)
    piece = pl.pallas_call(
        piece_kernel,
        in_specs=[anywhere] * 2,
        out_specs=whole,
        out_shape=half_shape,
        scratch_shapes=[pltpu.SemaphoreType.DMA],
        cost_estimate=pl.CostEstimate(flops=0, bytes_accessed=400_000, transcendentals=0),
        compiler_params=params,
        name="pick_piece",
    )(*in_hbm[1:3])
    arrived, across, beside, beside_across = {}, {}, {}, {}
    for distance in reversed(distances):
        if not is_power(count) or is_power(distance):
            arrived[distance] = along_seq(piece, distance)

    notes_shape = jax.ShapeDtypeStruct((count, SUBLANES, 128), jnp.float32)
    turned, tops, sums, acc, notes = pl.pallas_call(
        functools.partial(local_kernel, coef, rows),
        in_specs=[scalars] + [anywhere] * 3,
        out_specs=[whole] * 5,
        out_shape=[turned_shape, sum_shape, sum_shape, acc_shape, notes_shape],
        scratch_shapes=[
            pltpu.VMEM(key_rows.shape, key_rows.dtype),
            pltpu.VMEM((2, width, block_len), key_rows.dtype),
            pltpu.VMEM((2, all_rows, width), query_rows.dtype),
            pltpu.VMEM(key_rows.shape, key_rows.dtype),
            pltpu.SemaphoreType.DMA((2 + heads,)),
        ],
        cost_estimate=cost(3, 6_000_000),
        compiler_params=params,
        name="local_part",
    )(in_hbm[3], *in_hbm[:3])
    half_buffers = [
        pltpu.VMEM(half_shape.shape, half_shape.dtype),
        pltpu.VMEM(half_shape.shape, half_shape.dtype),
        pltpu.VMEM((2, width, block_len // 2), half_shape.dtype),
    ]

    def near_half(distance):
        return distance, arrived[distance], beside[distance]

    def far_half(distance):
        return distance, across[distance], beside_across[distance]

    def attended_with(sums, acc, visits):
        return pl.pallas_call(
            functools.partial(middle_kernel, coef, [visit[0] for visit in visits]),
            in_specs=[whole] * (4 + 2 * len(visits)),
            out_specs=[whole] * 2,
            out_shape=[sum_shape, acc_shape],
            scratch_shapes=half_buffers * len(visits),
            input_output_aliases={2: 0, 3: 1},
            cost_estimate=cost(len(visits), 4_000_000),
            compiler_params=params,
            name="visits_of_" + "_".join(str(visit[0]) for visit in visits),
        )(notes, turned, sums, acc, *(part for visit in visits for part in visit[1:]))

    def relay(distance):
        if distance in distances and distance not in arrived:
            near = distance & -distance
            arrived[distance] = along_seq(arrived[distance ^ near], near)

    def spread(distance):
        if distance in distances:
            across[distance] = along_head(arrived[distance])
            beside[distance] = along_inner(arrived[distance])

    def settle(distance):
        nonlocal acc
        across[distance], acc = lax.optimization_barrier((across[distance], acc))
        beside_across[distance] = along_inner(across[distance])

    last = distances[-1]
    arrived[2], acc = lax.optimization_barrier((arrived[2], acc))
    relay(3)
    arrived[1], arrived[2], acc = lax.optimization_barrier((arrived[1], arrived[2], acc))
    waiting = distances[:2]
    across[1] = along_head(arrived[1])
    across[2] = along_head(arrived[2])
    for distance in waiting:
        beside[distance] = along_inner(arrived[distance])
    sums, acc = attended_with(sums, acc, [near_half(d) for d in waiting])
    for ahead in distances[2:]:
        relay(ahead)
        settle(ahead - 2)
        arrived[ahead], acc = lax.optimization_barrier((arrived[ahead], acc))
        spread(ahead)
        across[ahead - 1], acc = lax.optimization_barrier((across[ahead - 1], acc))
        sums, acc = attended_with(sums, acc, [far_half(ahead - 2), near_half(ahead)])
    across[last], acc = lax.optimization_barrier((across[last], acc))
    for distance in distances[-2:]:
        beside_across[distance] = along_inner(across[distance])
    sums, acc = attended_with(sums, acc, [far_half(last - 1)])
    final = [last]

    flat = [part[d] for d in distances for part in (arrived, beside, across, beside_across)]
    attended, log_total = pl.pallas_call(
        functools.partial(last_kernel, coef, distances, final),
        in_specs=[anywhere] + [whole] * (5 + 2 * len(final)) + [anywhere] * (3 + len(flat)),
        out_specs=[anywhere, anywhere],
        out_shape=[jax.ShapeDtypeStruct(query_rows.shape, query_rows.dtype), top_shape],
        scratch_shapes=[
            pltpu.VMEM(query_rows.shape, query_rows.dtype),
            pltpu.VMEM(top_shape.shape, jnp.float32),
        ]
        + half_buffers * len(final)
        + [
            pltpu.VMEM((2, all_rows), jnp.float32),
            pltpu.VMEM((2 * block_len, width), key_rows.dtype),
            pltpu.VMEM((2 * block_len, width), key_rows.dtype),
            pltpu.VMEM((2, heads, rows, width), jnp.float32),
            pltpu.VMEM((2, heads, rows, 2 * width), jnp.float32),
            pltpu.SMEM(slot_block.shape, slot_block.dtype),
            pltpu.SemaphoreType.DMA,
            pltpu.SemaphoreType.DMA((2,)),
        ],
        cost_estimate=cost(1, 7_000_000),
        compiler_params=params,
        name="last_visitor",
    )(in_hbm[3], notes, turned, tops, sums, acc, *(part for d in final for part in far_half(d)[1:]), in_hbm[1], in_hbm[2], in_hbm[0], *flat)
    return attended, log_total


def solution(mesh):
    placed = (
        P(("groups", "seq"), "inner", "head"),
        P(("groups", "seq"), None, None),
        P(("groups", "seq"), None, None),
        P(),
    )
    return jax.shard_map(
        body,
        mesh=mesh,
        in_specs=placed,
        out_specs=(P(("groups", "seq"), "inner", "head"), P(("groups", "seq"), "head", "inner")),
        check_vma=False,
    )
```

```python
import functools
import math

import jax
import jax.numpy as jnp
from jax import lax
from jax.experimental import pallas as pl
from jax.experimental.pallas import tpu as pltpu
from jax.sharding import PartitionSpec as P

NEG = -1e30
SUM_LIMIT = 1e36
LO, HI = 0, 1
TILE = 256
SUBLANES = 8


def score_dot(q, k):
    return lax.dot_general(q, k, (((1,), (1,)), ((), ())), preferred_element_type=jnp.float32)


def value_dot(p, v):
    return jnp.dot(p, v, preferred_element_type=jnp.float32)


def widen(x, width):
    return jnp.concatenate([x] * (width // x.shape[1]), axis=1)


def is_power(count):
    return count & (count - 1) == 0


def source_of(index, distance, count):
    if is_power(count):
        return index ^ distance
    return lax.rem(index - distance + count, count)


def blocks_of(sb, seq_index):
    b0, b1 = sb[2 * seq_index], sb[2 * seq_index + 1]
    return jnp.where(b1 > b0, 1, 0), jnp.minimum(b0, b1), jnp.maximum(b0, b1)


def key_tiles(count):
    return [(start, min(TILE, count - start)) for start in range(0, count, TILE)]


def piece_kernel(k_hbm, v_hbm, piece, far_piece, sems):
    half = piece.shape[1]
    inner = lax.axis_index("inner")
    own_half = lax.rem(lax.axis_index("head"), 2)

    def copies(src):
        found = []
        for place, (part, target) in enumerate([(own_half, piece), (1 - own_half, far_piece)]):
            rows = pl.ds(pl.multiple_of(part * half, half), half)
            found.append(pltpu.make_async_copy(src.at[:, rows], target, sems.at[place]))
        return found

    for value, src in enumerate((k_hbm, v_hbm)):

        @pl.when(inner == value)
        def _():
            for copy in copies(src):
                copy.start()

    for copy in copies(k_hbm):
        copy.wait()


def weights_of(coef, s):
    p = jnp.exp2(s * coef)
    return p.astype(jnp.bfloat16), folded(jnp.add, p)


def with_ones(x):
    return jnp.concatenate([x, jnp.ones_like(x)], axis=1)


def minus_rows(top, height):
    high = top.astype(jnp.bfloat16).astype(jnp.float32)
    middle = (top - high).astype(jnp.bfloat16).astype(jnp.float32)
    low = top - high - middle
    row = lax.broadcasted_iota(jnp.int32, top.shape, 0)
    picked = jnp.where(row == 0, high, jnp.where(row == 1, middle, jnp.where(row == 2, low, 0.0)))
    zeros = jnp.zeros((height - top.shape[0], top.shape[1]), jnp.float32)
    return jnp.concatenate([-picked, zeros], axis=0).astype(jnp.bfloat16)


def down(x, height):
    return jnp.concatenate([x] * (height // x.shape[0]), axis=0)


def folded(combine, x):
    return functools.reduce(combine, [x[at : at + SUBLANES] for at in range(0, x.shape[0], SUBLANES)])


def with_sums(p, sums, v):
    return jnp.concatenate([value_dot(p, v), sums], axis=1)


def in_turn(chunks, score, finish):
    ready = score(*chunks[0])
    for place, chunk in enumerate(chunks):
        now = ready
        if place + 1 < len(chunks):
            ready = score(*chunks[place + 1])
        finish(now, *chunk)


def local_kernel(coef, rows, sb, q_hbm, k_hbm, v_hbm, turned_q, top_ref, sum_ref, acc_ref, notes, k_ref, turned_v, q_ref, v_ref, sems):
    _, all_rows, width = q_ref.shape
    copies = []
    for h in range(all_rows // rows):
        source, target = q_hbm.at[:, :, pl.ds(h * width, width)], q_ref.at[:, pl.ds(h * rows, rows)]
        copies.append(pltpu.make_async_copy(source, target, sems.at[2 + h]))
    copies.append(pltpu.make_async_copy(k_hbm, k_ref, sems.at[0]))
    copies.append(pltpu.make_async_copy(v_hbm, v_ref, sems.at[1]))
    for copy in copies:
        copy.start()
    for copy in copies:
        copy.wait()
    block_len = k_ref.shape[1]
    hi, _, _ = blocks_of(sb, lax.axis_index("seq"))
    slots = {HI: hi, LO: 1 - hi}
    tiles = key_tiles(block_len)
    me, count = lax.axis_index("seq"), lax.axis_size("seq")
    notes[0] = jnp.full(notes.shape[1:], hi, jnp.int32).astype(jnp.float32)
    for distance in range(1, count):
        notes[distance] = jnp.full(notes.shape[1:], visit_code(sb, me, distance, count), jnp.int32).astype(jnp.float32)
    for order in (HI, LO):
        turned_q[order, pl.ds(0, width)] = jnp.transpose(q_ref[slots[order]])
        turned_v[order] = jnp.transpose(v_ref[slots[order]])

    def keys(order, start, size):
        return k_ref[slots[order], pl.ds(start, size)]

    def values(order, start, size):
        return turned_v[order, :, start : start + size]

    def masked(order, start, size):
        lane = lax.broadcasted_iota(jnp.int32, (SUBLANES, all_rows), 1)
        heads_below = sum((lane >= at).astype(jnp.int32) for at in range(rows, all_rows, rows))
        row = lane - heads_below * rows + lax.axis_index("inner") * rows
        key = lax.broadcasted_iota(jnp.int32, (size, all_rows), 0) + start
        s = value_dot(keys(order, start, size), turned_q[order, pl.ds(0, width)])
        return jnp.where(key <= down(row, size), s, NEG)

    def highest(scores):
        top = functools.reduce(jnp.maximum, [folded(jnp.maximum, s) for s in scores])
        return jnp.broadcast_to(jnp.max(top, axis=0, keepdims=True), top.shape)

    def settle(order, scores, top):
        total, sums = None, None
        for (start, size), s in zip(tiles, scores):
            p, more = weights_of(coef, s - down(top, size))
            part = value_dot(values(order, start, size), p)
            total, sums = (part, more) if total is None else (total + part, sums + more)
        acc_ref[order] = total
        sum_ref[order] = sums

    def extend(order, scores):
        top = highest(scores)
        top_ref[order] = top
        turned_q[order, pl.ds(width, width)] = minus_rows(top, width)
        return top

    diag = [masked(HI, *tile) for tile in tiles]
    top = extend(HI, diag)
    low = [masked(LO, *tile) for tile in tiles]
    settle(HI, diag, top)
    low_top = extend(LO, low)

    def score(start, size):
        return value_dot(with_ones(keys(LO, start, size)), turned_q[HI])

    def finish(s, start, size):
        p, sums = weights_of(coef, s)
        acc_ref[HI] += value_dot(values(LO, start, size), p)
        sum_ref[HI] += sums

    settle(LO, low, low_top)
    in_turn(tiles, score, finish)


def visit_code(sb, me, distance, count):
    _, _, top_block = blocks_of(sb, me)
    other_hi, _, other_top = blocks_of(sb, source_of(me, distance, count))
    above = top_block > other_top
    other_lo = 1 - other_hi
    return other_lo + 2 * jnp.where(above, other_hi, other_lo) + 4 * jnp.where(above, HI, LO)


def noted(notes, place):
    return jnp.max(notes[place]).astype(jnp.int32)


def visit_chunks(distance, own, twin, notes, k_buf, v_buf, turned):
    code = noted(notes, distance)
    inner = lax.axis_index("inner")
    for value, (own_buf, twin_buf) in enumerate([(k_buf, v_buf), (v_buf, k_buf)]):

        @pl.when(inner == value)
        def _():
            own_buf[...] = own[...]
            twin_buf[...] = twin[...]

    for slot in range(2):
        turned[slot] = jnp.transpose(v_buf[slot])
    return (HI, code & 1), (code >> 2, (code >> 1) & 1)


def attend(coef, visits, notes, turned_q, sum_ref, acc_ref, buffers, done=None):
    chunks, ends = [], []
    laid_out = [visit_chunks(*visit, notes, *buffers[3 * i : 3 * i + 3]) for i, visit in enumerate(visits)]
    for place, pairs in enumerate(laid_out):
        k_buf, _, turned = buffers[3 * place : 3 * place + 3]
        tiles = key_tiles(k_buf.shape[1])
        for order, slot in pairs:
            for tile in tiles if ends else tiles[::-1]:
                chunks.append((len(ends), order, slot, k_buf, turned, *tile))
            ends.append(len(chunks) - 1)
    totals, seen = {}, []

    def score(place, order, slot, k_buf, turned, start, size):
        return value_dot(with_ones(k_buf[slot, pl.ds(start, size)]), turned_q[order])

    def finish(s, place, order, slot, k_buf, turned, start, size):
        p, sums = weights_of(coef, s)
        part = value_dot(turned[slot, :, pl.ds(start, size)], p)
        if place in totals:
            part, sums = totals[place][0] + part, totals[place][1] + sums
        totals[place] = part, sums
        seen.append(place)
        if len(seen) - 1 == ends[place]:
            acc_ref[order] += part
            sum_ref[order] += sums
            if done is not None:
                done(place - len(ends), laid_out[-1][1][0])

    in_turn(chunks, score, finish)


def first_row(x):
    return jnp.transpose(x)[:1]


def middle_kernel(coef, distances, notes, turned_q, sum_in, acc_in, *refs):
    count = len(distances)
    visits = [(d, refs[2 * i], refs[2 * i + 1]) for i, d in enumerate(distances)]
    sum_ref, acc_ref, *buffers = refs[2 * count :]
    attend(coef, visits, notes, turned_q, sum_ref, acc_ref, buffers)


def last_kernel(coef, distances, final, sb_ref, notes, turned_q, top_ref, sum_ref, acc_ref, *refs):
    visits = [(d, refs[2 * i], refs[2 * i + 1]) for i, d in enumerate(final)]
    refs = refs[2 * len(final) :]
    every, rest = refs[: 4 * len(distances) + 3], refs[4 * len(distances) + 3 :]
    out_hbm, lse_hbm, out_buf, lse_ref, *buffers, worst, k_buf, v_buf, run_top, run_acc, sb, sem, out_sems = rest
    _, rows, feats = out_buf.shape
    width = k_buf.shape[1]
    block_len, heads = k_buf.shape[0] // 2, feats // width
    half_len = block_len // 2
    count = lax.axis_size("seq")
    me = lax.axis_index("seq")
    own_half = lax.rem(lax.axis_index("head"), 2)
    inner = lax.axis_index("inner")
    hi = noted(notes, 0)
    lse_copy = pltpu.make_async_copy(lse_ref, lse_hbm, sem)

    def out_copy(slot):
        return pltpu.make_async_copy(out_buf.at[slot], out_hbm.at[slot], out_sems.at[slot])

    def emit(order, h, value, top):
        slot = hi if order == HI else 1 - hi
        sums = jnp.broadcast_to(jnp.sum(value[:, width:], axis=1, keepdims=True), (rows, width))
        out_buf[slot, :, h * width : (h + 1) * width] = (value[:, :width] / sums).astype(out_buf.dtype)
        lse_ref[slot, h : h + 1, :] = first_row(top * (coef * math.log(2.0)) + jnp.log(sums))

    def done(place, last_order):
        if place < -2:
            return
        order = 1 - last_order if place == -2 else last_order
        slot = jnp.where(order == HI, hi, 1 - hi)
        sums = jnp.sum(sum_ref[order], axis=0, keepdims=True)
        log_total = top_ref[order][:1] * (coef * math.log(2.0)) + jnp.log(sums)
        settled = jnp.transpose((acc_ref[order] * (1.0 / sums)).astype(out_buf.dtype))
        for h in range(heads):
            mine = slice(h * rows, (h + 1) * rows)
            lse_ref[slot, h : h + 1, :] = log_total[:, mine]
            out_buf[slot, :, h * width : (h + 1) * width] = settled[mine]
        worst[place + 2 : place + 3] = sums
        out_copy(slot).start()

    attend(coef, visits, notes, turned_q, sum_ref, acc_ref, buffers, done)
    fits = jnp.max(worst[...]) < SUM_LIMIT
    lse_copy.start()
    for slot in range(2):
        out_copy(slot).wait()
    lse_copy.wait()

    @pl.when(jnp.logical_not(fits))
    def _():
        def fetch(src, dst):
            copy = pltpu.make_async_copy(src, dst, sem)
            copy.start()
            copy.wait()

        fetch(sb_ref, sb)
        _, lo_block, hi_block = blocks_of(sb, me)

        def online(source):
            @pl.loop(0, 4 * heads)
            def _(i):
                h, slot, order = i // 4, lax.rem(i, 4) // 2, lax.rem(i, 2)
                own_block = jnp.where(order == HI, hi_block, lo_block)
                shift = (own_block - sb[2 * source + slot]) * block_len + inner * rows

                @pl.when(shift + rows > 0)
                def _():
                    own_slot = jnp.where(order == HI, hi, 1 - hi)
                    queries = out_buf[own_slot, :, pl.ds(pl.multiple_of(h * width, width), width)]
                    at = pl.ds(pl.multiple_of(slot * block_len, block_len), block_len)
                    s = score_dot(queries, k_buf[at])
                    row = lax.broadcasted_iota(jnp.int32, s.shape, 0) + shift
                    allowed = lax.broadcasted_iota(jnp.int32, s.shape, 1) <= row
                    s = jnp.where(allowed, s, NEG)
                    before = run_top[order, h]
                    top = jnp.maximum(before, jnp.broadcast_to(jnp.max(s, axis=1, keepdims=True), before.shape))
                    p = jnp.where(allowed, jnp.exp2((s - widen(top, block_len)) * coef), 0.0)
                    run_top[order, h] = top
                    shrink = widen(jnp.exp2((before - top) * coef), 2 * width)
                    lanes = functools.reduce(jnp.add, [p[:, x : x + width] for x in range(0, block_len, width)])
                    fresh = with_sums(p.astype(jnp.bfloat16), lanes, v_buf[at])
                    run_acc[order, h] = run_acc[order, h] * shrink + fresh

        run_top[...] = jnp.full_like(run_top, NEG)
        run_acc[...] = jnp.zeros_like(run_acc)
        def rows_of(slot, half):
            return pl.ds(pl.multiple_of((slot * 2 + half) * half_len, half_len), half_len)

        fetch(every[2], out_buf)
        for slot in range(2):
            fetch(every[0].at[slot], k_buf.at[pl.ds(slot * block_len, block_len)])
            fetch(every[1].at[slot], v_buf.at[pl.ds(slot * block_len, block_len)])
        online(me)
        for place, other in enumerate(distances):
            others = every[3 + 4 * place : 7 + 4 * place]
            for value, (own_buf, twin_buf) in enumerate([(k_buf, v_buf), (v_buf, k_buf)]):

                @pl.when(inner == value)
                def _():
                    for turn in range(2):
                        half = own_half if turn == 0 else 1 - own_half
                        for slot in range(2):
                            fetch(others[2 * turn].at[slot], own_buf.at[rows_of(slot, half)])
                            fetch(others[2 * turn + 1].at[slot], twin_buf.at[rows_of(slot, half)])

            online(source_of(me, other, count))
        for h in range(heads):
            for order in (LO, HI):
                emit(order, h, run_acc[order, h], run_top[order, h])
        for copy in (lse_copy, out_copy(0), out_copy(1)):
            copy.start()
        for copy in (lse_copy, out_copy(0), out_copy(1)):
            copy.wait()


def body(query_rows, key_rows, value_rows, slot_block):
    _, block_len, width = key_rows.shape
    _, rows, feats = query_rows.shape
    heads = feats // width
    all_rows = heads * rows
    count = lax.axis_size("seq")
    coef = math.log2(math.e) / math.sqrt(width)
    distances = list(range(1, count))

    def along_seq(block, distance):
        if is_power(count):
            route = [(i, i ^ distance) for i in range(count)]
        else:
            route = [(i, (i + distance) % count) for i in range(count)]
        with jax.named_scope("along_seq"):
            return lax.ppermute(block, "seq", route)

    def along_head(block):
        with jax.named_scope("along_head"):
            return lax.ppermute(block, "head", [(i, i ^ 1) for i in range(lax.axis_size("head"))])

    def along_inner(block):
        with jax.named_scope("along_inner"):
            return lax.ppermute(block, "inner", [(0, 1), (1, 0)])

    whole = pl.BlockSpec(memory_space=pltpu.VMEM)
    anywhere = pl.BlockSpec(memory_space=pl.ANY)
    scalars = pl.BlockSpec(memory_space=pltpu.SMEM)
    acc_shape = jax.ShapeDtypeStruct((2, width, all_rows), jnp.float32)
    sum_shape = jax.ShapeDtypeStruct((2, SUBLANES, all_rows), jnp.float32)
    turned_shape = jax.ShapeDtypeStruct((2, 2 * width, all_rows), query_rows.dtype)
    top_shape = jax.ShapeDtypeStruct((2, heads, rows), jnp.float32)
    params = pltpu.CompilerParams(vmem_limit_bytes=40 * 1024 * 1024)
    unit = rows * heads * block_len * width * 4
    exps = rows * heads * block_len

    def cost(units, size):
        return pl.CostEstimate(flops=int(2 * units * unit), bytes_accessed=size, transcendentals=int(units * exps))

    in_hbm = [
        pltpu.with_memory_space_constraint(x, pltpu.HBM) for x in (query_rows, key_rows, value_rows, slot_block)
    ]
    half_shape = jax.ShapeDtypeStruct((2, block_len // 2, width), key_rows.dtype)
    piece, far_piece = pl.pallas_call(
        piece_kernel,
        in_specs=[anywhere] * 2,
        out_specs=[whole] * 2,
        out_shape=[half_shape] * 2,
        scratch_shapes=[pltpu.SemaphoreType.DMA((2,))],
        cost_estimate=pl.CostEstimate(flops=0, bytes_accessed=400_000, transcendentals=0),
        compiler_params=params,
        name="pick_piece",
    )(*in_hbm[1:3])
    arrived, across, beside, beside_across = {}, {}, {}, {}
    for distance in reversed(distances):
        if not is_power(count) or is_power(distance):
            arrived[distance] = along_seq(piece, distance)

    notes_shape = jax.ShapeDtypeStruct((count, SUBLANES, 128), jnp.float32)
    turned, tops, sums, acc, notes = pl.pallas_call(
        functools.partial(local_kernel, coef, rows),
        in_specs=[scalars] + [anywhere] * 3,
        out_specs=[whole] * 5,
        out_shape=[turned_shape, sum_shape, sum_shape, acc_shape, notes_shape],
        scratch_shapes=[
            pltpu.VMEM(key_rows.shape, key_rows.dtype),
            pltpu.VMEM((2, width, block_len), key_rows.dtype),
            pltpu.VMEM((2, all_rows, width), query_rows.dtype),
            pltpu.VMEM(key_rows.shape, key_rows.dtype),
            pltpu.SemaphoreType.DMA((2 + heads,)),
        ],
        cost_estimate=cost(3, 6_000_000),
        compiler_params=params,
        name="local_part",
    )(in_hbm[3], *in_hbm[:3])
    half_buffers = [
        pltpu.VMEM(half_shape.shape, half_shape.dtype),
        pltpu.VMEM(half_shape.shape, half_shape.dtype),
        pltpu.VMEM((2, width, block_len // 2), half_shape.dtype),
    ]

    def near_half(distance):
        return distance, arrived[distance], beside[distance]

    def far_half(distance):
        return distance, across[distance], beside_across[distance]

    def attended_with(sums, acc, visits):
        return pl.pallas_call(
            functools.partial(middle_kernel, coef, [visit[0] for visit in visits]),
            in_specs=[whole] * (4 + 2 * len(visits)),
            out_specs=[whole] * 2,
            out_shape=[sum_shape, acc_shape],
            scratch_shapes=half_buffers * len(visits),
            input_output_aliases={2: 0, 3: 1},
            cost_estimate=cost(len(visits), 4_000_000),
            compiler_params=params,
            name="visits_of_" + "_".join(str(visit[0]) for visit in visits),
        )(notes, turned, sums, acc, *(part for visit in visits for part in visit[1:]))

    def relay(distance):
        if distance in distances and distance not in arrived:
            near = distance & -distance
            arrived[distance] = along_seq(arrived[distance ^ near], near)

    def spread(distance):
        if distance in distances:
            across[distance] = along_head(arrived[distance])
            beside[distance] = along_inner(arrived[distance])

    def settle(distance):
        nonlocal acc
        across[distance], acc = lax.optimization_barrier((across[distance], acc))
        beside_across[distance] = along_inner(across[distance])

    last = distances[-1]
    ready = sorted(arrived, reverse=True)
    *first, acc = lax.optimization_barrier((*(arrived[d] for d in ready), acc))
    arrived.update(zip(ready, first))

    def meet(distance):
        nonlocal acc
        arrived[distance], acc = lax.optimization_barrier((arrived[distance], acc))

    relay(3)
    across[2] = along_head(arrived[2])
    for distance in (1, 2):
        beside[distance] = along_inner(arrived[distance])
    sums, acc = attended_with(sums, acc, [near_half(1), near_half(2)])
    for ahead in distances[2:]:
        relay(ahead)
        meet(ahead)
        spread(ahead)
        if ahead == 3:
            far_piece, acc = lax.optimization_barrier((far_piece, acc))
            across[1] = along_seq(far_piece, 1)
        settle(ahead - 1)
        sums, acc = attended_with(sums, acc, [far_half(ahead - 1), near_half(ahead)])
    final = [1, last]
    across[last], across[1], acc = lax.optimization_barrier((across[last], across[1], acc))
    for distance in final:
        beside_across[distance] = along_inner(across[distance])

    flat = [part[d] for d in distances for part in (arrived, beside, across, beside_across)]
    attended, log_total = pl.pallas_call(
        functools.partial(last_kernel, coef, distances, final),
        in_specs=[anywhere] + [whole] * (5 + 2 * len(final)) + [anywhere] * (3 + len(flat)),
        out_specs=[anywhere, anywhere],
        out_shape=[jax.ShapeDtypeStruct(query_rows.shape, query_rows.dtype), top_shape],
        scratch_shapes=[
            pltpu.VMEM(query_rows.shape, query_rows.dtype),
            pltpu.VMEM(top_shape.shape, jnp.float32),
        ]
        + half_buffers * len(final)
        + [
            pltpu.VMEM((2, all_rows), jnp.float32),
            pltpu.VMEM((2 * block_len, width), key_rows.dtype),
            pltpu.VMEM((2 * block_len, width), key_rows.dtype),
            pltpu.VMEM((2, heads, rows, width), jnp.float32),
            pltpu.VMEM((2, heads, rows, 2 * width), jnp.float32),
            pltpu.SMEM(slot_block.shape, slot_block.dtype),
            pltpu.SemaphoreType.DMA,
            pltpu.SemaphoreType.DMA((2,)),
        ],
        cost_estimate=cost(1, 7_000_000),
        compiler_params=params,
        name="last_visitor",
    )(in_hbm[3], notes, turned, tops, sums, acc, *(part for d in final for part in far_half(d)[1:]), in_hbm[1], in_hbm[2], in_hbm[0], *flat)
    return attended, log_total


def solution(mesh):
    placed = (
        P(("groups", "seq"), "inner", "head"),
        P(("groups", "seq"), None, None),
        P(("groups", "seq"), None, None),
        P(),
    )
    return jax.shard_map(
        body,
        mesh=mesh,
        in_specs=placed,
        out_specs=(P(("groups", "seq"), "inner", "head"), P(("groups", "seq"), "head", "inner")),
        check_vma=False,
    )
```

```python
import functools
import math

import jax
import jax.numpy as jnp
from jax import lax
from jax.experimental import pallas as pl
from jax.experimental.pallas import tpu as pltpu
from jax.sharding import PartitionSpec as P

NEG = -1e30
SUM_LIMIT = 1e36
LO, HI = 0, 1
TILE = 256
SUBLANES = 8


def score_dot(q, k):
    return lax.dot_general(q, k, (((1,), (1,)), ((), ())), preferred_element_type=jnp.float32)


def value_dot(p, v):
    return jnp.dot(p, v, preferred_element_type=jnp.float32)


def widen(x, width):
    return jnp.concatenate([x] * (width // x.shape[1]), axis=1)


def is_power(count):
    return count & (count - 1) == 0


def source_of(index, distance, count):
    if is_power(count):
        return index ^ distance
    return lax.rem(index - distance + count, count)


def blocks_of(sb, seq_index):
    b0, b1 = sb[2 * seq_index], sb[2 * seq_index + 1]
    return jnp.where(b1 > b0, 1, 0), jnp.minimum(b0, b1), jnp.maximum(b0, b1)


def key_tiles(count):
    return [(start, min(TILE, count - start)) for start in range(0, count, TILE)]


def piece_kernel(k_hbm, v_hbm, sb_hbm, piece, sb_out, sems):
    half = piece.shape[1]
    inner = lax.axis_index("inner")
    mine = pl.ds(pl.multiple_of(lax.rem(lax.axis_index("head"), 2) * half, half), half)
    sb_copy = pltpu.make_async_copy(sb_hbm, sb_out, sems.at[1])
    for value, src in enumerate((k_hbm, v_hbm)):

        @pl.when(inner == value)
        def _():
            pltpu.make_async_copy(src.at[:, mine], piece, sems.at[0]).start()

    sb_copy.start()
    pltpu.make_async_copy(k_hbm.at[:, mine], piece, sems.at[0]).wait()
    sb_copy.wait()


def weights_of(coef, s):
    p = jnp.exp2(s * coef)
    return p.astype(jnp.bfloat16), folded(jnp.add, p)


def with_ones(x):
    return jnp.concatenate([x, jnp.ones_like(x)], axis=1)


def minus_rows(top, height):
    high = top.astype(jnp.bfloat16).astype(jnp.float32)
    middle = (top - high).astype(jnp.bfloat16).astype(jnp.float32)
    low = top - high - middle
    row = lax.broadcasted_iota(jnp.int32, top.shape, 0)
    picked = jnp.where(row == 0, high, jnp.where(row == 1, middle, jnp.where(row == 2, low, 0.0)))
    zeros = jnp.zeros((height - top.shape[0], top.shape[1]), jnp.float32)
    return jnp.concatenate([-picked, zeros], axis=0).astype(jnp.bfloat16)


def down(x, height):
    return jnp.concatenate([x] * (height // x.shape[0]), axis=0)


def folded(combine, x):
    return functools.reduce(combine, [x[at : at + SUBLANES] for at in range(0, x.shape[0], SUBLANES)])


def with_sums(p, sums, v):
    return jnp.concatenate([value_dot(p, v), sums], axis=1)


def in_turn(chunks, score, finish):
    ready = score(*chunks[0])
    for place, chunk in enumerate(chunks):
        now = ready
        if place + 1 < len(chunks):
            ready = score(*chunks[place + 1])
        finish(now, *chunk)


def local_kernel(coef, rows, sb, q_hbm, k_hbm, v_hbm, turned_q, top_ref, sum_ref, acc_ref, notes, k_ref, turned_v, q_ref, v_ref, sems):
    _, all_rows, width = q_ref.shape
    copies = []
    for h in range(all_rows // rows):
        source, target = q_hbm.at[:, :, pl.ds(h * width, width)], q_ref.at[:, pl.ds(h * rows, rows)]
        copies.append(pltpu.make_async_copy(source, target, sems.at[2 + h]))
    copies.append(pltpu.make_async_copy(k_hbm, k_ref, sems.at[0]))
    copies.append(pltpu.make_async_copy(v_hbm, v_ref, sems.at[1]))
    for copy in copies:
        copy.start()
    for copy in copies:
        copy.wait()
    block_len = k_ref.shape[1]
    hi, _, _ = blocks_of(sb, lax.axis_index("seq"))
    slots = {HI: hi, LO: 1 - hi}
    tiles = key_tiles(block_len)
    me, count = lax.axis_index("seq"), lax.axis_size("seq")
    notes[0] = jnp.full(notes.shape[1:], hi, jnp.int32).astype(jnp.float32)
    for distance in range(1, count):
        notes[distance] = jnp.full(notes.shape[1:], visit_code(sb, me, distance, count), jnp.int32).astype(jnp.float32)
    for order in (HI, LO):
        turned_q[order, pl.ds(0, width)] = jnp.transpose(q_ref[slots[order]])
        turned_v[order] = jnp.transpose(v_ref[slots[order]])

    def keys(order, start, size):
        return k_ref[slots[order], pl.ds(start, size)]

    def values(order, start, size):
        return turned_v[order, :, start : start + size]

    def masked(order, start, size):
        lane = lax.broadcasted_iota(jnp.int32, (SUBLANES, all_rows), 1)
        heads_below = sum((lane >= at).astype(jnp.int32) for at in range(rows, all_rows, rows))
        row = lane - heads_below * rows + lax.axis_index("inner") * rows
        key = lax.broadcasted_iota(jnp.int32, (size, all_rows), 0) + start
        s = value_dot(keys(order, start, size), turned_q[order, pl.ds(0, width)])
        return jnp.where(key <= down(row, size), s, NEG)

    def highest(scores):
        top = functools.reduce(jnp.maximum, [folded(jnp.maximum, s) for s in scores])
        return jnp.broadcast_to(jnp.max(top, axis=0, keepdims=True), top.shape)

    def settle(order, scores, top):
        total, sums = None, None
        for (start, size), s in zip(tiles, scores):
            p, more = weights_of(coef, s - down(top, size))
            part = value_dot(values(order, start, size), p)
            total, sums = (part, more) if total is None else (total + part, sums + more)
        acc_ref[order] = total
        sum_ref[order] = sums

    def extend(order, scores):
        top = highest(scores)
        top_ref[order] = top
        turned_q[order, pl.ds(width, width)] = minus_rows(top, width)
        return top

    diag = [masked(HI, *tile) for tile in tiles]
    top = extend(HI, diag)
    low = [masked(LO, *tile) for tile in tiles]
    settle(HI, diag, top)
    low_top = extend(LO, low)

    def score(start, size):
        return value_dot(with_ones(keys(LO, start, size)), turned_q[HI])

    def finish(s, start, size):
        p, sums = weights_of(coef, s)
        acc_ref[HI] += value_dot(values(LO, start, size), p)
        sum_ref[HI] += sums

    settle(LO, low, low_top)
    in_turn(tiles, score, finish)


def visit_code(sb, me, distance, count):
    _, _, top_block = blocks_of(sb, me)
    other_hi, _, other_top = blocks_of(sb, source_of(me, distance, count))
    above = top_block > other_top
    other_lo = 1 - other_hi
    return other_lo + 2 * jnp.where(above, other_hi, other_lo) + 4 * jnp.where(above, HI, LO)


def noted(notes, place):
    return jnp.max(notes[place]).astype(jnp.int32)


def visit_chunks(distance, own, twin, notes, k_buf, v_buf, turned):
    code = noted(notes, distance)
    inner = lax.axis_index("inner")
    for value, (own_buf, twin_buf) in enumerate([(k_buf, v_buf), (v_buf, k_buf)]):

        @pl.when(inner == value)
        def _():
            own_buf[...] = own[...]
            twin_buf[...] = twin[...]

    for slot in range(2):
        turned[slot] = jnp.transpose(v_buf[slot])
    return (HI, code & 1), (code >> 2, (code >> 1) & 1)


def attend(coef, visits, notes, turned_q, sum_ref, acc_ref, buffers, done=None):
    chunks, ends = [], []
    laid_out = [visit_chunks(*visit, notes, *buffers[3 * i : 3 * i + 3]) for i, visit in enumerate(visits)]
    all_rows = turned_q.shape[2]
    split = -(-all_rows // (2 * TILE)) * TILE
    for place, pairs in enumerate(laid_out):
        k_buf, _, turned = buffers[3 * place : 3 * place + 3]
        tiles = key_tiles(k_buf.shape[1])
        for turn, (order, slot) in enumerate(pairs):
            groups = [(0, all_rows)]
            if done is not None and (place, turn) == (len(laid_out) - 1, 1) and all_rows >= 4 * TILE:
                groups = [(0, split), (split, all_rows - split)]
            for group in groups:
                for tile in tiles:
                    chunks.append((len(ends), turn, order, slot, k_buf, turned, *group, *tile))
                ends.append(tiles[-1][0])
    totals = {}

    def score(place, turn, order, slot, k_buf, turned, lane, lanes, start, size):
        return value_dot(with_ones(k_buf[slot, pl.ds(start, size)]), turned_q[order, :, pl.ds(lane, lanes)])

    def finish(s, place, turn, order, slot, k_buf, turned, lane, lanes, start, size):
        p, sums = weights_of(coef, s)
        part = value_dot(turned[slot, :, pl.ds(start, size)], p)
        if start:
            part, sums = totals[place][0] + part, totals[place][1] + sums
        totals[place] = part, sums
        if start == ends[place]:
            acc_ref[order, :, pl.ds(lane, lanes)] += part
            sum_ref[order, :, pl.ds(lane, lanes)] += sums
            if done is not None:
                done(turn, laid_out[-1][1][0], lane + lanes)

    in_turn(chunks, score, finish)


def first_row(x):
    return jnp.transpose(x)[:1]


def middle_kernel(coef, distances, notes, turned_q, sum_in, acc_in, *refs):
    count = len(distances)
    visits = [(d, refs[2 * i], refs[2 * i + 1]) for i, d in enumerate(distances)]
    sum_ref, acc_ref, *buffers = refs[2 * count :]
    attend(coef, visits, notes, turned_q, sum_ref, acc_ref, buffers)


def last_kernel(coef, distances, final, sb_ref, notes, turned_q, top_ref, sum_ref, acc_ref, *refs):
    visits = [(d, refs[2 * i], refs[2 * i + 1]) for i, d in enumerate(final)]
    refs = refs[2 * len(final) :]
    every, rest = refs[: 4 * len(distances) + 3], refs[4 * len(distances) + 3 :]
    out_hbm, lse_hbm, out_buf, lse_ref, *buffers, worst, k_buf, v_buf, run_top, run_acc, sb, sem, out_sems = rest
    _, rows, feats = out_buf.shape
    width = k_buf.shape[1]
    block_len, heads = k_buf.shape[0] // 2, feats // width
    half_len = block_len // 2
    count = lax.axis_size("seq")
    me = lax.axis_index("seq")
    own_half = lax.rem(lax.axis_index("head"), 2)
    inner = lax.axis_index("inner")
    hi = noted(notes, 0)
    lse_copy = pltpu.make_async_copy(lse_ref, lse_hbm, sem)

    def out_copy(slot):
        return pltpu.make_async_copy(out_buf.at[slot], out_hbm.at[slot], out_sems.at[slot])

    def emit(order, h, value, top):
        slot = hi if order == HI else 1 - hi
        sums = jnp.broadcast_to(jnp.sum(value[:, width:], axis=1, keepdims=True), (rows, width))
        out_buf[slot, :, h * width : (h + 1) * width] = (value[:, :width] / sums).astype(out_buf.dtype)
        lse_ref[slot, h : h + 1, :] = first_row(top * (coef * math.log(2.0)) + jnp.log(sums))

    written, started = [0, 0], []

    def done(turn, last_order, covered):
        order = 1 - last_order if turn == 0 else last_order
        first, written[turn] = written[turn], covered // rows
        count_here = written[turn] - first
        lanes, columns = pl.ds(first * rows, count_here * rows), pl.ds(first * width, count_here * width)
        slot = jnp.where(order == HI, hi, 1 - hi)
        sums = jnp.sum(sum_ref[order, :, lanes], axis=0, keepdims=True)
        log_total = top_ref[order, :, lanes][:1] * (coef * math.log(2.0)) + jnp.log(sums)
        settled = jnp.transpose((acc_ref[order, :, lanes] * (1.0 / sums)).astype(out_buf.dtype))
        for h in range(count_here):
            mine = slice(h * rows, (h + 1) * rows)
            lse_ref[slot, first + h : first + h + 1, :] = log_total[:, mine]
            out_buf[slot, :, (first + h) * width : (first + h + 1) * width] = settled[mine]
        worst[turn : turn + 1, lanes] = sums
        target = out_hbm.at[slot, :, columns]
        copy = pltpu.make_async_copy(out_buf.at[slot, :, columns], target, out_sems.at[len(started)])
        copy.start()
        started.append(copy)

    attend(coef, visits, notes, turned_q, sum_ref, acc_ref, buffers, done)
    fits = jnp.max(worst[...]) < SUM_LIMIT
    lse_copy.start()
    for copy in started:
        copy.wait()
    lse_copy.wait()

    @pl.when(jnp.logical_not(fits))
    def _():
        def fetch(src, dst):
            copy = pltpu.make_async_copy(src, dst, sem)
            copy.start()
            copy.wait()

        fetch(sb_ref, sb)
        _, lo_block, hi_block = blocks_of(sb, me)

        def online(source):
            @pl.loop(0, 4 * heads)
            def _(i):
                h, slot, order = i // 4, lax.rem(i, 4) // 2, lax.rem(i, 2)
                own_block = jnp.where(order == HI, hi_block, lo_block)
                shift = (own_block - sb[2 * source + slot]) * block_len + inner * rows

                @pl.when(shift + rows > 0)
                def _():
                    own_slot = jnp.where(order == HI, hi, 1 - hi)
                    queries = out_buf[own_slot, :, pl.ds(pl.multiple_of(h * width, width), width)]
                    at = pl.ds(pl.multiple_of(slot * block_len, block_len), block_len)
                    s = score_dot(queries, k_buf[at])
                    row = lax.broadcasted_iota(jnp.int32, s.shape, 0) + shift
                    allowed = lax.broadcasted_iota(jnp.int32, s.shape, 1) <= row
                    s = jnp.where(allowed, s, NEG)
                    before = run_top[order, h]
                    top = jnp.maximum(before, jnp.broadcast_to(jnp.max(s, axis=1, keepdims=True), before.shape))
                    p = jnp.where(allowed, jnp.exp2((s - widen(top, block_len)) * coef), 0.0)
                    run_top[order, h] = top
                    shrink = widen(jnp.exp2((before - top) * coef), 2 * width)
                    lanes = functools.reduce(jnp.add, [p[:, x : x + width] for x in range(0, block_len, width)])
                    fresh = with_sums(p.astype(jnp.bfloat16), lanes, v_buf[at])
                    run_acc[order, h] = run_acc[order, h] * shrink + fresh

        run_top[...] = jnp.full_like(run_top, NEG)
        run_acc[...] = jnp.zeros_like(run_acc)
        def rows_of(slot, half):
            return pl.ds(pl.multiple_of((slot * 2 + half) * half_len, half_len), half_len)

        fetch(every[2], out_buf)
        for slot in range(2):
            fetch(every[0].at[slot], k_buf.at[pl.ds(slot * block_len, block_len)])
            fetch(every[1].at[slot], v_buf.at[pl.ds(slot * block_len, block_len)])
        online(me)
        for place, other in enumerate(distances):
            others = every[3 + 4 * place : 7 + 4 * place]
            for value, (own_buf, twin_buf) in enumerate([(k_buf, v_buf), (v_buf, k_buf)]):

                @pl.when(inner == value)
                def _():
                    for turn in range(2):
                        half = own_half if turn == 0 else 1 - own_half
                        for slot in range(2):
                            fetch(others[2 * turn].at[slot], own_buf.at[rows_of(slot, half)])
                            fetch(others[2 * turn + 1].at[slot], twin_buf.at[rows_of(slot, half)])

            online(source_of(me, other, count))
        for h in range(heads):
            for order in (LO, HI):
                emit(order, h, run_acc[order, h], run_top[order, h])
        for copy in (lse_copy, out_copy(0), out_copy(1)):
            copy.start()
        for copy in (lse_copy, out_copy(0), out_copy(1)):
            copy.wait()


def body(query_rows, key_rows, value_rows, slot_block):
    _, block_len, width = key_rows.shape
    _, rows, feats = query_rows.shape
    heads = feats // width
    all_rows = heads * rows
    count = lax.axis_size("seq")
    coef = math.log2(math.e) / math.sqrt(width)
    distances = list(range(1, count))

    def along_seq(block, distance):
        if is_power(count):
            route = [(i, i ^ distance) for i in range(count)]
        else:
            route = [(i, (i + distance) % count) for i in range(count)]
        with jax.named_scope("along_seq"):
            return lax.ppermute(block, "seq", route)

    def along_head(block):
        with jax.named_scope("along_head"):
            return lax.ppermute(block, "head", [(i, i ^ 1) for i in range(lax.axis_size("head"))])

    def along_inner(block):
        with jax.named_scope("along_inner"):
            return lax.ppermute(block, "inner", [(0, 1), (1, 0)])

    whole = pl.BlockSpec(memory_space=pltpu.VMEM)
    anywhere = pl.BlockSpec(memory_space=pl.ANY)
    scalars = pl.BlockSpec(memory_space=pltpu.SMEM)
    acc_shape = jax.ShapeDtypeStruct((2, width, all_rows), jnp.float32)
    sum_shape = jax.ShapeDtypeStruct((2, SUBLANES, all_rows), jnp.float32)
    turned_shape = jax.ShapeDtypeStruct((2, 2 * width, all_rows), query_rows.dtype)
    top_shape = jax.ShapeDtypeStruct((2, heads, rows), jnp.float32)
    params = pltpu.CompilerParams(vmem_limit_bytes=40 * 1024 * 1024)
    unit = rows * heads * block_len * width * 4
    exps = rows * heads * block_len

    def cost(units, size):
        return pl.CostEstimate(flops=int(2 * units * unit), bytes_accessed=size, transcendentals=int(units * exps))

    in_hbm = [
        pltpu.with_memory_space_constraint(x, pltpu.HBM) for x in (query_rows, key_rows, value_rows, slot_block)
    ]
    half_shape = jax.ShapeDtypeStruct((2, block_len // 2, width), key_rows.dtype)
    piece, sb_here = pl.pallas_call(
        piece_kernel,
        in_specs=[anywhere] * 3,
        out_specs=[whole] * 2,
        out_shape=[half_shape, jax.ShapeDtypeStruct(slot_block.shape, slot_block.dtype)],
        scratch_shapes=[pltpu.SemaphoreType.DMA((2,))],
        cost_estimate=pl.CostEstimate(flops=0, bytes_accessed=400_000, transcendentals=0),
        compiler_params=params,
        name="pick_piece",
    )(*in_hbm[1:])
    arrived, across, beside, beside_across = {}, {}, {}, {}
    for distance in reversed(distances):
        if not is_power(count) or is_power(distance):
            arrived[distance] = along_seq(piece, distance)

    notes_shape = jax.ShapeDtypeStruct((count, SUBLANES, 128), jnp.float32)
    turned, tops, sums, acc, notes = pl.pallas_call(
        functools.partial(local_kernel, coef, rows),
        in_specs=[scalars] + [anywhere] * 3,
        out_specs=[whole] * 5,
        out_shape=[turned_shape, sum_shape, sum_shape, acc_shape, notes_shape],
        scratch_shapes=[
            pltpu.VMEM(key_rows.shape, key_rows.dtype),
            pltpu.VMEM((2, width, block_len), key_rows.dtype),
            pltpu.VMEM((2, all_rows, width), query_rows.dtype),
            pltpu.VMEM(key_rows.shape, key_rows.dtype),
            pltpu.SemaphoreType.DMA((2 + heads,)),
        ],
        cost_estimate=cost(3, 6_000_000),
        compiler_params=params,
        name="local_part",
    )(sb_here, *in_hbm[:3])
    half_buffers = [
        pltpu.VMEM(half_shape.shape, half_shape.dtype),
        pltpu.VMEM(half_shape.shape, half_shape.dtype),
        pltpu.VMEM((2, width, block_len // 2), half_shape.dtype),
    ]

    def near_half(distance):
        return distance, arrived[distance], beside[distance]

    def far_half(distance):
        return distance, across[distance], beside_across[distance]

    def attended_with(sums, acc, visits):
        return pl.pallas_call(
            functools.partial(middle_kernel, coef, [visit[0] for visit in visits]),
            in_specs=[whole] * (4 + 2 * len(visits)),
            out_specs=[whole] * 2,
            out_shape=[sum_shape, acc_shape],
            scratch_shapes=half_buffers * len(visits),
            input_output_aliases={2: 0, 3: 1},
            cost_estimate=cost(len(visits), 4_000_000),
            compiler_params=params,
            name="visits_of_" + "_".join(str(visit[0]) for visit in visits),
        )(notes, turned, sums, acc, *(part for visit in visits for part in visit[1:]))

    def relay(distance):
        if distance in distances and distance not in arrived:
            near = distance & -distance
            arrived[distance] = along_seq(arrived[distance ^ near], near)

    def spread(distance):
        if distance in distances:
            across[distance] = along_head(arrived[distance])
            beside[distance] = along_inner(arrived[distance])

    def settle(distance):
        nonlocal acc
        across[distance], acc = lax.optimization_barrier((across[distance], acc))
        beside_across[distance] = along_inner(across[distance])

    last = distances[-1]
    for distance in sorted(arrived, reverse=True):
        arrived[distance], acc = lax.optimization_barrier((arrived[distance], acc))
    waiting = distances[:2]
    for distance in waiting:
        beside[distance] = along_inner(arrived[distance])
    across[1] = along_head(arrived[1])
    relay(3)
    across[2] = along_head(arrived[2])
    sums, acc = attended_with(sums, acc, [near_half(d) for d in waiting])
    for ahead in distances[2:]:
        relay(ahead)
        settle(ahead - 2)
        arrived[ahead], acc = lax.optimization_barrier((arrived[ahead], acc))
        spread(ahead)
        across[ahead - 1], acc = lax.optimization_barrier((across[ahead - 1], acc))
        sums, acc = attended_with(sums, acc, [far_half(ahead - 2), near_half(ahead)])
    across[last], acc = lax.optimization_barrier((across[last], acc))
    for distance in distances[-2:]:
        beside_across[distance] = along_inner(across[distance])
    sums, acc = attended_with(sums, acc, [far_half(last - 1)])
    final = [last]

    flat = [part[d] for d in distances for part in (arrived, beside, across, beside_across)]
    attended, log_total = pl.pallas_call(
        functools.partial(last_kernel, coef, distances, final),
        in_specs=[anywhere] + [whole] * (5 + 2 * len(final)) + [anywhere] * (3 + len(flat)),
        out_specs=[anywhere, anywhere],
        out_shape=[jax.ShapeDtypeStruct(query_rows.shape, query_rows.dtype), top_shape],
        scratch_shapes=[
            pltpu.VMEM(query_rows.shape, query_rows.dtype),
            pltpu.VMEM(top_shape.shape, jnp.float32),
        ]
        + half_buffers * len(final)
        + [
            pltpu.VMEM((2, all_rows), jnp.float32),
            pltpu.VMEM((2 * block_len, width), key_rows.dtype),
            pltpu.VMEM((2 * block_len, width), key_rows.dtype),
            pltpu.VMEM((2, heads, rows, width), jnp.float32),
            pltpu.VMEM((2, heads, rows, 2 * width), jnp.float32),
            pltpu.SMEM(slot_block.shape, slot_block.dtype),
            pltpu.SemaphoreType.DMA,
            pltpu.SemaphoreType.DMA((3,)),
        ],
        cost_estimate=cost(1, 7_000_000),
        compiler_params=params,
        name="last_visitor",
    )(sb_here, notes, turned, tops, sums, acc, *(part for d in final for part in far_half(d)[1:]), in_hbm[1], in_hbm[2], in_hbm[0], *flat)
    return attended, log_total


def solution(mesh):
    placed = (
        P(("groups", "seq"), "inner", "head"),
        P(("groups", "seq"), None, None),
        P(("groups", "seq"), None, None),
        P(),
    )
    return jax.shard_map(
        body,
        mesh=mesh,
        in_specs=placed,
        out_specs=(P(("groups", "seq"), "inner", "head"), P(("groups", "seq"), "head", "inner")),
        check_vma=False,
    )
```

```python
import functools
import math

import jax
import jax.numpy as jnp
from jax import lax
from jax.experimental import pallas as pl
from jax.experimental.pallas import tpu as pltpu
from jax.sharding import PartitionSpec as P

NEG = -1e30
SUM_LIMIT = 1e36
LO, HI = 0, 1
TILE = 256
SUBLANES = 8


def score_dot(q, k):
    return lax.dot_general(q, k, (((1,), (1,)), ((), ())), preferred_element_type=jnp.float32)


def value_dot(p, v):
    return jnp.dot(p, v, preferred_element_type=jnp.float32)


def widen(x, width):
    return jnp.concatenate([x] * (width // x.shape[1]), axis=1)


def is_power(count):
    return count & (count - 1) == 0


def source_of(index, distance, count):
    if is_power(count):
        return index ^ distance
    return lax.rem(index - distance + count, count)


def blocks_of(sb, seq_index):
    b0, b1 = sb[2 * seq_index], sb[2 * seq_index + 1]
    return jnp.where(b1 > b0, 1, 0), jnp.minimum(b0, b1), jnp.maximum(b0, b1)


def key_tiles(count):
    return [(start, min(TILE, count - start)) for start in range(0, count, TILE)]


def piece_kernel(k_hbm, v_hbm, sb_hbm, piece, sb_out, sems):
    half = piece.shape[1]
    inner = lax.axis_index("inner")
    mine = pl.ds(pl.multiple_of(lax.rem(lax.axis_index("head"), 2) * half, half), half)
    sb_copy = pltpu.make_async_copy(sb_hbm, sb_out, sems.at[1])
    for value, src in enumerate((k_hbm, v_hbm)):

        @pl.when(inner == value)
        def _():
            pltpu.make_async_copy(src.at[:, mine], piece, sems.at[0]).start()

    sb_copy.start()
    pltpu.make_async_copy(k_hbm.at[:, mine], piece, sems.at[0]).wait()
    sb_copy.wait()


def weights_of(coef, s):
    p = jnp.exp2(s * coef)
    return p.astype(jnp.bfloat16), folded(jnp.add, p)


def with_ones(x):
    return jnp.concatenate([x, jnp.ones_like(x)], axis=1)


def minus_rows(top, height):
    high = top.astype(jnp.bfloat16).astype(jnp.float32)
    middle = (top - high).astype(jnp.bfloat16).astype(jnp.float32)
    low = top - high - middle
    row = lax.broadcasted_iota(jnp.int32, top.shape, 0)
    picked = jnp.where(row == 0, high, jnp.where(row == 1, middle, jnp.where(row == 2, low, 0.0)))
    zeros = jnp.zeros((height - top.shape[0], top.shape[1]), jnp.float32)
    return jnp.concatenate([-picked, zeros], axis=0).astype(jnp.bfloat16)


def down(x, height):
    return jnp.concatenate([x] * (height // x.shape[0]), axis=0)


def folded(combine, x):
    return functools.reduce(combine, [x[at : at + SUBLANES] for at in range(0, x.shape[0], SUBLANES)])


def with_sums(p, sums, v):
    return jnp.concatenate([value_dot(p, v), sums], axis=1)


def in_turn(chunks, score, finish):
    ready = score(*chunks[0])
    for place, chunk in enumerate(chunks):
        now = ready
        if place + 1 < len(chunks):
            ready = score(*chunks[place + 1])
        finish(now, *chunk)


def local_kernel(coef, rows, sb, q_hbm, k_hbm, v_hbm, turned_q, top_ref, sum_ref, acc_ref, notes, k_ref, turned_v, q_ref, v_ref, sems):
    _, all_rows, width = q_ref.shape
    copies = []
    for h in range(all_rows // rows):
        source, target = q_hbm.at[:, :, pl.ds(h * width, width)], q_ref.at[:, pl.ds(h * rows, rows)]
        copies.append(pltpu.make_async_copy(source, target, sems.at[2 + h]))
    copies.append(pltpu.make_async_copy(k_hbm, k_ref, sems.at[0]))
    copies.append(pltpu.make_async_copy(v_hbm, v_ref, sems.at[1]))
    for copy in copies:
        copy.start()
    for copy in copies:
        copy.wait()
    block_len = k_ref.shape[1]
    hi, _, _ = blocks_of(sb, lax.axis_index("seq"))
    slots = {HI: hi, LO: 1 - hi}
    tiles = key_tiles(block_len)
    me, count = lax.axis_index("seq"), lax.axis_size("seq")
    notes[0] = jnp.full(notes.shape[1:], hi, jnp.int32).astype(jnp.float32)
    for distance in range(1, count):
        notes[distance] = jnp.full(notes.shape[1:], visit_code(sb, me, distance, count), jnp.int32).astype(jnp.float32)
    for order in (HI, LO):
        turned_q[order, pl.ds(0, width)] = jnp.transpose(q_ref[slots[order]])
        turned_v[order] = jnp.transpose(v_ref[slots[order]])

    def keys(order, start, size):
        return k_ref[slots[order], pl.ds(start, size)]

    def values(order, start, size):
        return turned_v[order, :, start : start + size]

    def masked(order, start, size):
        lane = lax.broadcasted_iota(jnp.int32, (SUBLANES, all_rows), 1)
        heads_below = sum((lane >= at).astype(jnp.int32) for at in range(rows, all_rows, rows))
        row = lane - heads_below * rows + lax.axis_index("inner") * rows
        key = lax.broadcasted_iota(jnp.int32, (size, all_rows), 0) + start
        s = value_dot(keys(order, start, size), turned_q[order, pl.ds(0, width)])
        return jnp.where(key <= down(row, size), s, NEG)

    def highest(scores):
        top = functools.reduce(jnp.maximum, [folded(jnp.maximum, s) for s in scores])
        return jnp.broadcast_to(jnp.max(top, axis=0, keepdims=True), top.shape)

    def settle(order, scores, top):
        total, sums = None, None
        for (start, size), s in zip(tiles, scores):
            p, more = weights_of(coef, s - down(top, size))
            part = value_dot(values(order, start, size), p)
            total, sums = (part, more) if total is None else (total + part, sums + more)
        acc_ref[order] = total
        sum_ref[order] = sums

    def extend(order, scores):
        top = highest(scores)
        top_ref[order] = top
        turned_q[order, pl.ds(width, width)] = minus_rows(top, width)
        return top

    diag = [masked(HI, *tile) for tile in tiles]
    top = extend(HI, diag)
    low = [masked(LO, *tile) for tile in tiles]
    settle(HI, diag, top)
    low_top = extend(LO, low)

    def score(start, size):
        return value_dot(with_ones(keys(LO, start, size)), turned_q[HI])

    def finish(s, start, size):
        p, sums = weights_of(coef, s)
        acc_ref[HI] += value_dot(values(LO, start, size), p)
        sum_ref[HI] += sums

    settle(LO, low, low_top)
    in_turn(tiles, score, finish)


def visit_code(sb, me, distance, count):
    _, _, top_block = blocks_of(sb, me)
    other_hi, _, other_top = blocks_of(sb, source_of(me, distance, count))
    above = top_block > other_top
    other_lo = 1 - other_hi
    return other_lo + 2 * jnp.where(above, other_hi, other_lo) + 4 * jnp.where(above, HI, LO)


def noted(notes, place):
    return jnp.max(notes[place]).astype(jnp.int32)


def visit_chunks(distance, own, twin, notes, k_buf, v_buf, turned):
    code = noted(notes, distance)
    inner = lax.axis_index("inner")
    for value, (own_buf, twin_buf) in enumerate([(k_buf, v_buf), (v_buf, k_buf)]):

        @pl.when(inner == value)
        def _():
            own_buf[...] = own[...]
            twin_buf[...] = twin[...]

    for slot in range(2):
        turned[slot] = jnp.transpose(v_buf[slot])
    return (HI, code & 1), (code >> 2, (code >> 1) & 1)


def attend(coef, visits, notes, turned_q, sum_ref, acc_ref, buffers, done=None):
    chunks, ends = [], []
    laid_out = [visit_chunks(*visit, notes, *buffers[3 * i : 3 * i + 3]) for i, visit in enumerate(visits)]
    for place, pairs in enumerate(laid_out):
        k_buf, _, turned = buffers[3 * place : 3 * place + 3]
        tiles = [(0, k_buf.shape[1])]
        for order, slot in pairs:
            for tile in tiles:
                chunks.append((len(ends), order, slot, k_buf, turned, *tile))
            ends.append(tiles[-1][0])
    totals = {}

    def score(place, order, slot, k_buf, turned, start, size):
        return value_dot(with_ones(k_buf[slot, pl.ds(start, size)]), turned_q[order])

    def finish(s, place, order, slot, k_buf, turned, start, size):
        p, sums = weights_of(coef, s)
        part = value_dot(turned[slot, :, pl.ds(start, size)], p)
        if start:
            part, sums = totals[place][0] + part, totals[place][1] + sums
        totals[place] = part, sums
        if start == ends[place]:
            acc_ref[order] += part
            sum_ref[order] += sums
            if done is not None:
                done(place - len(ends), laid_out[-1][1][0])

    in_turn(chunks, score, finish)


def first_row(x):
    return jnp.transpose(x)[:1]


def middle_kernel(coef, distances, notes, turned_q, sum_in, acc_in, *refs):
    count = len(distances)
    visits = [(d, refs[2 * i], refs[2 * i + 1]) for i, d in enumerate(distances)]
    sum_ref, acc_ref, *buffers = refs[2 * count :]
    attend(coef, visits, notes, turned_q, sum_ref, acc_ref, buffers)


def last_kernel(coef, distances, final, sb_ref, notes, turned_q, top_ref, sum_ref, acc_ref, *refs):
    visits = [(d, refs[2 * i], refs[2 * i + 1]) for i, d in enumerate(final)]
    refs = refs[2 * len(final) :]
    every, rest = refs[: 4 * len(distances) + 3], refs[4 * len(distances) + 3 :]
    out_hbm, lse_hbm, out_buf, lse_ref, *buffers, worst, k_buf, v_buf, run_top, run_acc, sb, sem, out_sems = rest
    _, rows, feats = out_buf.shape
    width = k_buf.shape[1]
    block_len, heads = k_buf.shape[0] // 2, feats // width
    half_len = block_len // 2
    count = lax.axis_size("seq")
    me = lax.axis_index("seq")
    own_half = lax.rem(lax.axis_index("head"), 2)
    inner = lax.axis_index("inner")
    hi = noted(notes, 0)
    lse_copy = pltpu.make_async_copy(lse_ref, lse_hbm, sem)

    def out_copy(slot):
        return pltpu.make_async_copy(out_buf.at[slot], out_hbm.at[slot], out_sems.at[slot])

    def emit(order, h, value, top):
        slot = hi if order == HI else 1 - hi
        sums = jnp.broadcast_to(jnp.sum(value[:, width:], axis=1, keepdims=True), (rows, width))
        out_buf[slot, :, h * width : (h + 1) * width] = (value[:, :width] / sums).astype(out_buf.dtype)
        lse_ref[slot, h : h + 1, :] = first_row(top * (coef * math.log(2.0)) + jnp.log(sums))

    def done(place, last_order):
        if place < -2:
            return
        order = 1 - last_order if place == -2 else last_order
        slot = jnp.where(order == HI, hi, 1 - hi)
        sums = jnp.sum(sum_ref[order], axis=0, keepdims=True)
        log_total = top_ref[order][:1] * (coef * math.log(2.0)) + jnp.log(sums)
        settled = jnp.transpose((acc_ref[order] * (1.0 / sums)).astype(out_buf.dtype))
        for h in range(heads):
            mine = slice(h * rows, (h + 1) * rows)
            lse_ref[slot, h : h + 1, :] = log_total[:, mine]
            out_buf[slot, :, h * width : (h + 1) * width] = settled[mine]
        worst[place + 2 : place + 3] = sums
        out_copy(slot).start()

    attend(coef, visits, notes, turned_q, sum_ref, acc_ref, buffers, done)
    fits = jnp.max(worst[...]) < SUM_LIMIT
    lse_copy.start()
    for slot in range(2):
        out_copy(slot).wait()
    lse_copy.wait()

    @pl.when(jnp.logical_not(fits))
    def _():
        def fetch(src, dst):
            copy = pltpu.make_async_copy(src, dst, sem)
            copy.start()
            copy.wait()

        fetch(sb_ref, sb)
        _, lo_block, hi_block = blocks_of(sb, me)

        def online(source):
            @pl.loop(0, 4 * heads)
            def _(i):
                h, slot, order = i // 4, lax.rem(i, 4) // 2, lax.rem(i, 2)
                own_block = jnp.where(order == HI, hi_block, lo_block)
                shift = (own_block - sb[2 * source + slot]) * block_len + inner * rows

                @pl.when(shift + rows > 0)
                def _():
                    own_slot = jnp.where(order == HI, hi, 1 - hi)
                    queries = out_buf[own_slot, :, pl.ds(pl.multiple_of(h * width, width), width)]
                    at = pl.ds(pl.multiple_of(slot * block_len, block_len), block_len)
                    s = score_dot(queries, k_buf[at])
                    row = lax.broadcasted_iota(jnp.int32, s.shape, 0) + shift
                    allowed = lax.broadcasted_iota(jnp.int32, s.shape, 1) <= row
                    s = jnp.where(allowed, s, NEG)
                    before = run_top[order, h]
                    top = jnp.maximum(before, jnp.broadcast_to(jnp.max(s, axis=1, keepdims=True), before.shape))
                    p = jnp.where(allowed, jnp.exp2((s - widen(top, block_len)) * coef), 0.0)
                    run_top[order, h] = top
                    shrink = widen(jnp.exp2((before - top) * coef), 2 * width)
                    lanes = functools.reduce(jnp.add, [p[:, x : x + width] for x in range(0, block_len, width)])
                    fresh = with_sums(p.astype(jnp.bfloat16), lanes, v_buf[at])
                    run_acc[order, h] = run_acc[order, h] * shrink + fresh

        run_top[...] = jnp.full_like(run_top, NEG)
        run_acc[...] = jnp.zeros_like(run_acc)
        def rows_of(slot, half):
            return pl.ds(pl.multiple_of((slot * 2 + half) * half_len, half_len), half_len)

        fetch(every[2], out_buf)
        for slot in range(2):
            fetch(every[0].at[slot], k_buf.at[pl.ds(slot * block_len, block_len)])
            fetch(every[1].at[slot], v_buf.at[pl.ds(slot * block_len, block_len)])
        online(me)
        for place, other in enumerate(distances):
            others = every[3 + 4 * place : 7 + 4 * place]
            for value, (own_buf, twin_buf) in enumerate([(k_buf, v_buf), (v_buf, k_buf)]):

                @pl.when(inner == value)
                def _():
                    for turn in range(2):
                        half = own_half if turn == 0 else 1 - own_half
                        for slot in range(2):
                            fetch(others[2 * turn].at[slot], own_buf.at[rows_of(slot, half)])
                            fetch(others[2 * turn + 1].at[slot], twin_buf.at[rows_of(slot, half)])

            online(source_of(me, other, count))
        for h in range(heads):
            for order in (LO, HI):
                emit(order, h, run_acc[order, h], run_top[order, h])
        for copy in (lse_copy, out_copy(0), out_copy(1)):
            copy.start()
        for copy in (lse_copy, out_copy(0), out_copy(1)):
            copy.wait()


def body(query_rows, key_rows, value_rows, slot_block):
    _, block_len, width = key_rows.shape
    _, rows, feats = query_rows.shape
    heads = feats // width
    all_rows = heads * rows
    count = lax.axis_size("seq")
    coef = math.log2(math.e) / math.sqrt(width)
    distances = list(range(1, count))

    def along_seq(block, distance):
        if is_power(count):
            route = [(i, i ^ distance) for i in range(count)]
        else:
            route = [(i, (i + distance) % count) for i in range(count)]
        with jax.named_scope("along_seq"):
            return lax.ppermute(block, "seq", route)

    def along_head(block):
        with jax.named_scope("along_head"):
            return lax.ppermute(block, "head", [(i, i ^ 1) for i in range(lax.axis_size("head"))])

    def along_inner(block):
        with jax.named_scope("along_inner"):
            return lax.ppermute(block, "inner", [(0, 1), (1, 0)])

    whole = pl.BlockSpec(memory_space=pltpu.VMEM)
    anywhere = pl.BlockSpec(memory_space=pl.ANY)
    scalars = pl.BlockSpec(memory_space=pltpu.SMEM)
    acc_shape = jax.ShapeDtypeStruct((2, width, all_rows), jnp.float32)
    sum_shape = jax.ShapeDtypeStruct((2, SUBLANES, all_rows), jnp.float32)
    turned_shape = jax.ShapeDtypeStruct((2, 2 * width, all_rows), query_rows.dtype)
    top_shape = jax.ShapeDtypeStruct((2, heads, rows), jnp.float32)
    params = pltpu.CompilerParams(vmem_limit_bytes=40 * 1024 * 1024)
    unit = rows * heads * block_len * width * 4
    exps = rows * heads * block_len

    def cost(units, size):
        return pl.CostEstimate(flops=int(2 * units * unit), bytes_accessed=size, transcendentals=int(units * exps))

    in_hbm = [
        pltpu.with_memory_space_constraint(x, pltpu.HBM) for x in (query_rows, key_rows, value_rows, slot_block)
    ]
    half_shape = jax.ShapeDtypeStruct((2, block_len // 2, width), key_rows.dtype)
    piece, sb_here = pl.pallas_call(
        piece_kernel,
        in_specs=[anywhere] * 3,
        out_specs=[whole] * 2,
        out_shape=[half_shape, jax.ShapeDtypeStruct(slot_block.shape, slot_block.dtype)],
        scratch_shapes=[pltpu.SemaphoreType.DMA((2,))],
        cost_estimate=pl.CostEstimate(flops=0, bytes_accessed=400_000, transcendentals=0),
        compiler_params=params,
        name="pick_piece",
    )(*in_hbm[1:])
    arrived, across, beside, beside_across = {}, {}, {}, {}
    for distance in reversed(distances):
        if not is_power(count) or is_power(distance):
            arrived[distance] = along_seq(piece, distance)

    notes_shape = jax.ShapeDtypeStruct((count, SUBLANES, 128), jnp.float32)
    turned, tops, sums, acc, notes = pl.pallas_call(
        functools.partial(local_kernel, coef, rows),
        in_specs=[scalars] + [anywhere] * 3,
        out_specs=[whole] * 5,
        out_shape=[turned_shape, sum_shape, sum_shape, acc_shape, notes_shape],
        scratch_shapes=[
            pltpu.VMEM(key_rows.shape, key_rows.dtype),
            pltpu.VMEM((2, width, block_len), key_rows.dtype),
            pltpu.VMEM((2, all_rows, width), query_rows.dtype),
            pltpu.VMEM(key_rows.shape, key_rows.dtype),
            pltpu.SemaphoreType.DMA((2 + heads,)),
        ],
        cost_estimate=cost(3, 6_000_000),
        compiler_params=params,
        name="local_part",
    )(sb_here, *in_hbm[:3])
    half_buffers = [
        pltpu.VMEM(half_shape.shape, half_shape.dtype),
        pltpu.VMEM(half_shape.shape, half_shape.dtype),
        pltpu.VMEM((2, width, block_len // 2), half_shape.dtype),
    ]

    def near_half(distance):
        return distance, arrived[distance], beside[distance]

    def far_half(distance):
        return distance, across[distance], beside_across[distance]

    def attended_with(sums, acc, visits):
        return pl.pallas_call(
            functools.partial(middle_kernel, coef, [visit[0] for visit in visits]),
            in_specs=[whole] * (4 + 2 * len(visits)),
            out_specs=[whole] * 2,
            out_shape=[sum_shape, acc_shape],
            scratch_shapes=half_buffers * len(visits),
            input_output_aliases={2: 0, 3: 1},
            cost_estimate=cost(len(visits), 4_000_000),
            compiler_params=params,
            name="visits_of_" + "_".join(str(visit[0]) for visit in visits),
        )(notes, turned, sums, acc, *(part for visit in visits for part in visit[1:]))

    def relay(distance):
        if distance in distances and distance not in arrived:
            near = distance & -distance
            arrived[distance] = along_seq(arrived[distance ^ near], near)

    def spread(distance):
        if distance in distances:
            across[distance] = along_head(arrived[distance])
            beside[distance] = along_inner(arrived[distance])

    def settle(distance):
        nonlocal acc
        across[distance], acc = lax.optimization_barrier((across[distance], acc))
        beside_across[distance] = along_inner(across[distance])

    last = distances[-1]
    for distance in sorted(arrived, reverse=True):
        arrived[distance], acc = lax.optimization_barrier((arrived[distance], acc))
    waiting = distances[:2]
    for distance in waiting:
        beside[distance] = along_inner(arrived[distance])
    across[1] = along_head(arrived[1])
    relay(3)
    across[2] = along_head(arrived[2])
    sums, acc = attended_with(sums, acc, [near_half(d) for d in waiting])
    for ahead in distances[2:]:
        relay(ahead)
        settle(ahead - 2)
        arrived[ahead], acc = lax.optimization_barrier((arrived[ahead], acc))
        spread(ahead)
        across[ahead - 1], acc = lax.optimization_barrier((across[ahead - 1], acc))
        sums, acc = attended_with(sums, acc, [far_half(ahead - 2), near_half(ahead)])
    across[last], acc = lax.optimization_barrier((across[last], acc))
    for distance in distances[-2:]:
        beside_across[distance] = along_inner(across[distance])
    sums, acc = attended_with(sums, acc, [far_half(last - 1)])
    final = [last]

    flat = [part[d] for d in distances for part in (arrived, beside, across, beside_across)]
    attended, log_total = pl.pallas_call(
        functools.partial(last_kernel, coef, distances, final),
        in_specs=[anywhere] + [whole] * (5 + 2 * len(final)) + [anywhere] * (3 + len(flat)),
        out_specs=[anywhere, anywhere],
        out_shape=[jax.ShapeDtypeStruct(query_rows.shape, query_rows.dtype), top_shape],
        scratch_shapes=[
            pltpu.VMEM(query_rows.shape, query_rows.dtype),
            pltpu.VMEM(top_shape.shape, jnp.float32),
        ]
        + half_buffers * len(final)
        + [
            pltpu.VMEM((2, all_rows), jnp.float32),
            pltpu.VMEM((2 * block_len, width), key_rows.dtype),
            pltpu.VMEM((2 * block_len, width), key_rows.dtype),
            pltpu.VMEM((2, heads, rows, width), jnp.float32),
            pltpu.VMEM((2, heads, rows, 2 * width), jnp.float32),
            pltpu.SMEM(slot_block.shape, slot_block.dtype),
            pltpu.SemaphoreType.DMA,
            pltpu.SemaphoreType.DMA((2,)),
        ],
        cost_estimate=cost(1, 7_000_000),
        compiler_params=params,
        name="last_visitor",
    )(sb_here, notes, turned, tops, sums, acc, *(part for d in final for part in far_half(d)[1:]), in_hbm[1], in_hbm[2], in_hbm[0], *flat)
    return attended, log_total


def solution(mesh):
    placed = (
        P(("groups", "seq"), "inner", "head"),
        P(("groups", "seq"), None, None),
        P(("groups", "seq"), None, None),
        P(),
    )
    return jax.shard_map(
        body,
        mesh=mesh,
        in_specs=placed,
        out_specs=(P(("groups", "seq"), "inner", "head"), P(("groups", "seq"), "head", "inner")),
        check_vma=False,
    )
```

```python
import functools
import math

import jax
import jax.numpy as jnp
from jax import lax
from jax.experimental import pallas as pl
from jax.experimental.pallas import tpu as pltpu
from jax.sharding import PartitionSpec as P

NEG = -1e30
SUM_LIMIT = 1e36
LO, HI = 0, 1
TILE = 256
SUBLANES = 8


def score_dot(q, k):
    return lax.dot_general(q, k, (((1,), (1,)), ((), ())), preferred_element_type=jnp.float32)


def value_dot(p, v):
    return jnp.dot(p, v, preferred_element_type=jnp.float32)


def widen(x, width):
    return jnp.concatenate([x] * (width // x.shape[1]), axis=1)


def is_power(count):
    return count & (count - 1) == 0


def source_of(index, distance, count):
    if is_power(count):
        return index ^ distance
    return lax.rem(index - distance + count, count)


def blocks_of(sb, seq_index):
    b0, b1 = sb[2 * seq_index], sb[2 * seq_index + 1]
    return jnp.where(b1 > b0, 1, 0), jnp.minimum(b0, b1), jnp.maximum(b0, b1)


def key_tiles(count):
    return [(start, min(TILE, count - start)) for start in range(0, count, TILE)]


def piece_kernel(k_hbm, v_hbm, sb_hbm, piece, sb_out, sems):
    half = piece.shape[1]
    inner = lax.axis_index("inner")
    mine = pl.ds(pl.multiple_of(lax.rem(lax.axis_index("head"), 2) * half, half), half)
    sb_copy = pltpu.make_async_copy(sb_hbm, sb_out, sems.at[1])
    for value, src in enumerate((k_hbm, v_hbm)):

        @pl.when(inner == value)
        def _():
            pltpu.make_async_copy(src.at[:, mine], piece, sems.at[0]).start()

    sb_copy.start()
    pltpu.make_async_copy(k_hbm.at[:, mine], piece, sems.at[0]).wait()
    sb_copy.wait()


def weights_of(coef, s):
    p = jnp.exp2(s * coef)
    return p.astype(jnp.bfloat16), folded(jnp.add, p)


def with_ones(x):
    return jnp.concatenate([x, jnp.ones_like(x)], axis=1)


def minus_rows(top, height):
    high = top.astype(jnp.bfloat16).astype(jnp.float32)
    middle = (top - high).astype(jnp.bfloat16).astype(jnp.float32)
    low = top - high - middle
    row = lax.broadcasted_iota(jnp.int32, top.shape, 0)
    picked = jnp.where(row == 0, high, jnp.where(row == 1, middle, jnp.where(row == 2, low, 0.0)))
    zeros = jnp.zeros((height - top.shape[0], top.shape[1]), jnp.float32)
    return jnp.concatenate([-picked, zeros], axis=0).astype(jnp.bfloat16)


def down(x, height):
    return jnp.concatenate([x] * (height // x.shape[0]), axis=0)


def folded(combine, x):
    return functools.reduce(combine, [x[at : at + SUBLANES] for at in range(0, x.shape[0], SUBLANES)])


def with_sums(p, sums, v):
    return jnp.concatenate([value_dot(p, v), sums], axis=1)


def in_turn(chunks, score, finish):
    ready = score(*chunks[0])
    for place, chunk in enumerate(chunks):
        now = ready
        if place + 1 < len(chunks):
            ready = score(*chunks[place + 1])
        finish(now, *chunk)


def local_kernel(coef, rows, sb, q_hbm, k_hbm, v_hbm, turned_q, top_ref, sum_ref, acc_ref, notes, k_ref, turned_v, q_ref, v_ref, sems):
    _, all_rows, width = q_ref.shape
    copies = []
    for h in range(all_rows // rows):
        source, target = q_hbm.at[:, :, pl.ds(h * width, width)], q_ref.at[:, pl.ds(h * rows, rows)]
        copies.append(pltpu.make_async_copy(source, target, sems.at[2 + h]))
    copies.append(pltpu.make_async_copy(k_hbm, k_ref, sems.at[0]))
    copies.append(pltpu.make_async_copy(v_hbm, v_ref, sems.at[1]))
    for copy in copies:
        copy.start()
    for copy in copies:
        copy.wait()
    block_len = k_ref.shape[1]
    hi, _, _ = blocks_of(sb, lax.axis_index("seq"))
    slots = {HI: hi, LO: 1 - hi}
    tiles = [(0, block_len)]
    me, count = lax.axis_index("seq"), lax.axis_size("seq")
    notes[0] = jnp.full(notes.shape[1:], hi, jnp.int32).astype(jnp.float32)
    for distance in range(1, count):
        notes[distance] = jnp.full(notes.shape[1:], visit_code(sb, me, distance, count), jnp.int32).astype(jnp.float32)
    for order in (HI, LO):
        turned_q[order, pl.ds(0, width)] = jnp.transpose(q_ref[slots[order]])
        turned_v[order] = jnp.transpose(v_ref[slots[order]])

    def keys(order, start, size):
        return k_ref[slots[order], pl.ds(start, size)]

    def values(order, start, size):
        return turned_v[order, :, start : start + size]

    def masked(order, start, size):
        lane = lax.broadcasted_iota(jnp.int32, (SUBLANES, all_rows), 1)
        heads_below = sum((lane >= at).astype(jnp.int32) for at in range(rows, all_rows, rows))
        row = lane - heads_below * rows + lax.axis_index("inner") * rows
        key = lax.broadcasted_iota(jnp.int32, (size, all_rows), 0) + start
        s = value_dot(keys(order, start, size), turned_q[order, pl.ds(0, width)])
        return jnp.where(key <= down(row, size), s, NEG)

    def highest(scores):
        top = functools.reduce(jnp.maximum, [folded(jnp.maximum, s) for s in scores])
        return jnp.broadcast_to(jnp.max(top, axis=0, keepdims=True), top.shape)

    def settle(order, scores, top):
        total, sums = None, None
        for (start, size), s in zip(tiles, scores):
            p, more = weights_of(coef, s - down(top, size))
            part = value_dot(values(order, start, size), p)
            total, sums = (part, more) if total is None else (total + part, sums + more)
        acc_ref[order] = total
        sum_ref[order] = sums

    def extend(order, scores):
        top = highest(scores)
        top_ref[order] = top
        turned_q[order, pl.ds(width, width)] = minus_rows(top, width)
        return top

    diag = [masked(HI, *tile) for tile in tiles]
    top = extend(HI, diag)
    low = [masked(LO, *tile) for tile in tiles]
    settle(HI, diag, top)
    low_top = extend(LO, low)

    def score(start, size):
        return value_dot(with_ones(keys(LO, start, size)), turned_q[HI])

    def finish(s, start, size):
        p, sums = weights_of(coef, s)
        acc_ref[HI] += value_dot(values(LO, start, size), p)
        sum_ref[HI] += sums

    settle(LO, low, low_top)
    in_turn(tiles, score, finish)


def visit_code(sb, me, distance, count):
    _, _, top_block = blocks_of(sb, me)
    other_hi, _, other_top = blocks_of(sb, source_of(me, distance, count))
    above = top_block > other_top
    other_lo = 1 - other_hi
    return other_lo + 2 * jnp.where(above, other_hi, other_lo) + 4 * jnp.where(above, HI, LO)


def noted(notes, place):
    return jnp.max(notes[place]).astype(jnp.int32)


def visit_chunks(distance, own, twin, notes, k_buf, v_buf, turned):
    code = noted(notes, distance)
    inner = lax.axis_index("inner")
    for value, (own_buf, twin_buf) in enumerate([(k_buf, v_buf), (v_buf, k_buf)]):

        @pl.when(inner == value)
        def _():
            own_buf[...] = own[...]
            twin_buf[...] = twin[...]

    for slot in range(2):
        turned[slot] = jnp.transpose(v_buf[slot])
    return (HI, code & 1), (code >> 2, (code >> 1) & 1)


def attend(coef, visits, notes, turned_q, sum_ref, acc_ref, buffers, done=None):
    chunks, ends = [], []
    laid_out = [visit_chunks(*visit, notes, *buffers[3 * i : 3 * i + 3]) for i, visit in enumerate(visits)]
    for place, pairs in enumerate(laid_out):
        k_buf, _, turned = buffers[3 * place : 3 * place + 3]
        tiles = [(0, k_buf.shape[1])]
        for order, slot in pairs:
            for tile in tiles:
                chunks.append((len(ends), order, slot, k_buf, turned, *tile))
            ends.append(tiles[-1][0])
    totals = {}

    def score(place, order, slot, k_buf, turned, start, size):
        return value_dot(with_ones(k_buf[slot, pl.ds(start, size)]), turned_q[order])

    def finish(s, place, order, slot, k_buf, turned, start, size):
        p, sums = weights_of(coef, s)
        part = value_dot(turned[slot, :, pl.ds(start, size)], p)
        if start:
            part, sums = totals[place][0] + part, totals[place][1] + sums
        totals[place] = part, sums
        if start == ends[place]:
            acc_ref[order] += part
            sum_ref[order] += sums
            if done is not None:
                done(place - len(ends), laid_out[-1][1][0])

    in_turn(chunks, score, finish)


def first_row(x):
    return jnp.transpose(x)[:1]


def middle_kernel(coef, distances, notes, turned_q, sum_in, acc_in, *refs):
    count = len(distances)
    visits = [(d, refs[2 * i], refs[2 * i + 1]) for i, d in enumerate(distances)]
    sum_ref, acc_ref, *buffers = refs[2 * count :]
    attend(coef, visits, notes, turned_q, sum_ref, acc_ref, buffers)


def last_kernel(coef, distances, final, sb_ref, notes, turned_q, top_ref, sum_ref, acc_ref, *refs):
    visits = [(d, refs[2 * i], refs[2 * i + 1]) for i, d in enumerate(final)]
    refs = refs[2 * len(final) :]
    every, rest = refs[: 4 * len(distances) + 3], refs[4 * len(distances) + 3 :]
    out_hbm, lse_hbm, out_buf, lse_ref, *buffers, worst, k_buf, v_buf, run_top, run_acc, sb, sem, out_sems = rest
    _, rows, feats = out_buf.shape
    width = k_buf.shape[1]
    block_len, heads = k_buf.shape[0] // 2, feats // width
    half_len = block_len // 2
    count = lax.axis_size("seq")
    me = lax.axis_index("seq")
    own_half = lax.rem(lax.axis_index("head"), 2)
    inner = lax.axis_index("inner")
    hi = noted(notes, 0)
    lse_copy = pltpu.make_async_copy(lse_ref, lse_hbm, sem)

    def out_copy(slot):
        return pltpu.make_async_copy(out_buf.at[slot], out_hbm.at[slot], out_sems.at[slot])

    def emit(order, h, value, top):
        slot = hi if order == HI else 1 - hi
        sums = jnp.broadcast_to(jnp.sum(value[:, width:], axis=1, keepdims=True), (rows, width))
        out_buf[slot, :, h * width : (h + 1) * width] = (value[:, :width] / sums).astype(out_buf.dtype)
        lse_ref[slot, h : h + 1, :] = first_row(top * (coef * math.log(2.0)) + jnp.log(sums))

    def done(place, last_order):
        if place < -2:
            return
        order = 1 - last_order if place == -2 else last_order
        slot = jnp.where(order == HI, hi, 1 - hi)
        sums = jnp.sum(sum_ref[order], axis=0, keepdims=True)
        log_total = top_ref[order][:1] * (coef * math.log(2.0)) + jnp.log(sums)
        settled = jnp.transpose((acc_ref[order] * (1.0 / sums)).astype(out_buf.dtype))
        for h in range(heads):
            mine = slice(h * rows, (h + 1) * rows)
            lse_ref[slot, h : h + 1, :] = log_total[:, mine]
            out_buf[slot, :, h * width : (h + 1) * width] = settled[mine]
        worst[place + 2 : place + 3] = sums
        out_copy(slot).start()

    attend(coef, visits, notes, turned_q, sum_ref, acc_ref, buffers, done)
    fits = jnp.max(worst[...]) < SUM_LIMIT
    lse_copy.start()
    for slot in range(2):
        out_copy(slot).wait()
    lse_copy.wait()

    @pl.when(jnp.logical_not(fits))
    def _():
        def fetch(src, dst):
            copy = pltpu.make_async_copy(src, dst, sem)
            copy.start()
            copy.wait()

        fetch(sb_ref, sb)
        _, lo_block, hi_block = blocks_of(sb, me)

        def online(source):
            @pl.loop(0, 4 * heads)
            def _(i):
                h, slot, order = i // 4, lax.rem(i, 4) // 2, lax.rem(i, 2)
                own_block = jnp.where(order == HI, hi_block, lo_block)
                shift = (own_block - sb[2 * source + slot]) * block_len + inner * rows

                @pl.when(shift + rows > 0)
                def _():
                    own_slot = jnp.where(order == HI, hi, 1 - hi)
                    queries = out_buf[own_slot, :, pl.ds(pl.multiple_of(h * width, width), width)]
                    at = pl.ds(pl.multiple_of(slot * block_len, block_len), block_len)
                    s = score_dot(queries, k_buf[at])
                    row = lax.broadcasted_iota(jnp.int32, s.shape, 0) + shift
                    allowed = lax.broadcasted_iota(jnp.int32, s.shape, 1) <= row
                    s = jnp.where(allowed, s, NEG)
                    before = run_top[order, h]
                    top = jnp.maximum(before, jnp.broadcast_to(jnp.max(s, axis=1, keepdims=True), before.shape))
                    p = jnp.where(allowed, jnp.exp2((s - widen(top, block_len)) * coef), 0.0)
                    run_top[order, h] = top
                    shrink = widen(jnp.exp2((before - top) * coef), 2 * width)
                    lanes = functools.reduce(jnp.add, [p[:, x : x + width] for x in range(0, block_len, width)])
                    fresh = with_sums(p.astype(jnp.bfloat16), lanes, v_buf[at])
                    run_acc[order, h] = run_acc[order, h] * shrink + fresh

        run_top[...] = jnp.full_like(run_top, NEG)
        run_acc[...] = jnp.zeros_like(run_acc)
        def rows_of(slot, half):
            return pl.ds(pl.multiple_of((slot * 2 + half) * half_len, half_len), half_len)

        fetch(every[2], out_buf)
        for slot in range(2):
            fetch(every[0].at[slot], k_buf.at[pl.ds(slot * block_len, block_len)])
            fetch(every[1].at[slot], v_buf.at[pl.ds(slot * block_len, block_len)])
        online(me)
        for place, other in enumerate(distances):
            others = every[3 + 4 * place : 7 + 4 * place]
            for value, (own_buf, twin_buf) in enumerate([(k_buf, v_buf), (v_buf, k_buf)]):

                @pl.when(inner == value)
                def _():
                    for turn in range(2):
                        half = own_half if turn == 0 else 1 - own_half
                        for slot in range(2):
                            fetch(others[2 * turn].at[slot], own_buf.at[rows_of(slot, half)])
                            fetch(others[2 * turn + 1].at[slot], twin_buf.at[rows_of(slot, half)])

            online(source_of(me, other, count))
        for h in range(heads):
            for order in (LO, HI):
                emit(order, h, run_acc[order, h], run_top[order, h])
        for copy in (lse_copy, out_copy(0), out_copy(1)):
            copy.start()
        for copy in (lse_copy, out_copy(0), out_copy(1)):
            copy.wait()


def body(query_rows, key_rows, value_rows, slot_block):
    _, block_len, width = key_rows.shape
    _, rows, feats = query_rows.shape
    heads = feats // width
    all_rows = heads * rows
    count = lax.axis_size("seq")
    coef = math.log2(math.e) / math.sqrt(width)
    distances = list(range(1, count))

    def along_seq(block, distance):
        if is_power(count):
            route = [(i, i ^ distance) for i in range(count)]
        else:
            route = [(i, (i + distance) % count) for i in range(count)]
        with jax.named_scope("along_seq"):
            return lax.ppermute(block, "seq", route)

    def along_head(block):
        with jax.named_scope("along_head"):
            return lax.ppermute(block, "head", [(i, i ^ 1) for i in range(lax.axis_size("head"))])

    def along_inner(block):
        with jax.named_scope("along_inner"):
            return lax.ppermute(block, "inner", [(0, 1), (1, 0)])

    whole = pl.BlockSpec(memory_space=pltpu.VMEM)
    anywhere = pl.BlockSpec(memory_space=pl.ANY)
    scalars = pl.BlockSpec(memory_space=pltpu.SMEM)
    acc_shape = jax.ShapeDtypeStruct((2, width, all_rows), jnp.float32)
    sum_shape = jax.ShapeDtypeStruct((2, SUBLANES, all_rows), jnp.float32)
    turned_shape = jax.ShapeDtypeStruct((2, 2 * width, all_rows), query_rows.dtype)
    top_shape = jax.ShapeDtypeStruct((2, heads, rows), jnp.float32)
    params = pltpu.CompilerParams(vmem_limit_bytes=40 * 1024 * 1024)
    unit = rows * heads * block_len * width * 4
    exps = rows * heads * block_len

    def cost(units, size):
        return pl.CostEstimate(flops=int(2 * units * unit), bytes_accessed=size, transcendentals=int(units * exps))

    in_hbm = [
        pltpu.with_memory_space_constraint(x, pltpu.HBM) for x in (query_rows, key_rows, value_rows, slot_block)
    ]
    half_shape = jax.ShapeDtypeStruct((2, block_len // 2, width), key_rows.dtype)
    piece, sb_here = pl.pallas_call(
        piece_kernel,
        in_specs=[anywhere] * 3,
        out_specs=[whole] * 2,
        out_shape=[half_shape, jax.ShapeDtypeStruct(slot_block.shape, slot_block.dtype)],
        scratch_shapes=[pltpu.SemaphoreType.DMA((2,))],
        cost_estimate=pl.CostEstimate(flops=0, bytes_accessed=400_000, transcendentals=0),
        compiler_params=params,
        name="pick_piece",
    )(*in_hbm[1:])
    arrived, across, beside, beside_across = {}, {}, {}, {}
    for distance in reversed(distances):
        if not is_power(count) or is_power(distance):
            arrived[distance] = along_seq(piece, distance)

    notes_shape = jax.ShapeDtypeStruct((count, SUBLANES, 128), jnp.float32)
    turned, tops, sums, acc, notes = pl.pallas_call(
        functools.partial(local_kernel, coef, rows),
        in_specs=[scalars] + [anywhere] * 3,
        out_specs=[whole] * 5,
        out_shape=[turned_shape, sum_shape, sum_shape, acc_shape, notes_shape],
        scratch_shapes=[
            pltpu.VMEM(key_rows.shape, key_rows.dtype),
            pltpu.VMEM((2, width, block_len), key_rows.dtype),
            pltpu.VMEM((2, all_rows, width), query_rows.dtype),
            pltpu.VMEM(key_rows.shape, key_rows.dtype),
            pltpu.SemaphoreType.DMA((2 + heads,)),
        ],
        cost_estimate=cost(3, 6_000_000),
        compiler_params=params,
        name="local_part",
    )(sb_here, *in_hbm[:3])
    half_buffers = [
        pltpu.VMEM(half_shape.shape, half_shape.dtype),
        pltpu.VMEM(half_shape.shape, half_shape.dtype),
        pltpu.VMEM((2, width, block_len // 2), half_shape.dtype),
    ]

    def near_half(distance):
        return distance, arrived[distance], beside[distance]

    def far_half(distance):
        return distance, across[distance], beside_across[distance]

    def attended_with(sums, acc, visits):
        return pl.pallas_call(
            functools.partial(middle_kernel, coef, [visit[0] for visit in visits]),
            in_specs=[whole] * (4 + 2 * len(visits)),
            out_specs=[whole] * 2,
            out_shape=[sum_shape, acc_shape],
            scratch_shapes=half_buffers * len(visits),
            input_output_aliases={2: 0, 3: 1},
            cost_estimate=cost(len(visits), 4_000_000),
            compiler_params=params,
            name="visits_of_" + "_".join(str(visit[0]) for visit in visits),
        )(notes, turned, sums, acc, *(part for visit in visits for part in visit[1:]))

    def relay(distance):
        if distance in distances and distance not in arrived:
            near = distance & -distance
            arrived[distance] = along_seq(arrived[distance ^ near], near)

    def spread(distance):
        if distance in distances:
            across[distance] = along_head(arrived[distance])
            beside[distance] = along_inner(arrived[distance])

    def settle(distance):
        nonlocal acc
        across[distance], acc = lax.optimization_barrier((across[distance], acc))
        beside_across[distance] = along_inner(across[distance])

    last = distances[-1]
    for distance in sorted(arrived, reverse=True):
        arrived[distance], acc = lax.optimization_barrier((arrived[distance], acc))
    waiting = distances[:2]
    for distance in waiting:
        beside[distance] = along_inner(arrived[distance])
    across[1] = along_head(arrived[1])
    relay(3)
    across[2] = along_head(arrived[2])
    sums, acc = attended_with(sums, acc, [near_half(d) for d in waiting])
    for ahead in distances[2:]:
        relay(ahead)
        settle(ahead - 2)
        arrived[ahead], acc = lax.optimization_barrier((arrived[ahead], acc))
        spread(ahead)
        across[ahead - 1], acc = lax.optimization_barrier((across[ahead - 1], acc))
        sums, acc = attended_with(sums, acc, [far_half(ahead - 2), near_half(ahead)])
    across[last], acc = lax.optimization_barrier((across[last], acc))
    for distance in distances[-2:]:
        beside_across[distance] = along_inner(across[distance])
    sums, acc = attended_with(sums, acc, [far_half(last - 1)])
    final = [last]

    flat = [part[d] for d in distances for part in (arrived, beside, across, beside_across)]
    attended, log_total = pl.pallas_call(
        functools.partial(last_kernel, coef, distances, final),
        in_specs=[anywhere] + [whole] * (5 + 2 * len(final)) + [anywhere] * (3 + len(flat)),
        out_specs=[anywhere, anywhere],
        out_shape=[jax.ShapeDtypeStruct(query_rows.shape, query_rows.dtype), top_shape],
        scratch_shapes=[
            pltpu.VMEM(query_rows.shape, query_rows.dtype),
            pltpu.VMEM(top_shape.shape, jnp.float32),
        ]
        + half_buffers * len(final)
        + [
            pltpu.VMEM((2, all_rows), jnp.float32),
            pltpu.VMEM((2 * block_len, width), key_rows.dtype),
            pltpu.VMEM((2 * block_len, width), key_rows.dtype),
            pltpu.VMEM((2, heads, rows, width), jnp.float32),
            pltpu.VMEM((2, heads, rows, 2 * width), jnp.float32),
            pltpu.SMEM(slot_block.shape, slot_block.dtype),
            pltpu.SemaphoreType.DMA,
            pltpu.SemaphoreType.DMA((2,)),
        ],
        cost_estimate=cost(1, 7_000_000),
        compiler_params=params,
        name="last_visitor",
    )(sb_here, notes, turned, tops, sums, acc, *(part for d in final for part in far_half(d)[1:]), in_hbm[1], in_hbm[2], in_hbm[0], *flat)
    return attended, log_total


def solution(mesh):
    placed = (
        P(("groups", "seq"), "inner", "head"),
        P(("groups", "seq"), None, None),
        P(("groups", "seq"), None, None),
        P(),
    )
    return jax.shard_map(
        body,
        mesh=mesh,
        in_specs=placed,
        out_specs=(P(("groups", "seq"), "inner", "head"), P(("groups", "seq"), "head", "inner")),
        check_vma=False,
    )
```
